32 devices in a mesh: img: 8 (over z, x), row: 4 (over y, core).
Axes of the slice: x: 2, y: 2, z: 4, core: 2. Of those that a mesh axis runs over, the one named last changes fastest.
Arguments:
- tokens: bfloat16 [16, 24, 24, 768], P('img', 'row'), may hold values from -6 to 6
- keep_mask: int32 [16, 24, 24], P('img', 'row'), may hold values from 0 to 1, as said below
- cotangent: bfloat16 [16, 24, 24, 768], P('img', 'row'), may hold values from -6 to 6
- qkv_weight: float32 [768, 2304], P('img', 'row'), may hold values from -0.21875 to 0.21875
- qkv_bias: float32 [2304], P(('img', 'row')), may hold values from -1.5 to 1.5
- proj_weight: float32 [768, 768], P('img', 'row'), may hold values from -1.75 to 1.75
- proj_bias: float32 [768], P(('img', 'row')), may hold values from -1.5 to 1.5
- attn_gain: float32 [768], P(('img', 'row')), may hold values from 0.1 to 1.9
- attn_shift: float32 [768], P(('img', 'row')), may hold values from -1.5 to 1.5
- mlp_gain: float32 [768], P(('img', 'row')), may hold values from 0.1 to 1.9
- mlp_shift: float32 [768], P(('img', 'row')), may hold values from -1.5 to 1.5
- up_weight: float32 [768, 3072], P('img', 'row'), may hold values from -0.21875 to 0.21875
- up_bias: float32 [3072], P(('img', 'row')), may hold values from -1.5 to 1.5
- down_weight: float32 [3072, 768], P('row', 'img'), may hold values from -0.109375 to 0.109375
- down_bias: float32 [768], P(('img', 'row')), may hold values from -1.5 to 1.5
- rope_freqs: float32 [768], P(('img', 'row')), may hold values from -1 to 1
Outputs:
- layer_out: bfloat16 [16, 24, 24, 768], P('img', 'row')
- tokens_grad: bfloat16 [16, 24, 24, 768], P('img', 'row')
- qkv_weight_grad: float32 [768, 2304], P('img', 'row')
- qkv_bias_grad: float32 [1536], P(('img', 'row'))
- value_bias_grad: float32 [768], P(('img', 'row'))
- proj_weight_grad: float32 [768, 768], P('img', 'row')
- proj_bias_grad: float32 [768], P(('img', 'row'))
- attn_gain_grad: float32 [768], P(('img', 'row'))
- attn_shift_grad: float32 [768], P(('img', 'row'))
- mlp_gain_grad: float32 [768], P(('img', 'row'))
- mlp_shift_grad: float32 [768], P(('img', 'row'))
- up_weight_grad: float32 [768, 3072], P('img', 'row')
- up_bias_grad: float32 [3072], P(('img', 'row'))
- down_weight_grad: float32 [3072, 768], P('row', 'img')
- down_bias_grad: float32 [768], P(('img', 'row'))
- rope_freqs_grad: float32 [768], P(('img', 'row'))
The draws below stay inside these ranges and needn't reach their ends.
Inputs may be any that keep to these rules, and one draw needn't show every extreme that they name: `keep_mask`: every image keeps all patches of one grid column drawn for it; each of its other patches is kept with one probability drawn per image from 1, 1/2, 1/4, 1/8, 1/16, 1/32.
All inputs are finite; a program needn't handle non-finite values.
Results may differ from the reference program's by a relative error of at most 0.018.
The reference program's roundings to bfloat16 on the way count: a program that leaves them out, or rounds other values in their place, can miss the bound.
Values may be sent and summed in bfloat16 or wider, within the bound.
No kernel may reach another device: no remote copies, remote signals or barrier semaphores. Data moves between devices by JAX's collectives and lax.ppermute only.
A program may use at most 192 MiB of HBM per device.

```python
import math
import jax
import jax.numpy as jnp
from jax import lax

D = 768
HEADS = 12
HEAD = 64
FF = 3072
GRID = 24
IMAGES = 16


def draw_keep_mask(key, part):
    key = jax.random.fold_in(key, 11)
    level_key, patch_key, column_key = jax.random.split(key, 3)
    levels = jax.random.randint(level_key, (IMAGES, 1, 1), 0, 6)
    chances = jax.random.randint(patch_key, (IMAGES, GRID, GRID), 0, 1024)
    threshold = jnp.right_shift(jnp.full((IMAGES, 1, 1), 1024, jnp.int32), levels)
    chosen = jax.random.randint(column_key, (IMAGES, 1, 1), 0, GRID)
    columns = jnp.arange(GRID, dtype=jnp.int32)[None, None, :]
    kept = jnp.logical_or(chances < threshold, columns == chosen)
    return kept.astype(jnp.int32)


def block_scale(key, extent, shards, low, top_value):
    factor_of = 1.0
    for dim, blocks in shards:
        draws = jax.random.uniform(jax.random.fold_in(jax.random.fold_in(key, 6), dim), (blocks,), jnp.float32, low / len(shards), top_value / len(shards))
        factor_of = factor_of * jnp.repeat(jnp.exp(draws), extent[dim] // blocks).reshape((-1,) + (1,) * (len(extent) - 1 - dim))
    return factor_of


def scatter_about(key, extent, width, limit, cuts=(), held_as=jnp.bfloat16):
    loudness = block_scale(key, extent, cuts, -0.22, 0.18) if cuts else 1.0
    drawn = jax.random.normal(key, extent, jnp.float32) * width * loudness
    return jnp.minimum(jnp.maximum(drawn, -limit), limit).astype(held_as)


def setup_inputs(seed: int = 0) -> dict:
    key_of = jax.random.split(jax.random.key(seed), 17)
    tokens = scatter_about(key_of[0], (IMAGES, GRID, GRID, D), 1.0, 6.0, ((0, 8), (1, 4)))
    keep_mask = draw_keep_mask(jax.random.fold_in(key_of[16], 71), 0)
    cotangent = scatter_about(key_of[2], (IMAGES, GRID, GRID, D), 1.0, 6.0, ((0, 8), (1, 4)))
    qkv_weight = scatter_about(key_of[3], (D, 3 * D), D ** -0.5, 0.21875, ((0, 8), (1, 4)), jnp.float32)
    qkv_bias = scatter_about(key_of[4], (3 * D,), 0.3, 1.5, ((0, 32),), jnp.float32)
    proj_weight = scatter_about(key_of[5], (D, D), (D // 64) ** -0.5, 1.75, ((0, 8), (1, 4)), jnp.float32)
    proj_bias = scatter_about(key_of[6], (D,), 0.3, 1.5, ((0, 32),), jnp.float32)
    attn_gain = jnp.clip(1.0 + 0.18 * jax.random.normal(key_of[7], (D,), jnp.float32), 0.1, 1.9)
    attn_shift = scatter_about(key_of[8], (D,), 0.3, 1.5, ((0, 32),), jnp.float32)
    mlp_gain = jnp.clip(1.0 + 0.18 * jax.random.normal(key_of[9], (D,), jnp.float32), 0.1, 1.9)
    mlp_shift = scatter_about(key_of[10], (D,), 0.3, 1.5, ((0, 32),), jnp.float32)
    up_weight = scatter_about(key_of[11], (D, FF), D ** -0.5, 0.21875, ((0, 8), (1, 4)), jnp.float32)
    up_bias = scatter_about(key_of[12], (FF,), 0.3, 1.5, ((0, 32),), jnp.float32)
    down_weight = scatter_about(key_of[13], (FF, D), FF ** -0.5, 0.109375, ((0, 4), (1, 8)), jnp.float32)
    down_bias = scatter_about(key_of[14], (D,), 0.3, 1.5, ((0, 32),), jnp.float32)
    rope_freqs = jnp.clip(jax.random.uniform(key_of[15], (D,), jnp.float32, -1.0, 1.0) * block_scale(key_of[15], (D,), ((0, 32),), -0.4, 0.0), -1.0, 1.0)
    return {"tokens": tokens, "keep_mask": keep_mask, "cotangent": cotangent, "qkv_weight": qkv_weight, "qkv_bias": qkv_bias, "proj_weight": proj_weight, "proj_bias": proj_bias, "attn_gain": attn_gain, "attn_shift": attn_shift, "mlp_gain": mlp_gain, "mlp_shift": mlp_shift, "up_weight": up_weight, "up_bias": up_bias, "down_weight": down_weight, "down_bias": down_bias, "rope_freqs": rope_freqs}


@jax.custom_vjp
def low(v):
    return lax.optimization_barrier(v.astype(jnp.bfloat16)).astype(jnp.float32)

@jax.custom_vjp
def low_back(v):
    return v

def low_keep(v):
    return (low(v), None)

def low_pass(kept, grad):
    return (grad,)

def back_keep(v):
    return (v, None)

def back_low(kept, grad):
    return (low(grad),)
low.defvjp(low_keep, low_pass)
low_back.defvjp(back_keep, back_low)

def layer_norm(values, gain_row, shift_row):
    center = values - lax.optimization_barrier(jnp.mean(values, -1, keepdims=True))
    inverse = lax.rsqrt(lax.optimization_barrier(jnp.mean(center * center, -1, keepdims=True)) + 1e-06)
    return center * inverse * gain_row + shift_row

def swap_halves(field, head_count):
    field_shape = field.shape
    halves = field.reshape(field_shape[:-1] + (head_count, 2, field_shape[-1] // (2 * head_count)))
    return jnp.flip(halves, -2).reshape(field_shape)

def project(field, matrix):
    return jnp.einsum('gsd,de->gse', field, matrix, precision=lax.Precision.HIGHEST)

def rope_tables(freqs):
    positions = jnp.arange(GRID * GRID, dtype=jnp.int32)
    col_pos = (positions % GRID).astype(jnp.float32)
    row_pos = (positions // GRID).astype(jnp.float32)
    freq_grid = freqs.reshape(2, HEADS, HEAD // 2)
    angles = col_pos[:, None, None] * freq_grid[0] + row_pos[:, None, None] * freq_grid[1]
    cosine = jnp.concatenate([jnp.cos(angles), jnp.cos(angles)], -1).reshape(GRID * GRID, D)
    sine = jnp.concatenate([-jnp.sin(angles), jnp.sin(angles)], -1).reshape(GRID * GRID, D)
    return (cosine, sine)

def one_group(weights, block_in, block_keep):
    qkv_weight, qkv_bias, proj_weight, proj_bias, attn_gain, attn_shift, mlp_gain, mlp_shift, up_weight, up_bias, down_weight, down_bias, rope_freqs = weights
    group_count = block_in.shape[0]
    seq_len = block_in.shape[1]
    cosine, sine = rope_tables(rope_freqs)
    acts_one = low(layer_norm(block_in, attn_gain, attn_shift))
    projected = low_back(project(acts_one, qkv_weight) + qkv_bias)
    queries = projected[..., :D]
    key_part = projected[..., D:2 * D]
    value_part = projected[..., 2 * D:]
    rot_query = low(queries * cosine + swap_halves(queries, HEADS) * sine).reshape(group_count, seq_len, HEADS, HEAD)
    rot_key = low(key_part * cosine + swap_halves(key_part, HEADS) * sine).reshape(group_count, seq_len, HEADS, HEAD)
    value_low = low(value_part).reshape(group_count, seq_len, HEADS, HEAD)
    scores = jnp.einsum('gshe,gnhe->ghsn', rot_query, rot_key, precision=lax.Precision.HIGHEST)
    scores = low_back(scores * (1.0 / math.sqrt(HEAD)))
    scores = jnp.where(block_keep[:, None, None, :] > 0, scores, -1e+30)
    soft_weights = jax.nn.softmax(scores, axis=-1)
    attended = jnp.einsum('ghsn,gnhe->gshe', low(soft_weights), value_low, precision=lax.Precision.HIGHEST)
    attended = attended.reshape(group_count, seq_len, D)
    residual_middle = block_in + low_back(project(low(low_back(attended)), proj_weight) + proj_bias)
    acts_two = low(layer_norm(residual_middle, mlp_gain, mlp_shift))
    hidden = low_back(project(acts_two, up_weight) + up_bias)
    branch = low_back(project(low(jax.nn.gelu(hidden, approximate=False)), down_weight) + down_bias)
    return block_keep[..., None] * (residual_middle + branch)

def reference(tokens, keep_mask, cotangent, qkv_weight, qkv_bias, proj_weight, proj_bias, attn_gain, attn_shift, mlp_gain, mlp_shift, up_weight, up_bias, down_weight, down_bias, rope_freqs):
    seq_len = GRID * GRID
    group_size = 8
    groups = IMAGES // group_size
    params = (qkv_weight, qkv_bias, proj_weight, proj_bias, attn_gain, attn_shift, mlp_gain, mlp_shift, up_weight, up_bias, down_weight, down_bias, rope_freqs)
    params_wide = tuple((member.astype(jnp.float32) for member in params))
    layer_inputs = tokens.reshape(IMAGES, seq_len, D).astype(jnp.float32)
    keeps = keep_mask.reshape(groups, group_size, seq_len).astype(jnp.float32)

    def forward(weights, field):
        rounded = tuple((low(member) for member in weights))
        checked = jax.checkpoint(one_group)

        def step(carry, block):
            return (carry, checked(rounded, block[0], block[1]))
        blocks_in = field.reshape(groups, group_size, seq_len, D)
        unused, outputs = lax.scan(step, jnp.zeros((), jnp.float32), (blocks_in, keeps))
        return outputs.reshape(IMAGES, seq_len, D)
    layer, pullback = jax.vjp(forward, params_wide, layer_inputs)
    weight_grads, input_grad = pullback(cotangent.reshape(IMAGES, seq_len, D).astype(jnp.float32))
    bias_grads = weight_grads[1]
    return (layer.astype(jnp.bfloat16).reshape(IMAGES, GRID, GRID, D), input_grad.astype(jnp.bfloat16).reshape(IMAGES, GRID, GRID, D), weight_grads[0], bias_grads[:2 * D], bias_grads[2 * D:], weight_grads[2], weight_grads[3], weight_grads[4], weight_grads[5], weight_grads[6], weight_grads[7], weight_grads[8], weight_grads[9], weight_grads[10], weight_grads[11], weight_grads[12])
```

```python
import jax
import jax.numpy as jnp
from jax import lax
from jax.sharding import PartitionSpec as P

HEADS = 12
NORM_EPSILON = 1e-06
MASKED_SCORE = -1e30
BF = jnp.bfloat16
F32 = jnp.float32


def layer_norm(values, gain, shift):
    center = values - jnp.mean(values, -1, keepdims=True)
    inverse = lax.rsqrt(jnp.mean(center * center, -1, keepdims=True) + NORM_EPSILON)
    normed = center * inverse
    return normed * gain + shift, normed, inverse


def norm_back(grad, normed, inverse, gain):
    scaled = grad * gain
    centred = scaled - jnp.mean(scaled, -1, keepdims=True)
    return inverse * (centred - normed * jnp.mean(scaled * normed, -1, keepdims=True))


def gelu_parts(pre):
    cdf = 0.5 * (1.0 + lax.erf(pre * 0.7071067811865476))
    pdf = jnp.exp(-0.5 * pre * pre) * 0.3989422804014327
    return pre * cdf, cdf + pre * pdf


def dot(left, right, dims):
    return lax.dot_general(left, right, (dims, ((), ())), preferred_element_type=F32)


def nn(left, right):
    return dot(left, right, ((1,), (0,)))


def nt(left, right):
    return dot(left, right, ((1,), (1,)))


def tn(left, right):
    return dot(left, right, ((0,), (0,)))


class Slice:
    def __init__(self, img_count):
        self.img_count = img_count
        self.bits = img_count.bit_length() - 1
        self.img = lax.axis_index("img")
        row = lax.axis_index("row")
        self.row = row
        self.y = row // 2
        self.c = row % 2
        high = list(range(self.bits - 1, 0, -1))
        self.orders = (high + [0, "y"], high + ["y", 0])

    def swap(self, array, step):
        if step == "c":
            return lax.ppermute(array, "row", [(r, r ^ 1) for r in range(4)])
        if step == "y":
            return lax.ppermute(array, "row", [(r, r ^ 2) for r in range(4)])
        return lax.ppermute(array, "img", [(i, i ^ (1 << step)) for i in range(self.img_count)])

    def gather(self, piece, order):
        held = piece[None]
        for step in order:
            held = jnp.concatenate([held, self.swap(held, step)], 0)
        return held

    def scatter(self, held, order):
        for step in reversed(order):
            half = held.shape[0] // 2
            came = self.swap(held[half:], step)
            held = (held[:half].astype(F32) + came.astype(F32)).astype(held.dtype)
        return held[0]

    def places(self, order):
        place = jnp.zeros((2, self.img_count), jnp.int32)
        img = jnp.arange(self.img_count, dtype=jnp.int32)[None, :] ^ self.img
        side = jnp.arange(2, dtype=jnp.int32)[:, None] ^ self.y
        for k, step in enumerate(order):
            bit = side if step == "y" else (img >> step) & 1
            place = place + (bit << k)
        return place

    def gather_rows(self, piece):
        rows, width = piece.shape
        half = rows // 2
        parts = []
        for order, part in zip(self.orders, (piece[:half], piece[half:])):
            held = self.gather(part, order)
            parts.append(jnp.take(held, self.places(order), axis=0))
        return jnp.concatenate(parts, 2).reshape(2, self.img_count * rows, width)

    def scatter_rows(self, whole):
        rows = whole.shape[1] // self.img_count
        half = rows // 2
        pieces = whole.reshape(2, self.img_count, rows, whole.shape[2])
        parts = []
        for order, part in zip(self.orders, (pieces[:, :, :half], pieces[:, :, half:])):
            place = self.places(order).reshape(-1)
            source = jnp.zeros_like(place).at[place].set(jnp.arange(place.size, dtype=jnp.int32))
            held = jnp.take(part.reshape((-1,) + part.shape[2:]), source, axis=0)
            parts.append(self.scatter(held, order))
        return jnp.concatenate(parts, 0)


def half_swap(array):
    half = array.shape[0] // 2
    return jnp.concatenate([array[half:], array[:half]], 0)


def make_body(img_count):
    def body(
        tokens, keep_mask, cotangent, qkv_weight, qkv_bias, proj_weight, proj_bias, attn_gain, attn_shift,
        mlp_gain, mlp_shift, up_weight, up_bias, down_weight, down_bias, rope_freqs,
    ):
        me = Slice(img_count)
        y, c = me.y, me.c
        images, band_rows, side, width = tokens.shape
        band = band_rows * side
        head = width // HEADS
        pairs = head // 2
        heads = HEADS // 2
        own_width = heads * head
        third = own_width // 2

        def pick(flag, zero, one):
            return jnp.where(flag == 0, zero, one)

        vectors = (qkv_bias, proj_bias, attn_gain, attn_shift, mlp_gain, mlp_shift, up_bias, down_bias, rope_freqs)
        lengths = [v.shape[0] for v in vectors]
        packed = jnp.concatenate([v.astype(BF) for v in vectors])[None]
        both = jnp.concatenate([packed, me.swap(packed, "c")], 0)
        order = me.orders[0]
        gathered = me.gather(both, order)
        gathered = jnp.take(gathered, me.places(order).T.reshape(-1), axis=0)
        gathered = pick(c, gathered, gathered[:, ::-1]).astype(F32)
        flat = []
        start = 0
        for length in lengths:
            flat.append(gathered[:, :, start : start + length].reshape(-1))
            start += length
        b_qkv, b_proj, g1, s1, g2, s2, b_up, b_down, freqs = flat
        own_b_qkv = b_qkv.reshape(3, 2, 2, third)
        own_b_qkv = pick(c, own_b_qkv[:, :, 0], own_b_qkv[:, :, 1]).reshape(-1)
        own_b_up = b_up.reshape(2, 2, -1)
        own_b_up = pick(c, own_b_up[:, 0], own_b_up[:, 1]).reshape(-1)
        own_freqs = freqs.reshape(2, 2, 2, heads // 2, pairs)
        own_freqs = pick(c, own_freqs[:, :, 0], own_freqs[:, :, 1]).reshape(2, heads, pairs)

        mask_rows = jnp.pad(keep_mask.reshape(images, 1, band).astype(BF), ((0, 0), (0, 15), (0, width - band)))
        pack = jnp.concatenate([tokens.reshape(images, band, width), cotangent.reshape(images, band, width), mask_rows], 1)
        mine, other = pick(y, pack[0], pack[1]), pick(y, pack[1], pack[0])
        near = jnp.stack([mine, me.swap(other, "y")], 0)
        bands = jnp.concatenate([near, me.swap(near, "c")], 0)
        x = bands[:, :band].reshape(4 * band, width).astype(F32)
        ct = bands[:, band : 2 * band].reshape(4 * band, width).astype(F32)
        kp = bands[:, 2 * band, :band].reshape(4 * band).astype(F32)
        length = 4 * band

        w = qkv_weight.astype(BF)
        t0, t1, t2 = w[:, :third], w[:, third : 2 * third], w[:, 2 * third :]
        came = me.swap(t1, "c")
        canonical = pick(c, jnp.concatenate([t0, t2, came], 1), jnp.concatenate([came, t0, t2], 1))
        first = me.gather_rows(jnp.concatenate([canonical, proj_weight.astype(BF)], 1))
        up = me.gather_rows(up_weight.astype(BF))
        down = me.gather_rows(down_weight.T.astype(BF))
        w_qkv = jnp.concatenate([first[0, :, : 3 * third], first[1, :, : 3 * third]], 1)
        proj_cols = first[:, :, 3 * third :]
        proj_other = me.swap(proj_cols, "c")
        block = proj_cols.shape[2]
        w_proj = pick(
            c,
            jnp.concatenate([proj_cols[0], proj_other[0], proj_cols[1], proj_other[1]], 1),
            jnp.concatenate([proj_other[0], proj_cols[0], proj_other[1], proj_cols[1]], 1),
        )
        w_up = jnp.concatenate([up[0], up[1]], 1)
        w_down = jnp.concatenate([down[0], down[1]], 1)

        n1, xh1, rs1 = layer_norm(x, g1, s1)
        a1 = n1.astype(BF)
        qkv = nn(a1, w_qkv) + own_b_qkv
        place = jnp.arange(band, dtype=jnp.int32)
        col_pos = jnp.tile((place % side).astype(F32), 4)
        row_pos = jnp.concatenate([(place // side + (me.row ^ k) * band_rows).astype(F32) for k in (0, 2, 1, 3)])
        theta = col_pos[:, None, None] * own_freqs[0] + row_pos[:, None, None] * own_freqs[1]
        cos, sin = jnp.cos(theta), jnp.sin(theta)

        def rotate(z):
            z = z.reshape(length, heads, 2, pairs)
            z1, z2 = z[:, :, 0], z[:, :, 1]
            return z1 * cos - z2 * sin, z1 * sin + z2 * cos

        q1, q2 = rotate(qkv[:, :own_width])
        k1, k2 = rotate(qkv[:, own_width : 2 * own_width])
        qr = jnp.concatenate([q1, q2], -1).astype(BF)
        kr = jnp.concatenate([k1, k2], -1).astype(BF)
        vb = qkv[:, 2 * own_width :].reshape(length, heads, head).astype(BF)
        scale = 1.0 / head**0.5
        scores = jnp.einsum("qhe,khe->hqk", qr, kr, preferred_element_type=F32) * scale
        scores = jnp.where(kp[None, None, :] > 0, scores, MASKED_SCORE)
        powers = jnp.exp(scores - jnp.max(scores, -1, keepdims=True))
        p = powers / jnp.sum(powers, -1, keepdims=True)
        pb = p.astype(BF)
        ob = jnp.einsum("hqk,khe->qhe", pb, vb, preferred_element_type=F32).reshape(length, own_width).astype(BF)
        ob_other = half_swap(me.swap(ob, "c"))
        ob_zero, ob_one = pick(c, ob, ob_other), pick(c, ob_other, ob)
        ob_all = jnp.concatenate([ob_zero[:, :third], ob_one[:, :third], ob_zero[:, third:], ob_one[:, third:]], 1)
        x1 = x + nn(ob_all, w_proj) + b_proj

        n2, xh2, rs2 = layer_norm(x1, g2, s2)
        a2 = n2.astype(BF)
        u = nn(a2, w_up) + own_b_up
        act, slope = gelu_parts(u)
        g = act.astype(BF)
        m = nt(g, w_down)
        half = length // 2
        dy = kp[:, None] * ct
        dm = dy.astype(BF)
        d_down = tn(dm, g)
        du = (nn(dm, w_down) * slope).astype(BF)
        d_up_bias = jnp.sum(du.astype(F32), 0)
        d_up = tn(a2, du)
        dn2 = nt(du, w_up)
        m_own = m[:half] + me.swap(m[half:].astype(BF), "c").astype(F32)
        out_half = (kp[:half, None] * (x1[:half] + m_own + b_down)).astype(BF)
        dn2 = dn2 + half_swap(me.swap(dn2.astype(BF), "c")).astype(F32)
        dx1 = dy + norm_back(dn2, xh2, rs2, g2)
        dx1b = dx1.astype(BF)

        w_proj_heads = w_proj.reshape(2, 2, third, width)
        w_proj_heads = pick(c, w_proj_heads[:, 0], w_proj_heads[:, 1]).reshape(own_width, width)
        dob = nt(dx1b, w_proj_heads).astype(BF).reshape(length, heads, head)
        dx1b_cols = dx1b.reshape(length, 2, 2, block)
        dx1b_cols = pick(c, dx1b_cols[:, :, 0], dx1b_cols[:, :, 1]).reshape(length, 2 * block)
        d_proj = tn(ob_all, dx1b_cols)
        dp = jnp.einsum("qhe,khe->hqk", dob, vb, preferred_element_type=F32)
        ds = (p * (dp - jnp.sum(p * dp, -1, keepdims=True))).astype(BF)
        dqr = jnp.einsum("hqk,khe->qhe", ds, kr, preferred_element_type=F32) * scale
        dkr = jnp.einsum("hqk,qhe->khe", ds, qr, preferred_element_type=F32) * scale
        dv = jnp.einsum("hqk,qhe->khe", pb, dob, preferred_element_type=F32)

        def rotate_back(grad, o1, o2):
            e1, e2 = grad[..., :pairs], grad[..., pairs:]
            back = jnp.concatenate([e1 * cos + e2 * sin, e2 * cos - e1 * sin], -1)
            return back.reshape(length, own_width), e2 * o1 - e1 * o2

        dq, tq = rotate_back(dqr, q1, q2)
        dk, tk = rotate_back(dkr, k1, k2)
        turn = (tq + tk).reshape(length, heads * pairs)
        d_freqs = jnp.stack([jnp.sum(col_pos[:, None] * turn, 0), jnp.sum(row_pos[:, None] * turn, 0)])
        dqkv = jnp.concatenate([dq, dk, dv.reshape(length, own_width)], 1).astype(BF)
        d_qkv_bias = jnp.sum(dqkv.astype(F32), 0)
        d_qkv = tn(a1, dqkv)
        dn1 = nt(dqkv, w_qkv)
        dn1_own = dn1[:half] + me.swap(dn1[half:].astype(BF), "c").astype(F32)
        tokens_half = (dx1[:half] + norm_back(dn1_own, xh1[:half], rs1[:half], g1)).astype(BF)

        def to_images(rows):
            came = me.swap(rows[band:], "y")
            return pick(y, jnp.stack([rows[:band], came]), jnp.stack([came, rows[:band]])).reshape(tokens.shape)

        layer_out = to_images(out_half)
        tokens_grad = to_images(tokens_half)

        d_up = me.scatter_rows(jnp.stack([d_up[:, : width], d_up[:, width:]]).astype(BF)).astype(F32)
        d_down = me.scatter_rows(jnp.stack([d_down[:, : width], d_down[:, width:]]).astype(BF)).astype(F32).T
        d_first = jnp.stack(
            [
                jnp.concatenate([d_qkv[:, : 3 * third], d_proj[:, :block]], 1),
                jnp.concatenate([d_qkv[:, 3 * third :], d_proj[:, block:]], 1),
            ]
        )
        d_first = me.scatter_rows(d_first.astype(BF))
        d0, d1, d2 = d_first[:, :third], d_first[:, third : 2 * third], d_first[:, 2 * third : 3 * third]
        came = me.swap(pick(c, d2, d0), "c")
        d_qkv = pick(c, jnp.concatenate([d0, came, d1], 1), jnp.concatenate([d1, came, d2], 1)).astype(F32)
        d_proj = d_first[:, 3 * third :].astype(F32)

        def own_part(value):
            zero = jnp.zeros_like(value)
            return pick(c, jnp.stack([value, zero], 2), jnp.stack([zero, value], 2))

        grads = (
            own_part(d_qkv_bias[: 2 * own_width].reshape(2, 2, third)),
            own_part(d_qkv_bias[2 * own_width :].reshape(1, 2, third)),
            jnp.sum(dx1b[:half].astype(F32), 0),
            jnp.sum(dn1_own * xh1[:half], 0),
            jnp.sum(dn1_own, 0),
            jnp.sum(dn2[:half] * xh2[:half], 0),
            jnp.sum(dn2[:half], 0),
            own_part(d_up_bias.reshape(1, 2, -1)),
            jnp.sum(dm[:half].astype(F32), 0),
            own_part(d_freqs.reshape(2, 2, heads // 2 * pairs)),
        )
        devices = img_count * 4
        sizes = [v.size // devices for v in grads]
        table = jnp.concatenate([v.reshape(devices, -1) for v in grads], 1).reshape(img_count, 2, 2, -1)
        table = pick(c, table, table[:, :, ::-1])
        place = me.places(order).reshape(-1)
        source = jnp.zeros_like(place).at[place].set(jnp.arange(place.size, dtype=jnp.int32))
        table = jnp.take(table.swapaxes(0, 1).reshape(img_count * 2, 2, -1), source, axis=0)
        table = table[:, 0] + me.swap(table[:, 1], "c")
        total = me.scatter(table, order)
        vector_out = []
        start = 0
        for size in sizes:
            vector_out.append(total[start : start + size])
            start += size
        v = vector_out
        return (
            layer_out, tokens_grad, d_qkv, v[0], v[1], d_proj, v[2], v[3], v[4], v[5], v[6], d_up, v[7], d_down, v[8], v[9],
        )

    return body


def solution(mesh):
    split = P(("img", "row"))
    both = P("img", "row")
    field = P("img", "row", None, None)
    return jax.shard_map(
        make_body(mesh.shape["img"]),
        mesh=mesh,
        in_specs=(
            field, P("img", "row", None), field, both, split, both, split, split, split, split, split, both, split,
            P("row", "img"), split, split,
        ),
        out_specs=(
            field, field, both, split, split, both, split, split, split, split, split, both, split, P("row", "img"),
            split, split,
        ),
        check_vma=False,
    )
```

```python
import functools

import jax
import jax.numpy as jnp
from jax import lax
from jax.experimental import pallas as pl
from jax.experimental.pallas import tpu as pltpu
from jax.sharding import PartitionSpec as P

HEADS = 12
NORM_EPSILON = 1e-06
MASKED_SCORE = -1e30
BF = jnp.bfloat16
F32 = jnp.float32
MIB = 2**20
VMEM = pl.BlockSpec(memory_space=pltpu.VMEM)
SMEM = pl.BlockSpec(memory_space=pltpu.SMEM)


def dot(left, right, dims):
    return lax.dot_general(left, right, (dims, ((), ())), preferred_element_type=F32)


def nn(left, right):
    return dot(left, right, ((1,), (0,)))


def nt(left, right):
    return dot(left, right, ((1,), (1,)))


def tn(left, right):
    return dot(left, right, ((0,), (0,)))


def normed_rows(values):
    center = values - jnp.mean(values, -1, keepdims=True)
    inverse = lax.rsqrt(jnp.mean(center * center, -1, keepdims=True) + NORM_EPSILON)
    return center * inverse, inverse


def norm_back(grad, normed, inverse, gain):
    scaled = grad * gain
    centred = scaled - jnp.mean(scaled, -1, keepdims=True)
    return inverse * (centred - normed * jnp.mean(scaled * normed, -1, keepdims=True))


def column_sum(value):
    return jnp.sum(value, 0, keepdims=True)


class Layout:
    def __init__(self, img_count, tokens, rows):
        self.img_count = img_count
        self.bits = img_count.bit_length() - 1
        self.rows = rows
        self.half_rows = rows // 2
        self.aligned = rows % 32 == 0
        self.images, self.band_rows, self.side, self.width = tokens.shape
        self.band = self.band_rows * self.side
        self.length = 4 * self.band
        self.head = self.width // HEADS
        self.own = self.width // 2
        self.third = self.own // 2
        self.high = list(range(self.bits - 1, 0, -1))

    def slots(self, img_rel, y_rel):
        high = 0
        for k, bit in enumerate(self.high):
            high = high + (((img_rel >> bit) & 1) << k)
        top = self.bits - 1
        return (high + ((img_rel & 1) << top), y_rel), (high + (y_rel << top), img_rel & 1)


def load_pieces(lay, me_ref, refs, y_side, columns, store):
    if not lay.aligned:
        store(0, refs[0][y_side, :, columns])
        return
    img, y = me_ref[0], me_ref[1]
    half = lay.half_rows
    for i in range(lay.img_count):
        for part, (slot, last) in enumerate(lay.slots(i ^ img, y_side ^ y)):
            held, came = refs[2 * part], refs[2 * part + 1]
            store(i * lay.rows + part * half, jnp.where(last == 0, held[slot, :, columns], came[slot, :, columns]))


def store_pieces(lay, me_ref, refs, y_side, columns, value):
    if not lay.aligned:
        refs[0][y_side, :, columns] = value
        return
    img, y = me_ref[0], me_ref[1]
    half = lay.half_rows
    for i in range(lay.img_count):
        for part, (slot, last) in enumerate(lay.slots(i ^ img, y_side ^ y)):
            start = i * lay.rows + part * half
            piece = value[start : start + half]

            @pl.when(last == 0)
            def _(ref=refs[2 * part], slot=slot, piece=piece):
                ref[slot, :, columns] = piece

            @pl.when(last == 1)
            def _(ref=refs[2 * part + 1], slot=slot, piece=piece):
                ref[slot, :, columns] = piece


def halves_of(lay, value):
    pairs = lay.head // 2
    lane = lax.broadcasted_iota(jnp.int32, value.shape, 1)
    width = value.shape[1]
    first = (lane & pairs) == 0
    return jnp.where(first, pltpu.roll(value, width - pairs, 1), pltpu.roll(value, pairs, 1))


def project_kernel(lay, n_w, me_ref, t0, t1, t2, t3, *refs):
    w_refs = refs[:n_w]
    g_ref, s_ref, b_ref, f_ref, a_ref, q_ref, k_ref, v_ref, w_out, p_out, cos_ref, sin_ref, w_all = refs[n_w:]
    band, side, own, third = lay.band, lay.side, lay.own, lay.third
    for y_side in range(2):

        def store(row, rows, y_side=y_side):
            w_all[y_side, row : row + rows.shape[0]] = rows

        load_pieces(lay, me_ref, w_refs, y_side, slice(None), store)
    for b, ref in enumerate((t0, t1, t2, t3)):
        normed, _ = normed_rows(ref[:band].astype(F32))
        a_ref[b * band : (b + 1) * band] = (normed * g_ref[...] + s_ref[...]).astype(BF)
    lane = lax.broadcasted_iota(jnp.int32, (side, own), 1)
    sign = jnp.where((lane & (lay.head // 2)) == 0, -1.0, 1.0).astype(F32)
    col = lax.broadcasted_iota(jnp.int32, (side, own), 0).astype(F32) * f_ref[0:1]
    col_cos, col_sin = jnp.cos(col), jnp.sin(col)
    row_index = me_ref[3]
    for b, flip in enumerate((0, 2, 1, 3)):
        first = ((row_index ^ flip) * lay.band_rows).astype(F32)
        rows = (lax.broadcasted_iota(jnp.int32, (8, own), 0).astype(F32) + first) * f_ref[1:2]
        row_cos, row_sin = jnp.cos(rows), jnp.sin(rows)
        for r in range(lay.band_rows):
            at = slice(b * band + r * side, b * band + (r + 1) * side)
            rc, rs = row_cos[r : r + 1], row_sin[r : r + 1]
            cos_ref[at] = col_cos * rc - col_sin * rs
            sin_ref[at] = (col_sin * rc + col_cos * rs) * sign
    acts = a_ref[...]
    w0, w1 = w_all[0, :, : 3 * third], w_all[1, :, : 3 * third]
    w_out[0], w_out[1] = w0, w1
    p_out[0], p_out[1] = w_all[0, :, 3 * third :], w_all[1, :, 3 * third :]
    left = nn(acts, w0) + b_ref[:, : 3 * third]
    right = nn(acts, w1) + b_ref[:, 3 * third :]
    query, key = left[:, :own], jnp.concatenate([left[:, own:], right[:, :third]], 1)
    cos, sin = cos_ref[...], sin_ref[...]
    q_ref[...] = (query * cos + halves_of(lay, query) * sin).astype(BF)
    k_ref[...] = (key * cos + halves_of(lay, key) * sin).astype(BF)
    v_ref[...] = right[:, third:].astype(BF)


def attend_kernel(lay, chunk, q_ref, k_ref, v_ref, bias_ref, o_ref, p_ref):
    head = lay.head
    pair = 2 * head
    scale = head**-0.5

    def step(n, carry):
        at = pl.ds(pl.multiple_of(n * pair, pair), pair)
        keys, values = k_ref[:, at], v_ref[:, at]
        for start in range(0, lay.length, chunk):
            rows = slice(start, start + chunk)
            query = q_ref[rows, at] * jnp.asarray(scale, BF)
            lane = lax.broadcasted_iota(jnp.int32, query.shape, 1)
            outs = []
            for h in range(2):
                mine = (lane < head) if h == 0 else (lane >= head)
                score = nt(jnp.where(mine, query, jnp.zeros_like(query)), keys) + bias_ref[...]
                power = jnp.exp(score - jnp.max(score, -1, keepdims=True))
                weights = (power * (1.0 / jnp.sum(power, -1, keepdims=True))).astype(BF)
                p_ref[2 * n + h, rows] = weights
                outs.append(nn(weights, values))
            o_ref[rows, at] = jnp.where(lane < head, outs[0], outs[1]).astype(BF)
        return carry

    lax.fori_loop(0, HEADS // 4, step, 0)


def middle_kernel(lay, me_ref, t0, t1, t2, t3, ob_ref, oo_ref, p_ref, po_ref, pb_ref, g_ref, s_ref, x1_ref, a2_ref, wp_ref):
    band, third, half = lay.band, lay.third, lay.length // 2
    c = me_ref[2]
    block = p_ref.shape[2]
    for y_side in range(2):
        mine, other = p_ref[y_side], po_ref[y_side]
        wp_ref[:, 2 * y_side * block : 2 * (y_side + 1) * block] = jnp.where(
            c == 0, jnp.concatenate([mine, other], 1), jnp.concatenate([other, mine], 1)
        )
    low = [pl.ds(pl.multiple_of((2 * s + c) * third, third), third) for s in range(2)]
    high = [pl.ds(pl.multiple_of((2 * s + 1 - c) * third, third), third) for s in range(2)]
    own_w = jnp.concatenate([wp_ref[low[0]], wp_ref[low[1]]], 0)
    other_w = jnp.concatenate([wp_ref[high[0]], wp_ref[high[1]]], 0)
    other = jnp.concatenate([oo_ref[half:], oo_ref[:half]], 0)
    x1_ref[...] = nn(ob_ref[...], own_w) + nn(other, other_w) + pb_ref[...]
    for b, ref in enumerate((t0, t1, t2, t3)):
        at = slice(b * band, (b + 1) * band)
        x1 = x1_ref[at] + ref[:band].astype(F32)
        x1_ref[at] = x1
        normed, _ = normed_rows(x1)
        a2_ref[at] = (normed * g_ref[...] + s_ref[...]).astype(BF)


def mlp_kernel(lay, n_w, chunk, me_ref, t0, t1, t2, t3, kp_ref, x1_ref, a2_ref, *refs):
    w_refs = refs[:n_w]
    ub_ref, db_ref = refs[n_w : n_w + 2]
    part_ref, msend_ref, dn_ref, dnsend_ref, ubg_ref, dbg_ref = refs[n_w + 2 : n_w + 8]
    grads = refs[n_w + 8 : n_w + 8 + n_w]
    dm_ref, at_ref, dt_ref, m_ref, u_w, d_w = refs[n_w + 8 + n_w :]
    band, width, half = lay.band, lay.width, lay.length // 2
    for b, ref in enumerate((t0, t1, t2, t3)):
        at = slice(b * band, (b + 1) * band)
        dm_ref[at] = (ref[band : 2 * band].astype(F32) * kp_ref[at]).astype(BF)
    at_ref[...] = a2_ref[...].T
    dt_ref[...] = dm_ref[...].T
    dbg_ref[...] = column_sum(dm_ref[:half].astype(F32))
    m_ref[...] = jnp.zeros_like(m_ref)
    dn_ref[...] = jnp.zeros_like(dn_ref)
    per_side = width // chunk

    for y_side in range(2):

        def store(row, rows):
            u_w[row : row + rows.shape[0]] = rows[:, :width]
            d_w[row : row + rows.shape[0]] = rows[:, width:]

        load_pieces(lay, me_ref, w_refs, y_side, slice(None), store)

        def step(n, carry, y_side=y_side):
            at = pl.ds(pl.multiple_of(n * chunk, chunk), chunk)
            b_at = pl.ds(pl.multiple_of(n * chunk + y_side * width, chunk), chunk)
            up, down = u_w[:, at], d_w[:, at]
            acts = a2_ref[...]
            dm = dm_ref[...]
            pre = nn(acts, up) + ub_ref[:, b_at]
            cdf = 0.5 * (1.0 + lax.erf(pre * 0.7071067811865476))
            slope = cdf + pre * (jnp.exp(-0.5 * pre * pre) * 0.3989422804014327)
            act = (pre * cdf).astype(BF)
            du = (nn(dm, down) * slope).astype(BF)
            ubg_ref[:, b_at] = column_sum(du.astype(F32))
            m_ref[...] += nt(act, down)
            dn_ref[...] += nt(du, up)
            store_pieces(lay, me_ref, grads, y_side, at, nn(at_ref[...], du).astype(BF))
            d_at = pl.ds(pl.multiple_of(n * chunk + width, chunk), chunk)
            store_pieces(lay, me_ref, grads, y_side, d_at, nn(dt_ref[...], act).astype(BF))
            return carry

        lax.fori_loop(0, per_side, step, 0)
    part_ref[...] = x1_ref[:half] + m_ref[:half] + db_ref[...]
    msend_ref[...] = m_ref[half:].astype(BF)
    dnsend_ref[...] = dn_ref[...].astype(BF)


def back_kernel(
    lay, n_g, chunk, me_ref, t0, t1, t2, t3, kp_ref, x1_ref, dn_ref, came_ref, g_ref, wp_ref, ob_ref, oo_ref, q_ref, k_ref, v_ref,
    p_ref, cos_ref, sin_ref, a_ref, *refs,
):
    dx_ref, pbg_ref, gg_ref, sg_ref, bg_ref, fg_ref, dqkv_ref = refs[:7]
    grads = refs[7 : 7 + n_g]
    dxb_ref, dob_ref, dq_ref, dk_ref, dv_ref = refs[7 + n_g :]
    band, side, own, third, half, head = lay.band, lay.side, lay.own, lay.third, lay.length // 2, lay.head
    c = me_ref[2]
    pair = 2 * head
    scale = head**-0.5
    gg, sg, pbg = 0.0, 0.0, 0.0
    for b, ref in enumerate((t0, t1, t2, t3)):
        at = slice(b * band, (b + 1) * band)
        away = slice((b ^ 2) * band, ((b ^ 2) + 1) * band)
        dn = dn_ref[at] + came_ref[away].astype(F32)
        normed, inverse = normed_rows(x1_ref[at])
        dx = ref[band : 2 * band].astype(F32) * kp_ref[at] + norm_back(dn, normed, inverse, g_ref[...])
        dxb = dx.astype(BF)
        dxb_ref[at] = dxb
        if b < 2:
            dx_ref[at] = dx
            gg = gg + column_sum(dn * normed)
            sg = sg + column_sum(dn)
            pbg = pbg + column_sum(dxb.astype(F32))
    gg_ref[...], sg_ref[...], pbg_ref[...] = gg, sg, pbg
    low = [pl.ds(pl.multiple_of((2 * s + c) * third, third), third) for s in range(2)]
    own_w = jnp.concatenate([wp_ref[low[0]], wp_ref[low[1]]], 0)
    dxb = dxb_ref[...]
    dob_ref[...] = nt(dxb, own_w).astype(BF)
    block = lay.width // 4
    zero = jnp.concatenate([dxb[:, :block], dxb[:, 2 * block : 3 * block]], 1)
    one = jnp.concatenate([dxb[:, block : 2 * block], dxb[:, 3 * block :]], 1)
    cols = jnp.where(c == 0, zero, one)
    other = jnp.concatenate([oo_ref[half:], oo_ref[:half]], 0)
    mine_g, other_g = tn(ob_ref[...], cols).astype(BF), tn(other, cols).astype(BF)
    zero, one = jnp.where(c == 0, mine_g, other_g), jnp.where(c == 0, other_g, mine_g)
    p_grad = jnp.concatenate([zero[:third], one[:third], zero[third:], one[third:]], 0)

    def step(n, carry):
        at = pl.ds(pl.multiple_of(n * pair, pair), pair)
        keys, values = k_ref[:, at], v_ref[:, at]
        for start in range(0, lay.length, chunk):
            rows = slice(start, start + chunk)
            query, dob = q_ref[rows, at], dob_ref[rows, at]
            lane = lax.broadcasted_iota(jnp.int32, query.shape, 1)
            dqs, dks, dvs = [], [], []
            for h in range(2):
                mine = (lane < head) if h == 0 else (lane >= head)
                weights = p_ref[2 * n + h, rows]
                soft = weights.astype(F32)
                dp = nt(jnp.where(mine, dob, jnp.zeros_like(dob)), values)
                ds = (soft * (dp - jnp.sum(soft * dp, -1, keepdims=True))).astype(BF)
                dqs.append(nn(ds, keys))
                dks.append(tn(ds, query))
                dvs.append(tn(weights, dob))
            dq_ref[rows, at] = jnp.where(lane < head, dqs[0], dqs[1]) * scale
            lane = lax.broadcasted_iota(jnp.int32, keys.shape, 1)
            dk = jnp.where(lane < head, dks[0], dks[1]) * scale
            dv = jnp.where(lane < head, dvs[0], dvs[1])
            if start == 0:
                dk_ref[:, at] = dk
                dv_ref[:, at] = dv
            else:
                dk_ref[:, at] += dk
                dv_ref[:, at] += dv
        return carry

    lax.fori_loop(0, HEADS // 4, step, 0)
    cos, sin = cos_ref[...], sin_ref[...]
    dq, dk = dq_ref[...], dk_ref[...]
    dqkv_ref[:, :own] = (dq * cos + halves_of(lay, dq * sin)).astype(BF)
    dqkv_ref[:, own : 2 * own] = (dk * cos + halves_of(lay, dk * sin)).astype(BF)
    dqkv_ref[:, 2 * own :] = dv_ref[...].astype(BF)
    dq_ref[...] = dq * halves_of(lay, q_ref[...].astype(F32)) + dk * halves_of(lay, k_ref[...].astype(F32))
    by_col = jnp.zeros((side, own), F32)
    by_row = jnp.zeros((side, own), F32)
    for b, flip in enumerate((0, 2, 1, 3)):
        first = ((me_ref[3] ^ flip) * lay.band_rows).astype(F32)
        for r in range(lay.band_rows):
            turn = dq_ref[b * band + r * side : b * band + (r + 1) * side]
            by_col = by_col + turn
            by_row = by_row + turn * (first + r)
    lane = lax.broadcasted_iota(jnp.int32, (2, own), 1)
    sign = jnp.where((lane & (head // 2)) == 0, -1.0, 1.0).astype(F32)
    place = lax.broadcasted_iota(jnp.int32, (side, own), 0).astype(F32)
    both = jnp.concatenate([column_sum(by_col * place), column_sum(by_row)], 0) * sign
    fg_ref[...] = both + halves_of(lay, both)
    bg_ref[...] = column_sum(dqkv_ref[...].astype(F32))
    acts = a_ref[...]
    for y_side in range(2):
        at = slice(y_side * 3 * third, (y_side + 1) * 3 * third)
        grad = tn(acts, dqkv_ref[:, at]).astype(BF)
        full = jnp.concatenate([grad, p_grad[:, y_side * block : (y_side + 1) * block]], 1)
        store_pieces(lay, me_ref, grads, y_side, slice(None), full)


def last_kernel(lay, dqkv_ref, w_ref, keep_ref, send_ref):
    third, half = lay.third, lay.length // 2
    grad = nt(dqkv_ref[:, : 3 * third], w_ref[0]) + nt(dqkv_ref[:, 3 * third :], w_ref[1])
    keep_ref[...] = grad[:half]
    send_ref[...] = grad[half:].astype(BF)


def finish_kernel(lay, t0, t1, keep_ref, came_ref, dx_ref, g_ref, out_ref, send_ref, gg_ref, sg_ref):
    band = lay.band
    gg, sg = 0.0, 0.0
    for b, ref in enumerate((t0, t1)):
        at = slice(b * band, (b + 1) * band)
        dn = keep_ref[at] + came_ref[at].astype(F32)
        normed, inverse = normed_rows(ref[:band].astype(F32))
        result = (dx_ref[at] + norm_back(dn, normed, inverse, g_ref[...])).astype(BF)
        if b == 0:
            out_ref[...] = result
        else:
            send_ref[...] = result
        gg = gg + column_sum(dn * normed)
        sg = sg + column_sum(dn)
    gg_ref[...], sg_ref[...] = gg, sg


def call(kernel, name, inputs, outs, scratch=(), smem=1, limit=40):
    return pl.pallas_call(
        kernel,
        out_shape=[jax.ShapeDtypeStruct(shape, dtype) for shape, dtype in outs],
        in_specs=[SMEM] * smem + [VMEM] * (len(inputs) - smem),
        out_specs=[VMEM] * len(outs),
        scratch_shapes=[pltpu.VMEM(shape, dtype) for shape, dtype in scratch],
        compiler_params=pltpu.CompilerParams(vmem_limit_bytes=limit * MIB),
        name=name,
    )(*inputs)


class Slice:
    def __init__(self, lay):
        self.lay = lay
        self.img = lax.axis_index("img")
        self.row = lax.axis_index("row")
        self.y = self.row // 2
        self.c = self.row % 2
        self.facts = jnp.stack([self.img, self.y, self.c, self.row]).astype(jnp.int32)
        self.orders = (lay.high + [0, "y"], lay.high + ["y", 0])

    def swap(self, array, step):
        if step == "c":
            return lax.ppermute(array, "row", [(r, r ^ 1) for r in range(4)])
        if step == "y":
            return lax.ppermute(array, "row", [(r, r ^ 2) for r in range(4)])
        return lax.ppermute(array, "img", [(i, i ^ (1 << step)) for i in range(self.lay.img_count)])

    def gather(self, piece, order):
        held = piece[None]
        for step in order:
            held = jnp.concatenate([held, self.swap(held, step)], 0)
        return held

    def scatter(self, held, order):
        for step in reversed(order):
            half = held.shape[0] // 2
            came = self.swap(held[half:], step)
            held = (held[:half].astype(F32) + came.astype(F32)).astype(held.dtype)
        return held[0]

    def places(self, order):
        place = jnp.zeros((2, self.lay.img_count), jnp.int32)
        img = jnp.arange(self.lay.img_count, dtype=jnp.int32)[None, :] ^ self.img
        side = jnp.arange(2, dtype=jnp.int32)[:, None] ^ self.y
        for k, step in enumerate(order):
            bit = side if step == "y" else (img >> step) & 1
            place = place + (bit << k)
        return place

    def sources(self, order):
        place = self.places(order).reshape(-1)
        return jnp.zeros_like(place).at[place].set(jnp.arange(place.size, dtype=jnp.int32))

    def gather_rows(self, piece):
        lay = self.lay
        base = self.gather(piece, lay.high)
        parts = []
        for part, order in enumerate(self.orders):
            held = base[:, part * lay.half_rows : (part + 1) * lay.half_rows]
            held = jnp.concatenate([held, self.swap(held, order[-2])], 0)
            parts += [held, self.swap(held, order[-1])]
        if lay.aligned:
            return parts
        whole = []
        for part, order in enumerate(self.orders):
            both = jnp.concatenate(parts[2 * part : 2 * part + 2], 0)
            whole.append(jnp.take(both, self.places(order), axis=0))
        return [jnp.concatenate(whole, 2).reshape(2, lay.img_count * lay.rows, piece.shape[1])]

    def grad_shapes(self, columns):
        lay = self.lay
        if lay.aligned:
            return [((lay.img_count, lay.half_rows, columns), BF)] * 4
        return [((2, lay.img_count * lay.rows, columns), BF)]

    def scatter_rows(self, parts):
        lay = self.lay
        if not lay.aligned:
            pieces = parts[0].reshape(2, lay.img_count, lay.rows, parts[0].shape[2])
            parts = []
            for part, order in enumerate(self.orders):
                mine = pieces[:, :, part * lay.half_rows : (part + 1) * lay.half_rows]
                mine = jnp.take(mine.reshape((-1,) + mine.shape[2:]), self.sources(order), axis=0)
                parts += [mine[: lay.img_count], mine[lay.img_count :]]
        sums = []
        for part, order in enumerate(self.orders):
            keep, send = parts[2 * part : 2 * part + 2]
            held = (keep.astype(F32) + self.swap(send, order[-1]).astype(F32)).astype(BF)
            half = lay.img_count // 2
            sums.append((held[:half].astype(F32) + self.swap(held[half:], order[-2]).astype(F32)).astype(BF))
        return self.scatter(jnp.concatenate(sums, 1), lay.high)


def make_body(img_count):
    def body(
        tokens, keep_mask, cotangent, qkv_weight, qkv_bias, proj_weight, proj_bias, attn_gain, attn_shift,
        mlp_gain, mlp_shift, up_weight, up_bias, down_weight, down_bias, rope_freqs,
    ):
        lay = Layout(img_count, tokens, qkv_weight.shape[0])
        me = Slice(lay)
        y, c, facts = me.y, me.c, me.facts
        images, band, width, length = lay.images, lay.band, lay.width, lay.length
        pairs = lay.head // 2
        heads = HEADS // 2
        own, third = lay.own, lay.third
        half = length // 2
        block = proj_weight.shape[1]
        hidden = up_weight.shape[1]

        def pick(flag, zero, one):
            return jnp.where(flag == 0, zero, one)

        w = qkv_weight.astype(BF)
        t0, t1, t2 = w[:, :third], w[:, third : 2 * third], w[:, 2 * third :]
        came = me.swap(t1, "c")
        canonical = pick(c, jnp.concatenate([t0, t2, came], 1), jnp.concatenate([came, t0, t2], 1))
        first = me.gather_rows(jnp.concatenate([canonical, proj_weight.astype(BF)], 1))
        second = me.gather_rows(jnp.concatenate([up_weight, down_weight.T], 1).astype(BF))

        vectors = (qkv_bias, proj_bias, attn_gain, attn_shift, mlp_gain, mlp_shift, up_bias, down_bias, rope_freqs)
        lengths = [v.shape[0] for v in vectors]
        packed = jnp.concatenate(vectors).astype(BF)[None]
        both = jnp.concatenate([packed, me.swap(packed, "c")], 0)
        order = me.orders[0]
        gathered = me.gather(both, order)
        gathered = jnp.take(gathered, me.places(order).T.reshape(-1), axis=0)
        gathered = pick(c, gathered, gathered[:, ::-1]).astype(F32)
        flat = []
        start = 0
        for size in lengths:
            flat.append(gathered[:, :, start : start + size].reshape(1, -1))
            start += size
        b_qkv, b_proj, g1, s1, g2, s2, b_up, b_down, freqs = flat
        own_b_qkv = b_qkv.reshape(3, 2, 2, third)
        own_b_qkv = pick(c, own_b_qkv[:, :, 0], own_b_qkv[:, :, 1]).reshape(1, -1)
        own_b_up = b_up.reshape(2, 2, -1)
        own_b_up = pick(c, own_b_up[:, 0], own_b_up[:, 1]).reshape(1, -1)
        own_freqs = freqs.reshape(2, 2, 2, heads // 2, 1, pairs)
        own_freqs = pick(c, own_freqs[:, :, 0], own_freqs[:, :, 1])
        own_freqs = jnp.broadcast_to(own_freqs, own_freqs.shape[:3] + (2, pairs)).reshape(2, own)

        mask_rows = jnp.pad(keep_mask.reshape(images, 1, band).astype(BF), ((0, 0), (0, 15), (0, width - band)))
        pack = jnp.concatenate([tokens.reshape(images, band, width), cotangent.reshape(images, band, width), mask_rows], 1)
        mine, other = pick(y, pack[0], pack[1]), pick(y, pack[1], pack[0])
        near = me.swap(other, "y")
        bands = [mine, near, me.swap(mine, "c"), me.swap(near, "c")]
        kp = jnp.concatenate([b[2 * band, :band] for b in bands]).astype(F32)
        mask_bias = jnp.where(kp > 0, 0.0, MASKED_SCORE).reshape(1, length)
        kp = kp.reshape(length, 1)

        n_w = len(first)
        a1, q, k, v, w_qkv, p_cols, cos, sin = call(
            functools.partial(project_kernel, lay, n_w), "qkv", [facts, *bands, *first, g1, s1, own_b_qkv, own_freqs],
            [((length, width), BF), ((length, own), BF), ((length, own), BF), ((length, own), BF), ((2, width, 3 * third), BF),
             ((2, width, block), BF), ((length, own), F32), ((length, own), F32)],
            [((2, width, 3 * third + block), BF)],
        )
        p_other = me.swap(p_cols, "c")
        ob, p = call(
            functools.partial(attend_kernel, lay, band), "attend", [q, k, v, mask_bias],
            [((length, own), BF), ((heads, length, length), BF)], smem=0,
        )
        ob_other = me.swap(ob, "c")
        x1, a2, w_proj = call(
            functools.partial(middle_kernel, lay), "middle", [facts, *bands, ob, ob_other, p_cols, p_other, b_proj, g2, s2],
            [((length, width), F32), ((length, width), BF), ((width, width), BF)],
        )
        part, m_send, dn, dn_send, d_up_bias, d_down_bias, *second_grads = call(
            functools.partial(mlp_kernel, lay, n_w, 256), "mlp", [facts, *bands, kp, x1, a2, *second, own_b_up, b_down],
            [((half, width), F32), ((half, width), BF), ((length, width), F32), ((length, width), BF), ((1, 2 * hidden), F32),
             ((1, width), F32), *me.grad_shapes(2 * hidden)],
            [((length, width), BF), ((width, length), BF), ((width, length), BF), ((length, width), F32), ((width, hidden), BF),
             ((width, hidden), BF)],
        )
        d_second = me.scatter_rows(second_grads)
        dn_came = me.swap(dn_send, "c")
        m_came = me.swap(m_send, "c")
        out_half = (kp[:half] * (part + m_came.astype(F32))).astype(BF)
        dx_half, d_proj_bias, d_g2, d_s2, d_qkv_bias, d_freqs, dqkv, *first_grads = call(
            functools.partial(back_kernel, lay, n_w, band), "back",
            [facts, *bands, kp, x1, dn, dn_came, g2, w_proj, ob, ob_other, q, k, v, p, cos, sin, a1],
            [((half, width), F32), ((1, width), F32), ((1, width), F32), ((1, width), F32), ((1, 3 * own), F32), ((2, own), F32),
             ((length, 3 * own), BF), *me.grad_shapes(3 * third + block)],
            [((length, width), BF), ((length, own), BF), ((length, own), F32), ((length, own), F32), ((length, own), F32)],
        )
        d_first = me.scatter_rows(first_grads)
        dn1_keep, dn1_send = call(
            functools.partial(last_kernel, lay), "last", [dqkv, w_qkv], [((half, width), F32), ((half, width), BF)], smem=0
        )
        dn1_came = me.swap(dn1_send, "c")
        tg_keep, tg_send, d_g1, d_s1 = call(
            functools.partial(finish_kernel, lay), "finish", [bands[0], bands[1], dn1_keep, dn1_came, dx_half, g1],
            [((band, width), BF), ((band, width), BF), ((1, width), F32), ((1, width), F32)], smem=0,
        )

        def to_images(keep, send):
            came = me.swap(send, "y")
            return pick(y, jnp.stack([keep, came]), jnp.stack([came, keep])).reshape(tokens.shape)

        layer_out = to_images(out_half[:band], out_half[band:])
        tokens_grad = to_images(tg_keep, tg_send)

        d_up = d_second[:, :hidden].astype(F32)
        d_down = d_second[:, hidden:].T.astype(F32)
        d0, d1, d2 = d_first[:, :third], d_first[:, third : 2 * third], d_first[:, 2 * third : 3 * third]
        came = me.swap(pick(c, d2, d0), "c")
        d_qkv = pick(c, jnp.concatenate([d0, came, d1], 1), jnp.concatenate([d1, came, d2], 1)).astype(F32)
        d_proj = d_first[:, 3 * third :].astype(F32)

        def own_part(value):
            zero = jnp.zeros_like(value)
            return pick(c, jnp.stack([value, zero], 2), jnp.stack([zero, value], 2))

        d_freqs = d_freqs.reshape(2, 2, heads // 2, 2, pairs)[:, :, :, 0]
        grads = (
            own_part(d_qkv_bias[:, : 2 * own].reshape(2, 2, third)),
            own_part(d_qkv_bias[:, 2 * own :].reshape(1, 2, third)),
            d_proj_bias,
            d_g1,
            d_s1,
            d_g2,
            d_s2,
            own_part(d_up_bias.reshape(1, 2, -1)),
            d_down_bias,
            own_part(d_freqs.reshape(2, 2, heads // 2 * pairs)),
        )
        devices = img_count * 4
        sizes = [g.size // devices for g in grads]
        table = jnp.concatenate([g.reshape(devices, -1) for g in grads], 1).reshape(img_count, 2, 2, -1)
        table = pick(c, table, table[:, :, ::-1])
        table = jnp.take(table.swapaxes(0, 1).reshape(img_count * 2, 2, -1), me.sources(order), axis=0)
        table = table[:, 0] + me.swap(table[:, 1], "c")
        total = me.scatter(table, order)
        r = []
        start = 0
        for size in sizes:
            r.append(total[start : start + size])
            start += size
        return (
            layer_out, tokens_grad, d_qkv, r[0], r[1], d_proj, r[2], r[3], r[4], r[5], r[6], d_up, r[7], d_down, r[8], r[9],
        )

    return body


def solution(mesh):
    split = P(("img", "row"))
    both = P("img", "row")
    field = P("img", "row", None, None)
    return jax.shard_map(
        make_body(mesh.shape["img"]),
        mesh=mesh,
        in_specs=(
            field, P("img", "row", None), field, both, split, both, split, split, split, split, split, both, split,
            P("row", "img"), split, split,
        ),
        out_specs=(
            field, field, both, split, split, both, split, split, split, split, split, both, split, P("row", "img"),
            split, split,
        ),
        check_vma=False,
    )
```

```python
import functools

import jax
import jax.numpy as jnp
import numpy as np
from jax import lax
from jax.experimental import pallas as pl
from jax.experimental.pallas import tpu as pltpu
from jax.sharding import PartitionSpec as P

HEADS = 12
NORM_EPSILON = 1e-06
MASKED_SCORE = -1e30
BF = jnp.bfloat16
F32 = jnp.float32
MIB = 2**20
VMEM = pl.BlockSpec(memory_space=pltpu.VMEM)
SMEM = pl.BlockSpec(memory_space=pltpu.SMEM)


def dot(left, right, dims):
    return lax.dot_general(left, right, (dims, ((), ())), preferred_element_type=F32)


def nn(left, right):
    return dot(left, right, ((1,), (0,)))


def nt(left, right):
    return dot(left, right, ((1,), (1,)))


def tn(left, right):
    return dot(left, right, ((0,), (0,)))


def normed_rows(values):
    center = values - jnp.mean(values, -1, keepdims=True)
    inverse = lax.rsqrt(jnp.mean(center * center, -1, keepdims=True) + NORM_EPSILON)
    return center * inverse, inverse


def norm_back(grad, normed, inverse, gain):
    scaled = grad * gain
    centred = scaled - jnp.mean(scaled, -1, keepdims=True)
    return inverse * (centred - normed * jnp.mean(scaled * normed, -1, keepdims=True))


def column_sum(value):
    return jnp.sum(value, 0, keepdims=True)


class Layout:
    def __init__(self, img_count, tokens, rows):
        self.img_count = img_count
        self.bits = img_count.bit_length() - 1
        self.rows = rows
        self.half_rows = rows // 2
        self.aligned = rows % 32 == 0
        self.images, self.band_rows, self.side, self.width = tokens.shape
        self.band = self.band_rows * self.side
        self.length = 4 * self.band
        self.head = self.width // HEADS
        self.own = self.width // 2
        self.third = self.own // 2
        self.high = list(range(self.bits - 1, 0, -1))
        self.tiles = (img_count, rows) if self.aligned else (1, self.width)

    def slots(self, img_rel, y_rel):
        high = 0
        for k, bit in enumerate(self.high):
            high = high + (((img_rel >> bit) & 1) << k)
        top = self.bits - 1
        return (high + ((img_rel & 1) << top), y_rel), (high + (y_rel << top), img_rel & 1)


def load_pieces(lay, me_ref, refs, y_rel, target):
    if not lay.aligned:
        target[...] = refs[0][me_ref[1] ^ y_rel]
        return
    half = lay.half_rows
    base = lay.img_count // 2
    for img_rel in range(lay.img_count):
        for part, (slot, last) in enumerate(lay.slots(img_rel, y_rel)):
            ref = refs[4 * part + 2 * last + slot // base]
            target[img_rel ^ me_ref[0], part * half : (part + 1) * half] = ref[slot % base]


def store_pieces(lay, me_ref, refs, y_rel, columns, source):
    if not lay.aligned:
        refs[0][me_ref[1] ^ y_rel, :, :, columns] = source[...]
        return
    half = lay.half_rows
    for img_rel in range(lay.img_count):
        for part, (slot, last) in enumerate(lay.slots(img_rel, y_rel)):
            refs[2 * part + last][slot, :, columns] = source[img_rel ^ me_ref[0], part * half : (part + 1) * half]


def halves_of(lay, value):
    pairs = lay.head // 2
    lane = lax.broadcasted_iota(jnp.int32, value.shape, 1)
    width = value.shape[1]
    first = (lane & pairs) == 0
    return jnp.where(first, pltpu.roll(value, width - pairs, 1), pltpu.roll(value, pairs, 1))


def pack_kernel(lay, me_ref, tok_ref, cot_ref, mask_ref, qkv_ref, proj_ref, up_ref, down_ref, *refs):
    vectors = refs[:9]
    mine_ref, other_ref, third_ref, first_ref, second_ref = refs[9:]
    y = me_ref[1]
    band, third, width = lay.band, lay.third, lay.width
    third_ref[:, :third] = qkv_ref[:, third : 2 * third].astype(BF)
    third_ref[:, third:] = jnp.zeros((lay.rows, third_ref.shape[1] - third), BF)
    first_ref[:, :third] = qkv_ref[:, :third].astype(BF)
    first_ref[:, third : 2 * third] = qkv_ref[:, 2 * third :].astype(BF)
    first_ref[:, 2 * third :] = proj_ref[...].astype(BF)
    second_ref[:, :width] = up_ref[...].astype(BF)
    second_ref[:, width:] = down_ref[...].astype(BF)
    packed = jnp.concatenate([v[...] for v in vectors], 1)
    packed = jnp.concatenate([packed, jnp.zeros((1, width - packed.shape[1]), F32)], 1)
    for ref, which in ((mine_ref, y), (other_ref, 1 - y)):
        ref[:band] = tok_ref[which]
        ref[band : 2 * band] = cot_ref[which]
        keep = mask_ref[which].astype(F32)
        flat = jnp.concatenate([keep[r : r + 1] for r in range(lay.band_rows)], 1)
        flat = jnp.concatenate([flat, jnp.zeros((1, width - band), F32)], 1)
        ref[2 * band :] = jnp.concatenate([flat, packed, jnp.zeros((14, width), F32)], 0).astype(BF)


def fit_kernel(lay, me_ref, came_ref, first_ref, out_ref):
    third = lay.third
    c = me_ref[2]
    t0, t2, came = first_ref[:, :third], first_ref[:, third : 2 * third], came_ref[:, :third]
    out_ref[:, : 3 * third] = jnp.where(c == 0, jnp.concatenate([t0, t2, came], 1), jnp.concatenate([came, t0, t2], 1))
    out_ref[:, 3 * third :] = first_ref[:, 2 * third :]


def merge_kernel(lay, *refs):
    pieces, (top_ref, bottom_ref) = refs[:-2], refs[-2:]
    half = lay.half_rows
    for k, ref in enumerate(pieces):
        top_ref[k] = ref[:half]
        bottom_ref[k] = ref[half:]


def owner_mask(lay, devices, table_row, me_ref):
    place = lax.broadcasted_iota(jnp.int32, (devices, 1), 0)
    row_rel, img_place = place & 3, place >> 2
    row = (((row_rel & 1) << 1) | (row_rel >> 1)) ^ me_ref[3]
    img_rel = jnp.zeros_like(place)
    for k, bit in enumerate(lay.high + [0]):
        img_rel = img_rel | (((img_place >> k) & 1) << bit)
    return ((img_rel ^ me_ref[0]) * 4 + row) == table_row


def unpack_kernel(lay, plan, me_ref, v_ref, table_ref, out_ref):
    c = me_ref[2]
    devices = v_ref.shape[0]
    for start, size, offset, count in plan:
        at = slice(start, start + size)
        owner = jnp.where(c == 0, table_ref[0:1, at], table_ref[2:3, at])
        entry = jnp.where(c == 0, table_ref[1:2, at], table_ref[3:4, at])
        place = lax.broadcasted_iota(jnp.int32, (count, size), 0)
        spread = (place == entry).astype(F32).astype(BF)
        rows = nn(v_ref[:, offset : offset + count], spread)
        out_ref[:, at] = column_sum(jnp.where(owner_mask(lay, devices, owner, me_ref), rows, 0.0))


def repack_kernel(lay, plan, me_ref, table_ref, *refs):
    grads, out_ref = refs[:-1], refs[-1]
    c = me_ref[2]
    devices = out_ref.shape[0]
    out_ref[...] = jnp.zeros_like(out_ref)
    for ref, (start, size, offset, count) in zip(grads, plan):
        at = slice(start, start + size)
        owner = jnp.where(c == 0, table_ref[0:1, at], table_ref[2:3, at])
        entry = jnp.where(c == 0, table_ref[1:2, at], table_ref[3:4, at])
        place = lax.broadcasted_iota(jnp.int32, (count, size), 0)
        spread = (place == entry).astype(F32).astype(BF)
        rows = jnp.where(owner_mask(lay, devices, owner, me_ref), ref[...], 0.0).astype(BF)
        out_ref[:, offset : offset + count] = nt(rows, spread)


def project_kernel(lay, n_w, me_ref, t0, t1, t2, t3, *refs):
    w_refs = refs[:n_w]
    vec_ref, a_ref, q_ref, k_ref, v_ref, w_out, p_out, cos_ref, sin_ref, kp_ref, bias_ref, w_all = refs[n_w:]
    band, side, own, third = lay.band, lay.side, lay.own, lay.third
    g_ref, s_ref, b_ref = (vec_ref[:, lay.at[n]] for n in ("attn_gain", "attn_shift", "qkv_bias"))
    f_ref = vec_ref[:, lay.at["freqs"]]
    keeps = []
    for b, ref in enumerate((t0, t1, t2, t3)):
        at = slice(b * band, (b + 1) * band)
        normed, _ = normed_rows(ref[:band].astype(F32))
        a_ref[at] = (normed * g_ref + s_ref).astype(BF)
        keep = ref[2 * band :, :band].astype(F32)
        kp_ref[at] = jnp.transpose(keep)[:, 0:1]
        keeps.append(keep[0:1])
    bias_ref[...] = jnp.where(jnp.concatenate(keeps, 1) > 0, 0.0, MASKED_SCORE)
    lane = lax.broadcasted_iota(jnp.int32, (side, own), 1)
    sign = jnp.where((lane & (lay.head // 2)) == 0, -1.0, 1.0).astype(F32)
    col = lax.broadcasted_iota(jnp.int32, (side, own), 0).astype(F32) * f_ref[:, :own]
    col_cos, col_sin = jnp.cos(col), jnp.sin(col)
    row_index = me_ref[3]
    for b, flip in enumerate((0, 2, 1, 3)):
        first = ((row_index ^ flip) * lay.band_rows).astype(F32)
        rows = (lax.broadcasted_iota(jnp.int32, (8, own), 0).astype(F32) + first) * f_ref[:, own:]
        row_cos, row_sin = jnp.cos(rows), jnp.sin(rows)
        for r in range(lay.band_rows):
            at = slice(b * band + r * side, b * band + (r + 1) * side)
            rc, rs = row_cos[r : r + 1], row_sin[r : r + 1]
            cos_ref[at] = col_cos * rc - col_sin * rs
            sin_ref[at] = (col_sin * rc + col_cos * rs) * sign
    block = lay.width // 4
    for y_rel in range(2):
        y_side = me_ref[1] ^ y_rel
        load_pieces(lay, me_ref, w_refs, y_rel, w_all.at[y_side])
    acts = a_ref[...]
    w0, w1 = w_all[0].reshape(lay.width, -1), w_all[1].reshape(lay.width, -1)
    p_out[:, :block], p_out[:, block:] = w0[:, 3 * third :], w1[:, 3 * third :]
    w0, w1 = w0[:, : 3 * third], w1[:, : 3 * third]
    w_out[0], w_out[1] = w0, w1
    left = nn(acts, w0) + b_ref[:, : 3 * third]
    right = nn(acts, w1) + b_ref[:, 3 * third :]
    query, key = left[:, :own], jnp.concatenate([left[:, own:], right[:, :third]], 1)
    cos, sin = cos_ref[...], sin_ref[...]
    q_ref[...] = (query * cos + halves_of(lay, query) * sin).astype(BF)
    k_ref[...] = (key * cos + halves_of(lay, key) * sin).astype(BF)
    v_ref[...] = right[:, third:].astype(BF)


def attend_kernel(lay, chunk, q_ref, k_ref, v_ref, bias_ref, o_ref, p_ref):
    head = lay.head
    pair = 2 * head
    scale = head**-0.5

    def step(n, carry):
        at = pl.ds(pl.multiple_of(n * pair, pair), pair)
        keys, values = k_ref[:, at], v_ref[:, at]
        for start in range(0, lay.length, chunk):
            rows = slice(start, start + chunk)
            query = q_ref[rows, at] * jnp.asarray(scale, BF)
            lane = lax.broadcasted_iota(jnp.int32, query.shape, 1)
            outs = []
            for h in range(2):
                mine = (lane < head) if h == 0 else (lane >= head)
                score = nt(jnp.where(mine, query, jnp.zeros_like(query)), keys) + bias_ref[...]
                power = jnp.exp(score - jnp.max(score, -1, keepdims=True))
                weights = (power * (1.0 / jnp.sum(power, -1, keepdims=True))).astype(BF)
                p_ref[2 * n + h, rows] = weights
                outs.append(nn(weights, values))
            o_ref[rows, at] = jnp.where(lane < head, outs[0], outs[1]).astype(BF)
        return carry

    lax.fori_loop(0, HEADS // 4, step, 0)


def middle_kernel(lay, me_ref, t0, t1, t2, t3, ob_ref, oo_ref, p_ref, po_ref, vec_ref, x1_ref, a2_ref, wp_ref):
    band, third, half = lay.band, lay.third, lay.length // 2
    c = me_ref[2]
    block = lay.width // 4
    pb_ref, g_ref, s_ref = (vec_ref[:, lay.at[n]] for n in ("proj_bias", "mlp_gain", "mlp_shift"))
    for y_side in range(2):
        mine, other = (ref[:, y_side * block : (y_side + 1) * block] for ref in (p_ref, po_ref))
        wp_ref[:, 2 * y_side * block : 2 * (y_side + 1) * block] = jnp.where(
            c == 0, jnp.concatenate([mine, other], 1), jnp.concatenate([other, mine], 1)
        )
    low = [pl.ds(pl.multiple_of((2 * s + c) * third, third), third) for s in range(2)]
    high = [pl.ds(pl.multiple_of((2 * s + 1 - c) * third, third), third) for s in range(2)]
    own_w = jnp.concatenate([wp_ref[low[0]], wp_ref[low[1]]], 0)
    other_w = jnp.concatenate([wp_ref[high[0]], wp_ref[high[1]]], 0)
    other = jnp.concatenate([oo_ref[half:], oo_ref[:half]], 0)
    x1_ref[...] = nn(ob_ref[...], own_w) + nn(other, other_w) + pb_ref
    for b, ref in enumerate((t0, t1, t2, t3)):
        at = slice(b * band, (b + 1) * band)
        x1 = x1_ref[at] + ref[:band].astype(F32)
        x1_ref[at] = x1
        normed, _ = normed_rows(x1)
        a2_ref[at] = (normed * g_ref + s_ref).astype(BF)


def mlp_kernel(lay, n_w, n_g, chunk, me_ref, t0, t1, t2, t3, kp_ref, x1_ref, a2_ref, *refs):
    w_refs = refs[:n_w]
    vec_ref, part_ref, msend_ref, dn_ref, dnsend_ref, ubg_ref, dbg_ref = refs[n_w : n_w + 7]
    grads = refs[n_w + 7 : n_w + 7 + n_g]
    dm_ref, at_ref, dt_ref, m_ref, w_all, g_tmp = refs[n_w + 7 + n_g :]
    band, width, half = lay.band, lay.width, lay.length // 2
    up_bias = lay.at["up_bias"].start
    for b, ref in enumerate((t0, t1, t2, t3)):
        at = slice(b * band, (b + 1) * band)
        dm_ref[at] = (ref[band : 2 * band].astype(F32) * kp_ref[at]).astype(BF)
    at_ref[...] = a2_ref[...].T
    dt_ref[...] = dm_ref[...].T
    dbg_ref[...] = column_sum(dm_ref[:half].astype(F32))
    m_ref[...] = jnp.zeros_like(m_ref)
    dn_ref[...] = jnp.zeros_like(dn_ref)
    shape = lay.tiles + (chunk,)

    for y_rel in range(2):
        load_pieces(lay, me_ref, w_refs, y_rel, w_all)

        def step(n, carry, y_rel=y_rel):
            at = pl.ds(pl.multiple_of(n * chunk, chunk), chunk)
            d_at = pl.ds(pl.multiple_of(n * chunk + width, chunk), chunk)
            b_at = n * chunk + (me_ref[1] ^ y_rel) * width
            up = w_all[:, :, at].reshape(width, chunk)
            down = w_all[:, :, d_at].reshape(width, chunk)
            acts = a2_ref[...]
            dm = dm_ref[...]
            pre = nn(acts, up) + vec_ref[:, pl.ds(pl.multiple_of(b_at + up_bias, 128), chunk)]
            cdf = 0.5 * (1.0 + lax.erf(pre * 0.7071067811865476))
            slope = cdf + pre * (jnp.exp(-0.5 * pre * pre) * 0.3989422804014327)
            act = (pre * cdf).astype(BF)
            du = (nn(dm, down) * slope).astype(BF)
            ubg_ref[:, pl.ds(pl.multiple_of(b_at, chunk), chunk)] = column_sum(du.astype(F32))
            m_ref[...] += nt(act, down)
            dn_ref[...] += nt(du, up)
            g_tmp[...] = nn(at_ref[...], du).astype(BF).reshape(shape)
            store_pieces(lay, me_ref, grads, y_rel, at, g_tmp)
            g_tmp[...] = nn(dt_ref[...], act).astype(BF).reshape(shape)
            store_pieces(lay, me_ref, grads, y_rel, d_at, g_tmp)
            return carry

        lax.fori_loop(0, width // chunk, step, 0)
    part_ref[...] = x1_ref[:half] + m_ref[:half] + vec_ref[:, lay.at["down_bias"]]
    msend_ref[...] = m_ref[half:].astype(BF)
    dnsend_ref[...] = dn_ref[...].astype(BF)


def back_kernel(
    lay, n_g, chunk, me_ref, t0, t1, t2, t3, kp_ref, x1_ref, dn_ref, came_ref, vec_ref, wp_ref, ob_ref, oo_ref, q_ref, k_ref, v_ref,
    p_ref, cos_ref, sin_ref, a_ref, *refs,
):
    dx_ref, pbg_ref, gg_ref, sg_ref, bqk_ref, bv_ref, fg_ref, dqkv_ref = refs[:8]
    grads = refs[8 : 8 + n_g]
    dxb_ref, dob_ref, dq_ref, dk_ref, dv_ref, g_tmp = refs[8 + n_g :]
    g_ref = vec_ref[:, lay.at["mlp_gain"]]
    band, side, own, third, half, head = lay.band, lay.side, lay.own, lay.third, lay.length // 2, lay.head
    c = me_ref[2]
    pair = 2 * head
    scale = head**-0.5
    gg, sg, pbg = 0.0, 0.0, 0.0
    for b, ref in enumerate((t0, t1, t2, t3)):
        at = slice(b * band, (b + 1) * band)
        away = slice((b ^ 2) * band, ((b ^ 2) + 1) * band)
        dn = dn_ref[at] + came_ref[away].astype(F32)
        normed, inverse = normed_rows(x1_ref[at])
        dx = ref[band : 2 * band].astype(F32) * kp_ref[at] + norm_back(dn, normed, inverse, g_ref)
        dxb = dx.astype(BF)
        dxb_ref[at] = dxb
        if b < 2:
            dx_ref[at] = dx
            gg = gg + column_sum(dn * normed)
            sg = sg + column_sum(dn)
            pbg = pbg + column_sum(dxb.astype(F32))
    gg_ref[...], sg_ref[...], pbg_ref[...] = gg, sg, pbg
    low = [pl.ds(pl.multiple_of((2 * s + c) * third, third), third) for s in range(2)]
    own_w = jnp.concatenate([wp_ref[low[0]], wp_ref[low[1]]], 0)
    dxb = dxb_ref[...]
    dob_ref[...] = nt(dxb, own_w).astype(BF)
    block = lay.width // 4
    zero = jnp.concatenate([dxb[:, :block], dxb[:, 2 * block : 3 * block]], 1)
    one = jnp.concatenate([dxb[:, block : 2 * block], dxb[:, 3 * block :]], 1)
    cols = jnp.where(c == 0, zero, one)
    other = jnp.concatenate([oo_ref[half:], oo_ref[:half]], 0)
    mine_g, other_g = tn(ob_ref[...], cols).astype(BF), tn(other, cols).astype(BF)
    zero, one = jnp.where(c == 0, mine_g, other_g), jnp.where(c == 0, other_g, mine_g)
    p_grad = jnp.concatenate([zero[:third], one[:third], zero[third:], one[third:]], 0)

    def step(n, carry):
        at = pl.ds(pl.multiple_of(n * pair, pair), pair)
        keys, values = k_ref[:, at], v_ref[:, at]
        for start in range(0, lay.length, chunk):
            rows = slice(start, start + chunk)
            query, dob = q_ref[rows, at], dob_ref[rows, at]
            lane = lax.broadcasted_iota(jnp.int32, query.shape, 1)
            dqs, dks, dvs = [], [], []
            for h in range(2):
                mine = (lane < head) if h == 0 else (lane >= head)
                weights = p_ref[2 * n + h, rows]
                soft = weights.astype(F32)
                dp = nt(jnp.where(mine, dob, jnp.zeros_like(dob)), values)
                ds = (soft * (dp - jnp.sum(soft * dp, -1, keepdims=True))).astype(BF)
                dqs.append(nn(ds, keys))
                dks.append(tn(ds, query))
                dvs.append(tn(weights, dob))
            dq_ref[rows, at] = jnp.where(lane < head, dqs[0], dqs[1]) * scale
            lane = lax.broadcasted_iota(jnp.int32, keys.shape, 1)
            dk = jnp.where(lane < head, dks[0], dks[1]) * scale
            dv = jnp.where(lane < head, dvs[0], dvs[1])
            if start == 0:
                dk_ref[:, at] = dk
                dv_ref[:, at] = dv
            else:
                dk_ref[:, at] += dk
                dv_ref[:, at] += dv
        return carry

    lax.fori_loop(0, HEADS // 4, step, 0)
    cos, sin = cos_ref[...], sin_ref[...]
    dq, dk = dq_ref[...], dk_ref[...]
    dqkv_ref[:, :own] = (dq * cos + halves_of(lay, dq * sin)).astype(BF)
    dqkv_ref[:, own : 2 * own] = (dk * cos + halves_of(lay, dk * sin)).astype(BF)
    dqkv_ref[:, 2 * own :] = dv_ref[...].astype(BF)
    dq_ref[...] = dq * halves_of(lay, q_ref[...].astype(F32)) + dk * halves_of(lay, k_ref[...].astype(F32))
    by_col = jnp.zeros((side, own), F32)
    by_row = jnp.zeros((side, own), F32)
    for b, flip in enumerate((0, 2, 1, 3)):
        first = ((me_ref[3] ^ flip) * lay.band_rows).astype(F32)
        for r in range(lay.band_rows):
            turn = dq_ref[b * band + r * side : b * band + (r + 1) * side]
            by_col = by_col + turn
            by_row = by_row + turn * (first + r)
    lane = lax.broadcasted_iota(jnp.int32, (2, own), 1)
    sign = jnp.where((lane & (head // 2)) == 0, -1.0, 1.0).astype(F32)
    place = lax.broadcasted_iota(jnp.int32, (side, own), 0).astype(F32)
    both = jnp.concatenate([column_sum(by_col * place), column_sum(by_row)], 0) * sign
    both = jnp.where(sign < 0, both + halves_of(lay, both), 0.0)
    fg_ref[:, :own], fg_ref[:, own:] = both[0:1], both[1:2]
    bqk_ref[...] = column_sum(dqkv_ref[:, : 2 * own].astype(F32))
    bv_ref[...] = column_sum(dqkv_ref[:, 2 * own :].astype(F32))
    acts = a_ref[...]
    sides = []
    for y_side in range(2):
        grad = tn(acts, dqkv_ref[:, y_side * 3 * third : (y_side + 1) * 3 * third]).astype(BF)
        sides.append(jnp.concatenate([grad, p_grad[:, y_side * block : (y_side + 1) * block]], 1))
    y = me_ref[1]
    for y_rel in range(2):
        g_tmp[...] = jnp.where((y ^ y_rel) == 0, sides[0], sides[1]).reshape(g_tmp.shape)
        store_pieces(lay, me_ref, grads, y_rel, slice(None), g_tmp)


def last_kernel(lay, dqkv_ref, w_ref, keep_ref, send_ref):
    third, half = lay.third, lay.length // 2
    grad = nt(dqkv_ref[:, : 3 * third], w_ref[0]) + nt(dqkv_ref[:, 3 * third :], w_ref[1])
    keep_ref[...] = grad[:half]
    send_ref[...] = grad[half:].astype(BF)


def finish_kernel(lay, t0, t1, keep_ref, came_ref, dx_ref, vec_ref, out_ref, send_ref, gg_ref, sg_ref):
    band = lay.band
    g_ref = vec_ref[:, lay.at["attn_gain"]]
    gg, sg = 0.0, 0.0
    for b, ref in enumerate((t0, t1)):
        at = slice(b * band, (b + 1) * band)
        dn = keep_ref[at] + came_ref[at].astype(F32)
        normed, inverse = normed_rows(ref[:band].astype(F32))
        result = (dx_ref[at] + norm_back(dn, normed, inverse, g_ref)).astype(BF)
        if b == 0:
            out_ref[...] = result
        else:
            send_ref[...] = result
        gg = gg + column_sum(dn * normed)
        sg = sg + column_sum(dn)
    gg_ref[...], sg_ref[...] = gg, sg


def call(kernel, name, inputs, outs, scratch=(), smem=1, limit=16, us=1):
    return pl.pallas_call(
        kernel,
        out_shape=[jax.ShapeDtypeStruct(shape, dtype) for shape, dtype in outs],
        in_specs=[SMEM] * smem + [VMEM] * (len(inputs) - smem),
        out_specs=[VMEM] * len(outs),
        scratch_shapes=[pltpu.VMEM(shape, dtype) for shape, dtype in scratch],
        compiler_params=pltpu.CompilerParams(vmem_limit_bytes=limit * MIB),
        cost_estimate=pl.CostEstimate(flops=us * 1000000000, bytes_accessed=1024, transcendentals=0),
        name=name,
    )(*inputs)


class Slice:
    def __init__(self, lay):
        self.lay = lay
        self.img = lax.axis_index("img")
        self.row = lax.axis_index("row")
        self.y = self.row // 2
        self.c = self.row % 2
        self.facts = jnp.stack([self.img, self.y, self.c, self.row]).astype(jnp.int32)
        self.orders = (lay.high + [0, "y"], lay.high + ["y", 0])

    def swap(self, array, step):
        if step == "c":
            return lax.ppermute(array, "row", [(r, r ^ 1) for r in range(4)])
        if step == "y":
            return lax.ppermute(array, "row", [(r, r ^ 2) for r in range(4)])
        return lax.ppermute(array, "img", [(i, i ^ (1 << step)) for i in range(self.lay.img_count)])

    def gather(self, piece, order):
        held = piece[None]
        for step in order:
            held = jnp.concatenate([held, self.swap(held, step)], 0)
        return held

    def scatter(self, held, order):
        for step in reversed(order):
            half = held.shape[0] // 2
            came = self.swap(held[half:], step)
            held = (held[:half].astype(F32) + came.astype(F32)).astype(held.dtype)
        return held[0]

    def places(self, order):
        place = jnp.zeros((2, self.lay.img_count), jnp.int32)
        img = jnp.arange(self.lay.img_count, dtype=jnp.int32)[None, :] ^ self.img
        side = jnp.arange(2, dtype=jnp.int32)[:, None] ^ self.y
        for k, step in enumerate(order):
            bit = side if step == "y" else (img >> step) & 1
            place = place + (bit << k)
        return place

    def sources(self, order):
        place = self.places(order).reshape(-1)
        return jnp.zeros_like(place).at[place].set(jnp.arange(place.size, dtype=jnp.int32))

    def gather_rows(self, piece, name):
        lay = self.lay
        if not lay.aligned:
            base = self.gather(piece, lay.high)
            whole = []
            for part, order in enumerate(self.orders):
                held = base[:, part * lay.half_rows : (part + 1) * lay.half_rows]
                held = self.gather(held, order[-2:]).reshape((-1,) + held.shape[1:])
                whole.append(jnp.take(held, self.places(order), axis=0))
            return [jnp.concatenate(whole, 2).reshape((2,) + lay.tiles + piece.shape[1:])]
        pieces = [piece]
        for step in lay.high:
            pieces += [self.swap(p, step) for p in pieces]
        shape = (len(pieces), lay.half_rows, piece.shape[1])
        halves = call(functools.partial(merge_kernel, lay), name, pieces, [(shape, BF)] * 2, smem=0)
        parts = []
        for order, held in zip(self.orders, halves):
            near = self.swap(held, order[-2])
            parts += [held, near, self.swap(held, order[-1]), self.swap(near, order[-1])]
        return parts

    def grad_shapes(self, columns):
        lay = self.lay
        if lay.aligned:
            return [((lay.img_count, lay.half_rows, columns), BF)] * 4
        return [((2,) + lay.tiles + (columns,), BF)]

    def scatter_rows(self, parts):
        lay = self.lay
        if not lay.aligned:
            pieces = parts[0].reshape(2, lay.img_count, lay.rows, parts[0].shape[3])
            parts = []
            for part, order in enumerate(self.orders):
                mine = pieces[:, :, part * lay.half_rows : (part + 1) * lay.half_rows]
                mine = jnp.take(mine.reshape((-1,) + mine.shape[2:]), self.sources(order), axis=0)
                parts += [mine[: lay.img_count], mine[lay.img_count :]]
        sums = []
        for part, order in enumerate(self.orders):
            keep, send = parts[2 * part : 2 * part + 2]
            held = (keep.astype(F32) + self.swap(send, order[-1]).astype(F32)).astype(BF)
            half = lay.img_count // 2
            sums.append((held[:half].astype(F32) + self.swap(held[half:], order[-2]).astype(F32)).astype(BF))
        return self.scatter(jnp.concatenate(sums, 1), lay.high)


NAMES = ("qkv_bias", "proj_bias", "attn_gain", "attn_shift", "mlp_gain", "mlp_shift", "up_bias", "down_bias", "freqs")


def plan_vectors(lay):
    width, third, pairs = lay.width, lay.third, lay.head // 2
    devices = lay.img_count * 4
    heads = np.arange(HEADS).reshape(2, 2, HEADS // 4)

    def by_core(count, shape):
        return [np.take(np.arange(count).reshape(shape), core, len(shape) - 2).reshape(-1) for core in range(2)]

    plain = [np.arange(width)] * 2
    up = by_core(4 * width, (2, 2, width))
    freqs = []
    for core in range(2):
        pick = np.arange(width).reshape(2, HEADS, pairs)[:, heads[:, core].reshape(-1)]
        freqs.append(np.stack([pick, pick], 2).reshape(-1))
    qkv, qk, v = (by_core(n * width, (n, 2, 2, third)) for n in (3, 2, 1))

    def lay_out(members):
        plan, tables, start, offset = [], [[], [], [], []], 0, 0
        for pick, count in members:
            count //= devices
            plan.append((start, pick[0].size, offset, count))
            for core in range(2):
                tables[2 * core].append(pick[core] // count)
                tables[2 * core + 1].append(pick[core] % count)
            start += pick[0].size
            offset += count
        return plan, jnp.asarray(np.stack([np.concatenate(t) for t in tables]).astype(np.int32))

    rest = [(plain, width)] * 5 + [(up, 4 * width), (plain, width), (freqs, width)]
    given = lay_out([(qkv, 3 * width)] + rest)
    lay.at = {name: slice(p[0], p[0] + p[1]) for name, p in zip(NAMES, given[0])}
    return given, lay_out([(qk, 2 * width), (v, width)] + rest)


def make_body(img_count):
    def body(
        tokens, keep_mask, cotangent, qkv_weight, qkv_bias, proj_weight, proj_bias, attn_gain, attn_shift,
        mlp_gain, mlp_shift, up_weight, up_bias, down_weight, down_bias, rope_freqs,
    ):
        lay = Layout(img_count, tokens, qkv_weight.shape[0])
        me = Slice(lay)
        y, c, facts = me.y, me.c, me.facts
        images, band, width, length = lay.images, lay.band, lay.width, lay.length
        heads = HEADS // 2
        own, third = lay.own, lay.third
        half = length // 2
        block = proj_weight.shape[1]
        hidden = up_weight.shape[1]
        devices = img_count * 4
        vectors = (qkv_bias, proj_bias, attn_gain, attn_shift, mlp_gain, mlp_shift, up_bias, down_bias, rope_freqs)
        (plan, table), (grad_plan, grad_table) = plan_vectors(lay)

        def pick(flag, zero, one):
            return jnp.where(flag == 0, zero, one)

        def kernel(function, name, inputs, outs, scratch=(), **options):
            return call(functools.partial(function, lay), name, inputs, outs, scratch, **options)

        pack_rows = 2 * band + 16
        mine, other, third_send, first_piece, second_piece = kernel(
            pack_kernel, "pack",
            [facts, tokens.reshape(images, band, width), cotangent.reshape(images, band, width), keep_mask, qkv_weight, proj_weight,
             up_weight, down_weight.T, *[v.reshape(1, -1) for v in vectors]],
            [((pack_rows, width), BF), ((pack_rows, width), BF), ((lay.rows, 2 * 128), BF), ((lay.rows, 2 * third + block), BF),
             ((lay.rows, 2 * hidden), BF)], limit=12,
        )
        third_came = me.swap(third_send, "c")
        near = me.swap(other, "y")
        bands = [mine, near, me.swap(mine, "c"), me.swap(near, "c")]
        (first_piece,) = kernel(fit_kernel, "fit", [facts, third_came, first_piece], [((lay.rows, 3 * third + block), BF)])
        first = me.gather_rows(first_piece, "merge_first")
        second = me.gather_rows(second_piece, "merge_second")
        held = jnp.concatenate([b[2 * band + 1 : 2 * band + 2] for b in bands], 0)[None]
        vec_order = lay.high + [0]
        for step in vec_order:
            held = jnp.concatenate([held, me.swap(held, step)], 0)
        (vec,) = call(
            functools.partial(unpack_kernel, lay, plan), "unpack", [facts, held.reshape(devices, width), table],
            [((1, table.shape[1]), F32)], limit=24,
        )

        n_w = len(first)
        n_g = len(me.grad_shapes(1))
        a1, q, k, v, w_qkv, p_cols, cos, sin, kp, mask_bias = call(
            functools.partial(project_kernel, lay, n_w), "qkv", [facts, *bands, *first, vec],
            [((length, width), BF), ((length, own), BF), ((length, own), BF), ((length, own), BF), ((2, width, 3 * third), BF),
             ((width, 2 * block), BF), ((length, own), F32), ((length, own), F32), ((length, 1), F32), ((1, length), F32)],
            [((2,) + lay.tiles + (3 * third + block,), BF)], limit=24, us=5,
        )
        p_other = me.swap(p_cols, "c")
        ob, p = call(
            functools.partial(attend_kernel, lay, band), "attend", [q, k, v, mask_bias],
            [((length, own), BF), ((heads, length, length), BF)], smem=0, limit=12, us=11,
        )
        ob_other = me.swap(ob, "c")
        x1, a2, w_proj = call(
            functools.partial(middle_kernel, lay), "middle", [facts, *bands, ob, ob_other, p_cols, p_other, vec],
            [((length, width), F32), ((length, width), BF), ((width, width), BF)], limit=16, us=3,
        )
        part, m_send, dn, dn_send, d_up_bias, d_down_bias, *second_grads = call(
            functools.partial(mlp_kernel, lay, n_w, n_g, 256), "mlp", [facts, *bands, kp, x1, a2, *second, vec],
            [((half, width), F32), ((half, width), BF), ((length, width), F32), ((length, width), BF), ((1, 2 * hidden), F32),
             ((1, width), F32), *me.grad_shapes(2 * hidden)],
            [((length, width), BF), ((width, length), BF), ((width, length), BF), ((length, width), F32),
             (lay.tiles + (2 * hidden,), BF), (lay.tiles + (256,), BF)], limit=32, us=24,
        )
        d_second = me.scatter_rows(second_grads)
        dn_came = me.swap(dn_send, "c")
        m_came = me.swap(m_send, "c")
        out_half = (kp[:half] * (part + m_came.astype(F32))).astype(BF)
        dx_half, d_proj_bias, d_g2, d_s2, d_qk_bias, d_v_bias, d_freqs, dqkv, *first_grads = call(
            functools.partial(back_kernel, lay, n_g, band), "back",
            [facts, *bands, kp, x1, dn, dn_came, vec, w_proj, ob, ob_other, q, k, v, p, cos, sin, a1],
            [((half, width), F32), ((1, width), F32), ((1, width), F32), ((1, width), F32), ((1, 2 * own), F32), ((1, own), F32),
             ((1, 2 * own), F32), ((length, 3 * own), BF), *me.grad_shapes(3 * third + block)],
            [((length, width), BF), ((length, own), BF), ((length, own), F32), ((length, own), F32), ((length, own), F32),
             (lay.tiles + (3 * third + block,), BF)], limit=32, us=24,
        )
        d_first = me.scatter_rows(first_grads)
        dn1_keep, dn1_send = call(
            functools.partial(last_kernel, lay), "last", [dqkv, w_qkv], [((half, width), F32), ((half, width), BF)], smem=0, us=2
        )
        dn1_came = me.swap(dn1_send, "c")
        tg_keep, tg_send, d_g1, d_s1 = call(
            functools.partial(finish_kernel, lay), "finish", [bands[0], bands[1], dn1_keep, dn1_came, dx_half, vec],
            [((band, width), BF), ((band, width), BF), ((1, width), F32), ((1, width), F32)], smem=0,
        )

        grads = [d_qk_bias, d_v_bias, d_proj_bias, d_g1, d_s1, d_g2, d_s2, d_up_bias, d_down_bias, d_freqs]
        sums = call(
            functools.partial(repack_kernel, lay, grad_plan), "repack", [facts, grad_table, *grads], [((devices, 384), F32)],
            limit=24,
        )[0].reshape(img_count, 4, 384)
        for step in reversed(vec_order):
            count = sums.shape[0] // 2
            sums = sums[:count] + me.swap(sums[count:], step)
        sums = sums[0]
        sums = sums[:2] + me.swap(sums[2:], "c")
        total = sums[0] + me.swap(sums[1], "y")
        r = [total[offset : offset + count] for _, _, offset, count in grad_plan]

        def to_images(keep, send):
            came = me.swap(send, "y")
            return pick(y, jnp.stack([keep, came]), jnp.stack([came, keep])).reshape(tokens.shape)

        layer_out = to_images(out_half[:band], out_half[band:])
        tokens_grad = to_images(tg_keep, tg_send)

        d_up = d_second[:, :hidden].astype(F32)
        d_down = d_second[:, hidden:].T.astype(F32)
        d0, d1, d2 = d_first[:, :third], d_first[:, third : 2 * third], d_first[:, 2 * third : 3 * third]
        came = me.swap(pick(c, d2, d0), "c")
        d_qkv = pick(c, jnp.concatenate([d0, came, d1], 1), jnp.concatenate([d1, came, d2], 1)).astype(F32)
        d_proj = d_first[:, 3 * third :].astype(F32)
        return (
            layer_out, tokens_grad, d_qkv, r[0], r[1], d_proj, r[2], r[3], r[4], r[5], r[6], d_up, r[7], d_down, r[8], r[9],
        )

    return body


def solution(mesh):
    split = P(("img", "row"))
    both = P("img", "row")
    field = P("img", "row", None, None)
    return jax.shard_map(
        make_body(mesh.shape["img"]),
        mesh=mesh,
        in_specs=(
            field, P("img", "row", None), field, both, split, both, split, split, split, split, split, both, split,
            P("row", "img"), split, split,
        ),
        out_specs=(
            field, field, both, split, split, both, split, split, split, split, split, both, split, P("row", "img"),
            split, split,
        ),
        check_vma=False,
    )
```

```python
import functools

import jax
import jax.numpy as jnp
import numpy as np
from jax import lax
from jax.experimental import pallas as pl
from jax.experimental.pallas import tpu as pltpu
from jax.sharding import PartitionSpec as P

HEADS = 12
NORM_EPSILON = 1e-06
MASKED_SCORE = -1e30
BF = jnp.bfloat16
F32 = jnp.float32
MIB = 2**20
VMEM = pl.BlockSpec(memory_space=pltpu.VMEM)
HBM = pl.BlockSpec(memory_space=pltpu.MemorySpace.HBM)
PACKED = 384


def dot(left, right, dims):
    return lax.dot_general(left, right, (dims, ((), ())), preferred_element_type=F32)


def nn(left, right):
    return dot(left, right, ((1,), (0,)))


def nt(left, right):
    return dot(left, right, ((1,), (1,)))


def tn(left, right):
    return dot(left, right, ((0,), (0,)))


def normed_rows(values):
    center = values - jnp.mean(values, -1, keepdims=True)
    inverse = lax.rsqrt(jnp.mean(center * center, -1, keepdims=True) + NORM_EPSILON)
    return center * inverse, inverse


def norm_back(grad, normed, inverse, gain):
    scaled = grad * gain
    centred = scaled - jnp.mean(scaled, -1, keepdims=True)
    return inverse * (centred - normed * jnp.mean(scaled * normed, -1, keepdims=True))


def column_sum(value):
    return jnp.sum(value, 0, keepdims=True)


def here():
    row = lax.axis_index("row")
    return lax.axis_index("img"), row >> 1, row & 1, row


class Layout:
    def __init__(self, img_count, tokens, rows):
        self.img_count = img_count
        self.bits = img_count.bit_length() - 1
        self.rows = rows
        self.half_rows = rows // 2
        self.aligned = rows % 32 == 0
        self.images, self.band_rows, self.side, self.width = tokens.shape
        self.band = self.band_rows * self.side
        self.length = 4 * self.band
        self.head = self.width // HEADS
        self.own = self.width // 2
        self.third = self.own // 2
        self.high = list(range(self.bits - 1, 0, -1))
        self.tiles = (img_count, rows) if self.aligned else (1, self.width)

    def slots(self, img_rel, y_rel):
        high = 0
        for k, bit in enumerate(self.high):
            high = high + (((img_rel >> bit) & 1) << k)
        top = self.bits - 1
        return (high + ((img_rel & 1) << top), y_rel), (high + (y_rel << top), img_rel & 1)


def load_pieces(lay, refs, y_rel, target):
    if not lay.aligned:
        target[...] = refs[0][here()[1] ^ y_rel]
        return
    half = lay.half_rows
    count = len(refs) // 2
    for img_rel in range(lay.img_count):
        for part, (slot, last) in enumerate(lay.slots(img_rel, y_rel)):
            which, slot = divmod((slot + last * lay.img_count) * count, 2 * lay.img_count)
            ref, slot = refs[part * count + which], slot // count
            target[img_rel ^ here()[0], part * half : (part + 1) * half] = ref[slot, :half]


def store_pieces(lay, refs, y_rel, columns, source):
    if not lay.aligned:
        refs[0][here()[1] ^ y_rel, :, :, columns] = source[...]
        return
    half = lay.half_rows
    for img_rel in range(lay.img_count):
        for part, (slot, last) in enumerate(lay.slots(img_rel, y_rel)):
            refs[2 * part + last][slot, :half, columns] = source[img_rel ^ here()[0], part * half : (part + 1) * half]


def halves_of(lay, value):
    pairs = lay.head // 2
    lane = lax.broadcasted_iota(jnp.int32, value.shape, 1)
    width = value.shape[1]
    first = (lane & pairs) == 0
    return jnp.where(first, pltpu.roll(value, width - pairs, 1), pltpu.roll(value, pairs, 1))


def pack_kernel(lay, *refs):
    tok, cot, mask, qkv, proj, up, down, *vectors = refs[:16]
    mine_ref, other_ref, third_ref, first_ref, second_ref = refs[16:21]
    mask_in, qkv_in, proj_in, up_in, down_in, *vectors_in = refs[21:35]
    sems = refs[35]
    y = here()[1]
    band, third, width, rows = lay.band, lay.third, lay.width, lay.rows
    pairs = [(qkv, qkv_in), (proj, proj_in), *zip(vectors, vectors_in), (up, up_in), (down, down_in), (mask, mask_in)]
    for ref, which in ((other_ref, 1 - y), (mine_ref, y)):
        pairs += [(tok.at[which], ref.at[:band]), (cot.at[which], ref.at[band : 2 * band])]
    copies = [pltpu.make_async_copy(source, target, sems.at[n]) for n, (source, target) in enumerate(pairs)]
    for copy in copies:
        copy.start()
    for copy in copies[:11]:
        copy.wait()
    packed = jnp.concatenate([v[...] for v in vectors_in], 1)
    packed = jnp.concatenate([packed, jnp.zeros((1, PACKED - packed.shape[1]), F32)], 1).astype(BF)
    third_ref[:, :third] = qkv_in[:, third : 2 * third].astype(BF)
    third_ref[:, third:] = jnp.zeros((rows, third_ref.shape[1] - third), BF)
    third_ref[0:1, third_ref.shape[1] - PACKED :] = packed
    first_ref[:rows, :third] = qkv_in[:, :third].astype(BF)
    first_ref[:rows, third : 2 * third] = qkv_in[:, 2 * third :].astype(BF)
    first_ref[:rows, 2 * third :] = proj_in[...].astype(BF)
    first_ref[rows:] = jnp.zeros((16, first_ref.shape[1]), BF)
    first_ref[rows : rows + 1, :PACKED] = packed
    for copy in copies[11:]:
        copy.wait()
    second_ref[:, :width] = up_in[...].astype(BF)
    second_ref[:, width:] = down_in[...].astype(BF)
    for ref, which in ((mine_ref, y), (other_ref, 1 - y)):
        keep = mask_in[which].astype(F32)
        flat = jnp.concatenate([keep[r : r + 1] for r in range(lay.band_rows)], 1)
        flat = jnp.concatenate([flat, jnp.zeros((1, width - band), F32)], 1)
        ref[2 * band :] = jnp.concatenate([flat, jnp.zeros((15, width), F32)], 0).astype(BF)


def fit_kernel(lay, came_ref, first_ref, out_ref):
    third, rows = lay.third, lay.rows
    c = here()[2]
    t0, t2, came = first_ref[:rows, :third], first_ref[:rows, third : 2 * third], came_ref[:, :third]
    out_ref[:rows, : 3 * third] = jnp.where(c == 0, jnp.concatenate([t0, t2, came], 1), jnp.concatenate([came, t0, t2], 1))
    out_ref[:rows, 3 * third :] = first_ref[:rows, 2 * third :]
    out_ref[rows:] = jnp.zeros((16, out_ref.shape[1]), BF)
    out_ref[rows : rows + 1, :PACKED] = first_ref[rows : rows + 1, :PACKED]
    out_ref[rows : rows + 1, PACKED : 2 * PACKED] = came_ref[0:1, came_ref.shape[1] - PACKED :]


def merge_kernel(lay, *refs):
    pieces, (top_ref, bottom_ref) = refs[:-2], refs[-2:]
    half = lay.half_rows
    for k, ref in enumerate(pieces):
        top_ref[k] = ref[:half]
        bottom_ref[k] = ref[half:]


def join_kernel(lay, *refs):
    for part in range(2):
        near, far = refs[2 * part : 2 * part + 2]
        refs[4 + part][: near.shape[0]] = near[...]
        refs[4 + part][near.shape[0] :] = far[...]


def owner_mask(lay, c_rel, table_row):
    place = lax.broadcasted_iota(jnp.int32, (2 * lay.img_count, 1), 0)
    row = here()[3] ^ (((place >> (lay.bits - 1)) & 1) * 2 + c_rel)
    img_rel = place >> lay.bits
    for k, bit in enumerate(lay.high):
        img_rel = img_rel | (((place >> k) & 1) << bit)
    return ((img_rel ^ here()[0]) * 4 + row) == table_row


def owners(table_ref, at, c):
    owner = jnp.where(c == 0, table_ref[0:1, at], table_ref[2:3, at])
    entry = jnp.where(c == 0, table_ref[1:2, at], table_ref[3:4, at])
    return owner, entry


def unpack_kernel(lay, plan, n_v, table_ref, *refs):
    v_refs, out_ref = refs[:n_v], refs[n_v]
    if lay.aligned:
        half = lay.half_rows
        gathered = jnp.concatenate([ref[k, half : half + 16][0:1] for ref in v_refs for k in range(ref.shape[0])], 0)
    else:
        gathered = v_refs[0][...]
    for start, size, offset, count in plan:
        at = slice(start, start + size)
        owner, entry = owners(table_ref, at, here()[2])
        spread = (lax.broadcasted_iota(jnp.int32, (count, size), 0) == entry).astype(F32).astype(BF)
        total = 0.0
        for c_rel in range(2):
            rows = nn(gathered[:, c_rel * PACKED + offset : c_rel * PACKED + offset + count], spread)
            total = total + column_sum(jnp.where(owner_mask(lay, c_rel, owner), rows, 0.0))
        out_ref[:, at] = total


def repack(lay, plan, table_ref, grads, refs):
    sides = []
    for c_rel in range(2):
        parts = []
        for grad, (start, size, offset, count) in zip(grads, plan):
            owner, entry = owners(table_ref, slice(start, start + size), here()[2])
            spread = (lax.broadcasted_iota(jnp.int32, (count, size), 0) == entry).astype(F32).astype(BF)
            rows = jnp.where(owner_mask(lay, c_rel, owner), grad, 0.0).astype(BF)
            parts.append(nt(rows, spread))
        used = sum(p.shape[1] for p in parts)
        sides += parts + [jnp.zeros((2 * lay.img_count, PACKED - used), F32)]
    rows = jnp.concatenate(sides, 1)
    if not lay.aligned:
        refs[1][...] = rows.astype(BF)
        return
    half, count = lay.half_rows, lay.img_count
    for j in range(2 * count):
        block = jnp.concatenate([rows[j : j + 1], jnp.zeros((15, rows.shape[1]), F32)], 0).astype(BF)
        refs[2 + j // count][j % count, half : half + 16, :] = block


def project_kernel(lay, n_w, t0, t1, t2, t3, *refs):
    w_refs = refs[:n_w]
    vec_ref, a_ref, q_ref, k_ref, v_ref, w_out, p_out, cos_ref, sin_ref, kp_ref, bias_ref, w_all = refs[n_w:]
    band, side, own, third = lay.band, lay.side, lay.own, lay.third
    g_ref, s_ref, b_ref = (vec_ref[:, lay.at[n]] for n in ("attn_gain", "attn_shift", "qkv_bias"))
    f_ref = vec_ref[:, lay.at["freqs"]]
    keeps = []
    for b, ref in enumerate((t0, t1, t2, t3)):
        at = slice(b * band, (b + 1) * band)
        normed, _ = normed_rows(ref[:band].astype(F32))
        a_ref[at] = (normed * g_ref + s_ref).astype(BF)
        keep = ref[2 * band :, :band].astype(F32)
        kp_ref[at] = jnp.transpose(keep)[:, 0:1]
        keeps.append(keep[0:1])
    bias_ref[...] = jnp.where(jnp.concatenate(keeps, 1) > 0, 0.0, MASKED_SCORE)
    lane = lax.broadcasted_iota(jnp.int32, (side, own), 1)
    sign = jnp.where((lane & (lay.head // 2)) == 0, -1.0, 1.0).astype(F32)
    col = lax.broadcasted_iota(jnp.int32, (side, own), 0).astype(F32) * f_ref[:, :own]
    col_cos, col_sin = jnp.cos(col), jnp.sin(col)
    row_index = here()[3]
    for b, flip in enumerate((0, 2, 1, 3)):
        first = ((row_index ^ flip) * lay.band_rows).astype(F32)
        rows = (lax.broadcasted_iota(jnp.int32, (8, own), 0).astype(F32) + first) * f_ref[:, own:]
        row_cos, row_sin = jnp.cos(rows), jnp.sin(rows)
        for r in range(lay.band_rows):
            at = slice(b * band + r * side, b * band + (r + 1) * side)
            rc, rs = row_cos[r : r + 1], row_sin[r : r + 1]
            cos_ref[at] = col_cos * rc - col_sin * rs
            sin_ref[at] = (col_sin * rc + col_cos * rs) * sign
    block = lay.width // 4
    for y_rel in range(2):
        y_side = here()[1] ^ y_rel
        load_pieces(lay, w_refs, y_rel, w_all.at[y_side])
    acts = a_ref[...]
    w0, w1 = w_all[0].reshape(lay.width, -1), w_all[1].reshape(lay.width, -1)
    p_out[:, :block], p_out[:, block:] = w0[:, 3 * third :], w1[:, 3 * third :]
    w0, w1 = w0[:, : 3 * third], w1[:, : 3 * third]
    w_out[0], w_out[1] = w0, w1
    left = nn(acts, w0) + b_ref[:, : 3 * third]
    right = nn(acts, w1) + b_ref[:, 3 * third :]
    query, key = left[:, :own], jnp.concatenate([left[:, own:], right[:, :third]], 1)
    cos, sin = cos_ref[...], sin_ref[...]
    q_ref[...] = (query * cos + halves_of(lay, query) * sin).astype(BF)
    k_ref[...] = (key * cos + halves_of(lay, key) * sin).astype(BF)
    v_ref[...] = right[:, third:].astype(BF)


def attend_kernel(lay, chunk, q_ref, k_ref, v_ref, bias_ref, o_ref, p_ref):
    head = lay.head
    pair = 2 * head
    scale = head**-0.5

    def step(n, carry):
        at = pl.ds(pl.multiple_of(n * pair, pair), pair)
        keys, values = k_ref[:, at], v_ref[:, at]
        for start in range(0, lay.length, chunk):
            rows = slice(start, start + chunk)
            query = q_ref[rows, at] * jnp.asarray(scale, BF)
            lane = lax.broadcasted_iota(jnp.int32, query.shape, 1)
            outs = []
            for h in range(2):
                mine = (lane < head) if h == 0 else (lane >= head)
                score = nt(jnp.where(mine, query, jnp.zeros_like(query)), keys) + bias_ref[...]
                power = jnp.exp(score - jnp.max(score, -1, keepdims=True))
                weights = (power * (1.0 / jnp.sum(power, -1, keepdims=True))).astype(BF)
                p_ref[2 * n + h, rows] = weights
                outs.append(nn(weights, values))
            o_ref[rows, at] = jnp.where(lane < head, outs[0], outs[1]).astype(BF)
        return carry

    lax.fori_loop(0, HEADS // 4, step, 0)


def middle_kernel(lay, t0, t1, t2, t3, ob_ref, oo_ref, p_ref, po_ref, vec_ref, x1_ref, a2_ref, wp_ref):
    band, third, half = lay.band, lay.third, lay.length // 2
    c = here()[2]
    block = lay.width // 4
    pb_ref, g_ref, s_ref = (vec_ref[:, lay.at[n]] for n in ("proj_bias", "mlp_gain", "mlp_shift"))
    for y_side in range(2):
        mine, other = (ref[:, y_side * block : (y_side + 1) * block] for ref in (p_ref, po_ref))
        wp_ref[:, 2 * y_side * block : 2 * (y_side + 1) * block] = jnp.where(
            c == 0, jnp.concatenate([mine, other], 1), jnp.concatenate([other, mine], 1)
        )
    low = [pl.ds(pl.multiple_of((2 * s + c) * third, third), third) for s in range(2)]
    high = [pl.ds(pl.multiple_of((2 * s + 1 - c) * third, third), third) for s in range(2)]
    own_w = jnp.concatenate([wp_ref[low[0]], wp_ref[low[1]]], 0)
    other_w = jnp.concatenate([wp_ref[high[0]], wp_ref[high[1]]], 0)
    other = jnp.concatenate([oo_ref[half:], oo_ref[:half]], 0)
    x1_ref[...] = nn(ob_ref[...], own_w) + nn(other, other_w) + pb_ref
    for b, ref in enumerate((t0, t1, t2, t3)):
        at = slice(b * band, (b + 1) * band)
        x1 = x1_ref[at] + ref[:band].astype(F32)
        x1_ref[at] = x1
        normed, _ = normed_rows(x1)
        a2_ref[at] = (normed * g_ref + s_ref).astype(BF)


def mlp_kernel(lay, n_w, n_g, chunk, t0, t1, t2, t3, kp_ref, x1_ref, a2_ref, *refs):
    w_refs = refs[:n_w]
    vec_ref, part_ref, msend_ref, dn_ref, dnsend_ref, ubg_ref, dbg_ref = refs[n_w : n_w + 7]
    grads = refs[n_w + 7 : n_w + 7 + n_g]
    dm_ref, at_ref, dt_ref, m_ref, w_all, g_tmp = refs[n_w + 7 + n_g :]
    band, width, half = lay.band, lay.width, lay.length // 2
    up_bias = lay.at["up_bias"].start
    for b, ref in enumerate((t0, t1, t2, t3)):
        at = slice(b * band, (b + 1) * band)
        dm_ref[at] = (ref[band : 2 * band].astype(F32) * kp_ref[at]).astype(BF)
    at_ref[...] = a2_ref[...].T
    dt_ref[...] = dm_ref[...].T
    dbg_ref[...] = column_sum(dm_ref[:half].astype(F32))
    m_ref[...] = jnp.zeros_like(m_ref)
    dn_ref[...] = jnp.zeros_like(dn_ref)
    shape = lay.tiles + (chunk,)

    for y_rel in range(2):
        load_pieces(lay, w_refs, y_rel, w_all)

        def step(n, carry, y_rel=y_rel):
            at = pl.ds(pl.multiple_of(n * chunk, chunk), chunk)
            d_at = pl.ds(pl.multiple_of(n * chunk + width, chunk), chunk)
            b_at = n * chunk + (here()[1] ^ y_rel) * width
            up = w_all[:, :, at].reshape(width, chunk)
            down = w_all[:, :, d_at].reshape(width, chunk)
            acts = a2_ref[...]
            dm = dm_ref[...]
            pre = nn(acts, up) + vec_ref[:, pl.ds(pl.multiple_of(b_at + up_bias, 128), chunk)]
            cdf = 0.5 * (1.0 + lax.erf(pre * 0.7071067811865476))
            slope = cdf + pre * (jnp.exp(-0.5 * pre * pre) * 0.3989422804014327)
            act = (pre * cdf).astype(BF)
            du = (nn(dm, down) * slope).astype(BF)
            ubg_ref[:, pl.ds(pl.multiple_of(b_at, chunk), chunk)] = column_sum(du.astype(F32))
            m_ref[...] += nt(act, down)
            dn_ref[...] += nt(du, up)
            g_tmp[...] = nn(at_ref[...], du).astype(BF).reshape(shape)
            store_pieces(lay, grads, y_rel, at, g_tmp)
            g_tmp[...] = nn(dt_ref[...], act).astype(BF).reshape(shape)
            store_pieces(lay, grads, y_rel, d_at, g_tmp)
            return carry

        lax.fori_loop(0, width // chunk, step, 0)
    part_ref[...] = x1_ref[:half] + m_ref[:half] + vec_ref[:, lay.at["down_bias"]]
    msend_ref[...] = m_ref[half:].astype(BF)
    dnsend_ref[...] = dn_ref[...].astype(BF)


def back_kernel(
    lay, plan, n_g, chunk, t0, t1, t2, t3, kp_ref, x1_ref, dn_ref, came_ref, vec_ref, wp_ref, ob_ref, oo_ref, q_ref, k_ref, v_ref,
    p_ref, cos_ref, sin_ref, a_ref, w_ref, table_ref, ubg_ref, dbg_ref, *refs,
):
    dx_ref, keep_ref, send_ref = refs[:3]
    grads = refs[3 : 3 + n_g]
    dxb_ref, dob_ref, dq_ref, dk_ref, dv_ref, g_tmp, dqkv_ref = refs[3 + n_g :]
    g_ref = vec_ref[:, lay.at["mlp_gain"]]
    band, side, own, third, half, head = lay.band, lay.side, lay.own, lay.third, lay.length // 2, lay.head
    c = here()[2]
    pair = 2 * head
    scale = head**-0.5
    gg, sg, pbg = 0.0, 0.0, 0.0
    for b, ref in enumerate((t0, t1, t2, t3)):
        at = slice(b * band, (b + 1) * band)
        away = slice((b ^ 2) * band, ((b ^ 2) + 1) * band)
        dn = dn_ref[at] + came_ref[away].astype(F32)
        normed, inverse = normed_rows(x1_ref[at])
        dx = ref[band : 2 * band].astype(F32) * kp_ref[at] + norm_back(dn, normed, inverse, g_ref)
        dxb = dx.astype(BF)
        dxb_ref[at] = dxb
        if b < 2:
            dx_ref[at] = dx
            gg = gg + column_sum(dn * normed)
            sg = sg + column_sum(dn)
            pbg = pbg + column_sum(dxb.astype(F32))
    low = [pl.ds(pl.multiple_of((2 * s + c) * third, third), third) for s in range(2)]
    own_w = jnp.concatenate([wp_ref[low[0]], wp_ref[low[1]]], 0)
    dxb = dxb_ref[...]
    dob_ref[...] = nt(dxb, own_w).astype(BF)
    block = lay.width // 4
    zero = jnp.concatenate([dxb[:, :block], dxb[:, 2 * block : 3 * block]], 1)
    one = jnp.concatenate([dxb[:, block : 2 * block], dxb[:, 3 * block :]], 1)
    cols = jnp.where(c == 0, zero, one)
    other = jnp.concatenate([oo_ref[half:], oo_ref[:half]], 0)
    mine_g, other_g = tn(ob_ref[...], cols).astype(BF), tn(other, cols).astype(BF)
    zero, one = jnp.where(c == 0, mine_g, other_g), jnp.where(c == 0, other_g, mine_g)
    p_grad = jnp.concatenate([zero[:third], one[:third], zero[third:], one[third:]], 0)

    def step(n, carry):
        at = pl.ds(pl.multiple_of(n * pair, pair), pair)
        keys, values = k_ref[:, at], v_ref[:, at]
        for start in range(0, lay.length, chunk):
            rows = slice(start, start + chunk)
            query, dob = q_ref[rows, at], dob_ref[rows, at]
            lane = lax.broadcasted_iota(jnp.int32, query.shape, 1)
            dqs, dks, dvs = [], [], []
            for h in range(2):
                mine = (lane < head) if h == 0 else (lane >= head)
                weights = p_ref[2 * n + h, rows]
                soft = weights.astype(F32)
                dp = nt(jnp.where(mine, dob, jnp.zeros_like(dob)), values)
                ds = (soft * (dp - jnp.sum(soft * dp, -1, keepdims=True))).astype(BF)
                dqs.append(nn(ds, keys))
                dks.append(tn(ds, query))
                dvs.append(tn(weights, dob))
            dq_ref[rows, at] = jnp.where(lane < head, dqs[0], dqs[1]) * scale
            lane = lax.broadcasted_iota(jnp.int32, keys.shape, 1)
            dk = jnp.where(lane < head, dks[0], dks[1]) * scale
            dv = jnp.where(lane < head, dvs[0], dvs[1])
            if start == 0:
                dk_ref[:, at] = dk
                dv_ref[:, at] = dv
            else:
                dk_ref[:, at] += dk
                dv_ref[:, at] += dv
        return carry

    lax.fori_loop(0, HEADS // 4, step, 0)
    cos, sin = cos_ref[...], sin_ref[...]
    dq, dk = dq_ref[...], dk_ref[...]
    dqkv_ref[:, :own] = (dq * cos + halves_of(lay, dq * sin)).astype(BF)
    dqkv_ref[:, own : 2 * own] = (dk * cos + halves_of(lay, dk * sin)).astype(BF)
    dqkv_ref[:, 2 * own :] = dv_ref[...].astype(BF)
    dq_ref[...] = dq * halves_of(lay, q_ref[...].astype(F32)) + dk * halves_of(lay, k_ref[...].astype(F32))
    by_col = jnp.zeros((side, own), F32)
    by_row = jnp.zeros((side, own), F32)
    for b, flip in enumerate((0, 2, 1, 3)):
        first = ((here()[3] ^ flip) * lay.band_rows).astype(F32)
        for r in range(lay.band_rows):
            turn = dq_ref[b * band + r * side : b * band + (r + 1) * side]
            by_col = by_col + turn
            by_row = by_row + turn * (first + r)
    lane = lax.broadcasted_iota(jnp.int32, (2, own), 1)
    sign = jnp.where((lane & (head // 2)) == 0, -1.0, 1.0).astype(F32)
    place = lax.broadcasted_iota(jnp.int32, (side, own), 0).astype(F32)
    both = jnp.concatenate([column_sum(by_col * place), column_sum(by_row)], 0) * sign
    both = jnp.where(sign < 0, both + halves_of(lay, both), 0.0)
    freqs = jnp.concatenate([both[0:1], both[1:2]], 1)
    bqk = column_sum(dqkv_ref[:, : 2 * own].astype(F32))
    bv = column_sum(dqkv_ref[:, 2 * own :].astype(F32))
    grad = nt(dqkv_ref[:, : 3 * third], w_ref[0]) + nt(dqkv_ref[:, 3 * third :], w_ref[1])
    keep_ref[...] = grad[:half]
    send_ref[...] = grad[half:].astype(BF)
    g1, s1 = 0.0, 0.0
    for b, ref in enumerate((t0, t1, t2, t3)):
        part = grad[b * band : (b + 1) * band]
        normed, _ = normed_rows(ref[:band].astype(F32))
        g1 = g1 + column_sum(part * normed)
        s1 = s1 + column_sum(part)
    repack(lay, plan, table_ref, [bqk, bv, pbg, g1, s1, gg, sg, ubg_ref[...], dbg_ref[...], freqs], grads)
    acts = a_ref[...]
    sides = []
    for y_side in range(2):
        grad = tn(acts, dqkv_ref[:, y_side * 3 * third : (y_side + 1) * 3 * third]).astype(BF)
        sides.append(jnp.concatenate([grad, p_grad[:, y_side * block : (y_side + 1) * block]], 1))
    y = here()[1]
    for y_rel in range(2):
        g_tmp[...] = jnp.where((y ^ y_rel) == 0, sides[0], sides[1]).reshape(g_tmp.shape)
        store_pieces(lay, grads, y_rel, slice(None), g_tmp)


def finish_kernel(lay, t0, t1, keep_ref, came_ref, dx_ref, vec_ref, out_ref, send_ref):
    band = lay.band
    g_ref = vec_ref[:, lay.at["attn_gain"]]
    for b, ref in enumerate((t0, t1)):
        at = slice(b * band, (b + 1) * band)
        dn = keep_ref[at] + came_ref[at].astype(F32)
        normed, inverse = normed_rows(ref[:band].astype(F32))
        result = (dx_ref[at] + norm_back(dn, normed, inverse, g_ref)).astype(BF)
        if b == 0:
            out_ref[...] = result
        else:
            send_ref[...] = result


def tail_send_kernel(lay, sum_ref, out_ref):
    third, rows = lay.third, lay.rows
    out_ref[:, :third] = jnp.where(here()[2] == 0, sum_ref[:rows, 2 * third : 3 * third], sum_ref[:rows, :third])
    out_ref[:, third:] = jnp.zeros((rows, out_ref.shape[1] - third), BF)
    out_ref[0:1, out_ref.shape[1] - PACKED :] = sum_ref[rows : rows + 1, PACKED : 2 * PACKED]


def tail_kernel(lay, plan, sum_ref, came_ref, qkv_ref, proj_ref, *outs):
    third, rows = lay.third, lay.rows
    d0, d1, d2 = (sum_ref[:rows, k * third : (k + 1) * third] for k in range(3))
    c = here()[2]
    qkv_ref[:, :third] = jnp.where(c == 0, d0, d1).astype(F32)
    qkv_ref[:, third : 2 * third] = came_ref[:, :third].astype(F32)
    qkv_ref[:, 2 * third :] = jnp.where(c == 0, d1, d2).astype(F32)
    proj_ref[...] = sum_ref[:rows, 3 * third :].astype(F32)
    total = sum_ref[rows : rows + 1, :PACKED].astype(F32) + came_ref[0:1, came_ref.shape[1] - PACKED :].astype(F32)
    for ref, (_, _, offset, count) in zip(outs, plan):
        ref[...] = total[:, offset : offset + count]


def call(kernel, name, inputs, outs, scratch=(), limit=16, hbm=False):
    return pl.pallas_call(
        kernel,
        out_shape=[jax.ShapeDtypeStruct(shape, dtype) for shape, dtype in outs],
        in_specs=[HBM if hbm else VMEM] * len(inputs),
        out_specs=[VMEM] * len(outs),
        scratch_shapes=[s if not isinstance(s, tuple) else pltpu.VMEM(*s) for s in scratch],
        compiler_params=pltpu.CompilerParams(vmem_limit_bytes=limit * MIB),
        cost_estimate=pl.CostEstimate(flops=1000, bytes_accessed=1024, transcendentals=0),
        name=name,
    )(*inputs)


def after(value, *others):
    return lax.optimization_barrier((value, *others))[0]


class Slice:
    def __init__(self, lay):
        self.lay = lay
        self.img = lax.axis_index("img")
        self.row = lax.axis_index("row")
        self.y = self.row // 2
        self.c = self.row % 2
        self.orders = (lay.high + [0, "y"], lay.high + ["y", 0])

    def swap(self, array, step):
        if step == "c":
            return lax.ppermute(array, "row", [(r, r ^ 1) for r in range(4)])
        if step == "y":
            return lax.ppermute(array, "row", [(r, r ^ 2) for r in range(4)])
        return lax.ppermute(array, "img", [(i, i ^ (1 << step)) for i in range(self.lay.img_count)])

    def gather(self, piece, order):
        held = piece[None]
        for step in order:
            held = jnp.concatenate([held, self.swap(held, step)], 0)
        return held

    def scatter(self, held, order):
        for step in reversed(order):
            half = held.shape[0] // 2
            came = self.swap(held[half:], step)
            held = (held[:half].astype(F32) + came.astype(F32)).astype(held.dtype)
        return held[0]

    def places(self, order):
        place = jnp.zeros((2, self.lay.img_count), jnp.int32)
        img = jnp.arange(self.lay.img_count, dtype=jnp.int32)[None, :] ^ self.img
        side = jnp.arange(2, dtype=jnp.int32)[:, None] ^ self.y
        for k, step in enumerate(order):
            bit = side if step == "y" else (img >> step) & 1
            place = place + (bit << k)
        return place

    def sources(self, order):
        place = self.places(order).reshape(-1)
        return jnp.zeros_like(place).at[place].set(jnp.arange(place.size, dtype=jnp.int32))

    def gather_rows(self, piece, name, joined=False, early=lambda pieces: pieces, late=lambda pieces: pieces):
        lay = self.lay
        if not lay.aligned:
            extra = [] if piece.shape[0] == lay.rows else [self.gather(piece[lay.rows], self.orders[1])]
            piece = piece[: lay.rows]
            base = self.gather(piece, lay.high)
            whole = []
            for part, order in enumerate(self.orders):
                held = base[:, part * lay.half_rows : (part + 1) * lay.half_rows]
                held = self.gather(held, order[-2:]).reshape((-1,) + held.shape[1:])
                whole.append(jnp.take(held, self.places(order), axis=0))
            return [jnp.concatenate(whole, 2).reshape((2,) + lay.tiles + piece.shape[1:])] + extra
        pieces = [piece]
        for step in lay.high:
            pieces += [self.swap(p, step) for p in pieces]
            pieces = early(pieces)
        shapes = [((len(pieces), rows, piece.shape[1]), BF) for rows in (lay.half_rows, piece.shape[0] - lay.half_rows)]
        halves = call(functools.partial(merge_kernel, lay), name, pieces, shapes)
        near = [self.swap(held, order[-2]) for order, held in zip(self.orders, halves)]
        if joined:
            shapes = [((2 * h.shape[0],) + h.shape[1:], BF) for h in halves]
            halves = call(functools.partial(join_kernel, lay), name, late([halves[0], near[0], halves[1], near[1]]), shapes)
            parts = [[held, self.swap(held, order[-1])] for order, held in zip(self.orders, halves)]
        else:
            parts = [
                [held, came, self.swap(held, order[-1]), self.swap(came, order[-1])]
                for order, held, came in zip(self.orders, halves, near)
            ]
        return parts[0] + parts[1]

    def grad_shapes(self, columns, extra=0):
        lay = self.lay
        if lay.aligned:
            return [((lay.img_count, lay.half_rows + more, columns), BF) for more in (0, 0, extra, extra)]
        return [((2,) + lay.tiles + (columns,), BF)] + [((2 * lay.img_count, columns), BF)] * (extra > 0)

    def scatter_rows(self, parts):
        lay = self.lay
        extra = []
        if not lay.aligned:
            if len(parts) > 1:
                row = self.scatter(parts[1], self.orders[1])[None]
                extra = [jnp.pad(row, ((0, 15), (0, 0)))]
            pieces = parts[0].reshape(2, lay.img_count, lay.rows, parts[0].shape[3])
            parts = []
            for part, order in enumerate(self.orders):
                mine = pieces[:, :, part * lay.half_rows : (part + 1) * lay.half_rows]
                mine = jnp.take(mine.reshape((-1,) + mine.shape[2:]), self.sources(order), axis=0)
                parts += [mine[: lay.img_count], mine[lay.img_count :]]
        sums = []
        for part, order in enumerate(self.orders):
            keep, send = parts[2 * part : 2 * part + 2]
            held = (keep.astype(F32) + self.swap(send, order[-1]).astype(F32)).astype(BF)
            half = lay.img_count // 2
            sums.append((held[:half].astype(F32) + self.swap(held[half:], order[-2]).astype(F32)).astype(BF))
        total = self.scatter(jnp.concatenate(sums, 1), lay.high)
        return jnp.concatenate([total] + extra, 0) if extra else total


NAMES = ("qkv_bias", "proj_bias", "attn_gain", "attn_shift", "mlp_gain", "mlp_shift", "up_bias", "down_bias", "freqs")


def plan_vectors(lay):
    width, third, pairs = lay.width, lay.third, lay.head // 2
    devices = lay.img_count * 4
    heads = np.arange(HEADS).reshape(2, 2, HEADS // 4)

    def by_core(count, shape):
        return [np.take(np.arange(count).reshape(shape), core, len(shape) - 2).reshape(-1) for core in range(2)]

    plain = [np.arange(width)] * 2
    up = by_core(4 * width, (2, 2, width))
    freqs = []
    for core in range(2):
        pick = np.arange(width).reshape(2, HEADS, pairs)[:, heads[:, core].reshape(-1)]
        freqs.append(np.stack([pick, pick], 2).reshape(-1))
    qkv, qk, v = (by_core(n * width, (n, 2, 2, third)) for n in (3, 2, 1))

    def lay_out(members):
        plan, tables, start, offset = [], [[], [], [], []], 0, 0
        for pick, count in members:
            count //= devices
            plan.append((start, pick[0].size, offset, count))
            for core in range(2):
                tables[2 * core].append(pick[core] // count)
                tables[2 * core + 1].append(pick[core] % count)
            start += pick[0].size
            offset += count
        return plan, jnp.asarray(np.stack([np.concatenate(t) for t in tables]).astype(np.int32))

    rest = [(plain, width)] * 5 + [(up, 4 * width), (plain, width), (freqs, width)]
    given = lay_out([(qkv, 3 * width)] + rest)
    lay.at = {name: slice(p[0], p[0] + p[1]) for name, p in zip(NAMES, given[0])}
    return given, lay_out([(qk, 2 * width), (v, width)] + rest)


def make_body(img_count):
    def body(
        tokens, keep_mask, cotangent, qkv_weight, qkv_bias, proj_weight, proj_bias, attn_gain, attn_shift,
        mlp_gain, mlp_shift, up_weight, up_bias, down_weight, down_bias, rope_freqs,
    ):
        lay = Layout(img_count, tokens, qkv_weight.shape[0])
        me = Slice(lay)
        y = me.y
        images, band, width, length = lay.images, lay.band, lay.width, lay.length
        heads = HEADS // 2
        own, third = lay.own, lay.third
        half = length // 2
        block = proj_weight.shape[1]
        hidden = up_weight.shape[1]
        vectors = (qkv_bias, proj_bias, attn_gain, attn_shift, mlp_gain, mlp_shift, up_bias, down_bias, rope_freqs)
        (plan, table), (grad_plan, grad_table) = plan_vectors(lay)

        def pick(flag, zero, one):
            return jnp.where(flag == 0, zero, one)

        def kernel(function, name, inputs, outs, scratch=(), **options):
            return call(functools.partial(function, lay), name, inputs, outs, scratch, **options)

        pack_rows = 2 * band + 16
        mine, other, third_send, first_piece, second_piece = kernel(
            pack_kernel, "pack",
            [tokens.reshape(images, band, width), cotangent.reshape(images, band, width), keep_mask, qkv_weight, proj_weight,
             up_weight, down_weight.T, *[v.reshape(1, -1) for v in vectors]],
            [((pack_rows, width), BF), ((pack_rows, width), BF), ((lay.rows, 256 + PACKED), BF),
             ((lay.rows + 16, 2 * third + block), BF), ((lay.rows, 2 * hidden), BF)],
            [(keep_mask.shape, jnp.int32), (qkv_weight.shape, F32), (proj_weight.shape, F32), (up_weight.shape, F32),
             (down_weight.T.shape, F32), *[((1, v.shape[0]), F32) for v in vectors], pltpu.SemaphoreType.DMA((18,))],
            limit=60, hbm=True,
        )
        third_came = me.swap(third_send, "c")
        near = me.swap(other, "y")
        bands = [mine, near, me.swap(mine, "c"), me.swap(near, "c")]
        (first_piece,) = kernel(fit_kernel, "fit", [third_came, first_piece], [((lay.rows + 16, 3 * third + block), BF)])
        marks = {}

        def note_first(pieces):
            if len(pieces) == img_count // 2:
                marks["high"] = pieces[1]
                pieces[0] = after(pieces[0], near)
            return pieces

        first = me.gather_rows(first_piece, "merge_first", early=note_first)
        if lay.aligned:
            second_piece = after(second_piece, marks["high"])
            first_near = (first[1], first[5])

        def hold_second(pieces):
            if len(pieces) == 2:
                pieces[1] = after(pieces[1], *first_near)
            return pieces

        second = me.gather_rows(second_piece, "merge_second", True, hold_second)
        first, vec_parts = (first, first[4:]) if lay.aligned else (first[:1], first[1:])
        (vec,) = call(
            functools.partial(unpack_kernel, lay, plan, len(vec_parts)), "unpack", [table, *vec_parts],
            [((1, table.shape[1]), F32)], limit=24,
        )

        n_w, n_s = len(first), len(second)
        n_g = len(me.grad_shapes(1))
        a1, q, k, v, w_qkv, p_cols, cos, sin, kp, mask_bias = call(
            functools.partial(project_kernel, lay, n_w), "qkv", [*bands, *first, vec],
            [((length, width), BF), ((length, own), BF), ((length, own), BF), ((length, own), BF), ((2, width, 3 * third), BF),
             ((width, 2 * block), BF), ((length, own), F32), ((length, own), F32), ((length, 1), F32), ((1, length), F32)],
            [((2,) + lay.tiles + (3 * third + block,), BF)], limit=16,
        )
        p_other = me.swap(p_cols, "c")
        ob, p = call(
            functools.partial(attend_kernel, lay, band), "attend", [q, k, v, mask_bias],
            [((length, own), BF), ((heads, length, length), BF)], limit=8,
        )
        ob_other = me.swap(ob, "c")
        x1, a2, w_proj = call(
            functools.partial(middle_kernel, lay), "middle", [*bands, ob, ob_other, p_cols, p_other, vec],
            [((length, width), F32), ((length, width), BF), ((width, width), BF)], limit=10,
        )
        part, m_send, dn, dn_send, d_up_bias, d_down_bias, *second_grads = call(
            functools.partial(mlp_kernel, lay, n_s, n_g, 256), "mlp", [*bands, kp, x1, a2, *second, vec],
            [((half, width), F32), ((half, width), BF), ((length, width), F32), ((length, width), BF), ((1, 2 * hidden), F32),
             ((1, width), F32), *me.grad_shapes(2 * hidden)],
            [((length, width), BF), ((width, length), BF), ((width, length), BF), ((length, width), F32),
             (lay.tiles + (2 * hidden,), BF), (lay.tiles + (256,), BF)], limit=18,
        )
        d_second = me.scatter_rows(second_grads)
        dn_came = me.swap(dn_send, "c")
        m_came = me.swap(m_send, "c")
        out_half = (kp[:half] * (part + m_came.astype(F32))).astype(BF)
        grad_shapes = me.grad_shapes(3 * third + block, 16)
        dx_half, dn1_keep, dn1_send, *first_grads = call(
            functools.partial(back_kernel, lay, grad_plan, len(grad_shapes), band), "back",
            [*bands, kp, x1, dn, dn_came, vec, w_proj, ob, ob_other, q, k, v, p, cos, sin, a1, w_qkv, grad_table, d_up_bias,
             d_down_bias],
            [((half, width), F32), ((half, width), F32), ((half, width), BF), *grad_shapes],
            [((length, width), BF), ((length, own), BF), ((length, own), F32), ((length, own), F32), ((length, own), F32),
             (lay.tiles + (3 * third + block,), BF), ((length, 3 * own), BF)], limit=24,
        )
        d_first = me.scatter_rows(first_grads)
        dn1_came = me.swap(dn1_send, "c")
        tg_keep, tg_send = call(
            functools.partial(finish_kernel, lay), "finish", [bands[0], bands[1], dn1_keep, dn1_came, dx_half, vec],
            [((band, width), BF), ((band, width), BF)],
        )

        def to_images(keep, send):
            came = me.swap(send, "y")
            return pick(y, jnp.stack([keep, came]), jnp.stack([came, keep])).reshape(tokens.shape)

        layer_out = to_images(out_half[:band], out_half[band:])
        tokens_grad = to_images(tg_keep, tg_send)

        d_up = d_second[:, :hidden].astype(F32)
        d_down = d_second[:, hidden:].T.astype(F32)
        (tail_send,) = kernel(tail_send_kernel, "tail_send", [d_first], [((lay.rows, 256 + PACKED), BF)])
        tail_came = me.swap(tail_send, "c")
        d_qkv, d_proj, *r = call(
            functools.partial(tail_kernel, lay, grad_plan), "tail", [d_first, tail_came],
            [((lay.rows, 3 * third), F32), ((lay.rows, block), F32), *[((1, count), F32) for _, _, _, count in grad_plan]],
        )
        r = [v.reshape(-1) for v in r]
        return (
            layer_out, tokens_grad, d_qkv, r[0], r[1], d_proj, r[2], r[3], r[4], r[5], r[6], d_up, r[7], d_down, r[8], r[9],
        )

    return body


def solution(mesh):
    split = P(("img", "row"))
    both = P("img", "row")
    field = P("img", "row", None, None)
    return jax.shard_map(
        make_body(mesh.shape["img"]),
        mesh=mesh,
        in_specs=(
            field, P("img", "row", None), field, both, split, both, split, split, split, split, split, both, split,
            P("row", "img"), split, split,
        ),
        out_specs=(
            field, field, both, split, split, both, split, split, split, split, split, both, split, P("row", "img"),
            split, split,
        ),
        check_vma=False,
    )
```

```python
import functools

import jax
import jax.numpy as jnp
import numpy as np
from jax import lax
from jax.experimental import pallas as pl
from jax.experimental.pallas import tpu as pltpu
from jax.sharding import PartitionSpec as P

HEADS = 12
PARTS = 2
NORM_EPSILON = 1e-06
MASKED_SCORE = -1e30
BF = jnp.bfloat16
F32 = jnp.float32
MIB = 2**20
VMEM = pl.BlockSpec(memory_space=pltpu.VMEM)
HBM = pl.BlockSpec(memory_space=pltpu.MemorySpace.HBM)
PACKED = 384
EXTRA = 8


def dot(left, right, dims):
    return lax.dot_general(left, right, (dims, ((), ())), preferred_element_type=F32)


def nn(left, right):
    return dot(left, right, ((1,), (0,)))


def nt(left, right):
    return dot(left, right, ((1,), (1,)))


def tn(left, right):
    return dot(left, right, ((0,), (0,)))


def normed_rows(values):
    center = values - jnp.mean(values, -1, keepdims=True)
    inverse = lax.rsqrt(jnp.mean(center * center, -1, keepdims=True) + NORM_EPSILON)
    return center * inverse, inverse


def norm_back(grad, normed, inverse, gain):
    scaled = grad * gain
    centred = scaled - jnp.mean(scaled, -1, keepdims=True)
    return inverse * (centred - normed * jnp.mean(scaled * normed, -1, keepdims=True))


def column_sum(value):
    return jnp.sum(value, 0, keepdims=True)


def here():
    row = lax.axis_index("row")
    return lax.axis_index("img"), row >> 1, row & 1, row


class Layout:
    def __init__(self, img_count, tokens, rows):
        self.img_count = img_count
        self.bits = img_count.bit_length() - 1
        self.rows = rows
        self.half_rows = rows // 2
        self.aligned = rows % 32 == 0 and img_count == 8
        self.images, self.band_rows, self.side, self.width = tokens.shape
        self.band = self.band_rows * self.side
        self.length = 4 * self.band
        self.head = self.width // HEADS
        self.own = self.width // 2
        self.third = self.own // 2
        self.high = list(range(self.bits - 1, 0, -1))
        self.first = (self.high + [0, "y"], self.high + ["y", 0])
        self.second = ([0] + self.high + ["y"], ["y"] + self.high + [0])
        self.gathered = (self.first, self.second)
        self.reduced = (self.second, self.first)
        self.tiles = (img_count, rows) if self.aligned else (1, self.width)

    def slots(self, orders, img_rel, y_rel):
        found = []
        for order in orders:
            bits = [y_rel if step == "y" else (img_rel >> step) & 1 for step in order]
            found.append((sum(bit << k for k, bit in enumerate(bits[:-1])), bits[-1]))
        return found


def load_pieces(lay, orders, refs, y_rel, target, columns=slice(None)):
    if not lay.aligned:
        target[...] = refs[0][here()[1] ^ y_rel, :, :, columns]
        return
    half = lay.half_rows
    count = len(refs) // 2
    for img_rel in range(lay.img_count):
        for part, (slot, last) in enumerate(lay.slots(orders, img_rel, y_rel)):
            which, slot = divmod((slot + last * lay.img_count) * count, 2 * lay.img_count)
            ref, slot = refs[part * count + which], slot // count
            target[img_rel ^ here()[0], part * half : (part + 1) * half] = ref[slot, :half, columns]


def store_pieces(lay, orders, refs, y_rel, columns, source):
    if not lay.aligned:
        refs[0][here()[1] ^ y_rel, :, :, columns] = source[...]
        return
    half = lay.half_rows
    for img_rel in range(lay.img_count):
        for part, (slot, last) in enumerate(lay.slots(orders, img_rel, y_rel)):
            refs[2 * part + last][slot, :half, columns] = source[img_rel ^ here()[0], part * half : (part + 1) * half]


def halves_of(lay, value):
    pairs = lay.head // 2
    lane = lax.broadcasted_iota(jnp.int32, value.shape, 1)
    width = value.shape[1]
    first = (lane & pairs) == 0
    return jnp.where(first, pltpu.roll(value, width - pairs, 1), pltpu.roll(value, pairs, 1))


def pack_kernel(lay, *refs):
    tok, cot, mask, qkv, proj, up, down, *vectors = refs[:16]
    mine_ref, other_ref, third_ref, first_ref = refs[16:20]
    second, refs = refs[20:23], refs[23:]
    mask_in, qkv_in, proj_in, up_in, down_in, *vectors_in = refs[:14]
    sems = refs[14]
    y = here()[1]
    band, third, width, rows = lay.band, lay.third, lay.width, lay.rows
    pairs = [(qkv, qkv_in), (proj, proj_in), *zip(vectors, vectors_in), (up, up_in), (down, down_in), (mask, mask_in)]
    for ref, which in ((other_ref, 1 - y), (mine_ref, y)):
        pairs += [(tok.at[which], ref.at[:band]), (cot.at[which], ref.at[band : 2 * band])]
    copies = [pltpu.make_async_copy(source, target, sems.at[n]) for n, (source, target) in enumerate(pairs)]
    for copy in copies:
        copy.start()
    for copy in copies[:11]:
        copy.wait()
    packed = jnp.concatenate([v[...] for v in vectors_in], 1)
    packed = jnp.concatenate([packed, jnp.zeros((1, PACKED - packed.shape[1]), F32)], 1).astype(BF)
    third_ref[:, :third] = qkv_in[:, third : 2 * third].astype(BF)
    third_ref[:, third:] = jnp.zeros((rows, third_ref.shape[1] - third), BF)
    third_ref[0:1, third_ref.shape[1] - PACKED :] = packed
    first_ref[:rows, :third] = qkv_in[:, :third].astype(BF)
    first_ref[:rows, third : 2 * third] = qkv_in[:, 2 * third :].astype(BF)
    first_ref[rows:] = jnp.zeros((EXTRA, first_ref.shape[1]), BF)
    first_ref[rows : rows + 1, :PACKED] = packed
    for copy in copies[11:]:
        copy.wait()
    step = width // PARTS
    for ref, part, first_row in zip(second, (0, 1, 1), (0, 0, lay.half_rows)):
        at = slice(part * step, (part + 1) * step)
        side = slice(first_row, first_row + ref.shape[0])
        ref[:, :step] = up_in[side, at].astype(BF)
        ref[:, step : 2 * step] = down_in[side, at].astype(BF)
    second[0][:, 2 * step :] = proj_in[...].astype(BF)
    for ref, which in ((mine_ref, y), (other_ref, 1 - y)):
        keep = mask_in[which].astype(F32)
        flat = jnp.concatenate([keep[r : r + 1] for r in range(lay.band_rows)], 1)
        flat = jnp.concatenate([flat, jnp.zeros((1, width - band), F32)], 1)
        ref[2 * band :] = jnp.concatenate([flat, jnp.zeros((15, width), F32)], 0).astype(BF)


def fit_kernel(lay, came_ref, first_ref, out_ref):
    third, rows = lay.third, lay.rows
    c = here()[2]
    t0, t2, came = first_ref[:rows, :third], first_ref[:rows, third : 2 * third], came_ref[:, :third]
    out_ref[:rows, : 3 * third] = jnp.where(c == 0, jnp.concatenate([t0, t2, came], 1), jnp.concatenate([came, t0, t2], 1))
    theirs = came_ref[0:1, came_ref.shape[1] - PACKED :]
    rest = jnp.zeros((EXTRA - 2, PACKED), F32).astype(BF)
    out_ref[rows:] = jnp.zeros((EXTRA, out_ref.shape[1]), BF)
    out_ref[rows:, :PACKED] = jnp.concatenate([first_ref[rows : rows + 1, :PACKED], theirs, rest], 0)


def merge_kernel(lay, *refs):
    pieces, (top_ref, bottom_ref) = refs[:-2], refs[-2:]
    half = lay.half_rows
    for k, ref in enumerate(pieces):
        if len(ref.shape) == 2:
            top_ref[k] = ref[:half]
            bottom_ref[k] = ref[half:]
        else:
            count = ref.shape[0]
            top_ref[k * count : (k + 1) * count] = ref[:, :half]
            bottom_ref[k * count : (k + 1) * count] = ref[:, half:]


def start_kernel(lay, top, top_came, bottom, bottom_came, out_ref):
    half = lay.half_rows
    out_ref[0, :half], out_ref[1, :half] = top[...], top_came[...]
    out_ref[0, half:], out_ref[1, half:] = bottom[...], bottom_came[...]


def join_kernel(*refs):
    for part in range(2):
        own, came = refs[2 * part : 2 * part + 2]
        refs[4 + part][: own.shape[0]] = own[...]
        refs[4 + part][own.shape[0] :] = came[...]


def fold_kernel(*refs):
    for part in range(2):
        keep, came = refs[2 * part : 2 * part + 2]
        count = keep.shape[0] // 2
        for half in range(2):
            at = slice(half * count, (half + 1) * count)
            refs[4 + 2 * part + half][...] = (keep[at].astype(F32) + came[at].astype(F32)).astype(BF)


def rejoin_kernel(*refs):
    count, top = refs[0].shape[:2]
    for part in range(2):
        keep, came = refs[2 * part : 2 * part + 2]
        rows = slice(0, top) if part == 0 else slice(top, None)
        for half in range(2):
            at = slice(half * count // 2, (half + 1) * count // 2)
            refs[4 + half][:, rows] = (keep[at].astype(F32) + came[at].astype(F32)).astype(BF)


def halve_kernel(keep_ref, came_ref, *outs):
    count = keep_ref.shape[0] // len(outs)
    for half, ref in enumerate(outs):
        at = slice(half * count, (half + 1) * count)
        total = (keep_ref[at].astype(F32) + came_ref[at].astype(F32)).astype(BF)
        ref[...] = total.reshape(ref.shape)


def split_kernel(keep_ref, came_ref, out_ref, top_ref, bottom_ref):
    half = top_ref.shape[0]
    out_ref[...] = (keep_ref[0].astype(F32) + came_ref[0].astype(F32)).astype(BF)
    top_ref[...] = (keep_ref[1, :half].astype(F32) + came_ref[1, :half].astype(F32)).astype(BF)
    bottom_ref[...] = (keep_ref[1, half:].astype(F32) + came_ref[1, half:].astype(F32)).astype(BF)


def owner_mask(lay, c_rel, table_row):
    place = lax.broadcasted_iota(jnp.int32, (2 * lay.img_count, 1), 0)
    img_rel = jnp.zeros_like(place)
    row = here()[3] ^ c_rel
    for k, step in enumerate(lay.first[1]):
        bit = (place >> k) & 1
        if step == "y":
            row = row ^ (bit * 2)
        else:
            img_rel = img_rel | (bit << step)
    return ((img_rel ^ here()[0]) * 4 + row) == table_row


def owners(table_ref, at, c):
    owner = jnp.where(c == 0, table_ref[0:1, at], table_ref[2:3, at])
    entry = jnp.where(c == 0, table_ref[1:2, at], table_ref[3:4, at])
    return owner, entry


def unpack_kernel(lay, plan, n_v, table_ref, *refs):
    v_refs, out_ref = refs[:n_v], refs[n_v]
    if lay.aligned:
        half = lay.half_rows
        rows = [ref[k, half : half + EXTRA, :PACKED].astype(F32) for ref in v_refs for k in range(ref.shape[0])]
        gathered = [jnp.concatenate([row[c_rel : c_rel + 1] for row in rows], 0).astype(BF) for c_rel in range(2)]
    else:
        gathered = [v_refs[0][:, c_rel, :PACKED] for c_rel in range(2)]
    for start, size, offset, count in plan:
        at = slice(start, start + size)
        owner, entry = owners(table_ref, at, here()[2])
        spread = (lax.broadcasted_iota(jnp.int32, (count, size), 0) == entry).astype(F32).astype(BF)
        total = 0.0
        for c_rel in range(2):
            rows = nn(gathered[c_rel][:, offset : offset + count], spread)
            total = total + column_sum(jnp.where(owner_mask(lay, c_rel, owner), rows, 0.0))
        out_ref[:, at] = total


def repack(lay, plan, table_ref, grads, refs):
    sides = []
    for c_rel in range(2):
        parts = []
        for grad, (start, size, offset, count) in zip(grads, plan):
            owner, entry = owners(table_ref, slice(start, start + size), here()[2])
            spread = (lax.broadcasted_iota(jnp.int32, (count, size), 0) == entry).astype(F32).astype(BF)
            rows = jnp.where(owner_mask(lay, c_rel, owner), grad, 0.0).astype(BF)
            parts.append(nt(rows, spread))
        used = sum(p.shape[1] for p in parts)
        sides.append(jnp.concatenate(parts + [jnp.zeros((2 * lay.img_count, PACKED - used), F32)], 1))
    if not lay.aligned:
        refs[1][...] = jnp.zeros(refs[1].shape, BF)
        for c_rel in range(2):
            refs[1][:, c_rel, :PACKED] = sides[c_rel].astype(BF)
        return
    half, count = lay.half_rows, lay.img_count
    for j in range(2 * count):
        ref = refs[2 + j // count]
        block = jnp.concatenate([side[j : j + 1] for side in sides] + [jnp.zeros((EXTRA - 2, PACKED), F32)], 0).astype(BF)
        ref[j % count, half:] = jnp.zeros((EXTRA, ref.shape[2]), BF)
        ref[j % count, half:, :PACKED] = block


def project_kernel(lay, n_w, t0, t1, t2, t3, *refs):
    w_refs = refs[:n_w]
    vec_ref, a_ref, q_ref, k_ref, v_ref, w_out, cos_ref, sin_ref, kp_ref, bias_ref, w_all = refs[n_w:]
    band, side, own, third = lay.band, lay.side, lay.own, lay.third
    g_ref, s_ref, b_ref = (vec_ref[:, lay.at[n]] for n in ("attn_gain", "attn_shift", "qkv_bias"))
    f_ref = vec_ref[:, lay.at["freqs"]]
    keeps = []
    for b, ref in enumerate((t0, t1, t2, t3)):
        at = slice(b * band, (b + 1) * band)
        normed, _ = normed_rows(ref[:band].astype(F32))
        a_ref[at] = (normed * g_ref + s_ref).astype(BF)
        keep = ref[2 * band :, :band].astype(F32)
        kp_ref[at] = jnp.transpose(keep)[:, 0:1]
        keeps.append(keep[0:1])
    bias_ref[...] = jnp.where(jnp.concatenate(keeps, 1) > 0, 0.0, MASKED_SCORE)
    lane = lax.broadcasted_iota(jnp.int32, (side, own), 1)
    sign = jnp.where((lane & (lay.head // 2)) == 0, -1.0, 1.0).astype(F32)
    col = lax.broadcasted_iota(jnp.int32, (side, own), 0).astype(F32) * f_ref[:, :own]
    col_cos, col_sin = jnp.cos(col), jnp.sin(col)
    row_index = here()[3]
    for b, flip in enumerate((0, 2, 1, 3)):
        first = ((row_index ^ flip) * lay.band_rows).astype(F32)
        rows = (lax.broadcasted_iota(jnp.int32, (8, own), 0).astype(F32) + first) * f_ref[:, own:]
        row_cos, row_sin = jnp.cos(rows), jnp.sin(rows)
        for r in range(lay.band_rows):
            at = slice(b * band + r * side, b * band + (r + 1) * side)
            rc, rs = row_cos[r : r + 1], row_sin[r : r + 1]
            cos_ref[at] = col_cos * rc - col_sin * rs
            sin_ref[at] = (col_sin * rc + col_cos * rs) * sign
    for y_rel in range(2):
        y_side = here()[1] ^ y_rel
        load_pieces(lay, lay.first, w_refs, y_rel, w_all.at[y_side])
    acts = a_ref[...]
    w0, w1 = w_all[0].reshape(lay.width, -1), w_all[1].reshape(lay.width, -1)
    w_out[0], w_out[1] = w0, w1
    left = nn(acts, w0) + b_ref[:, : 3 * third]
    right = nn(acts, w1) + b_ref[:, 3 * third :]
    query, key = left[:, :own], jnp.concatenate([left[:, own:], right[:, :third]], 1)
    cos, sin = cos_ref[...], sin_ref[...]
    q_ref[...] = (query * cos + halves_of(lay, query) * sin).astype(BF)
    k_ref[...] = (key * cos + halves_of(lay, key) * sin).astype(BF)
    v_ref[...] = right[:, third:].astype(BF)


def proj_kernel(lay, n_w, *refs):
    out_ref, w_all = refs[n_w:]
    block = lay.width // 4
    columns = slice(refs[0].shape[-1] - block, None)
    for y_rel in range(2):
        y_side = here()[1] ^ y_rel
        load_pieces(lay, lay.gathered[0], refs[:n_w], y_rel, w_all.at[y_side], columns)
    for y_side in range(2):
        out_ref[:, y_side * block : (y_side + 1) * block] = w_all[y_side].reshape(lay.width, block)


def attend_kernel(lay, chunk, q_ref, k_ref, v_ref, bias_ref, o_ref, p_ref):
    head = lay.head
    pair = 2 * head
    scale = head**-0.5

    def step(n, carry):
        at = pl.ds(pl.multiple_of(n * pair, pair), pair)
        keys, values = k_ref[:, at], v_ref[:, at]
        for start in range(0, lay.length, chunk):
            rows = slice(start, start + chunk)
            query = q_ref[rows, at] * jnp.asarray(scale, BF)
            lane = lax.broadcasted_iota(jnp.int32, query.shape, 1)
            outs = []
            for h in range(2):
                mine = (lane < head) if h == 0 else (lane >= head)
                score = nt(jnp.where(mine, query, jnp.zeros_like(query)), keys) + bias_ref[...]
                power = jnp.exp(score - jnp.max(score, -1, keepdims=True))
                weights = (power * (1.0 / jnp.sum(power, -1, keepdims=True))).astype(BF)
                p_ref[2 * n + h, rows] = weights
                outs.append(nn(weights, values))
            o_ref[rows, at] = jnp.where(lane < head, outs[0], outs[1]).astype(BF)
        return carry

    lax.fori_loop(0, HEADS // 4, step, 0)


def middle_kernel(lay, t0, t1, t2, t3, ob_ref, oo_ref, p_ref, po_ref, vec_ref, kp_ref, x1_ref, a2_ref, at_ref, dm_ref, dt_ref, dbg_ref, wp_ref):
    band, third, half = lay.band, lay.third, lay.length // 2
    c = here()[2]
    block = lay.width // 4
    pb_ref, g_ref, s_ref = (vec_ref[:, lay.at[n]] for n in ("proj_bias", "mlp_gain", "mlp_shift"))
    for y_side in range(2):
        mine, other = (ref[:, y_side * block : (y_side + 1) * block] for ref in (p_ref, po_ref))
        wp_ref[:, 2 * y_side * block : 2 * (y_side + 1) * block] = jnp.where(
            c == 0, jnp.concatenate([mine, other], 1), jnp.concatenate([other, mine], 1)
        )
    low = [pl.ds(pl.multiple_of((2 * s + c) * third, third), third) for s in range(2)]
    high = [pl.ds(pl.multiple_of((2 * s + 1 - c) * third, third), third) for s in range(2)]
    own_w = jnp.concatenate([wp_ref[low[0]], wp_ref[low[1]]], 0)
    other_w = jnp.concatenate([wp_ref[high[0]], wp_ref[high[1]]], 0)
    other = jnp.concatenate([oo_ref[half:], oo_ref[:half]], 0)
    x1_ref[...] = nn(ob_ref[...], own_w) + nn(other, other_w) + pb_ref
    for b, ref in enumerate((t0, t1, t2, t3)):
        at = slice(b * band, (b + 1) * band)
        x1 = x1_ref[at] + ref[:band].astype(F32)
        x1_ref[at] = x1
        normed, _ = normed_rows(x1)
        a2_ref[at] = (normed * g_ref + s_ref).astype(BF)
        dm_ref[at] = (ref[band : 2 * band].astype(F32) * kp_ref[at]).astype(BF)
    at_ref[...] = a2_ref[...].T
    dt_ref[...] = dm_ref[...].T
    dbg_ref[...] = column_sum(dm_ref[:half].astype(F32))


def mlp_kernel(lay, part, n_w, n_g, x1_ref, a2_ref, at_ref, dm_ref, dt_ref, vec_ref, *refs):
    w_refs, refs = refs[:n_w], refs[n_w:]
    last = part == PARTS - 1
    if part:
        (m_in, dn_in), refs = refs[:2], refs[2:]
    grads, refs = refs[:n_g], refs[n_g:]
    ubg_ref, refs = refs[0], refs[1:]
    if last:
        part_ref, msend_ref, dn_ref, dnsend_ref, m_ref, w_all, g_tmp = refs
    else:
        m_ref, dn_ref, w_all, g_tmp = refs
    width, half = lay.width, lay.length // 2
    chunk = width // PARTS
    up_bias = lay.at["up_bias"].start + part * chunk
    for y_rel in range(2):
        load_pieces(lay, lay.gathered[part], w_refs, y_rel, w_all, slice(0, 2 * chunk))
        y_side = here()[1] ^ y_rel
        up = w_all[:, :, :chunk].reshape(width, chunk)
        down = w_all[:, :, chunk:].reshape(width, chunk)
        pre = nn(a2_ref[...], up) + vec_ref[:, pl.ds(pl.multiple_of(y_side * width + up_bias, 128), chunk)]
        cdf = 0.5 * (1.0 + lax.erf(pre * 0.7071067811865476))
        slope = cdf + pre * (jnp.exp(-0.5 * pre * pre) * 0.3989422804014327)
        act = (pre * cdf).astype(BF)
        du = (nn(dm_ref[...], down) * slope).astype(BF)
        ubg_ref[:, pl.ds(pl.multiple_of(y_side * chunk, 128), chunk)] = column_sum(du.astype(F32))
        g_tmp[...] = nn(at_ref[...], du).astype(BF).reshape(g_tmp.shape)
        store_pieces(lay, lay.reduced[part], grads, y_rel, slice(0, chunk), g_tmp)
        g_tmp[...] = nn(dt_ref[...], act).astype(BF).reshape(g_tmp.shape)
        store_pieces(lay, lay.reduced[part], grads, y_rel, slice(chunk, None), g_tmp)
        m, dn = nt(act, down), nt(du, up)
        if y_rel == 0:
            m_ref[...] = m + m_in[...] if part else m
            dn_ref[...] = dn + dn_in[...] if part else dn
        else:
            m_ref[...] += m
            dn_ref[...] += dn
    if last:
        part_ref[...] = x1_ref[:half] + m_ref[:half] + vec_ref[:, lay.at["down_bias"]]
        msend_ref[...] = m_ref[half:].astype(BF)
        dnsend_ref[...] = dn_ref[...].astype(BF)


def attend_back(lay, chunk, first, count, base, q_ref, k_ref, v_ref, p_ref, dob_ref, dq_ref, dk_ref, dv_ref):
    head = lay.head
    pair = 2 * head
    scale = head**-0.5

    def step(n, carry):
        at = pl.ds(pl.multiple_of(n * pair, pair), pair)
        out = pl.ds(pl.multiple_of((n - base) * pair, pair), pair)
        keys, values = k_ref[:, at], v_ref[:, at]
        for start in range(0, lay.length, chunk):
            rows = slice(start, start + chunk)
            query, dob = q_ref[rows, at], dob_ref[rows, at]
            lane = lax.broadcasted_iota(jnp.int32, query.shape, 1)
            dqs, dks, dvs = [], [], []
            for h in range(2):
                mine = (lane < head) if h == 0 else (lane >= head)
                weights = p_ref[2 * n + h, rows]
                soft = weights.astype(F32)
                dp = nt(jnp.where(mine, dob, jnp.zeros_like(dob)), values)
                ds = (soft * (dp - jnp.sum(soft * dp, -1, keepdims=True))).astype(BF)
                dqs.append(nn(ds, keys))
                dks.append(tn(ds, query))
                dvs.append(tn(weights, dob))
            dq_ref[rows, out] = jnp.where(lane < head, dqs[0], dqs[1]) * scale
            lane = lax.broadcasted_iota(jnp.int32, keys.shape, 1)
            dk = jnp.where(lane < head, dks[0], dks[1]) * scale
            dv = jnp.where(lane < head, dvs[0], dvs[1])
            if start == 0:
                dk_ref[:, out] = dk
                dv_ref[:, out] = dv
            else:
                dk_ref[:, out] += dk
                dv_ref[:, out] += dv
        return carry

    lax.fori_loop(first, first + count, step, 0)


def back_kernel(
    lay, chunk, n_g, t0, t1, t2, t3, kp_ref, x1_ref, dn_ref, came_ref, vec_ref, wp_ref, ob_ref, oo_ref, q_ref, k_ref, v_ref, p_ref,
    *refs,
):
    grads_in, grads, refs = refs[:n_g], refs[n_g : 2 * n_g], refs[2 * n_g :]
    dx_ref, dob_ref, sums_ref, dq_ref, dk_ref, dv_ref, dxb_ref, g_tmp = refs
    for before, ref in zip(grads_in, grads):
        ref[..., : before.shape[-1]] = before[...]
    g_ref = vec_ref[:, lay.at["mlp_gain"]]
    band, third, half = lay.band, lay.third, lay.length // 2
    c = here()[2]
    gg, sg, pbg = 0.0, 0.0, 0.0
    for b, ref in enumerate((t0, t1, t2, t3)):
        at = slice(b * band, (b + 1) * band)
        away = slice((b ^ 2) * band, ((b ^ 2) + 1) * band)
        dn = dn_ref[at] + came_ref[away].astype(F32)
        normed, inverse = normed_rows(x1_ref[at])
        dx = ref[band : 2 * band].astype(F32) * kp_ref[at] + norm_back(dn, normed, inverse, g_ref)
        dxb = dx.astype(BF)
        dxb_ref[at] = dxb
        if b < 2:
            dx_ref[at] = dx
            gg = gg + column_sum(dn * normed)
            sg = sg + column_sum(dn)
            pbg = pbg + column_sum(dxb.astype(F32))
    low = [pl.ds(pl.multiple_of((2 * s + c) * third, third), third) for s in range(2)]
    own_w = jnp.concatenate([wp_ref[low[0]], wp_ref[low[1]]], 0)
    dxb = dxb_ref[...]
    dob_ref[...] = nt(dxb, own_w).astype(BF)
    block = lay.width // 4
    zero = jnp.concatenate([dxb[:, :block], dxb[:, 2 * block : 3 * block]], 1)
    one = jnp.concatenate([dxb[:, block : 2 * block], dxb[:, 3 * block :]], 1)
    cols = jnp.where(c == 0, zero, one)
    other = jnp.concatenate([oo_ref[half:], oo_ref[:half]], 0)
    mine_g, other_g = tn(ob_ref[...], cols).astype(BF), tn(other, cols).astype(BF)
    zero, one = jnp.where(c == 0, mine_g, other_g), jnp.where(c == 0, other_g, mine_g)
    p_grad = jnp.concatenate([zero[:third], one[:third], zero[third:], one[third:]], 0)
    columns = slice(grads_in[0].shape[-1], None)
    sides = [p_grad[:, :block], p_grad[:, block:]]
    for y_rel in range(2):
        g_tmp[...] = jnp.where((here()[1] ^ y_rel) == 0, sides[0], sides[1]).reshape(g_tmp.shape)
        store_pieces(lay, lay.reduced[1], grads, y_rel, columns, g_tmp)
    sums_ref[...] = jnp.concatenate([gg, sg, pbg], 0)
    attend_back(lay, chunk, 0, 1, 0, q_ref, k_ref, v_ref, p_ref, dob_ref, dq_ref, dk_ref, dv_ref)


def back_heads_kernel(lay, chunk, q_ref, k_ref, v_ref, p_ref, dob_ref, dq_ref, dk_ref, dv_ref):
    attend_back(lay, chunk, 1, HEADS // 4 - 1, 1, q_ref, k_ref, v_ref, p_ref, dob_ref, dq_ref, dk_ref, dv_ref)


def back_rest_kernel(
    lay, plan, n_g, t0, t1, t2, t3, q_ref, k_ref, cos_ref, sin_ref, a_ref, w_ref, table_ref, ubg0, ubg1, dbg_ref, sums_ref,
    dq0, dk0, dv0, dq1, dk1, dv1, *refs,
):
    keep_ref, send_ref = refs[:2]
    grads = refs[2 : 2 + n_g]
    dq_ref, g_tmp, dqkv_ref = refs[2 + n_g :]
    band, side, own, third, half, head = lay.band, lay.side, lay.own, lay.third, lay.length // 2, lay.head
    gg, sg, pbg = sums_ref[0:1], sums_ref[1:2], sums_ref[2:3]
    step = lay.width // PARTS
    ubg = jnp.concatenate([ref[:, y_side * step : (y_side + 1) * step] for y_side in range(2) for ref in (ubg0, ubg1)], 1)
    cos, sin = cos_ref[...], sin_ref[...]
    dq, dk, dv = (jnp.concatenate([a[...], b[...]], 1) for a, b in ((dq0, dq1), (dk0, dk1), (dv0, dv1)))
    dqkv_ref[:, :own] = (dq * cos + halves_of(lay, dq * sin)).astype(BF)
    dqkv_ref[:, own : 2 * own] = (dk * cos + halves_of(lay, dk * sin)).astype(BF)
    dqkv_ref[:, 2 * own :] = dv.astype(BF)
    dq_ref[...] = dq * halves_of(lay, q_ref[...].astype(F32)) + dk * halves_of(lay, k_ref[...].astype(F32))
    by_col = jnp.zeros((side, own), F32)
    by_row = jnp.zeros((side, own), F32)
    for b, flip in enumerate((0, 2, 1, 3)):
        first = ((here()[3] ^ flip) * lay.band_rows).astype(F32)
        for r in range(lay.band_rows):
            turn = dq_ref[b * band + r * side : b * band + (r + 1) * side]
            by_col = by_col + turn
            by_row = by_row + turn * (first + r)
    lane = lax.broadcasted_iota(jnp.int32, (2, own), 1)
    sign = jnp.where((lane & (head // 2)) == 0, -1.0, 1.0).astype(F32)
    place = lax.broadcasted_iota(jnp.int32, (side, own), 0).astype(F32)
    both = jnp.concatenate([column_sum(by_col * place), column_sum(by_row)], 0) * sign
    both = jnp.where(sign < 0, both + halves_of(lay, both), 0.0)
    freqs = jnp.concatenate([both[0:1], both[1:2]], 1)
    bqk = column_sum(dqkv_ref[:, : 2 * own].astype(F32))
    bv = column_sum(dqkv_ref[:, 2 * own :].astype(F32))
    grad = nt(dqkv_ref[:, : 3 * third], w_ref[0]) + nt(dqkv_ref[:, 3 * third :], w_ref[1])
    keep_ref[...] = grad[:half]
    send_ref[...] = grad[half:].astype(BF)
    g1, s1 = 0.0, 0.0
    for b, ref in enumerate((t0, t1, t2, t3)):
        part = grad[b * band : (b + 1) * band]
        normed, _ = normed_rows(ref[:band].astype(F32))
        g1 = g1 + column_sum(part * normed)
        s1 = s1 + column_sum(part)
    repack(lay, plan, table_ref, [bqk, bv, pbg, g1, s1, gg, sg, ubg, dbg_ref[...], freqs], grads)
    acts = a_ref[...]
    sides = []
    for y_side in range(2):
        grad = tn(acts, dqkv_ref[:, y_side * 3 * third : (y_side + 1) * 3 * third]).astype(BF)
        sides.append(grad)
    y = here()[1]
    for y_rel in range(2):
        g_tmp[...] = jnp.where((y ^ y_rel) == 0, sides[0], sides[1]).reshape(g_tmp.shape)
        store_pieces(lay, lay.first, grads, y_rel, slice(None), g_tmp)


def finish_kernel(lay, t0, t1, keep_ref, came_ref, dx_ref, vec_ref, out_ref, send_ref):
    band = lay.band
    g_ref = vec_ref[:, lay.at["attn_gain"]]
    for b, ref in enumerate((t0, t1)):
        at = slice(b * band, (b + 1) * band)
        dn = keep_ref[at] + came_ref[at].astype(F32)
        normed, inverse = normed_rows(ref[:band].astype(F32))
        result = (dx_ref[at] + norm_back(dn, normed, inverse, g_ref)).astype(BF)
        if b == 0:
            out_ref[...] = result
        else:
            send_ref[...] = result


def tail_second_kernel(lay, counts, *refs):
    up_ref, down_ref, proj_ref = refs[-3:]
    step = up_ref.shape[1] // PARTS
    half = lay.half_rows
    for part, count in enumerate(counts):
        at = slice(part * step, (part + 1) * step)
        keep, *came = refs[sum(counts[:part]) : sum(counts[: part + 1])]
        if not came:
            up_ref[:, at], down_ref[:, at] = keep[:, :step].astype(F32), keep[:, step : 2 * step].astype(F32)
        for rows, ref in zip((slice(0, half), slice(half, None)), came):
            up_ref[rows, at] = keep[rows, :step].astype(F32) + ref[:, :step].astype(F32)
            down_ref[rows, at] = keep[rows, step:].astype(F32) + ref[:, step:].astype(F32)
        if part:
            proj_ref[...] = keep[:, 2 * step :].astype(F32)


def tail_send_kernel(lay, sum_ref, out_ref):
    third, rows = lay.third, lay.rows
    out_ref[:, :third] = jnp.where(here()[2] == 0, sum_ref[:rows, 2 * third : 3 * third], sum_ref[:rows, :third])
    out_ref[:, third:] = jnp.zeros((rows, out_ref.shape[1] - third), BF)
    theirs = sum_ref[rows:, :PACKED].astype(F32)[1:2]
    out_ref[0:1, out_ref.shape[1] - PACKED :] = theirs.astype(BF)


def tail_kernel(lay, plan, sum_ref, came_ref, qkv_ref, *outs):
    third, rows = lay.third, lay.rows
    d0, d1, d2 = (sum_ref[:rows, k * third : (k + 1) * third] for k in range(3))
    c = here()[2]
    qkv_ref[:, :third] = jnp.where(c == 0, d0, d1).astype(F32)
    qkv_ref[:, third : 2 * third] = came_ref[:, :third].astype(F32)
    qkv_ref[:, 2 * third :] = jnp.where(c == 0, d1, d2).astype(F32)
    total = sum_ref[rows:, :PACKED].astype(F32)[0:1] + came_ref[0:1, came_ref.shape[1] - PACKED :].astype(F32)
    for ref, (_, _, offset, count) in zip(outs, plan):
        ref[...] = total[:, offset : offset + count]


def call(kernel, name, inputs, outs, scratch=(), limit=16, hbm=False):
    return pl.pallas_call(
        kernel,
        out_shape=[jax.ShapeDtypeStruct(shape, dtype) for shape, dtype in outs],
        in_specs=[HBM if hbm else VMEM] * len(inputs),
        out_specs=[VMEM] * len(outs),
        scratch_shapes=[s if not isinstance(s, tuple) else pltpu.VMEM(*s) for s in scratch],
        compiler_params=pltpu.CompilerParams(vmem_limit_bytes=limit * MIB),
        cost_estimate=pl.CostEstimate(flops=1000, bytes_accessed=1024, transcendentals=0),
        name=name,
    )(*inputs)


def after(value, *others):
    return lax.optimization_barrier((value, *others))[0]


class Slice:
    def __init__(self, lay):
        self.lay = lay
        self.img = lax.axis_index("img")
        self.row = lax.axis_index("row")
        self.y = self.row // 2
        self.c = self.row % 2
        self.orders = lay.first

    def swap(self, array, step):
        if step == "c":
            return lax.ppermute(array, "row", [(r, r ^ 1) for r in range(4)])
        if step == "y":
            return lax.ppermute(array, "row", [(r, r ^ 2) for r in range(4)])
        return lax.ppermute(array, "img", [(i, i ^ (1 << step)) for i in range(self.lay.img_count)])

    def gather(self, piece, order):
        held = piece[None]
        for step in order:
            held = jnp.concatenate([held, self.swap(held, step)], 0)
        return held

    def scatter(self, held, order):
        for step in reversed(order):
            half = held.shape[0] // 2
            came = self.swap(held[half:], step)
            held = (held[:half].astype(F32) + came.astype(F32)).astype(held.dtype)
        return held[0]

    def places(self, order):
        place = jnp.zeros((2, self.lay.img_count), jnp.int32)
        img = jnp.arange(self.lay.img_count, dtype=jnp.int32)[None, :] ^ self.img
        side = jnp.arange(2, dtype=jnp.int32)[:, None] ^ self.y
        for k, step in enumerate(order):
            bit = side if step == "y" else (img >> step) & 1
            place = place + (bit << k)
        return place

    def sources(self, order):
        place = self.places(order).reshape(-1)
        return jnp.zeros_like(place).at[place].set(jnp.arange(place.size, dtype=jnp.int32))

    def gather_whole(self, piece):
        lay = self.lay
        base = self.gather(piece, lay.high)
        whole = []
        for part, order in enumerate(self.orders):
            held = base[:, part * lay.half_rows : (part + 1) * lay.half_rows]
            held = self.gather(held, order[-2:]).reshape((-1,) + held.shape[1:])
            whole.append(jnp.take(held, self.places(order), axis=0))
        return jnp.concatenate(whole, 2).reshape((2,) + lay.tiles + piece.shape[1:])

    def high(self, piece, *others):
        one, two = (self.swap(piece, step) for step in self.lay.high)
        return [piece, one, two, self.swap(after(one, two, *others), self.lay.high[1])]

    def merge(self, pieces, name):
        lay = self.lay
        rows, columns = pieces[0].shape[-2:]
        count = len(pieces) * (pieces[0].shape[0] if pieces[0].ndim == 3 else 1)
        shapes = [((count, n, columns), BF) for n in (lay.half_rows, rows - lay.half_rows)]
        return call(functools.partial(merge_kernel, lay), name, pieces, shapes)

    def pairs(self, orders, place, top, bottom):
        return [self.swap(top, orders[0][place]), self.swap(bottom, orders[1][place])]

    def grad_shapes(self, columns, extra=0):
        lay = self.lay
        if lay.aligned:
            return [((lay.img_count, lay.half_rows + more, columns), BF) for more in (0, 0, extra, extra)]
        return [((2,) + lay.tiles + (columns,), BF)] + [((2 * lay.img_count, 2, columns), BF)] * (extra > 0)

    def scatter_rows(self, parts):
        lay = self.lay
        extra = []
        if not lay.aligned:
            if len(parts) > 1:
                extra = [jnp.pad(self.scatter(parts[1], self.orders[1]), ((0, EXTRA - 2), (0, 0)))]
            pieces = parts[0].reshape(2, lay.img_count, lay.rows, parts[0].shape[3])
            parts = []
            for part, order in enumerate(self.orders):
                mine = pieces[:, :, part * lay.half_rows : (part + 1) * lay.half_rows]
                mine = jnp.take(mine.reshape((-1,) + mine.shape[2:]), self.sources(order), axis=0)
                parts += [mine[: lay.img_count], mine[lay.img_count :]]
        sums = []
        for part, order in enumerate(self.orders):
            keep, send = parts[2 * part : 2 * part + 2]
            held = (keep.astype(F32) + self.swap(send, order[-1]).astype(F32)).astype(BF)
            half = lay.img_count // 2
            sums.append((held[:half].astype(F32) + self.swap(held[half:], order[-2]).astype(F32)).astype(BF))
        total = self.scatter(jnp.concatenate(sums, 1), lay.high)
        return jnp.concatenate([total] + extra, 0) if extra else total

    def fold(self, grads, came, name):
        shapes = [((g.shape[0] // 2,) + g.shape[1:], BF) for g in grads]
        return call(fold_kernel, name + "_fold", [grads[0], came[0], grads[2], came[1]], shapes)

    def rejoin(self, top, top_came, bottom, bottom_came, name):
        count, rows, columns = top.shape
        shape = (count // 2, rows + bottom.shape[1], columns)
        return call(rejoin_kernel, name + "_rejoin", [top, top_came, bottom, bottom_came], [(shape, BF)] * 2)

    def halve(self, keep, came, name):
        shape = (keep.shape[0] // 2,) + keep.shape[1:]
        return call(halve_kernel, name + "_halve", [keep, came], [(shape, BF)] * 2)

    def split(self, keep, came, name):
        _, rows, columns = keep.shape
        half = self.lay.half_rows
        shapes = [((n, columns), BF) for n in (rows, half, rows - half)]
        out, top, bottom = call(split_kernel, name + "_split", [keep, came], shapes)
        return [out] + self.pairs(self.lay.second, 0, top, bottom)

    def end(self, keep, came, name):
        return call(halve_kernel, name + "_end", [keep, came], [(keep.shape[1:], BF)])[0]


NAMES = ("qkv_bias", "proj_bias", "attn_gain", "attn_shift", "mlp_gain", "mlp_shift", "up_bias", "down_bias", "freqs")


def plan_vectors(lay):
    width, third, pairs = lay.width, lay.third, lay.head // 2
    devices = lay.img_count * 4
    heads = np.arange(HEADS).reshape(2, 2, HEADS // 4)

    def by_core(count, shape):
        return [np.take(np.arange(count).reshape(shape), core, len(shape) - 2).reshape(-1) for core in range(2)]

    plain = [np.arange(width)] * 2
    up = by_core(4 * width, (2, 2, width))
    freqs = []
    for core in range(2):
        pick = np.arange(width).reshape(2, HEADS, pairs)[:, heads[:, core].reshape(-1)]
        freqs.append(np.stack([pick, pick], 2).reshape(-1))
    qkv, qk, v = (by_core(n * width, (n, 2, 2, third)) for n in (3, 2, 1))

    def lay_out(members):
        plan, tables, start, offset = [], [[], [], [], []], 0, 0
        for pick, count in members:
            count //= devices
            plan.append((start, pick[0].size, offset, count))
            for core in range(2):
                tables[2 * core].append(pick[core] // count)
                tables[2 * core + 1].append(pick[core] % count)
            start += pick[0].size
            offset += count
        return plan, jnp.asarray(np.stack([np.concatenate(t) for t in tables]).astype(np.int32))

    rest = [(plain, width)] * 5 + [(up, 4 * width), (plain, width), (freqs, width)]
    given = lay_out([(qkv, 3 * width)] + rest)
    lay.at = {name: slice(p[0], p[0] + p[1]) for name, p in zip(NAMES, given[0])}
    return given, lay_out([(qk, 2 * width), (v, width)] + rest)


def make_body(img_count):
    def body(
        tokens, keep_mask, cotangent, qkv_weight, qkv_bias, proj_weight, proj_bias, attn_gain, attn_shift,
        mlp_gain, mlp_shift, up_weight, up_bias, down_weight, down_bias, rope_freqs,
    ):
        lay = Layout(img_count, tokens, qkv_weight.shape[0])
        me = Slice(lay)
        y = me.y
        images, band, width, length = lay.images, lay.band, lay.width, lay.length
        heads = HEADS // 2
        own, third = lay.own, lay.third
        half = length // 2
        block = proj_weight.shape[1]
        hidden = up_weight.shape[1]
        vectors = (qkv_bias, proj_bias, attn_gain, attn_shift, mlp_gain, mlp_shift, up_bias, down_bias, rope_freqs)
        (plan, table), (grad_plan, grad_table) = plan_vectors(lay)

        def pick(flag, zero, one):
            return jnp.where(flag == 0, zero, one)

        def kernel(function, name, inputs, outs, scratch=(), **options):
            return call(functools.partial(function, lay), name, inputs, outs, scratch, **options)

        pack_rows = 2 * band + 16
        mine, other, third_send, first_piece, *second_pieces = kernel(
            pack_kernel, "pack",
            [tokens.reshape(images, band, width), cotangent.reshape(images, band, width), keep_mask, qkv_weight, proj_weight,
             up_weight, down_weight.T, *[v.reshape(1, -1) for v in vectors]],
            [((pack_rows, width), BF), ((pack_rows, width), BF), ((lay.rows, 256 + PACKED), BF),
             ((lay.rows + EXTRA, 2 * third), BF),
             ((lay.rows, hidden + block), BF), ((lay.half_rows, hidden), BF), ((lay.rows - lay.half_rows, hidden), BF)],
            [(keep_mask.shape, jnp.int32), (qkv_weight.shape, F32), (proj_weight.shape, F32), (up_weight.shape, F32),
             (down_weight.T.shape, F32), *[((1, v.shape[0]), F32) for v in vectors], pltpu.SemaphoreType.DMA((18,))],
            limit=60, hbm=True,
        )
        third_came = me.swap(third_send, "c")
        near = me.swap(other, "y")
        bands = [mine, near, me.swap(mine, "c"), me.swap(near, "c")]
        (first_piece,) = kernel(fit_kernel, "fit", [third_came, first_piece], [((lay.rows + EXTRA, 3 * third), BF)])
        step = width // PARTS
        if lay.aligned:
            part0, top1, bottom1 = second_pieces
            near1 = me.pairs(lay.second, 0, top1, bottom1)
            pieces = me.high(first_piece, *near1)
            high0 = me.high(after(part0, pieces[1]))
            top, bottom = me.merge([after(pieces[0], near)] + pieces[1:], "merge_first")
            came = me.pairs(lay.first, -2, top, bottom)
            top = after(top, high0[1])
            shapes = [((2 * held.shape[0],) + held.shape[1:], BF) for held in (top, bottom)]
            top, bottom = call(join_kernel, "join_first", [top, came[0], bottom, came[1]], shapes)
            came = me.pairs(lay.first, -1, top, bottom)
            first = [top, came[0], bottom, came[1]]
            top0, bottom0 = me.merge(high0, "merge0")
            (both1,) = kernel(
                start_kernel, "start1", [after(top1, high0[3]), near1[0], bottom1, near1[1]], [((2, lay.rows, 2 * step), BF)]
            )
            vec_parts = [after(first[2], top0, bottom0), first[3]]
        else:
            first = [me.gather_whole(first_piece[: lay.rows])]
            vec_parts = [me.gather(first_piece[lay.rows : lay.rows + 2], me.orders[1])]
            second = [[me.gather_whole(p)] for p in (second_pieces[0], jnp.concatenate(second_pieces[1:], 0))]
        (vec,) = call(
            functools.partial(unpack_kernel, lay, plan, len(vec_parts)), "unpack", [table, *vec_parts],
            [((1, table.shape[1]), F32)], limit=24,
        )

        n_w = len(first)
        n_g = len(me.grad_shapes(1))
        a1, q, k, v, w_qkv, cos, sin, kp, mask_bias = call(
            functools.partial(project_kernel, lay, n_w), "qkv", [*bands, *first, vec],
            [((length, width), BF), ((length, own), BF), ((length, own), BF), ((length, own), BF), ((2, width, 3 * third), BF),
             ((length, own), F32), ((length, own), F32), ((length, 1), F32), ((1, length), F32)],
            [((2,) + lay.tiles + (3 * third,), BF)], limit=16,
        )
        ob, p = call(
            functools.partial(attend_kernel, lay, band), "attend", [q, k, v, mask_bias],
            [((length, own), BF), ((heads, length, length), BF)], limit=8,
        )
        if lay.aligned:
            near0 = me.pairs(lay.first, -2, top0, bottom0)
            far0 = me.pairs(lay.first, -1, top0, bottom0)
            both0 = me.pairs(lay.first, -1, *[after(n, ob) for n in near0])
            ob_other = me.swap(after(ob, *near0, *far0), "c")
            second = [[top0, near0[0], far0[0], both0[0], bottom0, near0[1], far0[1], both0[1]]]
        else:
            ob_other = me.swap(ob, "c")
        (p_cols,) = call(
            functools.partial(proj_kernel, lay, len(second[0])), "proj", second[0], [((width, 2 * block), BF)],
            [((2,) + lay.tiles + (block,), BF)],
        )
        p_other = me.swap(p_cols, "c")
        x1, a2, a2_t, dm, dm_t, d_down_bias, w_proj = call(
            functools.partial(middle_kernel, lay), "middle", [*bands, ob, ob_other, p_cols, p_other, vec, kp],
            [((length, width), F32), ((length, width), BF), ((width, length), BF), ((length, width), BF), ((width, length), BF),
             ((1, width), F32), ((width, width), BF)], limit=10,
        )
        if lay.aligned:
            high1 = me.high(both1, q)
            top1, bottom1 = me.merge([after(high1[0], p_cols)] + high1[1:], "merge1")
            last1 = me.pairs(lay.second, -1, top1, bottom1)
            second.append([top1, last1[0], bottom1, last1[1]])
        sums, second_grads, d_up_bias = [], [], []
        step = width // PARTS
        for part in range(PARTS):
            shapes = me.grad_shapes(2 * step) + [((1, 2 * step), F32)]
            scratch = [(lay.tiles + (2 * step,), BF), (lay.tiles + (step,), BF)]
            if part == PARTS - 1:
                shapes += [((half, width), F32), ((half, width), BF), ((length, width), F32), ((length, width), BF)]
                scratch = [((length, width), F32)] + scratch
            else:
                shapes += [((length, width), F32)] * 2
            outs = call(
                functools.partial(mlp_kernel, lay, part, len(second[part]), n_g), "mlp%d" % part,
                [x1, a2, a2_t, dm, dm_t, vec, *second[part], *sums], shapes, scratch, limit=18,
            )
            second_grads.append(outs[:n_g])
            d_up_bias.append(outs[n_g])
            sums = outs[n_g + 1 :]
        part, m_send, dn, dn_send = sums
        if lay.aligned:
            g = second_grads[0]
            came0 = me.pairs(lay.second, -1, g[1], g[3])
        dn_came = me.swap(dn_send, "c")
        m_came = me.swap(m_send, "c")
        out_half = (kp[:half] * (part + m_came.astype(F32))).astype(BF)
        pair = 2 * lay.head
        *outs, dx_half, dob, norm_sums, dq0, dk0, dv0 = call(
            functools.partial(back_kernel, lay, band, n_g), "back",
            [*bands, kp, x1, dn, dn_came, vec, w_proj, ob, ob_other, q, k, v, p, *second_grads[1]],
            [*me.grad_shapes(2 * step + block), ((half, width), F32), ((length, own), BF), ((3, width), F32), ((length, pair), F32),
             ((length, pair), F32), ((length, pair), F32)],
            [((length, width), BF), (lay.tiles + (block,), BF)], limit=20,
        )
        second_grads[1] = outs
        if lay.aligned:
            came1 = me.pairs(lay.first, -1, outs[1], outs[3])
        else:
            d_second = [[me.scatter_rows(g)] for g in second_grads]
        if lay.aligned:
            g = second_grads[0]
            keep0, send0 = me.rejoin(g[0], after(came0[0], dob), g[2], came0[1], "part0")
            dob = after(dob, keep0, send0)
            came0 = me.swap(send0, lay.high[1])
        dq1, dk1, dv1 = call(
            functools.partial(back_heads_kernel, lay, band), "back_heads", [q, k, v, p, dob], [((length, own - pair), F32)] * 3
        )
        if lay.aligned:
            g = second_grads[1]
            folded1 = me.fold(g, [after(came1[0], dq1), came1[1]], "part1")
            dq1 = after(dq1, *folded1)
            came1 = me.pairs(lay.first, -2, folded1[1], folded1[3])
        grad_shapes = me.grad_shapes(3 * third, EXTRA)
        dn1_keep, dn1_send, *first_grads = call(
            functools.partial(back_rest_kernel, lay, grad_plan, len(grad_shapes)), "back_rest",
            [*bands, q, k, cos, sin, a1, w_qkv, grad_table, *d_up_bias, d_down_bias, norm_sums, dq0, dk0, dv0, dq1, dk1, dv1],
            [((half, width), F32), ((half, width), BF), *grad_shapes],
            [((length, own), F32), (lay.tiles + (3 * third,), BF), ((length, 3 * own), BF)], limit=24,
        )
        if lay.aligned:
            g = first_grads
            came = me.pairs(lay.first, -1, after(g[1], came0, *came1), after(g[3], came0, *came1))
            keep0, send0 = me.halve(keep0, came0, "part0")
            came0 = me.swap(send0, lay.high[0])
            keep1, send1 = me.rejoin(folded1[0], came1[0], folded1[2], came1[1], "part1")
            came1 = me.swap(send1, lay.high[1])
            folded = me.fold(g, came, "first")
            came = me.pairs(lay.first, -2, after(folded[1], came0, came1), after(folded[3], came0, came1))
            d_second = [me.split(keep0, came0, "part0")]
            keep1, send1 = me.halve(keep1, came1, "part1")
            came1 = me.swap(send1, lay.high[0])
            keep, send = me.rejoin(folded[0], came[0], folded[2], came[1], "first")
            keep, send = me.halve(keep, me.swap(after(send, came1), lay.high[1]), "first")
            d_second.append([me.end(keep1, came1, "part1")])
            d_first = me.end(keep, me.swap(send, lay.high[0]), "first")
        else:
            d_first = me.scatter_rows(first_grads)
        dn1_came = me.swap(dn1_send, "c")
        tg_keep, tg_send = call(
            functools.partial(finish_kernel, lay), "finish", [bands[0], bands[1], dn1_keep, dn1_came, dx_half, vec],
            [((band, width), BF), ((band, width), BF)],
        )

        def to_images(keep, send):
            came = me.swap(send, "y")
            return pick(y, jnp.stack([keep, came]), jnp.stack([came, keep])).reshape(tokens.shape)

        layer_out = to_images(out_half[:band], out_half[band:])
        tokens_grad = to_images(tg_keep, tg_send)

        d_up, d_down, d_proj = call(
            functools.partial(tail_second_kernel, lay, [len(d) for d in d_second]), "tail_second",
            [held for d in d_second for held in d], [((lay.rows, n), F32) for n in (hidden, hidden, block)]
        )
        d_down = d_down.T
        (tail_send,) = kernel(tail_send_kernel, "tail_send", [d_first], [((lay.rows, 256 + PACKED), BF)])
        tail_came = me.swap(tail_send, "c")
        d_qkv, *r = call(
            functools.partial(tail_kernel, lay, grad_plan), "tail", [d_first, tail_came],
            [((lay.rows, 3 * third), F32), *[((1, count), F32) for _, _, _, count in grad_plan]],
        )
        r = [v.reshape(-1) for v in r]
        return (
            layer_out, tokens_grad, d_qkv, r[0], r[1], d_proj, r[2], r[3], r[4], r[5], r[6], d_up, r[7], d_down, r[8], r[9],
        )

    return body


def solution(mesh):
    split = P(("img", "row"))
    both = P("img", "row")
    field = P("img", "row", None, None)
    return jax.shard_map(
        make_body(mesh.shape["img"]),
        mesh=mesh,
        in_specs=(
            field, P("img", "row", None), field, both, split, both, split, split, split, split, split, both, split,
            P("row", "img"), split, split,
        ),
        out_specs=(
            field, field, both, split, split, both, split, split, split, split, split, both, split, P("row", "img"),
            split, split,
        ),
        check_vma=False,
    )
```

```python
import functools

import jax
import jax.numpy as jnp
import numpy as np
from jax import lax
from jax.experimental import pallas as pl
from jax.experimental.pallas import tpu as pltpu
from jax.sharding import PartitionSpec as P

HEADS = 12
PARTS = (3, 3)
NORM_EPSILON = 1e-06
MASKED_SCORE = -1e30
BF = jnp.bfloat16
F32 = jnp.float32
MIB = 2**20
VMEM = pl.BlockSpec(memory_space=pltpu.VMEM)
HBM = pl.BlockSpec(memory_space=pltpu.MemorySpace.HBM)
PACKED = 384
EXTRA = 8


def dot(left, right, dims):
    return lax.dot_general(left, right, (dims, ((), ())), preferred_element_type=F32)


def nn(left, right):
    return dot(left, right, ((1,), (0,)))


def nt(left, right):
    return dot(left, right, ((1,), (1,)))


def tn(left, right):
    return dot(left, right, ((0,), (0,)))


def normed_rows(values):
    center = values - jnp.mean(values, -1, keepdims=True)
    inverse = lax.rsqrt(jnp.mean(center * center, -1, keepdims=True) + NORM_EPSILON)
    return center * inverse, inverse


def norm_back(grad, normed, inverse, gain):
    scaled = grad * gain
    centred = scaled - jnp.mean(scaled, -1, keepdims=True)
    return inverse * (centred - normed * jnp.mean(scaled * normed, -1, keepdims=True))


def column_sum(value):
    return jnp.sum(value, 0, keepdims=True)


def here():
    row = lax.axis_index("row")
    return lax.axis_index("img"), row >> 1, row & 1, row


class Layout:
    def __init__(self, img_count, tokens, rows):
        self.img_count = img_count
        self.bits = img_count.bit_length() - 1
        self.rows = rows
        self.half_rows = rows // 2
        self.aligned = rows % 32 == 0 and img_count == 8
        self.images, self.band_rows, self.side, self.width = tokens.shape
        self.band = self.band_rows * self.side
        self.length = 4 * self.band
        self.head = self.width // HEADS
        self.own = self.width // 2
        self.third = self.own // 2
        self.high = list(range(self.bits - 1, 0, -1))
        self.first = (self.high + [0, "y"], self.high + ["y", 0])
        self.second = ([0] + self.high + ["y"], ["y"] + self.high + [0])
        sizes = [self.width * sixths // 6 for sixths in PARTS]
        self.parts = [slice(sum(sizes[:n]), sum(sizes[: n + 1])) for n in range(len(sizes))]
        self.gathered = (self.first, self.second)
        self.reduced = (self.second, self.first)
        self.tiles = (img_count, rows) if self.aligned else (1, self.width)

    def slots(self, orders, img_rel, y_rel):
        found = []
        for order in orders:
            bits = [y_rel if step == "y" else (img_rel >> step) & 1 for step in order]
            found.append((sum(bit << k for k, bit in enumerate(bits[:-1])), bits[-1]))
        return found


def load_pieces(lay, orders, refs, y_rel, target, columns=slice(None)):
    if not lay.aligned:
        target[...] = refs[0][here()[1] ^ y_rel, :, :, columns]
        return
    half = lay.half_rows
    count = len(refs) // 2
    for img_rel in range(lay.img_count):
        for part, (slot, last) in enumerate(lay.slots(orders, img_rel, y_rel)):
            which, slot = divmod((slot + last * lay.img_count) * count, 2 * lay.img_count)
            ref, slot = refs[part * count + which], slot // count
            target[img_rel ^ here()[0], part * half : (part + 1) * half] = ref[slot, :half, columns]


def store_pieces(lay, orders, refs, y_rel, columns, source):
    if not lay.aligned:
        refs[0][here()[1] ^ y_rel, :, :, columns] = source[...]
        return
    half = lay.half_rows
    for img_rel in range(lay.img_count):
        for part, (slot, last) in enumerate(lay.slots(orders, img_rel, y_rel)):
            refs[2 * part + last][slot, :half, columns] = source[img_rel ^ here()[0], part * half : (part + 1) * half]


def halves_of(lay, value):
    pairs = lay.head // 2
    lane = lax.broadcasted_iota(jnp.int32, value.shape, 1)
    width = value.shape[1]
    first = (lane & pairs) == 0
    return jnp.where(first, pltpu.roll(value, width - pairs, 1), pltpu.roll(value, pairs, 1))


def pack_kernel(lay, *refs):
    tok, cot, mask, qkv, proj, up, down, *vectors = refs[:16]
    mine_ref, other_ref, third_ref, first_ref = refs[16:20]
    second, refs = [*refs[20:22], other_ref.at[2 * lay.band + 16 :]], refs[22:]
    mask_in, qkv_in, proj_in, up_in, down_in, *vectors_in = refs[:14]
    sems = refs[14]
    y = here()[1]
    band, third, width, rows = lay.band, lay.third, lay.width, lay.rows
    pairs = [(qkv, qkv_in), (proj, proj_in), *zip(vectors, vectors_in), (up, up_in), (down, down_in), (mask, mask_in)]
    for ref, which in ((other_ref, 1 - y), (mine_ref, y)):
        pairs += [(tok.at[which], ref.at[:band]), (cot.at[which], ref.at[band : 2 * band])]
    copies = [pltpu.make_async_copy(source, target, sems.at[n]) for n, (source, target) in enumerate(pairs)]
    for copy in copies:
        copy.start()
    for copy in copies[:11]:
        copy.wait()
    packed = jnp.concatenate([v[...] for v in vectors_in], 1)
    packed = jnp.concatenate([packed, jnp.zeros((1, PACKED - packed.shape[1]), F32)], 1).astype(BF)
    third_ref[:, :third] = qkv_in[:, third : 2 * third].astype(BF)
    third_ref[:, third:] = jnp.zeros((rows, third_ref.shape[1] - third), BF)
    third_ref[0:1, third_ref.shape[1] - PACKED :] = packed
    first_ref[:rows, :third] = qkv_in[:, :third].astype(BF)
    first_ref[:rows, third : 2 * third] = qkv_in[:, 2 * third :].astype(BF)
    first_ref[rows:] = jnp.zeros((EXTRA, first_ref.shape[1]), BF)
    first_ref[rows : rows + 1, :PACKED] = packed
    for copy in copies[11:]:
        copy.wait()
    for ref, part, first_row in zip(second, (0, 1, 1), (0, 0, lay.half_rows)):
        at = lay.parts[part]
        step = at.stop - at.start
        side = slice(first_row, first_row + ref.shape[0])
        ref[:, :step] = up_in[side, at].astype(BF)
        ref[:, step : 2 * step] = down_in[side, at].astype(BF)
        if part == 0:
            ref[:, 2 * step :] = proj_in[side].astype(BF)
    for ref, which in ((mine_ref, y), (other_ref, 1 - y)):
        keep = [jnp.where(which == 0, mask_in[r, 0:1], mask_in[r, 1:2]).astype(F32) for r in range(lay.band_rows)]
        flat = jnp.concatenate(keep, 1)
        flat = jnp.concatenate([flat, jnp.zeros((1, width - band), F32)], 1)
        ref[2 * band : 2 * band + 16] = jnp.concatenate([flat, jnp.zeros((15, width), F32)], 0).astype(BF)


def fit_kernel(lay, came_ref, first_ref, out_ref):
    third, rows = lay.third, lay.rows
    c = here()[2]
    t0, t2, came = first_ref[:rows, :third], first_ref[:rows, third : 2 * third], came_ref[:, :third]
    out_ref[:rows, : 3 * third] = jnp.where(c == 0, jnp.concatenate([t0, t2, came], 1), jnp.concatenate([came, t0, t2], 1))
    theirs = came_ref[0:1, came_ref.shape[1] - PACKED :]
    rest = jnp.zeros((EXTRA - 2, PACKED), F32).astype(BF)
    out_ref[rows:] = jnp.zeros((EXTRA, out_ref.shape[1]), BF)
    out_ref[rows:, :PACKED] = jnp.concatenate([first_ref[rows : rows + 1, :PACKED], theirs, rest], 0)


def merge_kernel(lay, *refs):
    pieces, (top_ref, bottom_ref) = refs[:-2], refs[-2:]
    half = lay.half_rows
    for k, ref in enumerate(pieces):
        if len(ref.shape) == 2:
            top_ref[k] = ref[:half]
            bottom_ref[k] = ref[half:]
        else:
            count = ref.shape[0]
            top_ref[k * count : (k + 1) * count] = ref[:, :half]
            bottom_ref[k * count : (k + 1) * count] = ref[:, half:]


def start_kernel(lay, top, top_came, bottom, bottom_came, out_ref):
    half = lay.half_rows
    out_ref[0, :half], out_ref[1, :half] = top[...], top_came[...]
    first = 2 * lay.band + 16
    out_ref[0, half:], out_ref[1, half:] = bottom[first:], bottom_came[first:]


def join_kernel(*refs):
    for part in range(2):
        own, came = refs[2 * part : 2 * part + 2]
        refs[4 + part][: own.shape[0]] = own[...]
        refs[4 + part][own.shape[0] :] = came[...]


def fold_kernel(*refs):
    for part in range(2):
        keep, came = refs[2 * part : 2 * part + 2]
        count = keep.shape[0] // 2
        for half in range(2):
            at = slice(half * count, (half + 1) * count)
            refs[4 + 2 * part + half][...] = (keep[at].astype(F32) + came[at].astype(F32)).astype(BF)


def rejoin_kernel(n, *refs):
    outs = refs[len(refs) - n :]
    top = refs[0].shape[1]
    count = refs[0].shape[0] // n
    column = 0
    for k in range(0, len(refs) - n, 4):
        columns = slice(column, column + refs[k].shape[2])
        column = columns.stop
        for part in range(2):
            keep, came = refs[k + 2 * part : k + 2 * part + 2]
            rows = slice(0, top) if part == 0 else slice(top, None)
            for share, out in enumerate(outs):
                at = slice(share * count, (share + 1) * count)
                out[:, rows, columns] = (keep[at].astype(F32) + came[at].astype(F32)).astype(BF)


def end_kernel(*refs):
    refs[-1][...] = sum(ref[0].astype(F32) for ref in refs[:-1]).astype(BF)


def halve_kernel(keep_ref, came_ref, *outs):
    count = keep_ref.shape[0] // len(outs)
    for half, ref in enumerate(outs):
        at = slice(half * count, (half + 1) * count)
        total = (keep_ref[at].astype(F32) + came_ref[at].astype(F32)).astype(BF)
        ref[...] = total.reshape(ref.shape)


def split_kernel(keep_ref, came_ref, out_ref, top_ref, bottom_ref):
    half = top_ref.shape[0]
    out_ref[...] = (keep_ref[0].astype(F32) + came_ref[0].astype(F32)).astype(BF)
    top_ref[...] = (keep_ref[1, :half].astype(F32) + came_ref[1, :half].astype(F32)).astype(BF)
    bottom_ref[...] = (keep_ref[1, half:].astype(F32) + came_ref[1, half:].astype(F32)).astype(BF)


def owner_mask(lay, c_rel, table_row):
    place = lax.broadcasted_iota(jnp.int32, (2 * lay.img_count, 1), 0)
    img_rel = jnp.zeros_like(place)
    row = here()[3] ^ c_rel
    for k, step in enumerate(lay.first[1]):
        bit = (place >> k) & 1
        if step == "y":
            row = row ^ (bit * 2)
        else:
            img_rel = img_rel | (bit << step)
    return ((img_rel ^ here()[0]) * 4 + row) == table_row


def owners(table_ref, at, c):
    owner = jnp.where(c == 0, table_ref[0:1, at], table_ref[2:3, at])
    entry = jnp.where(c == 0, table_ref[1:2, at], table_ref[3:4, at])
    return owner, entry


def unpack_kernel(lay, plan, n_v, table_ref, *refs):
    v_refs, out_ref = refs[:n_v], refs[n_v]
    if lay.aligned:
        half = lay.half_rows
        rows = [ref[k, half : half + EXTRA, :PACKED].astype(F32) for ref in v_refs for k in range(ref.shape[0])]
        gathered = [jnp.concatenate([row[c_rel : c_rel + 1] for row in rows], 0).astype(BF) for c_rel in range(2)]
    else:
        gathered = [v_refs[0][:, c_rel, :PACKED] for c_rel in range(2)]
    for start, size, offset, count in plan:
        at = slice(start, start + size)
        owner, entry = owners(table_ref, at, here()[2])
        spread = (lax.broadcasted_iota(jnp.int32, (count, size), 0) == entry).astype(F32).astype(BF)
        total = 0.0
        for c_rel in range(2):
            rows = nn(gathered[c_rel][:, offset : offset + count], spread)
            total = total + column_sum(jnp.where(owner_mask(lay, c_rel, owner), rows, 0.0))
        out_ref[:, at] = total


def repack(lay, plan, table_ref, grads, refs):
    sides = []
    for c_rel in range(2):
        parts = []
        for grad, (start, size, offset, count) in zip(grads, plan):
            owner, entry = owners(table_ref, slice(start, start + size), here()[2])
            spread = (lax.broadcasted_iota(jnp.int32, (count, size), 0) == entry).astype(F32).astype(BF)
            rows = jnp.where(owner_mask(lay, c_rel, owner), grad, 0.0).astype(BF)
            parts.append(nt(rows, spread))
        used = sum(p.shape[1] for p in parts)
        sides.append(jnp.concatenate(parts + [jnp.zeros((2 * lay.img_count, PACKED - used), F32)], 1))
    if not lay.aligned:
        refs[1][...] = jnp.zeros(refs[1].shape, BF)
        for c_rel in range(2):
            refs[1][:, c_rel, :PACKED] = sides[c_rel].astype(BF)
        return
    half, count = lay.half_rows, lay.img_count
    for j in range(2 * count):
        ref = refs[2 + j // count]
        block = jnp.concatenate([side[j : j + 1] for side in sides] + [jnp.zeros((EXTRA - 2, PACKED), F32)], 0).astype(BF)
        ref[j % count, half:] = jnp.zeros((EXTRA, ref.shape[2]), BF)
        ref[j % count, half:, :PACKED] = block


def project_kernel(lay, n_w, t0, t1, t2, t3, *refs):
    w_refs = refs[:n_w]
    vec_ref, a_ref, q_ref, k_ref, v_ref, w_out, cos_ref, sin_ref, kp_ref, bias_ref, w_all = refs[n_w:]
    band, side, own, third = lay.band, lay.side, lay.own, lay.third
    g_ref, s_ref, b_ref = (vec_ref[:, lay.at[n]] for n in ("attn_gain", "attn_shift", "qkv_bias"))
    f_ref = vec_ref[:, lay.at["freqs"]]
    keeps = []
    for b, ref in enumerate((t0, t1, t2, t3)):
        at = slice(b * band, (b + 1) * band)
        normed, _ = normed_rows(ref[:band].astype(F32))
        a_ref[at] = (normed * g_ref + s_ref).astype(BF)
        keep = ref[2 * band : 2 * band + 16, :band].astype(F32)
        kp_ref[at] = jnp.transpose(keep)[:, 0:1]
        keeps.append(keep[0:1])
    bias_ref[...] = jnp.where(jnp.concatenate(keeps, 1) > 0, 0.0, MASKED_SCORE)
    lane = lax.broadcasted_iota(jnp.int32, (side, own), 1)
    sign = jnp.where((lane & (lay.head // 2)) == 0, -1.0, 1.0).astype(F32)
    col = lax.broadcasted_iota(jnp.int32, (side, own), 0).astype(F32) * f_ref[:, :own]
    col_cos, col_sin = jnp.cos(col), jnp.sin(col)
    row_index = here()[3]
    for b, flip in enumerate((0, 2, 1, 3)):
        first = ((row_index ^ flip) * lay.band_rows).astype(F32)
        rows = (lax.broadcasted_iota(jnp.int32, (8, own), 0).astype(F32) + first) * f_ref[:, own:]
        row_cos, row_sin = jnp.cos(rows), jnp.sin(rows)
        for r in range(lay.band_rows):
            at = slice(b * band + r * side, b * band + (r + 1) * side)
            rc, rs = row_cos[r : r + 1], row_sin[r : r + 1]
            cos_ref[at] = col_cos * rc - col_sin * rs
            sin_ref[at] = (col_sin * rc + col_cos * rs) * sign
    for y_rel in range(2):
        y_side = here()[1] ^ y_rel
        load_pieces(lay, lay.first, w_refs, y_rel, w_all.at[y_side])
    acts = a_ref[...]
    w0, w1 = w_all[0].reshape(lay.width, -1), w_all[1].reshape(lay.width, -1)
    w_out[0], w_out[1] = w0, w1
    left = nn(acts, w0) + b_ref[:, : 3 * third]
    right = nn(acts, w1) + b_ref[:, 3 * third :]
    query, key = left[:, :own], jnp.concatenate([left[:, own:], right[:, :third]], 1)
    cos, sin = cos_ref[...], sin_ref[...]
    q_ref[...] = (query * cos + halves_of(lay, query) * sin).astype(BF)
    k_ref[...] = (key * cos + halves_of(lay, key) * sin).astype(BF)
    v_ref[...] = right[:, third:].astype(BF)


def proj_kernel(lay, n_w, *refs):
    out_ref, w_all = refs[n_w:]
    block = lay.width // 4
    columns = slice(refs[0].shape[-1] - block, None)
    for y_rel in range(2):
        y_side = here()[1] ^ y_rel
        load_pieces(lay, lay.gathered[0], refs[:n_w], y_rel, w_all.at[y_side], columns)
    for y_side in range(2):
        out_ref[:, y_side * block : (y_side + 1) * block] = w_all[y_side].reshape(lay.width, block)


def attend_kernel(lay, chunk, first, count, q_ref, k_ref, v_ref, bias_ref, o_ref, p_ref):
    head = lay.head
    pair = 2 * head
    scale = head**-0.5

    def step(n, carry):
        at = pl.ds(pl.multiple_of(n * pair, pair), pair)
        out = pl.ds(pl.multiple_of((n - first) * pair, pair), pair)
        keys, values = k_ref[:, at], v_ref[:, at]
        for start in range(0, lay.length, chunk):
            rows = slice(start, start + chunk)
            query = q_ref[rows, at] * jnp.asarray(scale, BF)
            lane = lax.broadcasted_iota(jnp.int32, query.shape, 1)
            outs = []
            for h in range(2):
                mine = (lane < head) if h == 0 else (lane >= head)
                score = nt(jnp.where(mine, query, jnp.zeros_like(query)), keys) + bias_ref[...]
                power = jnp.exp(score - jnp.max(score, -1, keepdims=True))
                weights = (power * (1.0 / jnp.sum(power, -1, keepdims=True))).astype(BF)
                p_ref[2 * (n - first) + h, rows] = weights
                outs.append(nn(weights, values))
            o_ref[rows, out] = jnp.where(lane < head, outs[0], outs[1]).astype(BF)
        return carry

    lax.fori_loop(first, first + count, step, 0)


def both_heads(half, ob0, ob1, oo0, oo1):
    other = jnp.concatenate([oo0[...], oo1[...]], 1)
    return jnp.concatenate([ob0[...], ob1[...]], 1), jnp.concatenate([other[half:], other[:half]], 0)


def middle_kernel(lay, t0, t1, t2, t3, ob0, ob1, oo0, oo1, p_ref, po_ref, vec_ref, kp_ref, x1_ref, a2_ref, at_ref, dm_ref, dt_ref, dbg_ref, wp_ref):
    band, third, half = lay.band, lay.third, lay.length // 2
    c = here()[2]
    block = lay.width // 4
    pb_ref, g_ref, s_ref = (vec_ref[:, lay.at[n]] for n in ("proj_bias", "mlp_gain", "mlp_shift"))
    for y_side in range(2):
        mine, other = (ref[:, y_side * block : (y_side + 1) * block] for ref in (p_ref, po_ref))
        wp_ref[:, 2 * y_side * block : 2 * (y_side + 1) * block] = jnp.where(
            c == 0, jnp.concatenate([mine, other], 1), jnp.concatenate([other, mine], 1)
        )
    low = [pl.ds(pl.multiple_of((2 * s + c) * third, third), third) for s in range(2)]
    high = [pl.ds(pl.multiple_of((2 * s + 1 - c) * third, third), third) for s in range(2)]
    own_w = jnp.concatenate([wp_ref[low[0]], wp_ref[low[1]]], 0)
    other_w = jnp.concatenate([wp_ref[high[0]], wp_ref[high[1]]], 0)
    mine, other = both_heads(half, ob0, ob1, oo0, oo1)
    x1_ref[...] = nn(mine, own_w) + nn(other, other_w) + pb_ref
    for b, ref in enumerate((t0, t1, t2, t3)):
        at = slice(b * band, (b + 1) * band)
        x1 = x1_ref[at] + ref[:band].astype(F32)
        x1_ref[at] = x1
        normed, _ = normed_rows(x1)
        a2_ref[at] = (normed * g_ref + s_ref).astype(BF)
        dm_ref[at] = (ref[band : 2 * band].astype(F32) * kp_ref[at]).astype(BF)
    at_ref[...] = a2_ref[...].T
    dt_ref[...] = dm_ref[...].T
    dbg_ref[...] = column_sum(dm_ref[:half].astype(F32))


def mlp_kernel(lay, part, n_w, n_g, x1_ref, a2_ref, at_ref, dm_ref, dt_ref, vec_ref, *refs):
    w_refs, refs = refs[:n_w], refs[n_w:]
    last = part == len(PARTS) - 1
    if part:
        (m_in, dn_in), refs = refs[:2], refs[2:]
    count = n_g if last else 2 * n_g
    grads, refs = refs[:count], refs[count:]
    ubg_ref, refs = refs[0], refs[1:]
    if last:
        part_ref, msend_ref, dn_ref, dnsend_ref, m_ref, w_all, g_tmp = refs
    else:
        m_ref, dn_ref, w_all, g_tmp = refs
    width, half = lay.width, lay.length // 2
    chunk = lay.parts[part].stop - lay.parts[part].start
    up_bias = lay.at["up_bias"].start + lay.parts[part].start
    for y_rel in range(2):
        load_pieces(lay, lay.gathered[part], w_refs, y_rel, w_all, slice(0, 2 * chunk))
        y_side = here()[1] ^ y_rel
        up = w_all[:, :, :chunk].reshape(width, chunk)
        down = w_all[:, :, chunk:].reshape(width, chunk)
        pre = nn(a2_ref[...], up) + vec_ref[:, pl.ds(pl.multiple_of(y_side * width + up_bias, 128), chunk)]
        cdf = 0.5 * (1.0 + lax.erf(pre * 0.7071067811865476))
        slope = cdf + pre * (jnp.exp(-0.5 * pre * pre) * 0.3989422804014327)
        act = (pre * cdf).astype(BF)
        du = (nn(dm_ref[...], down) * slope).astype(BF)
        ubg_ref[:, pl.ds(pl.multiple_of(y_side * chunk, 128), chunk)] = column_sum(du.astype(F32))
        g_tmp[...] = nn(at_ref[...], du).astype(BF).reshape(g_tmp.shape)
        own, at = (grads[:n_g], slice(None)) if not last else (grads, slice(0, chunk))
        store_pieces(lay, lay.reduced[part], own, y_rel, at, g_tmp)
        g_tmp[...] = nn(dt_ref[...], act).astype(BF).reshape(g_tmp.shape)
        own, at = (grads[n_g:], slice(None)) if not last else (grads, slice(chunk, None))
        store_pieces(lay, lay.reduced[part], own, y_rel, at, g_tmp)
        m, dn = nt(act, down), nt(du, up)
        if y_rel == 0:
            m_ref[...] = m + m_in[...] if part else m
            dn_ref[...] = dn + dn_in[...] if part else dn
        else:
            m_ref[...] += m
            dn_ref[...] += dn
    if last:
        part_ref[...] = x1_ref[:half] + m_ref[:half] + vec_ref[:, lay.at["down_bias"]]
        msend_ref[...] = m_ref[half:].astype(BF)
        dnsend_ref[...] = dn_ref[...].astype(BF)


def attend_back(lay, chunk, first, count, base, q_ref, k_ref, v_ref, p_ref, dob_ref, dq_ref, dk_ref, dv_ref):
    head = lay.head
    pair = 2 * head
    scale = head**-0.5

    def step(n, carry):
        at = pl.ds(pl.multiple_of(n * pair, pair), pair)
        out = pl.ds(pl.multiple_of((n - base) * pair, pair), pair)
        keys, values = k_ref[:, at], v_ref[:, at]
        for start in range(0, lay.length, chunk):
            rows = slice(start, start + chunk)
            query, dob = q_ref[rows, at], dob_ref[rows, at]
            lane = lax.broadcasted_iota(jnp.int32, query.shape, 1)
            dqs, dks, dvs = [], [], []
            for h in range(2):
                mine = (lane < head) if h == 0 else (lane >= head)
                weights = p_ref[2 * (n - base) + h, rows]
                soft = weights.astype(F32)
                dp = nt(jnp.where(mine, dob, jnp.zeros_like(dob)), values)
                ds = (soft * (dp - jnp.sum(soft * dp, -1, keepdims=True))).astype(BF)
                dqs.append(nn(ds, keys))
                dks.append(tn(ds, query))
                dvs.append(tn(weights, dob))
            dq_ref[rows, out] = jnp.where(lane < head, dqs[0], dqs[1]) * scale
            lane = lax.broadcasted_iota(jnp.int32, keys.shape, 1)
            dk = jnp.where(lane < head, dks[0], dks[1]) * scale
            dv = jnp.where(lane < head, dvs[0], dvs[1])
            if start == 0:
                dk_ref[:, out] = dk
                dv_ref[:, out] = dv
            else:
                dk_ref[:, out] += dk
                dv_ref[:, out] += dv
        return carry

    lax.fori_loop(first, first + count, step, 0)


def back_kernel(
    lay, chunk, n_g, t0, t1, t2, t3, kp_ref, x1_ref, dn_ref, came_ref, vec_ref, wp_ref, ob0, ob1, oo0, oo1, q_ref, k_ref, v_ref,
    p_ref, *refs,
):
    grads_in, grads, refs = refs[:n_g], refs[n_g : 2 * n_g], refs[2 * n_g :]
    dx_ref, dob_ref, sums_ref, dq_ref, dk_ref, dv_ref, dxb_ref, g_tmp = refs
    for before, ref in zip(grads_in, grads):
        ref[..., : before.shape[-1]] = before[...]
    g_ref = vec_ref[:, lay.at["mlp_gain"]]
    band, third, half = lay.band, lay.third, lay.length // 2
    c = here()[2]
    gg, sg, pbg = 0.0, 0.0, 0.0
    for b, ref in enumerate((t0, t1, t2, t3)):
        at = slice(b * band, (b + 1) * band)
        away = slice((b ^ 2) * band, ((b ^ 2) + 1) * band)
        dn = dn_ref[at] + came_ref[away].astype(F32)
        normed, inverse = normed_rows(x1_ref[at])
        dx = ref[band : 2 * band].astype(F32) * kp_ref[at] + norm_back(dn, normed, inverse, g_ref)
        dxb = dx.astype(BF)
        dxb_ref[at] = dxb
        if b < 2:
            dx_ref[at] = dx
            gg = gg + column_sum(dn * normed)
            sg = sg + column_sum(dn)
            pbg = pbg + column_sum(dxb.astype(F32))
    low = [pl.ds(pl.multiple_of((2 * s + c) * third, third), third) for s in range(2)]
    own_w = jnp.concatenate([wp_ref[low[0]], wp_ref[low[1]]], 0)
    dxb = dxb_ref[...]
    dob_ref[...] = nt(dxb, own_w).astype(BF)
    block = lay.width // 4
    zero = jnp.concatenate([dxb[:, :block], dxb[:, 2 * block : 3 * block]], 1)
    one = jnp.concatenate([dxb[:, block : 2 * block], dxb[:, 3 * block :]], 1)
    cols = jnp.where(c == 0, zero, one)
    mine, other = both_heads(half, ob0, ob1, oo0, oo1)
    mine_g, other_g = tn(mine, cols).astype(BF), tn(other, cols).astype(BF)
    zero, one = jnp.where(c == 0, mine_g, other_g), jnp.where(c == 0, other_g, mine_g)
    p_grad = jnp.concatenate([zero[:third], one[:third], zero[third:], one[third:]], 0)
    columns = slice(grads_in[0].shape[-1], None)
    sides = [p_grad[:, :block], p_grad[:, block:]]
    for y_rel in range(2):
        g_tmp[...] = jnp.where((here()[1] ^ y_rel) == 0, sides[0], sides[1]).reshape(g_tmp.shape)
        store_pieces(lay, lay.reduced[1], grads, y_rel, columns, g_tmp)
    sums_ref[...] = jnp.concatenate([gg, sg, pbg], 0)
    attend_back(lay, chunk, 0, 1, 0, q_ref, k_ref, v_ref, p_ref, dob_ref, dq_ref, dk_ref, dv_ref)


def back_heads_kernel(lay, chunk, q_ref, k_ref, v_ref, p_ref, dob_ref, dq_ref, dk_ref, dv_ref):
    attend_back(lay, chunk, 1, HEADS // 4 - 1, 1, q_ref, k_ref, v_ref, p_ref, dob_ref, dq_ref, dk_ref, dv_ref)


def back_rest_kernel(
    lay, plan, n_g, t0, t1, t2, t3, q_ref, k_ref, cos_ref, sin_ref, a_ref, w_ref, table_ref, ubg0, ubg1, dbg_ref, sums_ref,
    dq0, dk0, dv0, dq1, dk1, dv1, *refs,
):
    keep_ref, send_ref = refs[:2]
    grads = refs[2 : 2 + n_g]
    dq_ref, g_tmp, dqkv_ref = refs[2 + n_g :]
    band, side, own, third, half, head = lay.band, lay.side, lay.own, lay.third, lay.length // 2, lay.head
    gg, sg, pbg = sums_ref[0:1], sums_ref[1:2], sums_ref[2:3]
    sizes = [ref.shape[1] // 2 for ref in (ubg0, ubg1)]
    ubg = [ref[:, y_side * size : (y_side + 1) * size] for y_side in range(2) for ref, size in zip((ubg0, ubg1), sizes)]
    ubg = jnp.concatenate(ubg, 1)
    cos, sin = cos_ref[...], sin_ref[...]
    dq, dk, dv = (jnp.concatenate([a[...], b[...]], 1) for a, b in ((dq0, dq1), (dk0, dk1), (dv0, dv1)))
    dqkv_ref[:, :own] = (dq * cos + halves_of(lay, dq * sin)).astype(BF)
    dqkv_ref[:, own : 2 * own] = (dk * cos + halves_of(lay, dk * sin)).astype(BF)
    dqkv_ref[:, 2 * own :] = dv.astype(BF)
    dq_ref[...] = dq * halves_of(lay, q_ref[...].astype(F32)) + dk * halves_of(lay, k_ref[...].astype(F32))
    by_col = jnp.zeros((side, own), F32)
    by_row = jnp.zeros((side, own), F32)
    for b, flip in enumerate((0, 2, 1, 3)):
        first = ((here()[3] ^ flip) * lay.band_rows).astype(F32)
        for r in range(lay.band_rows):
            turn = dq_ref[b * band + r * side : b * band + (r + 1) * side]
            by_col = by_col + turn
            by_row = by_row + turn * (first + r)
    lane = lax.broadcasted_iota(jnp.int32, (2, own), 1)
    sign = jnp.where((lane & (head // 2)) == 0, -1.0, 1.0).astype(F32)
    place = lax.broadcasted_iota(jnp.int32, (side, own), 0).astype(F32)
    both = jnp.concatenate([column_sum(by_col * place), column_sum(by_row)], 0) * sign
    both = jnp.where(sign < 0, both + halves_of(lay, both), 0.0)
    freqs = jnp.concatenate([both[0:1], both[1:2]], 1)
    bqk = column_sum(dqkv_ref[:, : 2 * own].astype(F32))
    bv = column_sum(dqkv_ref[:, 2 * own :].astype(F32))
    grad = nt(dqkv_ref[:, : 3 * third], w_ref[0]) + nt(dqkv_ref[:, 3 * third :], w_ref[1])
    keep_ref[...] = grad[:half]
    send_ref[...] = grad[half:].astype(BF)
    g1, s1 = 0.0, 0.0
    for b, ref in enumerate((t0, t1, t2, t3)):
        part = grad[b * band : (b + 1) * band]
        normed, _ = normed_rows(ref[:band].astype(F32))
        g1 = g1 + column_sum(part * normed)
        s1 = s1 + column_sum(part)
    repack(lay, plan, table_ref, [bqk, bv, pbg, g1, s1, gg, sg, ubg, dbg_ref[...], freqs], grads)
    acts = a_ref[...]
    sides = []
    for y_side in range(2):
        grad = tn(acts, dqkv_ref[:, y_side * 3 * third : (y_side + 1) * 3 * third]).astype(BF)
        sides.append(grad)
    y = here()[1]
    for y_rel in range(2):
        g_tmp[...] = jnp.where((y ^ y_rel) == 0, sides[0], sides[1]).reshape(g_tmp.shape)
        store_pieces(lay, lay.first, grads, y_rel, slice(None), g_tmp)


def finish_kernel(lay, t0, t1, keep_ref, came_ref, dx_ref, vec_ref, out_ref, send_ref):
    band = lay.band
    g_ref = vec_ref[:, lay.at["attn_gain"]]
    for b, ref in enumerate((t0, t1)):
        at = slice(b * band, (b + 1) * band)
        dn = keep_ref[at] + came_ref[at].astype(F32)
        normed, inverse = normed_rows(ref[:band].astype(F32))
        result = (dx_ref[at] + norm_back(dn, normed, inverse, g_ref)).astype(BF)
        if b == 0:
            out_ref[...] = result
        else:
            send_ref[...] = result


def tail_second_kernel(lay, counts, *refs):
    up_ref, down_ref, proj_ref = refs[-3:]
    half = lay.half_rows
    for part, count in enumerate(counts):
        at = lay.parts[part]
        step = at.stop - at.start
        keep, *came = refs[sum(counts[:part]) : sum(counts[: part + 1])]
        if not came:
            up_ref[:, at], down_ref[:, at] = keep[:, :step].astype(F32), keep[:, step : 2 * step].astype(F32)
        for rows, ref in zip((slice(0, half), slice(half, None)), came):
            up_ref[rows, at] = keep[rows, :step].astype(F32) + ref[:, :step].astype(F32)
            down_ref[rows, at] = keep[rows, step:].astype(F32) + ref[:, step:].astype(F32)
        if part:
            proj_ref[...] = keep[:, 2 * step :].astype(F32)


def tail_send_kernel(lay, sum_ref, out_ref):
    third, rows = lay.third, lay.rows
    out_ref[:, :third] = jnp.where(here()[2] == 0, sum_ref[:rows, 2 * third : 3 * third], sum_ref[:rows, :third])
    out_ref[:, third:] = jnp.zeros((rows, out_ref.shape[1] - third), BF)
    theirs = sum_ref[rows:, :PACKED].astype(F32)[1:2]
    out_ref[0:1, out_ref.shape[1] - PACKED :] = theirs.astype(BF)


def tail_kernel(lay, plan, sum_ref, came_ref, qkv_ref, *outs):
    third, rows = lay.third, lay.rows
    d0, d1, d2 = (sum_ref[:rows, k * third : (k + 1) * third] for k in range(3))
    c = here()[2]
    qkv_ref[:, :third] = jnp.where(c == 0, d0, d1).astype(F32)
    qkv_ref[:, third : 2 * third] = came_ref[:, :third].astype(F32)
    qkv_ref[:, 2 * third :] = jnp.where(c == 0, d1, d2).astype(F32)
    total = sum_ref[rows:, :PACKED].astype(F32)[0:1] + came_ref[0:1, came_ref.shape[1] - PACKED :].astype(F32)
    for ref, (_, _, offset, count) in zip(outs, plan):
        ref[...] = total[:, offset : offset + count]


def call(kernel, name, inputs, outs, scratch=(), limit=16, hbm=False):
    return pl.pallas_call(
        kernel,
        out_shape=[jax.ShapeDtypeStruct(shape, dtype) for shape, dtype in outs],
        in_specs=[HBM if hbm else VMEM] * len(inputs),
        out_specs=[VMEM] * len(outs),
        scratch_shapes=[s if not isinstance(s, tuple) else pltpu.VMEM(*s) for s in scratch],
        compiler_params=pltpu.CompilerParams(vmem_limit_bytes=limit * MIB),
        cost_estimate=pl.CostEstimate(flops=1000, bytes_accessed=1024, transcendentals=0),
        name=name,
    )(*inputs)


def after(value, *others):
    return lax.optimization_barrier((value, *others))[0]


class Slice:
    def __init__(self, lay):
        self.lay = lay
        self.img = lax.axis_index("img")
        self.row = lax.axis_index("row")
        self.y = self.row // 2
        self.c = self.row % 2
        self.orders = lay.first

    def swap(self, array, step):
        if step == "c":
            return lax.ppermute(array, "row", [(r, r ^ 1) for r in range(4)])
        if step == "y":
            return lax.ppermute(array, "row", [(r, r ^ 2) for r in range(4)])
        mask = sum(1 << bit for bit in self.lay.high) if step == "high" else 1 << step
        return lax.ppermute(array, "img", [(i, i ^ mask) for i in range(self.lay.img_count)])

    def gather(self, piece, order):
        held = piece[None]
        for step in order:
            held = jnp.concatenate([held, self.swap(held, step)], 0)
        return held

    def scatter(self, held, order):
        for step in reversed(order):
            half = held.shape[0] // 2
            came = self.swap(held[half:], step)
            held = (held[:half].astype(F32) + came.astype(F32)).astype(held.dtype)
        return held[0]

    def places(self, order):
        place = jnp.zeros((2, self.lay.img_count), jnp.int32)
        img = jnp.arange(self.lay.img_count, dtype=jnp.int32)[None, :] ^ self.img
        side = jnp.arange(2, dtype=jnp.int32)[:, None] ^ self.y
        for k, step in enumerate(order):
            bit = side if step == "y" else (img >> step) & 1
            place = place + (bit << k)
        return place

    def sources(self, order):
        place = self.places(order).reshape(-1)
        return jnp.zeros_like(place).at[place].set(jnp.arange(place.size, dtype=jnp.int32))

    def gather_whole(self, piece):
        lay = self.lay
        base = self.gather(piece, lay.high)
        whole = []
        for part, order in enumerate(self.orders):
            held = base[:, part * lay.half_rows : (part + 1) * lay.half_rows]
            held = self.gather(held, order[-2:]).reshape((-1,) + held.shape[1:])
            whole.append(jnp.take(held, self.places(order), axis=0))
        return jnp.concatenate(whole, 2).reshape((2,) + lay.tiles + piece.shape[1:])

    def high(self, *pieces):
        steps = self.lay.high + ["high"]
        return [self.swap(piece, step) for piece, step in zip(pieces * 3 if len(pieces) == 1 else pieces, steps)]

    def merge(self, pieces, name):
        lay = self.lay
        rows, columns = pieces[0].shape[-2:]
        count = len(pieces) * (pieces[0].shape[0] if pieces[0].ndim == 3 else 1)
        shapes = [((count, n, columns), BF) for n in (lay.half_rows, rows - lay.half_rows)]
        return call(functools.partial(merge_kernel, lay), name, pieces, shapes)

    def pairs(self, orders, place, top, bottom):
        return [self.swap(top, orders[0][place]), self.swap(bottom, orders[1][place])]

    def grad_shapes(self, columns, extra=0):
        lay = self.lay
        if lay.aligned:
            return [((lay.img_count, lay.half_rows + more, columns), BF) for more in (0, 0, extra, extra)]
        return [((2,) + lay.tiles + (columns,), BF)] + [((2 * lay.img_count, 2, columns), BF)] * (extra > 0)

    def scatter_rows(self, parts):
        lay = self.lay
        extra = []
        if not lay.aligned:
            if len(parts) > 1:
                extra = [jnp.pad(self.scatter(parts[1], self.orders[1]), ((0, EXTRA - 2), (0, 0)))]
            pieces = parts[0].reshape(2, lay.img_count, lay.rows, parts[0].shape[3])
            parts = []
            for part, order in enumerate(self.orders):
                mine = pieces[:, :, part * lay.half_rows : (part + 1) * lay.half_rows]
                mine = jnp.take(mine.reshape((-1,) + mine.shape[2:]), self.sources(order), axis=0)
                parts += [mine[: lay.img_count], mine[lay.img_count :]]
        sums = []
        for part, order in enumerate(self.orders):
            keep, send = parts[2 * part : 2 * part + 2]
            held = (keep.astype(F32) + self.swap(send, order[-1]).astype(F32)).astype(BF)
            half = lay.img_count // 2
            sums.append((held[:half].astype(F32) + self.swap(held[half:], order[-2]).astype(F32)).astype(BF))
        total = self.scatter(jnp.concatenate(sums, 1), lay.high)
        return jnp.concatenate([total] + extra, 0) if extra else total

    def fold(self, grads, came, name):
        shapes = [((g.shape[0] // 2,) + g.shape[1:], BF) for g in grads]
        return call(fold_kernel, name + "_fold", [grads[0], came[0], grads[2], came[1]], shapes)

    def rejoin(self, groups, name, n=2):
        count, rows, _ = groups[0][0].shape
        shape = (count // n, rows + groups[0][2].shape[1], sum(group[0].shape[2] for group in groups))
        arrays = [array for group in groups for array in group]
        return list(call(functools.partial(rejoin_kernel, n), name + "_rejoin", arrays, [(shape, BF)] * n))

    def halve(self, keep, came, name):
        shape = (keep.shape[0] // 2,) + keep.shape[1:]
        return call(halve_kernel, name + "_halve", [keep, came], [(shape, BF)] * 2)

    def split(self, keep, came, name):
        _, rows, columns = keep.shape
        half = self.lay.half_rows
        shapes = [((n, columns), BF) for n in (rows, half, rows - half)]
        out, top, bottom = call(split_kernel, name + "_split", [keep, came], shapes)
        return [out] + self.pairs(self.lay.second, 0, top, bottom)

    def end(self, shares, name):
        return call(end_kernel, name + "_end", shares, [(shares[0].shape[1:], BF)])[0]


NAMES = ("qkv_bias", "proj_bias", "attn_gain", "attn_shift", "mlp_gain", "mlp_shift", "up_bias", "down_bias", "freqs")


def plan_vectors(lay):
    width, third, pairs = lay.width, lay.third, lay.head // 2
    devices = lay.img_count * 4
    heads = np.arange(HEADS).reshape(2, 2, HEADS // 4)

    def by_core(count, shape):
        return [np.take(np.arange(count).reshape(shape), core, len(shape) - 2).reshape(-1) for core in range(2)]

    plain = [np.arange(width)] * 2
    up = by_core(4 * width, (2, 2, width))
    freqs = []
    for core in range(2):
        pick = np.arange(width).reshape(2, HEADS, pairs)[:, heads[:, core].reshape(-1)]
        freqs.append(np.stack([pick, pick], 2).reshape(-1))
    qkv, qk, v = (by_core(n * width, (n, 2, 2, third)) for n in (3, 2, 1))

    def lay_out(members):
        plan, tables, start, offset = [], [[], [], [], []], 0, 0
        for pick, count in members:
            count //= devices
            plan.append((start, pick[0].size, offset, count))
            for core in range(2):
                tables[2 * core].append(pick[core] // count)
                tables[2 * core + 1].append(pick[core] % count)
            start += pick[0].size
            offset += count
        return plan, jnp.asarray(np.stack([np.concatenate(t) for t in tables]).astype(np.int32))

    rest = [(plain, width)] * 5 + [(up, 4 * width), (plain, width), (freqs, width)]
    given = lay_out([(qkv, 3 * width)] + rest)
    lay.at = {name: slice(p[0], p[0] + p[1]) for name, p in zip(NAMES, given[0])}
    return given, lay_out([(qk, 2 * width), (v, width)] + rest)


def make_body(img_count):
    def body(
        tokens, keep_mask, cotangent, qkv_weight, qkv_bias, proj_weight, proj_bias, attn_gain, attn_shift,
        mlp_gain, mlp_shift, up_weight, up_bias, down_weight, down_bias, rope_freqs,
    ):
        lay = Layout(img_count, tokens, qkv_weight.shape[0])
        me = Slice(lay)
        y = me.y
        images, band, width, length = lay.images, lay.band, lay.width, lay.length
        heads = HEADS // 2
        own, third = lay.own, lay.third
        half = length // 2
        block = proj_weight.shape[1]
        hidden = up_weight.shape[1]
        vectors = (qkv_bias, proj_bias, attn_gain, attn_shift, mlp_gain, mlp_shift, up_bias, down_bias, rope_freqs)
        (plan, table), (grad_plan, grad_table) = plan_vectors(lay)

        def pick(flag, zero, one):
            return jnp.where(flag == 0, zero, one)

        def kernel(function, name, inputs, outs, scratch=(), **options):
            return call(functools.partial(function, lay), name, inputs, outs, scratch, **options)

        pack_rows = 2 * band + 16
        sizes = [part.stop - part.start for part in lay.parts]
        mine, other, third_send, first_piece, *second_pieces = kernel(
            pack_kernel, "pack",
            [tokens.reshape(images, band, width), cotangent.reshape(images, band, width), keep_mask.transpose(1, 0, 2), qkv_weight, proj_weight,
             up_weight, down_weight.T, *[v.reshape(1, -1) for v in vectors]],
            [((pack_rows, width), BF), ((pack_rows + lay.rows - lay.half_rows, width), BF), ((lay.rows, 256 + PACKED), BF),
             ((lay.rows + EXTRA, 2 * third), BF),
             ((lay.rows, 2 * sizes[0] + block), BF), ((lay.half_rows, 2 * sizes[1]), BF)],
            [((lay.band_rows, images, lay.side), jnp.int32), (qkv_weight.shape, F32), (proj_weight.shape, F32), (up_weight.shape, F32),
             (down_weight.T.shape, F32), *[((1, v.shape[0]), F32) for v in vectors], pltpu.SemaphoreType.DMA((18,))],
            limit=60, hbm=True,
        )
        third_came = me.swap(third_send, "c")
        (first_piece,) = kernel(fit_kernel, "fit", [third_came, first_piece], [((lay.rows + EXTRA, 3 * third), BF)])
        mine_came = me.swap(mine, "c")
        near = me.swap(after(other, first_piece, mine_came), "y")
        bands = [mine, near, mine_came]
        if lay.aligned:
            part0, top1 = second_pieces
            near1 = me.swap(top1, lay.second[0][0])
            came = me.high(first_piece)
            bands.append(me.swap(after(near, *came), "c"))
            part0 = after(part0, came[0])
            top, bottom = me.merge([first_piece] + came, "merge_first")
            came = me.pairs(lay.first, -2, top, bottom)
            high0 = [me.swap(part0, step) for step in lay.high]
            top = after(top, bands[3], near1, *high0)
            shapes = [((2 * held.shape[0],) + held.shape[1:], BF) for held in (top, bottom)]
            top, bottom = call(join_kernel, "join_first", [top, came[0], bottom, came[1]], shapes)
            came = me.pairs(lay.first, -1, top, bottom)
            first = [top, came[0], bottom, came[1]]
            high0.append(me.swap(after(high0[0], top), lay.high[1]))
            top0, bottom0 = me.merge([part0] + high0, "merge0")
            shape = (2, lay.rows, top1.shape[1])
            (both1,) = kernel(start_kernel, "start1", [after(top1, high0[0]), near1, other, near], [(shape, BF)])
            vec_parts = [after(first[2], first[1], top0, bottom0, both1), first[3]]
        else:
            bands.append(me.swap(near, "c"))
            first = [me.gather_whole(first_piece[: lay.rows])]
            vec_parts = [me.gather(first_piece[lay.rows : lay.rows + 2], me.orders[1])]
            second = [[me.gather_whole(p)] for p in (second_pieces[0], jnp.concatenate([second_pieces[1], other[pack_rows:]], 0))]
        (vec,) = call(
            functools.partial(unpack_kernel, lay, plan, len(vec_parts)), "unpack", [table, *vec_parts],
            [((1, table.shape[1]), F32)], limit=24,
        )

        n_w = len(first)
        n_g = len(me.grad_shapes(1))
        a1, q, k, v, w_qkv, cos, sin, kp, mask_bias = call(
            functools.partial(project_kernel, lay, n_w), "qkv", [*bands, *first, vec],
            [((length, width), BF), ((length, own), BF), ((length, own), BF), ((length, own), BF), ((2, width, 3 * third), BF),
             ((length, own), F32), ((length, own), F32), ((length, 1), F32), ((1, length), F32)],
            [((2,) + lay.tiles + (3 * third,), BF)], limit=16,
        )
        def attend(first, count, q):
            return call(
                functools.partial(attend_kernel, lay, band, first, count), "attend%d" % first, [q, k, v, mask_bias],
                [((length, count * 2 * lay.head), BF), ((2 * count, length, length), BF)], limit=8,
            )

        ob0, p0 = attend(0, 1, q)
        oo0 = me.swap(ob0, "c")
        if lay.aligned:
            near0 = me.pairs(lay.first, -2, top0, bottom0)
            high1 = [both1] + [me.swap(both1, step) for step in lay.high]
            shapes = [((2 * held.shape[0],) + held.shape[1:], BF) for held in (top0, bottom0)]
            top0 = after(top0, ob0, high1[1], high1[2])
            top0, bottom0 = call(join_kernel, "join0", [top0, near0[0], bottom0, near0[1]], shapes)
            last0 = me.pairs(lay.first, -1, top0, bottom0)
            second = [[top0, last0[0], bottom0, last0[1]]]
            ob1, p1 = attend(1, HEADS // 4 - 1, after(q, top0, bottom0))
            high1.append(me.swap(after(high1[1], ob1), lay.high[1]))
            top1, bottom1 = me.merge(high1, "merge1")
            last1 = me.pairs(lay.second, -1, top1, bottom1)
            second.append([top1, last1[0], bottom1, last1[1]])
            gate = [ob1, top1, bottom1]
        else:
            ob1, p1 = attend(1, HEADS // 4 - 1, q)
            gate = [ob1]
        oo1 = me.swap(ob1, "c")
        (p_cols,) = call(
            functools.partial(proj_kernel, lay, len(second[0])), "proj", [after(second[0][0], *gate)] + second[0][1:], [((width, 2 * block), BF)],
            [((2,) + lay.tiles + (block,), BF)],
        )
        p_other = me.swap(p_cols, "c")
        x1, a2, a2_t, dm, dm_t, d_down_bias, w_proj = call(
            functools.partial(middle_kernel, lay), "middle", [*bands, ob0, ob1, oo0, oo1, p_cols, p_other, vec, kp],
            [((length, width), F32), ((length, width), BF), ((width, length), BF), ((length, width), BF), ((width, length), BF),
             ((1, width), F32), ((width, width), BF)], limit=10,
        )
        sums, second_grads, d_up_bias = [], [], []
        for part, at in enumerate(lay.parts):
            step = at.stop - at.start
            shapes = (me.grad_shapes(2 * step) if part else me.grad_shapes(step) * 2) + [((1, 2 * step), F32)]
            scratch = [(lay.tiles + (2 * step,), BF), (lay.tiles + (step,), BF)]
            if part == len(PARTS) - 1:
                shapes += [((half, width), F32), ((half, width), BF), ((length, width), F32), ((length, width), BF)]
                scratch = [((length, width), F32)] + scratch
            else:
                shapes += [((length, width), F32)] * 2
            outs = call(
                functools.partial(mlp_kernel, lay, part, len(second[part]), n_g), "mlp%d" % part,
                [x1, a2, a2_t, dm, dm_t, vec, *second[part], *sums], shapes, scratch, limit=18,
            )
            count = n_g if part else 2 * n_g
            second_grads.append(outs[:count])
            d_up_bias.append(outs[count])
            sums = outs[count + 1 :]
        part, m_send, dn, dn_send = sums
        if lay.aligned:
            g = second_grads[0]
            came0 = me.pairs(lay.second, -1, g[1], g[3])
            dn_send = after(dn_send, *came0)
            came0 += me.pairs(lay.second, -1, g[5], g[7])
        dn_came = me.swap(dn_send, "c")
        m_came = me.swap(m_send, "c")
        out_half = (kp[:half] * (part + m_came.astype(F32))).astype(BF)
        pair = 2 * lay.head
        *outs, dx_half, dob, norm_sums, dq0, dk0, dv0 = call(
            functools.partial(back_kernel, lay, band, n_g), "back",
            [*bands, kp, x1, dn, dn_came, vec, w_proj, ob0, ob1, oo0, oo1, q, k, v, p0, *second_grads[1]],
            [*me.grad_shapes(2 * sizes[1] + block), ((half, width), F32), ((length, own), BF), ((3, width), F32), ((length, pair), F32),
             ((length, pair), F32), ((length, pair), F32)],
            [((length, width), BF), (lay.tiles + (block,), BF)], limit=20,
        )
        second_grads[1] = outs
        if lay.aligned:
            came1 = me.pairs(lay.first, -1, *[after(send, *came0[2:]) for send in (outs[1], outs[3])])
        else:
            g = [jnp.concatenate(second_grads[0], 3)], second_grads[1]
            d_second = [[me.scatter_rows(held)] for held in g]
        if lay.aligned:
            g = second_grads[0]
            came0[0] = after(came0[0], dob)
            keep0, send0 = me.rejoin([[g[k], came0[k // 2], g[k + 2], came0[k // 2 + 1]] for k in (0, 4)], "part0")
            dob = after(dob, keep0, send0)
            came0 = me.swap(send0, lay.high[1])
        dq1, dk1, dv1 = call(
            functools.partial(back_heads_kernel, lay, band), "back_heads", [q, k, v, p1, dob], [((length, own - pair), F32)] * 3
        )
        grad_shapes = me.grad_shapes(3 * third, EXTRA)
        dn1_keep, dn1_send, *first_grads = call(
            functools.partial(back_rest_kernel, lay, grad_plan, len(grad_shapes)), "back_rest",
            [*bands, q, k, cos, sin, a1, w_qkv, grad_table, *d_up_bias, d_down_bias, norm_sums, dq0, dk0, dv0, dq1, dk1, dv1],
            [((half, width), F32), ((half, width), BF), *grad_shapes],
            [((length, own), F32), (lay.tiles + (3 * third,), BF), ((length, 3 * own), BF)], limit=24,
        )
        if lay.aligned:
            g, came1[0] = second_grads[1], after(came1[0], first_grads[0])
            folded1 = me.fold(g, came1, "part1")
            came1 = me.pairs(lay.first, -2, folded1[1], folded1[3])
            g = first_grads
            came = me.pairs(lay.first, -1, *[after(send, came0, folded1[0]) for send in (g[1], g[3])])
            keep0, send0 = me.halve(keep0, came0, "part0")
            came0 = me.swap(send0, lay.high[0])
            keep1, send1 = me.rejoin([[folded1[0], came1[0], folded1[2], came1[1]]], "part1")
            came1 = me.swap(send1, lay.high[1])
            folded = me.fold(g, came, "first")
            came = me.pairs(lay.first, -2, *[after(send, came0, came1) for send in (folded[1], folded[3])])
            d_second = [me.split(keep0, came0, "part0")]
            keep1, send1 = me.halve(keep1, came1, "part1")
            came1 = me.swap(send1, lay.high[0])
            shares = me.rejoin([[folded[0], came[0], folded[2], came[1]]], "first", 4)
            d_second.append([me.end([keep1, came1], "part1")])
            shares[1] = after(shares[1], *d_second[0], d_second[1][0])
            d_first = me.end([shares[0]] + me.high(*shares[1:]), "first")
        else:
            d_first = me.scatter_rows(first_grads)
        dn1_came = me.swap(dn1_send, "c")
        tg_keep, tg_send = call(
            functools.partial(finish_kernel, lay), "finish", [bands[0], bands[1], dn1_keep, dn1_came, dx_half, vec],
            [((band, width), BF), ((band, width), BF)],
        )

        def to_images(keep, send):
            came = me.swap(send, "y")
            return pick(y, jnp.stack([keep, came]), jnp.stack([came, keep])).reshape(tokens.shape)

        layer_out = to_images(out_half[:band], out_half[band:])
        tokens_grad = to_images(tg_keep, tg_send)

        d_up, d_down, d_proj = call(
            functools.partial(tail_second_kernel, lay, [len(d) for d in d_second]), "tail_second",
            [held for d in d_second for held in d], [((lay.rows, n), F32) for n in (hidden, hidden, block)]
        )
        d_down = d_down.T
        (tail_send,) = kernel(tail_send_kernel, "tail_send", [d_first], [((lay.rows, 256 + PACKED), BF)])
        tail_came = me.swap(tail_send, "c")
        d_qkv, *r = call(
            functools.partial(tail_kernel, lay, grad_plan), "tail", [d_first, tail_came],
            [((lay.rows, 3 * third), F32), *[((1, count), F32) for _, _, _, count in grad_plan]],
        )
        r = [v.reshape(-1) for v in r]
        return (
            layer_out, tokens_grad, d_qkv, r[0], r[1], d_proj, r[2], r[3], r[4], r[5], r[6], d_up, r[7], d_down, r[8], r[9],
        )

    return body


def solution(mesh):
    split = P(("img", "row"))
    both = P("img", "row")
    field = P("img", "row", None, None)
    return jax.shard_map(
        make_body(mesh.shape["img"]),
        mesh=mesh,
        in_specs=(
            field, P("img", "row", None), field, both, split, both, split, split, split, split, split, both, split,
            P("row", "img"), split, split,
        ),
        out_specs=(
            field, field, both, split, split, both, split, split, split, split, split, both, split, P("row", "img"),
            split, split,
        ),
        check_vma=False,
    )
```

```python
import functools

import jax
import jax.numpy as jnp
import numpy as np
from jax import lax
from jax.experimental import pallas as pl
from jax.experimental.pallas import tpu as pltpu
from jax.sharding import PartitionSpec as P

HEADS = 12
PARTS = (3, 3)
NORM_EPSILON = 1e-06
MASKED_SCORE = -1e30
BF = jnp.bfloat16
F32 = jnp.float32
MIB = 2**20
VMEM = pl.BlockSpec(memory_space=pltpu.VMEM)
HBM = pl.BlockSpec(memory_space=pltpu.MemorySpace.HBM)
PACKED = 384
EXTRA = 8


def dot(left, right, dims):
    return lax.dot_general(left, right, (dims, ((), ())), preferred_element_type=F32)


def nn(left, right):
    return dot(left, right, ((1,), (0,)))


def nt(left, right):
    return dot(left, right, ((1,), (1,)))


def tn(left, right):
    return dot(left, right, ((0,), (0,)))


def normed_rows(values):
    center = values - jnp.mean(values, -1, keepdims=True)
    inverse = lax.rsqrt(jnp.mean(center * center, -1, keepdims=True) + NORM_EPSILON)
    return center * inverse, inverse


def norm_back(grad, normed, inverse, gain):
    scaled = grad * gain
    centred = scaled - jnp.mean(scaled, -1, keepdims=True)
    return inverse * (centred - normed * jnp.mean(scaled * normed, -1, keepdims=True))


def column_sum(value):
    return jnp.sum(value, 0, keepdims=True)


def here():
    row = lax.axis_index("row")
    return lax.axis_index("img"), row >> 1, row & 1, row


class Layout:
    def __init__(self, img_count, tokens, rows):
        self.img_count = img_count
        self.bits = img_count.bit_length() - 1
        self.rows = rows
        self.half_rows = rows // 2
        self.aligned = rows % 32 == 0 and img_count == 8
        self.images, self.band_rows, self.side, self.width = tokens.shape
        self.band = self.band_rows * self.side
        self.length = 4 * self.band
        self.head = self.width // HEADS
        self.own = self.width // 2
        self.third = self.own // 2
        self.high = list(range(self.bits - 1, 0, -1))
        self.first = (self.high + [0, "y"], self.high + ["y", 0])
        self.second = ([0] + self.high + ["y"], ["y"] + self.high + [0])
        sizes = [self.width * sixths // 6 for sixths in PARTS]
        self.parts = [slice(sum(sizes[:n]), sum(sizes[: n + 1])) for n in range(len(sizes))]
        self.gathered = (self.first, self.second)
        self.reduced = (self.second, self.first)
        self.tiles = (img_count, rows) if self.aligned else (1, self.width)

    def slots(self, orders, img_rel, y_rel):
        found = []
        for order in orders:
            bits = [y_rel if step == "y" else (img_rel >> step) & 1 for step in order]
            found.append((sum(bit << k for k, bit in enumerate(bits[:-1])), bits[-1]))
        return found


def load_pieces(lay, orders, refs, y_rel, target, columns=slice(None)):
    if not lay.aligned:
        target[...] = refs[0][here()[1] ^ y_rel, :, :, columns]
        return
    half = lay.half_rows
    count = len(refs) // 2
    for img_rel in range(lay.img_count):
        for part, (slot, last) in enumerate(lay.slots(orders, img_rel, y_rel)):
            which, slot = divmod((slot + last * lay.img_count) * count, 2 * lay.img_count)
            ref, slot = refs[part * count + which], slot // count
            target[img_rel ^ here()[0], part * half : (part + 1) * half] = ref[slot, :half, columns]


def store_pieces(lay, orders, refs, y_rel, columns, source):
    if not lay.aligned:
        refs[0][here()[1] ^ y_rel, :, :, columns] = source[...]
        return
    half = lay.half_rows
    for img_rel in range(lay.img_count):
        for part, (slot, last) in enumerate(lay.slots(orders, img_rel, y_rel)):
            refs[2 * part + last][slot, :half, columns] = source[img_rel ^ here()[0], part * half : (part + 1) * half]


def halves_of(lay, value):
    pairs = lay.head // 2
    lane = lax.broadcasted_iota(jnp.int32, value.shape, 1)
    width = value.shape[1]
    first = (lane & pairs) == 0
    return jnp.where(first, pltpu.roll(value, width - pairs, 1), pltpu.roll(value, pairs, 1))


def pack_kernel(lay, *refs):
    tok, cot, mask, qkv, proj, up, down, *vectors = refs[:16]
    mine_ref, other_ref, third_ref, first_ref = refs[16:20]
    second, refs = [*refs[20:22], other_ref.at[2 * lay.band + 16 :]], refs[22:]
    mask_in, qkv_in, proj_in, up_in, down_in, *vectors_in = refs[:14]
    sems = refs[14]
    y = here()[1]
    band, third, width, rows = lay.band, lay.third, lay.width, lay.rows
    pairs = [(qkv, qkv_in), (proj, proj_in), *zip(vectors, vectors_in), (up, up_in), (down, down_in), (mask, mask_in)]
    for ref, which in ((other_ref, 1 - y), (mine_ref, y)):
        pairs += [(tok.at[which], ref.at[:band]), (cot.at[which], ref.at[band : 2 * band])]
    copies = [pltpu.make_async_copy(source, target, sems.at[n]) for n, (source, target) in enumerate(pairs)]
    for copy in copies:
        copy.start()
    for copy in copies[:11]:
        copy.wait()
    packed = jnp.concatenate([v[...] for v in vectors_in], 1)
    packed = jnp.concatenate([packed, jnp.zeros((1, PACKED - packed.shape[1]), F32)], 1).astype(BF)
    third_ref[:, :third] = qkv_in[:, third : 2 * third].astype(BF)
    third_ref[:, third:] = jnp.zeros((rows, third_ref.shape[1] - third), BF)
    third_ref[0:1, third_ref.shape[1] - PACKED :] = packed
    first_ref[:rows, :third] = qkv_in[:, :third].astype(BF)
    first_ref[:rows, third : 2 * third] = qkv_in[:, 2 * third :].astype(BF)
    first_ref[rows:] = jnp.zeros((EXTRA, first_ref.shape[1]), BF)
    first_ref[rows : rows + 1, :PACKED] = packed
    for copy in copies[11:]:
        copy.wait()
    for ref, part, first_row in zip(second, (0, 1, 1), (0, 0, lay.half_rows)):
        at = lay.parts[part]
        step = at.stop - at.start
        side = slice(first_row, first_row + ref.shape[0])
        ref[:, :step] = up_in[side, at].astype(BF)
        ref[:, step : 2 * step] = down_in[side, at].astype(BF)
        if part == 0:
            ref[:, 2 * step :] = proj_in[side].astype(BF)
    for ref, which in ((mine_ref, y), (other_ref, 1 - y)):
        keep = [jnp.where(which == 0, mask_in[r, 0:1], mask_in[r, 1:2]).astype(F32) for r in range(lay.band_rows)]
        flat = jnp.concatenate(keep, 1)
        flat = jnp.concatenate([flat, jnp.zeros((1, width - band), F32)], 1)
        ref[2 * band : 2 * band + 16] = jnp.concatenate([flat, jnp.zeros((15, width), F32)], 0).astype(BF)


def fit_kernel(lay, came_ref, first_ref, out_ref):
    third, rows = lay.third, lay.rows
    c = here()[2]
    t0, t2, came = first_ref[:rows, :third], first_ref[:rows, third : 2 * third], came_ref[:, :third]
    out_ref[:rows, : 3 * third] = jnp.where(c == 0, jnp.concatenate([t0, t2, came], 1), jnp.concatenate([came, t0, t2], 1))
    theirs = came_ref[0:1, came_ref.shape[1] - PACKED :]
    rest = jnp.zeros((EXTRA - 2, PACKED), F32).astype(BF)
    out_ref[rows:] = jnp.zeros((EXTRA, out_ref.shape[1]), BF)
    out_ref[rows:, :PACKED] = jnp.concatenate([first_ref[rows : rows + 1, :PACKED], theirs, rest], 0)


def merge_kernel(lay, *refs):
    pieces, (top_ref, bottom_ref) = refs[:-2], refs[-2:]
    half = lay.half_rows
    for k, ref in enumerate(pieces):
        if len(ref.shape) == 2:
            top_ref[k] = ref[:half]
            bottom_ref[k] = ref[half:]
        else:
            count = ref.shape[0]
            top_ref[k * count : (k + 1) * count] = ref[:, :half]
            bottom_ref[k * count : (k + 1) * count] = ref[:, half:]


def start_kernel(lay, top, top_came, bottom, bottom_came, out_ref):
    half = lay.half_rows
    out_ref[0, :half], out_ref[1, :half] = top[...], top_came[...]
    first = 2 * lay.band + 16
    out_ref[0, half:], out_ref[1, half:] = bottom[first:], bottom_came[first:]


def join_kernel(*refs):
    for part in range(2):
        own, came = refs[2 * part : 2 * part + 2]
        refs[4 + part][: own.shape[0]] = own[...]
        refs[4 + part][own.shape[0] :] = came[...]


def fold_kernel(*refs):
    for part in range(2):
        keep, came = refs[2 * part : 2 * part + 2]
        count = keep.shape[0] // 2
        for half in range(2):
            at = slice(half * count, (half + 1) * count)
            refs[4 + 2 * part + half][...] = (keep[at].astype(F32) + came[at].astype(F32)).astype(BF)


def rejoin_kernel(n, *refs):
    outs = refs[len(refs) - n :]
    top = refs[0].shape[1]
    count = refs[0].shape[0] // n
    column = 0
    for k in range(0, len(refs) - n, 4):
        columns = slice(column, column + refs[k].shape[2])
        column = columns.stop
        for part in range(2):
            keep, came = refs[k + 2 * part : k + 2 * part + 2]
            rows = slice(0, top) if part == 0 else slice(top, None)
            for share, out in enumerate(outs):
                at = slice(share * count, (share + 1) * count)
                out[:, rows, columns] = (keep[at].astype(F32) + came[at].astype(F32)).astype(BF)


def end_kernel(*refs):
    refs[-1][...] = sum(ref[0].astype(F32) for ref in refs[:-1]).astype(BF)


def halve_kernel(keep_ref, came_ref, *outs):
    count = keep_ref.shape[0] // len(outs)
    for half, ref in enumerate(outs):
        at = slice(half * count, (half + 1) * count)
        total = (keep_ref[at].astype(F32) + came_ref[at].astype(F32)).astype(BF)
        ref[...] = total.reshape(ref.shape)


def split_kernel(keep_ref, came_ref, out_ref, top_ref, bottom_ref):
    half = top_ref.shape[0]
    out_ref[...] = (keep_ref[0].astype(F32) + came_ref[0].astype(F32)).astype(BF)
    top_ref[...] = (keep_ref[1, :half].astype(F32) + came_ref[1, :half].astype(F32)).astype(BF)
    bottom_ref[...] = (keep_ref[1, half:].astype(F32) + came_ref[1, half:].astype(F32)).astype(BF)


def owner_mask(lay, c_rel, table_row):
    place = lax.broadcasted_iota(jnp.int32, (2 * lay.img_count, 1), 0)
    img_rel = jnp.zeros_like(place)
    row = here()[3] ^ c_rel
    for k, step in enumerate(lay.first[1]):
        bit = (place >> k) & 1
        if step == "y":
            row = row ^ (bit * 2)
        else:
            img_rel = img_rel | (bit << step)
    return ((img_rel ^ here()[0]) * 4 + row) == table_row


def owners(table_ref, at, c):
    owner = jnp.where(c == 0, table_ref[0:1, at], table_ref[2:3, at])
    entry = jnp.where(c == 0, table_ref[1:2, at], table_ref[3:4, at])
    return owner, entry


def unpack_kernel(lay, plan, n_v, table_ref, *refs):
    v_refs, out_ref = refs[:n_v], refs[n_v]
    if lay.aligned:
        half = lay.half_rows
        rows = [ref[k, half : half + EXTRA, :PACKED].astype(F32) for ref in v_refs for k in range(ref.shape[0])]
        gathered = [jnp.concatenate([row[c_rel : c_rel + 1] for row in rows], 0).astype(BF) for c_rel in range(2)]
    else:
        gathered = [v_refs[0][:, c_rel, :PACKED] for c_rel in range(2)]
    for start, size, offset, count in plan:
        at = slice(start, start + size)
        owner, entry = owners(table_ref, at, here()[2])
        spread = (lax.broadcasted_iota(jnp.int32, (count, size), 0) == entry).astype(F32).astype(BF)
        total = 0.0
        for c_rel in range(2):
            rows = nn(gathered[c_rel][:, offset : offset + count], spread)
            total = total + column_sum(jnp.where(owner_mask(lay, c_rel, owner), rows, 0.0))
        out_ref[:, at] = total


def repack(lay, plan, table_ref, grads, refs):
    sides = []
    for c_rel in range(2):
        parts = []
        for grad, (start, size, offset, count) in zip(grads, plan):
            owner, entry = owners(table_ref, slice(start, start + size), here()[2])
            spread = (lax.broadcasted_iota(jnp.int32, (count, size), 0) == entry).astype(F32).astype(BF)
            rows = jnp.where(owner_mask(lay, c_rel, owner), grad, 0.0).astype(BF)
            parts.append(nt(rows, spread))
        used = sum(p.shape[1] for p in parts)
        sides.append(jnp.concatenate(parts + [jnp.zeros((2 * lay.img_count, PACKED - used), F32)], 1))
    if not lay.aligned:
        refs[1][...] = jnp.zeros(refs[1].shape, BF)
        for c_rel in range(2):
            refs[1][:, c_rel, :PACKED] = sides[c_rel].astype(BF)
        return
    half, count = lay.half_rows, lay.img_count
    for j in range(2 * count):
        ref = refs[2 + j // count]
        block = jnp.concatenate([side[j : j + 1] for side in sides] + [jnp.zeros((EXTRA - 2, PACKED), F32)], 0).astype(BF)
        ref[j % count, half:] = jnp.zeros((EXTRA, ref.shape[2]), BF)
        ref[j % count, half:, :PACKED] = block


def project_kernel(lay, n_w, t0, t1, t2, t3, *refs):
    w_refs = refs[:n_w]
    vec_ref, a_ref, q_ref, k_ref, v_ref, w_out, cos_ref, sin_ref, kp_ref, bias_ref, w_all = refs[n_w:]
    band, side, own, third = lay.band, lay.side, lay.own, lay.third
    g_ref, s_ref, b_ref = (vec_ref[:, lay.at[n]] for n in ("attn_gain", "attn_shift", "qkv_bias"))
    f_ref = vec_ref[:, lay.at["freqs"]]
    keeps = []
    for b, ref in enumerate((t0, t1, t2, t3)):
        at = slice(b * band, (b + 1) * band)
        normed, _ = normed_rows(ref[:band].astype(F32))
        a_ref[at] = (normed * g_ref + s_ref).astype(BF)
        keep = ref[2 * band : 2 * band + 16, :band].astype(F32)
        kp_ref[at] = jnp.transpose(keep)[:, 0:1]
        keeps.append(keep[0:1])
    bias_ref[...] = jnp.where(jnp.concatenate(keeps, 1) > 0, 0.0, MASKED_SCORE)
    lane = lax.broadcasted_iota(jnp.int32, (side, own), 1)
    sign = jnp.where((lane & (lay.head // 2)) == 0, -1.0, 1.0).astype(F32)
    col = lax.broadcasted_iota(jnp.int32, (side, own), 0).astype(F32) * f_ref[:, :own]
    col_cos, col_sin = jnp.cos(col), jnp.sin(col)
    row_index = here()[3]
    for b, flip in enumerate((0, 2, 1, 3)):
        first = ((row_index ^ flip) * lay.band_rows).astype(F32)
        rows = (lax.broadcasted_iota(jnp.int32, (8, own), 0).astype(F32) + first) * f_ref[:, own:]
        row_cos, row_sin = jnp.cos(rows), jnp.sin(rows)
        for r in range(lay.band_rows):
            at = slice(b * band + r * side, b * band + (r + 1) * side)
            rc, rs = row_cos[r : r + 1], row_sin[r : r + 1]
            cos_ref[at] = col_cos * rc - col_sin * rs
            sin_ref[at] = (col_sin * rc + col_cos * rs) * sign
    for y_rel in range(2):
        y_side = here()[1] ^ y_rel
        load_pieces(lay, lay.first, w_refs, y_rel, w_all.at[y_side])
    acts = a_ref[...]
    w0, w1 = w_all[0].reshape(lay.width, -1), w_all[1].reshape(lay.width, -1)
    w_out[0], w_out[1] = w0, w1
    left = nn(acts, w0) + b_ref[:, : 3 * third]
    right = nn(acts, w1) + b_ref[:, 3 * third :]
    query, key = left[:, :own], jnp.concatenate([left[:, own:], right[:, :third]], 1)
    cos, sin = cos_ref[...], sin_ref[...]
    q_ref[...] = (query * cos + halves_of(lay, query) * sin).astype(BF)
    k_ref[...] = (key * cos + halves_of(lay, key) * sin).astype(BF)
    v_ref[...] = right[:, third:].astype(BF)


def proj_kernel(lay, n_w, *refs):
    out_ref, w_all = refs[n_w:]
    block = lay.width // 4
    columns = slice(refs[0].shape[-1] - block, None)
    for y_rel in range(2):
        y_side = here()[1] ^ y_rel
        load_pieces(lay, lay.gathered[0], refs[:n_w], y_rel, w_all.at[y_side], columns)
    for y_side in range(2):
        out_ref[:, y_side * block : (y_side + 1) * block] = w_all[y_side].reshape(lay.width, block)


def attend_kernel(lay, first, count, q_ref, k_ref, v_ref, bias_ref, o_ref, p_ref):
    head = lay.head
    pair = 2 * head
    scale = head**-0.5

    def step(n, carry):
        at = pl.ds(pl.multiple_of(n * pair, pair), pair)
        out = pl.ds(pl.multiple_of((n - first) * pair, pair), pair)
        keys, values = k_ref[:, at], v_ref[:, at]
        query = q_ref[:, at] * jnp.asarray(scale, BF)
        lane = lax.broadcasted_iota(jnp.int32, query.shape, 1)
        outs = []
        for h in range(2):
            mine = (lane < head) if h == 0 else (lane >= head)
            score = nt(jnp.where(mine, query, jnp.zeros_like(query)), keys) + bias_ref[...]
            power = jnp.exp(score - jnp.max(score, -1, keepdims=True))
            weights = (power * (1.0 / jnp.sum(power, -1, keepdims=True))).astype(BF)
            p_ref[2 * (n - first) + h] = weights
            outs.append(nn(weights, values))
        o_ref[:, out] = jnp.where(lane < head, outs[0], outs[1]).astype(BF)
        return carry

    lax.fori_loop(first, first + count, step, 0)


def both_heads(half, ob0, ob1, oo0, oo1):
    other = jnp.concatenate([oo0[...], oo1[...]], 1)
    return jnp.concatenate([ob0[...], ob1[...]], 1), jnp.concatenate([other[half:], other[:half]], 0)


def middle_kernel(lay, t0, t1, t2, t3, ob0, ob1, oo0, oo1, p_ref, po_ref, vec_ref, kp_ref, x1_ref, a2_ref, at_ref, dm_ref, dt_ref, dbg_ref, wp_ref):
    band, third, half = lay.band, lay.third, lay.length // 2
    c = here()[2]
    block = lay.width // 4
    pb_ref, g_ref, s_ref = (vec_ref[:, lay.at[n]] for n in ("proj_bias", "mlp_gain", "mlp_shift"))
    for y_side in range(2):
        mine, other = (ref[:, y_side * block : (y_side + 1) * block] for ref in (p_ref, po_ref))
        wp_ref[:, 2 * y_side * block : 2 * (y_side + 1) * block] = jnp.where(
            c == 0, jnp.concatenate([mine, other], 1), jnp.concatenate([other, mine], 1)
        )
    low = [pl.ds(pl.multiple_of((2 * s + c) * third, third), third) for s in range(2)]
    high = [pl.ds(pl.multiple_of((2 * s + 1 - c) * third, third), third) for s in range(2)]
    own_w = jnp.concatenate([wp_ref[low[0]], wp_ref[low[1]]], 0)
    other_w = jnp.concatenate([wp_ref[high[0]], wp_ref[high[1]]], 0)
    mine, other = both_heads(half, ob0, ob1, oo0, oo1)
    x1_ref[...] = nn(mine, own_w) + nn(other, other_w) + pb_ref
    for b, ref in enumerate((t0, t1, t2, t3)):
        at = slice(b * band, (b + 1) * band)
        x1 = x1_ref[at] + ref[:band].astype(F32)
        x1_ref[at] = x1
        normed, _ = normed_rows(x1)
        a2_ref[at] = (normed * g_ref + s_ref).astype(BF)
        dm_ref[at] = (ref[band : 2 * band].astype(F32) * kp_ref[at]).astype(BF)
    at_ref[...] = a2_ref[...].T
    dt_ref[...] = dm_ref[...].T
    dbg_ref[...] = column_sum(dm_ref[:half].astype(F32))


def mlp_kernel(lay, part, n_w, n_g, x1_ref, a2_ref, at_ref, dm_ref, dt_ref, vec_ref, *refs):
    w_refs, refs = refs[:n_w], refs[n_w:]
    last = part == len(PARTS) - 1
    if part:
        (m_in, dn_in), refs = refs[:2], refs[2:]
    count = n_g if last else 2 * n_g
    grads, refs = refs[:count], refs[count:]
    ubg_ref, refs = refs[0], refs[1:]
    if last:
        part_ref, msend_ref, dn_ref, dnsend_ref, m_ref, w_all, g_tmp = refs
    else:
        m_ref, dn_ref, w_all, g_tmp = refs
    width, half = lay.width, lay.length // 2
    chunk = lay.parts[part].stop - lay.parts[part].start
    up_bias = lay.at["up_bias"].start + lay.parts[part].start
    for y_rel in range(2):
        load_pieces(lay, lay.gathered[part], w_refs, y_rel, w_all, slice(0, 2 * chunk))
        y_side = here()[1] ^ y_rel
        up = w_all[:, :, :chunk].reshape(width, chunk)
        down = w_all[:, :, chunk:].reshape(width, chunk)
        pre = nn(a2_ref[...], up) + vec_ref[:, pl.ds(pl.multiple_of(y_side * width + up_bias, 128), chunk)]
        cdf = 0.5 * (1.0 + lax.erf(pre * 0.7071067811865476))
        slope = cdf + pre * (jnp.exp(-0.5 * pre * pre) * 0.3989422804014327)
        act = (pre * cdf).astype(BF)
        du = (nn(dm_ref[...], down) * slope).astype(BF)
        ubg_ref[:, pl.ds(pl.multiple_of(y_side * chunk, 128), chunk)] = column_sum(du.astype(F32))
        g_tmp[...] = nn(at_ref[...], du).astype(BF).reshape(g_tmp.shape)
        own, at = (grads[:n_g], slice(None)) if not last else (grads, slice(0, chunk))
        store_pieces(lay, lay.reduced[part], own, y_rel, at, g_tmp)
        g_tmp[...] = nn(dt_ref[...], act).astype(BF).reshape(g_tmp.shape)
        own, at = (grads[n_g:], slice(None)) if not last else (grads, slice(chunk, None))
        store_pieces(lay, lay.reduced[part], own, y_rel, at, g_tmp)
        m, dn = nt(act, down), nt(du, up)
        if y_rel == 0:
            m_ref[...] = m + m_in[...] if part else m
            dn_ref[...] = dn + dn_in[...] if part else dn
        else:
            m_ref[...] += m
            dn_ref[...] += dn
    if last:
        part_ref[...] = x1_ref[:half] + m_ref[:half] + vec_ref[:, lay.at["down_bias"]]
        msend_ref[...] = m_ref[half:].astype(BF)
        dnsend_ref[...] = dn_ref[...].astype(BF)


def attend_back(lay, first, count, base, q_ref, k_ref, v_ref, p_ref, dob_ref, dq_ref, dk_ref, dv_ref):
    head = lay.head
    pair = 2 * head
    scale = head**-0.5

    def step(n, carry):
        at = pl.ds(pl.multiple_of(n * pair, pair), pair)
        out = pl.ds(pl.multiple_of((n - base) * pair, pair), pair)
        keys, values = k_ref[:, at], v_ref[:, at]
        query, dob = q_ref[:, at], dob_ref[:, at]
        query_t, dob_t = query.T, dob.T
        lane = lax.broadcasted_iota(jnp.int32, query.shape, 1)
        row = lax.broadcasted_iota(jnp.int32, query_t.shape, 0)
        dqs, dks, dvs = [], [], []
        for h in range(2):
            mine = (lane < head) if h == 0 else (lane >= head)
            weights = p_ref[2 * (n - base) + h]
            soft = weights.astype(F32)
            dp = nt(jnp.where(mine, dob, jnp.zeros_like(dob)), values)
            ds = (soft * (dp - jnp.sum(soft * dp, -1, keepdims=True))).astype(BF)
            dqs.append(nn(ds, keys))
            dks.append(nn(query_t, ds))
            dvs.append(nn(dob_t, weights))
        dq_ref[:, out] = jnp.where(lane < head, dqs[0], dqs[1]) * scale
        dk_ref[:, out] = (jnp.where(row < head, dks[0], dks[1]) * scale).T
        dv_ref[:, out] = jnp.where(row < head, dvs[0], dvs[1]).T
        return carry

    lax.fori_loop(first, first + count, step, 0)


def back_kernel(
    lay, t0, t1, t2, t3, kp_ref, x1_ref, dn_ref, came_ref, vec_ref, wp_ref, ob0, ob1, oo0, oo1, q_ref, k_ref, v_ref,
    p_ref, dx_ref, dob_ref, pg_ref, sums_ref, dq_ref, dk_ref, dv_ref, dxb_ref,
):
    g_ref = vec_ref[:, lay.at["mlp_gain"]]
    band, third, half = lay.band, lay.third, lay.length // 2
    c = here()[2]
    gg, sg, pbg = 0.0, 0.0, 0.0
    for b, ref in enumerate((t0, t1, t2, t3)):
        at = slice(b * band, (b + 1) * band)
        away = slice((b ^ 2) * band, ((b ^ 2) + 1) * band)
        dn = dn_ref[at] + came_ref[away].astype(F32)
        normed, inverse = normed_rows(x1_ref[at])
        dx = ref[band : 2 * band].astype(F32) * kp_ref[at] + norm_back(dn, normed, inverse, g_ref)
        dxb = dx.astype(BF)
        dxb_ref[at] = dxb
        if b < 2:
            dx_ref[at] = dx
            gg = gg + column_sum(dn * normed)
            sg = sg + column_sum(dn)
            pbg = pbg + column_sum(dxb.astype(F32))
    low = [pl.ds(pl.multiple_of((2 * s + c) * third, third), third) for s in range(2)]
    own_w = jnp.concatenate([wp_ref[low[0]], wp_ref[low[1]]], 0)
    dxb = dxb_ref[...]
    dob_ref[...] = nt(dxb, own_w).astype(BF)
    block = lay.width // 4
    zero = jnp.concatenate([dxb[:, :block], dxb[:, 2 * block : 3 * block]], 1)
    one = jnp.concatenate([dxb[:, block : 2 * block], dxb[:, 3 * block :]], 1)
    cols = jnp.where(c == 0, zero, one)
    mine, other = both_heads(half, ob0, ob1, oo0, oo1)
    mine_g, other_g = tn(mine, cols).astype(BF), tn(other, cols).astype(BF)
    zero, one = jnp.where(c == 0, mine_g, other_g), jnp.where(c == 0, other_g, mine_g)
    p_grad = jnp.concatenate([zero[:third], one[:third], zero[third:], one[third:]], 0)
    pg_ref[...] = p_grad
    sums_ref[...] = jnp.concatenate([gg, sg, pbg], 0)
    attend_back(lay, 0, 1, 0, q_ref, k_ref, v_ref, p_ref, dob_ref, dq_ref, dk_ref, dv_ref)


def back_heads_kernel(lay, q_ref, k_ref, v_ref, p_ref, dob_ref, dq_ref, dk_ref, dv_ref):
    attend_back(lay, 1, HEADS // 4 - 1, 1, q_ref, k_ref, v_ref, p_ref, dob_ref, dq_ref, dk_ref, dv_ref)


def back_rest_kernel(
    lay, plan, n_g, t0, t1, t2, t3, q_ref, k_ref, cos_ref, sin_ref, a_ref, w_ref, table_ref, ubg0, ubg1, dbg_ref, pg_ref, sums_ref,
    dq0, dk0, dv0, dq1, dk1, dv1, *refs,
):
    keep_ref, send_ref = refs[:2]
    grads = refs[2 : 2 + n_g]
    dq_ref, g_tmp, dqkv_ref = refs[2 + n_g :]
    band, side, own, third, half, head = lay.band, lay.side, lay.own, lay.third, lay.length // 2, lay.head
    gg, sg, pbg = sums_ref[0:1], sums_ref[1:2], sums_ref[2:3]
    block = lay.width // 4
    sizes = [ref.shape[1] // 2 for ref in (ubg0, ubg1)]
    ubg = [ref[:, y_side * size : (y_side + 1) * size] for y_side in range(2) for ref, size in zip((ubg0, ubg1), sizes)]
    ubg = jnp.concatenate(ubg, 1)
    cos, sin = cos_ref[...], sin_ref[...]
    dq, dk, dv = (jnp.concatenate([a[...], b[...]], 1) for a, b in ((dq0, dq1), (dk0, dk1), (dv0, dv1)))
    dqkv_ref[:, :own] = (dq * cos + halves_of(lay, dq * sin)).astype(BF)
    dqkv_ref[:, own : 2 * own] = (dk * cos + halves_of(lay, dk * sin)).astype(BF)
    dqkv_ref[:, 2 * own :] = dv.astype(BF)
    dq_ref[...] = dq * halves_of(lay, q_ref[...].astype(F32)) + dk * halves_of(lay, k_ref[...].astype(F32))
    by_col = jnp.zeros((side, own), F32)
    by_row = jnp.zeros((side, own), F32)
    for b, flip in enumerate((0, 2, 1, 3)):
        first = ((here()[3] ^ flip) * lay.band_rows).astype(F32)
        for r in range(lay.band_rows):
            turn = dq_ref[b * band + r * side : b * band + (r + 1) * side]
            by_col = by_col + turn
            by_row = by_row + turn * (first + r)
    lane = lax.broadcasted_iota(jnp.int32, (2, own), 1)
    sign = jnp.where((lane & (head // 2)) == 0, -1.0, 1.0).astype(F32)
    place = lax.broadcasted_iota(jnp.int32, (side, own), 0).astype(F32)
    both = jnp.concatenate([column_sum(by_col * place), column_sum(by_row)], 0) * sign
    both = jnp.where(sign < 0, both + halves_of(lay, both), 0.0)
    freqs = jnp.concatenate([both[0:1], both[1:2]], 1)
    bqk = column_sum(dqkv_ref[:, : 2 * own].astype(F32))
    bv = column_sum(dqkv_ref[:, 2 * own :].astype(F32))
    grad = nt(dqkv_ref[:, : 3 * third], w_ref[0]) + nt(dqkv_ref[:, 3 * third :], w_ref[1])
    keep_ref[...] = grad[:half]
    send_ref[...] = grad[half:].astype(BF)
    g1, s1 = 0.0, 0.0
    for b, ref in enumerate((t0, t1, t2, t3)):
        part = grad[b * band : (b + 1) * band]
        normed, _ = normed_rows(ref[:band].astype(F32))
        g1 = g1 + column_sum(part * normed)
        s1 = s1 + column_sum(part)
    repack(lay, plan, table_ref, [bqk, bv, pbg, g1, s1, gg, sg, ubg, dbg_ref[...], freqs], grads)
    acts = a_ref[...]
    sides = []
    for y_side in range(2):
        grad = tn(acts, dqkv_ref[:, y_side * 3 * third : (y_side + 1) * 3 * third]).astype(BF)
        sides.append(jnp.concatenate([grad, pg_ref[:, y_side * block : (y_side + 1) * block]], 1))
    y = here()[1]
    for y_rel in range(2):
        g_tmp[...] = jnp.where((y ^ y_rel) == 0, sides[0], sides[1]).reshape(g_tmp.shape)
        store_pieces(lay, lay.first, grads, y_rel, slice(None), g_tmp)


def finish_kernel(lay, t0, t1, keep_ref, came_ref, dx_ref, vec_ref, out_ref, send_ref):
    band = lay.band
    g_ref = vec_ref[:, lay.at["attn_gain"]]
    for b, ref in enumerate((t0, t1)):
        at = slice(b * band, (b + 1) * band)
        dn = keep_ref[at] + came_ref[at].astype(F32)
        normed, inverse = normed_rows(ref[:band].astype(F32))
        result = (dx_ref[at] + norm_back(dn, normed, inverse, g_ref)).astype(BF)
        if b == 0:
            out_ref[...] = result
        else:
            send_ref[...] = result


def tail_second_kernel(lay, counts, *refs):
    up_ref, down_ref = refs[-2:]
    half = lay.half_rows
    for part, count in enumerate(counts):
        at = lay.parts[part]
        step = at.stop - at.start
        keep, *came = refs[sum(counts[:part]) : sum(counts[: part + 1])]
        if not came:
            up_ref[:, at], down_ref[:, at] = keep[:, :step].astype(F32), keep[:, step:].astype(F32)
        for rows, ref in zip((slice(0, half), slice(half, None)), came):
            up_ref[rows, at] = keep[rows, :step].astype(F32) + ref[:, :step].astype(F32)
            down_ref[rows, at] = keep[rows, step:].astype(F32) + ref[:, step:].astype(F32)


def tail_send_kernel(lay, sum_ref, out_ref):
    third, rows = lay.third, lay.rows
    out_ref[:, :third] = jnp.where(here()[2] == 0, sum_ref[:rows, 2 * third : 3 * third], sum_ref[:rows, :third])
    out_ref[:, third:] = jnp.zeros((rows, out_ref.shape[1] - third), BF)
    theirs = sum_ref[rows:, :PACKED].astype(F32)[1:2]
    out_ref[0:1, out_ref.shape[1] - PACKED :] = theirs.astype(BF)


def tail_kernel(lay, plan, sum_ref, came_ref, qkv_ref, proj_ref, *outs):
    third, rows = lay.third, lay.rows
    d0, d1, d2 = (sum_ref[:rows, k * third : (k + 1) * third] for k in range(3))
    c = here()[2]
    qkv_ref[:, :third] = jnp.where(c == 0, d0, d1).astype(F32)
    qkv_ref[:, third : 2 * third] = came_ref[:, :third].astype(F32)
    qkv_ref[:, 2 * third :] = jnp.where(c == 0, d1, d2).astype(F32)
    proj_ref[...] = sum_ref[:rows, 3 * third :].astype(F32)
    total = sum_ref[rows:, :PACKED].astype(F32)[0:1] + came_ref[0:1, came_ref.shape[1] - PACKED :].astype(F32)
    for ref, (_, _, offset, count) in zip(outs, plan):
        ref[...] = total[:, offset : offset + count]


def call(kernel, name, inputs, outs, scratch=(), limit=16, hbm=False):
    return pl.pallas_call(
        kernel,
        out_shape=[jax.ShapeDtypeStruct(shape, dtype) for shape, dtype in outs],
        in_specs=[HBM if hbm else VMEM] * len(inputs),
        out_specs=[VMEM] * len(outs),
        scratch_shapes=[s if not isinstance(s, tuple) else pltpu.VMEM(*s) for s in scratch],
        compiler_params=pltpu.CompilerParams(vmem_limit_bytes=limit * MIB),
        cost_estimate=pl.CostEstimate(flops=1000, bytes_accessed=1024, transcendentals=0),
        name=name,
    )(*inputs)


def after(value, *others):
    return lax.optimization_barrier((value, *others))[0]


class Slice:
    def __init__(self, lay):
        self.lay = lay
        self.img = lax.axis_index("img")
        self.row = lax.axis_index("row")
        self.y = self.row // 2
        self.c = self.row % 2
        self.orders = lay.first

    def swap(self, array, step):
        if step == "c":
            return lax.ppermute(array, "row", [(r, r ^ 1) for r in range(4)])
        if step == "y":
            return lax.ppermute(array, "row", [(r, r ^ 2) for r in range(4)])
        mask = sum(1 << bit for bit in self.lay.high) if step == "high" else 1 << step
        return lax.ppermute(array, "img", [(i, i ^ mask) for i in range(self.lay.img_count)])

    def gather(self, piece, order):
        held = piece[None]
        for step in order:
            held = jnp.concatenate([held, self.swap(held, step)], 0)
        return held

    def scatter(self, held, order):
        for step in reversed(order):
            half = held.shape[0] // 2
            came = self.swap(held[half:], step)
            held = (held[:half].astype(F32) + came.astype(F32)).astype(held.dtype)
        return held[0]

    def places(self, order):
        place = jnp.zeros((2, self.lay.img_count), jnp.int32)
        img = jnp.arange(self.lay.img_count, dtype=jnp.int32)[None, :] ^ self.img
        side = jnp.arange(2, dtype=jnp.int32)[:, None] ^ self.y
        for k, step in enumerate(order):
            bit = side if step == "y" else (img >> step) & 1
            place = place + (bit << k)
        return place

    def sources(self, order):
        place = self.places(order).reshape(-1)
        return jnp.zeros_like(place).at[place].set(jnp.arange(place.size, dtype=jnp.int32))

    def gather_whole(self, piece):
        lay = self.lay
        base = self.gather(piece, lay.high)
        whole = []
        for part, order in enumerate(self.orders):
            held = base[:, part * lay.half_rows : (part + 1) * lay.half_rows]
            held = self.gather(held, order[-2:]).reshape((-1,) + held.shape[1:])
            whole.append(jnp.take(held, self.places(order), axis=0))
        return jnp.concatenate(whole, 2).reshape((2,) + lay.tiles + piece.shape[1:])

    def high(self, *pieces):
        steps = self.lay.high + ["high"]
        return [self.swap(piece, step) for piece, step in zip(pieces * 3 if len(pieces) == 1 else pieces, steps)]

    def merge(self, pieces, name):
        lay = self.lay
        rows, columns = pieces[0].shape[-2:]
        count = len(pieces) * (pieces[0].shape[0] if pieces[0].ndim == 3 else 1)
        shapes = [((count, n, columns), BF) for n in (lay.half_rows, rows - lay.half_rows)]
        return call(functools.partial(merge_kernel, lay), name, pieces, shapes)

    def pairs(self, orders, place, top, bottom):
        return [self.swap(top, orders[0][place]), self.swap(bottom, orders[1][place])]

    def grad_shapes(self, columns, extra=0):
        lay = self.lay
        if lay.aligned:
            return [((lay.img_count, lay.half_rows + more, columns), BF) for more in (0, 0, extra, extra)]
        return [((2,) + lay.tiles + (columns,), BF)] + [((2 * lay.img_count, 2, columns), BF)] * (extra > 0)

    def scatter_rows(self, parts):
        lay = self.lay
        extra = []
        if not lay.aligned:
            if len(parts) > 1:
                extra = [jnp.pad(self.scatter(parts[1], self.orders[1]), ((0, EXTRA - 2), (0, 0)))]
            pieces = parts[0].reshape(2, lay.img_count, lay.rows, parts[0].shape[3])
            parts = []
            for part, order in enumerate(self.orders):
                mine = pieces[:, :, part * lay.half_rows : (part + 1) * lay.half_rows]
                mine = jnp.take(mine.reshape((-1,) + mine.shape[2:]), self.sources(order), axis=0)
                parts += [mine[: lay.img_count], mine[lay.img_count :]]
        sums = []
        for part, order in enumerate(self.orders):
            keep, send = parts[2 * part : 2 * part + 2]
            held = (keep.astype(F32) + self.swap(send, order[-1]).astype(F32)).astype(BF)
            half = lay.img_count // 2
            sums.append((held[:half].astype(F32) + self.swap(held[half:], order[-2]).astype(F32)).astype(BF))
        total = self.scatter(jnp.concatenate(sums, 1), lay.high)
        return jnp.concatenate([total] + extra, 0) if extra else total

    def fold(self, grads, came, name):
        shapes = [((g.shape[0] // 2,) + g.shape[1:], BF) for g in grads]
        return call(fold_kernel, name + "_fold", [grads[0], came[0], grads[2], came[1]], shapes)

    def rejoin(self, groups, name, n=2):
        count, rows, _ = groups[0][0].shape
        shape = (count // n, rows + groups[0][2].shape[1], sum(group[0].shape[2] for group in groups))
        arrays = [array for group in groups for array in group]
        return list(call(functools.partial(rejoin_kernel, n), name + "_rejoin", arrays, [(shape, BF)] * n))

    def halve(self, keep, came, name):
        shape = (keep.shape[0] // 2,) + keep.shape[1:]
        return call(halve_kernel, name + "_halve", [keep, came], [(shape, BF)] * 2)

    def split(self, keep, came, name):
        _, rows, columns = keep.shape
        half = self.lay.half_rows
        shapes = [((n, columns), BF) for n in (rows, half, rows - half)]
        out, top, bottom = call(split_kernel, name + "_split", [keep, came], shapes)
        return [out] + self.pairs(self.lay.second, 0, top, bottom)

    def end(self, shares, name):
        return call(end_kernel, name + "_end", shares, [(shares[0].shape[1:], BF)])[0]


NAMES = ("qkv_bias", "proj_bias", "attn_gain", "attn_shift", "mlp_gain", "mlp_shift", "up_bias", "down_bias", "freqs")


def plan_vectors(lay):
    width, third, pairs = lay.width, lay.third, lay.head // 2
    devices = lay.img_count * 4
    heads = np.arange(HEADS).reshape(2, 2, HEADS // 4)

    def by_core(count, shape):
        return [np.take(np.arange(count).reshape(shape), core, len(shape) - 2).reshape(-1) for core in range(2)]

    plain = [np.arange(width)] * 2
    up = by_core(4 * width, (2, 2, width))
    freqs = []
    for core in range(2):
        pick = np.arange(width).reshape(2, HEADS, pairs)[:, heads[:, core].reshape(-1)]
        freqs.append(np.stack([pick, pick], 2).reshape(-1))
    qkv, qk, v = (by_core(n * width, (n, 2, 2, third)) for n in (3, 2, 1))

    def lay_out(members):
        plan, tables, start, offset = [], [[], [], [], []], 0, 0
        for pick, count in members:
            count //= devices
            plan.append((start, pick[0].size, offset, count))
            for core in range(2):
                tables[2 * core].append(pick[core] // count)
                tables[2 * core + 1].append(pick[core] % count)
            start += pick[0].size
            offset += count
        return plan, jnp.asarray(np.stack([np.concatenate(t) for t in tables]).astype(np.int32))

    rest = [(plain, width)] * 5 + [(up, 4 * width), (plain, width), (freqs, width)]
    given = lay_out([(qkv, 3 * width)] + rest)
    lay.at = {name: slice(p[0], p[0] + p[1]) for name, p in zip(NAMES, given[0])}
    return given, lay_out([(qk, 2 * width), (v, width)] + rest)


def make_body(img_count):
    def body(
        tokens, keep_mask, cotangent, qkv_weight, qkv_bias, proj_weight, proj_bias, attn_gain, attn_shift,
        mlp_gain, mlp_shift, up_weight, up_bias, down_weight, down_bias, rope_freqs,
    ):
        lay = Layout(img_count, tokens, qkv_weight.shape[0])
        me = Slice(lay)
        y = me.y
        images, band, width, length = lay.images, lay.band, lay.width, lay.length
        heads = HEADS // 2
        own, third = lay.own, lay.third
        half = length // 2
        block = proj_weight.shape[1]
        hidden = up_weight.shape[1]
        vectors = (qkv_bias, proj_bias, attn_gain, attn_shift, mlp_gain, mlp_shift, up_bias, down_bias, rope_freqs)
        (plan, table), (grad_plan, grad_table) = plan_vectors(lay)

        def pick(flag, zero, one):
            return jnp.where(flag == 0, zero, one)

        def kernel(function, name, inputs, outs, scratch=(), **options):
            return call(functools.partial(function, lay), name, inputs, outs, scratch, **options)

        pack_rows = 2 * band + 16
        sizes = [part.stop - part.start for part in lay.parts]
        mine, other, third_send, first_piece, *second_pieces = kernel(
            pack_kernel, "pack",
            [tokens.reshape(images, band, width), cotangent.reshape(images, band, width), keep_mask.transpose(1, 0, 2), qkv_weight, proj_weight,
             up_weight, down_weight.T, *[v.reshape(1, -1) for v in vectors]],
            [((pack_rows, width), BF), ((pack_rows + lay.rows - lay.half_rows, width), BF), ((lay.rows, 256 + PACKED), BF),
             ((lay.rows + EXTRA, 2 * third), BF),
             ((lay.rows, 2 * sizes[0] + block), BF), ((lay.half_rows, 2 * sizes[1]), BF)],
            [((lay.band_rows, images, lay.side), jnp.int32), (qkv_weight.shape, F32), (proj_weight.shape, F32), (up_weight.shape, F32),
             (down_weight.T.shape, F32), *[((1, v.shape[0]), F32) for v in vectors], pltpu.SemaphoreType.DMA((18,))],
            limit=60, hbm=True,
        )
        third_came = me.swap(third_send, "c")
        (first_piece,) = kernel(fit_kernel, "fit", [third_came, first_piece], [((lay.rows + EXTRA, 3 * third), BF)])
        mine_came = me.swap(mine, "c")
        near = me.swap(after(other, first_piece, mine_came), "y")
        bands = [mine, near, mine_came]
        if lay.aligned:
            part0, top1 = second_pieces
            near1 = me.swap(top1, lay.second[0][0])
            came = me.high(first_piece)
            bands.append(me.swap(after(near, *came), "c"))
            part0 = after(part0, came[0])
            top, bottom = me.merge([first_piece] + came, "merge_first")
            came = me.pairs(lay.first, -2, top, bottom)
            high0 = [me.swap(part0, step) for step in lay.high]
            top = after(top, bands[3], near1, *high0)
            shapes = [((2 * held.shape[0],) + held.shape[1:], BF) for held in (top, bottom)]
            top, bottom = call(join_kernel, "join_first", [top, came[0], bottom, came[1]], shapes)
            came = me.pairs(lay.first, -1, top, bottom)
            first = [top, came[0], bottom, came[1]]
            high0.append(me.swap(after(high0[0], top), lay.high[1]))
            top0, bottom0 = me.merge([part0] + high0, "merge0")
            shape = (2, lay.rows, top1.shape[1])
            (both1,) = kernel(start_kernel, "start1", [after(top1, high0[0]), near1, other, near], [(shape, BF)])
            vec_parts = [after(first[2], first[1], top0, bottom0, both1), first[3]]
        else:
            bands.append(me.swap(near, "c"))
            first = [me.gather_whole(first_piece[: lay.rows])]
            vec_parts = [me.gather(first_piece[lay.rows : lay.rows + 2], me.orders[1])]
            second = [[me.gather_whole(p)] for p in (second_pieces[0], jnp.concatenate([second_pieces[1], other[pack_rows:]], 0))]
        (vec,) = call(
            functools.partial(unpack_kernel, lay, plan, len(vec_parts)), "unpack", [table, *vec_parts],
            [((1, table.shape[1]), F32)], limit=24,
        )

        n_w = len(first)
        n_g = len(me.grad_shapes(1))
        a1, q, k, v, w_qkv, cos, sin, kp, mask_bias = call(
            functools.partial(project_kernel, lay, n_w), "qkv", [*bands, *first, vec],
            [((length, width), BF), ((length, own), BF), ((length, own), BF), ((length, own), BF), ((2, width, 3 * third), BF),
             ((length, own), F32), ((length, own), F32), ((length, 1), F32), ((1, length), F32)],
            [((2,) + lay.tiles + (3 * third,), BF)], limit=16,
        )
        def attend(first, count, q):
            return call(
                functools.partial(attend_kernel, lay, first, count), "attend%d" % first, [q, k, v, mask_bias],
                [((length, count * 2 * lay.head), BF), ((2 * count, length, length), BF)], limit=8,
            )

        ob0, p0 = attend(0, 1, q)
        oo0 = me.swap(ob0, "c")
        if lay.aligned:
            near0 = me.pairs(lay.first, -2, top0, bottom0)
            high1 = [both1] + [me.swap(both1, step) for step in lay.high]
            shapes = [((2 * held.shape[0],) + held.shape[1:], BF) for held in (top0, bottom0)]
            top0 = after(top0, ob0, high1[1], high1[2])
            top0, bottom0 = call(join_kernel, "join0", [top0, near0[0], bottom0, near0[1]], shapes)
            last0 = me.pairs(lay.first, -1, top0, bottom0)
            second = [[top0, last0[0], bottom0, last0[1]]]
            ob1, p1 = attend(1, HEADS // 4 - 1, after(q, top0, bottom0))
            high1.append(me.swap(after(high1[1], ob1), lay.high[1]))
            top1, bottom1 = me.merge(high1, "merge1")
            last1 = me.pairs(lay.second, -1, top1, bottom1)
            second.append([top1, last1[0], bottom1, last1[1]])
            gate = [ob1, top1, bottom1]
        else:
            ob1, p1 = attend(1, HEADS // 4 - 1, q)
            gate = [ob1]
        oo1 = me.swap(ob1, "c")
        (p_cols,) = call(
            functools.partial(proj_kernel, lay, len(second[0])), "proj", [after(second[0][0], *gate)] + second[0][1:], [((width, 2 * block), BF)],
            [((2,) + lay.tiles + (block,), BF)],
        )
        p_other = me.swap(p_cols, "c")
        x1, a2, a2_t, dm, dm_t, d_down_bias, w_proj = call(
            functools.partial(middle_kernel, lay), "middle", [*bands, ob0, ob1, oo0, oo1, p_cols, p_other, vec, kp],
            [((length, width), F32), ((length, width), BF), ((width, length), BF), ((length, width), BF), ((width, length), BF),
             ((1, width), F32), ((width, width), BF)], limit=10,
        )
        sums, second_grads, d_up_bias = [], [], []
        for part, at in enumerate(lay.parts):
            step = at.stop - at.start
            shapes = (me.grad_shapes(2 * step) if part else me.grad_shapes(step) * 2) + [((1, 2 * step), F32)]
            scratch = [(lay.tiles + (2 * step,), BF), (lay.tiles + (step,), BF)]
            if part == len(PARTS) - 1:
                shapes += [((half, width), F32), ((half, width), BF), ((length, width), F32), ((length, width), BF)]
                scratch = [((length, width), F32)] + scratch
            else:
                shapes += [((length, width), F32)] * 2
            outs = call(
                functools.partial(mlp_kernel, lay, part, len(second[part]), n_g), "mlp%d" % part,
                [x1, a2, a2_t, dm, dm_t, vec, *second[part], *sums], shapes, scratch, limit=18,
            )
            count = n_g if part else 2 * n_g
            second_grads.append(outs[:count])
            d_up_bias.append(outs[count])
            sums = outs[count + 1 :]
        part, m_send, dn, dn_send = sums
        if lay.aligned:
            g = second_grads[0]
            came0 = me.pairs(lay.second, -1, g[1], g[3])
            dn_send = after(dn_send, *came0)
            came0 += me.pairs(lay.second, -1, g[5], g[7])
        dn_came = me.swap(dn_send, "c")
        m_came = me.swap(m_send, "c")
        out_half = (kp[:half] * (part + m_came.astype(F32))).astype(BF)
        pair = 2 * lay.head
        dx_half, dob, p_grad, norm_sums, dq0, dk0, dv0 = call(
            functools.partial(back_kernel, lay), "back",
            [*bands, kp, x1, dn, dn_came, vec, w_proj, ob0, ob1, oo0, oo1, q, k, v, p0],
            [((half, width), F32), ((length, own), BF), ((width, 2 * block), BF), ((3, width), F32), ((length, pair), F32),
             ((length, pair), F32), ((length, pair), F32)],
            [((length, width), BF)], limit=20,
        )
        if lay.aligned:
            g = second_grads[1]
            came1 = me.pairs(lay.first, -1, *[after(send, dn_came) for send in (g[1], g[3])])
        else:
            g = [jnp.concatenate(second_grads[0], 3)], second_grads[1]
            d_second = [[me.scatter_rows(held)] for held in g]
        if lay.aligned:
            g = second_grads[0]
            came0[0] = after(came0[0], dob)
            keep0, send0 = me.rejoin([[g[k], came0[k // 2], g[k + 2], came0[k // 2 + 1]] for k in (0, 4)], "part0")
            dob = after(dob, keep0, send0)
            came0 = me.swap(send0, lay.high[1])
        dq1, dk1, dv1 = call(
            functools.partial(back_heads_kernel, lay), "back_heads", [q, k, v, p1, dob], [((length, own - pair), F32)] * 3
        )
        if lay.aligned:
            came1[0] = after(came1[0], dq1)
            folded1 = me.fold(second_grads[1], came1, "part1")
            dq1 = after(dq1, *folded1)
            came1 = me.pairs(lay.first, -2, folded1[1], folded1[3])
        grad_shapes = me.grad_shapes(3 * third + block, EXTRA)
        dn1_keep, dn1_send, *first_grads = call(
            functools.partial(back_rest_kernel, lay, grad_plan, len(grad_shapes)), "back_rest",
            [*bands, q, k, cos, sin, a1, w_qkv, grad_table, *d_up_bias, d_down_bias, p_grad, norm_sums, dq0, dk0, dv0, dq1, dk1, dv1],
            [((half, width), F32), ((half, width), BF), *grad_shapes],
            [((length, own), F32), (lay.tiles + (3 * third + block,), BF), ((length, 3 * own), BF)], limit=24,
        )
        if lay.aligned:
            g = first_grads
            came = me.pairs(lay.first, -1, *[after(send, came0, *came1) for send in (g[1], g[3])])
            keep0, send0 = me.halve(keep0, came0, "part0")
            came0 = me.swap(send0, lay.high[0])
            keep1, send1 = me.rejoin([[folded1[0], came1[0], folded1[2], came1[1]]], "part1")
            came1 = me.swap(send1, lay.high[1])
            folded = me.fold(g, came, "first")
            came = me.pairs(lay.first, -2, *[after(send, came0, came1) for send in (folded[1], folded[3])])
            d_second = [me.split(keep0, came0, "part0")]
            keep1, send1 = me.halve(keep1, came1, "part1")
            came1 = me.swap(send1, lay.high[0])
            shares = me.rejoin([[folded[0], came[0], folded[2], came[1]]], "first", 4)
            d_second.append([me.end([keep1, came1], "part1")])
            shares[1] = after(shares[1], *d_second[0], d_second[1][0])
            d_first = me.end([shares[0]] + me.high(*shares[1:]), "first")
        else:
            d_first = me.scatter_rows(first_grads)
        dn1_came = me.swap(dn1_send, "c")
        tg_keep, tg_send = call(
            functools.partial(finish_kernel, lay), "finish", [bands[0], bands[1], dn1_keep, dn1_came, dx_half, vec],
            [((band, width), BF), ((band, width), BF)],
        )

        def to_images(keep, send):
            came = me.swap(send, "y")
            return pick(y, jnp.stack([keep, came]), jnp.stack([came, keep])).reshape(tokens.shape)

        layer_out = to_images(out_half[:band], out_half[band:])
        tokens_grad = to_images(tg_keep, tg_send)

        d_up, d_down = call(
            functools.partial(tail_second_kernel, lay, [len(d) for d in d_second]), "tail_second",
            [held for d in d_second for held in d], [((lay.rows, n), F32) for n in (hidden, hidden)]
        )
        d_down = d_down.T
        (tail_send,) = kernel(tail_send_kernel, "tail_send", [d_first], [((lay.rows, 256 + PACKED), BF)])
        tail_came = me.swap(tail_send, "c")
        d_qkv, d_proj, *r = call(
            functools.partial(tail_kernel, lay, grad_plan), "tail", [d_first, tail_came],
            [((lay.rows, 3 * third), F32), ((lay.rows, block), F32), *[((1, count), F32) for _, _, _, count in grad_plan]],
        )
        r = [v.reshape(-1) for v in r]
        return (
            layer_out, tokens_grad, d_qkv, r[0], r[1], d_proj, r[2], r[3], r[4], r[5], r[6], d_up, r[7], d_down, r[8], r[9],
        )

    return body


def solution(mesh):
    split = P(("img", "row"))
    both = P("img", "row")
    field = P("img", "row", None, None)
    return jax.shard_map(
        make_body(mesh.shape["img"]),
        mesh=mesh,
        in_specs=(
            field, P("img", "row", None), field, both, split, both, split, split, split, split, split, both, split,
            P("row", "img"), split, split,
        ),
        out_specs=(
            field, field, both, split, split, both, split, split, split, split, split, both, split, P("row", "img"),
            split, split,
        ),
        check_vma=False,
    )
```

```python
import functools

import jax
import jax.numpy as jnp
import numpy as np
from jax import lax
from jax.experimental import pallas as pl
from jax.experimental.pallas import tpu as pltpu
from jax.sharding import PartitionSpec as P

HEADS = 12
PARTS = (3, 3)
NORM_EPSILON = 1e-06
MASKED_SCORE = -1e30
BF = jnp.bfloat16
F32 = jnp.float32
MIB = 2**20
VMEM = pl.BlockSpec(memory_space=pltpu.VMEM)
HBM = pl.BlockSpec(memory_space=pltpu.MemorySpace.HBM)
PACKED = 384
SPARE = 64
EXTRA = 8


def dot(left, right, dims):
    return lax.dot_general(left, right, (dims, ((), ())), preferred_element_type=F32)


def nn(left, right):
    return dot(left, right, ((1,), (0,)))


def nt(left, right):
    return dot(left, right, ((1,), (1,)))


def tn(left, right):
    return dot(left, right, ((0,), (0,)))


def normed_rows(values):
    center = values - jnp.mean(values, -1, keepdims=True)
    inverse = lax.rsqrt(jnp.mean(center * center, -1, keepdims=True) + NORM_EPSILON)
    return center * inverse, inverse


def norm_back(grad, normed, inverse, gain):
    scaled = grad * gain
    centred = scaled - jnp.mean(scaled, -1, keepdims=True)
    return inverse * (centred - normed * jnp.mean(scaled * normed, -1, keepdims=True))


def column_sum(value):
    return jnp.sum(value, 0, keepdims=True)


def here():
    row = lax.axis_index("row")
    return lax.axis_index("img"), row >> 1, row & 1, row


class Layout:
    def __init__(self, img_count, tokens, rows):
        self.img_count = img_count
        self.bits = img_count.bit_length() - 1
        self.rows = rows
        self.half_rows = rows // 2
        self.aligned = rows % 32 == 0 and img_count == 8
        self.images, self.band_rows, self.side, self.width = tokens.shape
        self.band = self.band_rows * self.side
        self.length = 4 * self.band
        self.head = self.width // HEADS
        self.own = self.width // 2
        self.third = self.own // 2
        self.high = list(range(self.bits - 1, 0, -1))
        self.first = (self.high + [0, "y"], self.high + ["y", 0])
        self.second = ([0] + self.high + ["y"], ["y"] + self.high + [0])
        sizes = [self.width * sixths // 6 for sixths in PARTS]
        self.parts = [slice(sum(sizes[:n]), sum(sizes[: n + 1])) for n in range(len(sizes))]
        self.gathered = (self.first, self.second)
        self.reduced = (self.second, self.first)
        self.tiles = (img_count, rows) if self.aligned else (1, self.width)

    def slots(self, orders, img_rel, y_rel):
        found = []
        for order in orders:
            bits = [y_rel if step == "y" else (img_rel >> step) & 1 for step in order]
            found.append((sum(bit << k for k, bit in enumerate(bits[:-1])), bits[-1]))
        return found


def load_pieces(lay, orders, refs, y_rel, target, columns=slice(None)):
    if not lay.aligned:
        target[...] = refs[0][here()[1] ^ y_rel, :, :, columns]
        return
    half = lay.half_rows
    count = len(refs) // 2
    for img_rel in range(lay.img_count):
        for part, (slot, last) in enumerate(lay.slots(orders, img_rel, y_rel)):
            which, slot = divmod((slot + last * lay.img_count) * count, 2 * lay.img_count)
            ref, slot = refs[part * count + which], slot // count
            target[img_rel ^ here()[0], part * half : (part + 1) * half] = ref[slot, :half, columns]


def store_pieces(lay, orders, refs, y_rel, columns, source):
    if not lay.aligned:
        refs[0][here()[1] ^ y_rel, :, :, columns] = source[...]
        return
    half = lay.half_rows
    for img_rel in range(lay.img_count):
        for part, (slot, last) in enumerate(lay.slots(orders, img_rel, y_rel)):
            refs[2 * part + last][slot, :half, columns] = source[img_rel ^ here()[0], part * half : (part + 1) * half]


def halves_of(lay, value):
    pairs = lay.head // 2
    lane = lax.broadcasted_iota(jnp.int32, value.shape, 1)
    width = value.shape[1]
    first = (lane & pairs) == 0
    return jnp.where(first, pltpu.roll(value, width - pairs, 1), pltpu.roll(value, pairs, 1))


def pack_kernel(lay, *refs):
    tok, cot, mask, qkv, proj, up, down, *vectors = refs[:16]
    mine_ref, other_ref, third_ref, first_ref = refs[16:20]
    second, refs = [*refs[20:22], other_ref.at[2 * lay.band + 16 :]], refs[22:]
    mask_in, qkv_in, proj_in, up_in, down_in, *vectors_in = refs[:14]
    sems = refs[14]
    y = here()[1]
    band, third, width, rows = lay.band, lay.third, lay.width, lay.rows
    pairs = [(qkv, qkv_in), (proj, proj_in), *zip(vectors, vectors_in), (up, up_in), (down, down_in), (mask, mask_in)]
    for ref, which in ((other_ref, 1 - y), (mine_ref, y)):
        pairs += [(tok.at[which], ref.at[:band]), (cot.at[which], ref.at[band : 2 * band])]
    copies = [pltpu.make_async_copy(source, target, sems.at[n]) for n, (source, target) in enumerate(pairs)]
    for copy in copies:
        copy.start()
    for copy in copies[:11]:
        copy.wait()
    packed = jnp.concatenate([v[...] for v in vectors_in], 1)
    packed = jnp.concatenate([packed, jnp.zeros((1, PACKED - packed.shape[1]), F32)], 1).astype(BF)
    third_ref[:, :third] = qkv_in[:, third : 2 * third].astype(BF)
    third_ref[:, third:] = jnp.zeros((rows, third_ref.shape[1] - third), BF)
    third_ref[0:1, third_ref.shape[1] - PACKED :] = packed
    first_ref[:rows, :third] = qkv_in[:, :third].astype(BF)
    first_ref[:rows, third : 2 * third] = qkv_in[:, 2 * third :].astype(BF)
    first_ref[rows:] = jnp.zeros((EXTRA, first_ref.shape[1]), BF)
    first_ref[rows : rows + 1, :PACKED] = packed
    for copy in copies[11:]:
        copy.wait()
    for ref, part, first_row in zip(second, (0, 1, 1), (0, 0, lay.half_rows)):
        at = lay.parts[part]
        step = at.stop - at.start
        side = slice(first_row, first_row + ref.shape[0])
        ref[:, :step] = up_in[side, at].astype(BF)
        ref[:, step : 2 * step] = down_in[side, at].astype(BF)
        if part == 0:
            ref[:, 2 * step :] = proj_in[side].astype(BF)
    for ref, which in ((mine_ref, y), (other_ref, 1 - y)):
        keep = [jnp.where(which == 0, mask_in[r, 0:1], mask_in[r, 1:2]).astype(F32) for r in range(lay.band_rows)]
        flat = jnp.concatenate(keep, 1)
        flat = jnp.concatenate([flat, jnp.zeros((1, width - band), F32)], 1)
        ref[2 * band : 2 * band + 16] = jnp.concatenate([flat, jnp.zeros((15, width), F32)], 0).astype(BF)


def fit_kernel(lay, came_ref, first_ref, out_ref):
    third, rows = lay.third, lay.rows
    c = here()[2]
    t0, t2, came = first_ref[:rows, :third], first_ref[:rows, third : 2 * third], came_ref[:, :third]
    out_ref[:, : 3 * third] = jnp.where(c == 0, jnp.concatenate([t0, t2, came], 1), jnp.concatenate([came, t0, t2], 1))
    lines = [first_ref[rows : rows + 1, :PACKED].astype(F32), came_ref[0:1, came_ref.shape[1] - PACKED :].astype(F32)]
    lines = [line[:, k : k + SPARE] for line in lines for k in range(0, PACKED, SPARE)]
    if rows > len(lines):
        lines.append(jnp.zeros((rows - len(lines), SPARE), F32))
    out_ref[:, 3 * third :] = jnp.concatenate(lines, 0).astype(BF)


def merge_kernel(lay, *refs):
    pieces, (top_ref, bottom_ref) = refs[:-2], refs[-2:]
    half = lay.half_rows
    for k, ref in enumerate(pieces):
        if len(ref.shape) == 2:
            top_ref[k] = ref[:half]
            bottom_ref[k] = ref[half:]
        else:
            count = ref.shape[0]
            top_ref[k * count : (k + 1) * count] = ref[:, :half]
            bottom_ref[k * count : (k + 1) * count] = ref[:, half:]


def start_kernel(lay, top, top_came, bottom, bottom_came, out_ref):
    half = lay.half_rows
    out_ref[0, :half], out_ref[1, :half] = top[...], top_came[...]
    first = 2 * lay.band + 16
    out_ref[0, half:], out_ref[1, half:] = bottom[first:], bottom_came[first:]


def join_kernel(*refs):
    for part in range(2):
        own, came = refs[2 * part : 2 * part + 2]
        refs[4 + part][: own.shape[0]] = own[...]
        refs[4 + part][own.shape[0] :] = came[...]


def fold_kernel(*refs):
    for part in range(2):
        keep, came = refs[2 * part : 2 * part + 2]
        count = keep.shape[0] // 2
        for half in range(2):
            at = slice(half * count, (half + 1) * count)
            refs[4 + 2 * part + half][...] = (keep[at].astype(F32) + came[at].astype(F32)).astype(BF)


def rejoin_kernel(n, *refs):
    outs = refs[len(refs) - n :]
    top = refs[0].shape[1]
    count = refs[0].shape[0] // n
    column = 0
    for k in range(0, len(refs) - n, 4):
        columns = slice(column, column + refs[k].shape[2])
        column = columns.stop
        for part in range(2):
            keep, came = refs[k + 2 * part : k + 2 * part + 2]
            rows = slice(0, top) if part == 0 else slice(top, None)
            for share, out in enumerate(outs):
                at = slice(share * count, (share + 1) * count)
                out[:, rows, columns] = (keep[at].astype(F32) + came[at].astype(F32)).astype(BF)


def end_kernel(*refs):
    refs[-1][...] = sum(ref[0].astype(F32) for ref in refs[:-1]).astype(BF)


def halve_kernel(keep_ref, came_ref, *outs):
    count = keep_ref.shape[0] // len(outs)
    for half, ref in enumerate(outs):
        at = slice(half * count, (half + 1) * count)
        total = (keep_ref[at].astype(F32) + came_ref[at].astype(F32)).astype(BF)
        ref[...] = total.reshape(ref.shape)


def split_kernel(keep_ref, came_ref, out_ref, top_ref, bottom_ref):
    half = top_ref.shape[0]
    out_ref[...] = (keep_ref[0].astype(F32) + came_ref[0].astype(F32)).astype(BF)
    top_ref[...] = (keep_ref[1, :half].astype(F32) + came_ref[1, :half].astype(F32)).astype(BF)
    bottom_ref[...] = (keep_ref[1, half:].astype(F32) + came_ref[1, half:].astype(F32)).astype(BF)


def owner_mask(lay, order, c_rel, table_row):
    place = lax.broadcasted_iota(jnp.int32, (2 * lay.img_count, 1), 0)
    img_rel = jnp.zeros_like(place)
    row = here()[3] ^ c_rel
    for k, step in enumerate(order):
        bit = (place >> k) & 1
        if step == "y":
            row = row ^ (bit * 2)
        else:
            img_rel = img_rel | (bit << step)
    return ((img_rel ^ here()[0]) * 4 + row) == table_row


def owners(table_ref, at, c):
    owner = jnp.where(c == 0, table_ref[0:1, at], table_ref[2:3, at])
    entry = jnp.where(c == 0, table_ref[1:2, at], table_ref[3:4, at])
    return owner, entry


def unpack_kernel(lay, plan, n_v, table_ref, *refs):
    v_refs, out_ref = refs[:n_v], refs[n_v]
    lines = PACKED // SPARE
    if lay.aligned:
        blocks = [ref[k, :16, ref.shape[2] - SPARE :].astype(F32) for ref in v_refs for k in range(ref.shape[0])]
        blocks = [jnp.concatenate([block[n : n + 1] for block in blocks], 0) for n in range(2 * lines)]
    else:
        blocks = [v_refs[0][:, n].astype(F32) for n in range(2 * lines)]
    gathered = [jnp.concatenate(blocks[c_rel * lines : (c_rel + 1) * lines], 1).astype(BF) for c_rel in range(2)]
    for start, size, offset, count in plan:
        at = slice(start, start + size)
        owner, entry = owners(table_ref, at, here()[2])
        spread = (lax.broadcasted_iota(jnp.int32, (count, size), 0) == entry).astype(F32).astype(BF)
        total = 0.0
        for c_rel in range(2):
            rows = nn(gathered[c_rel][:, offset : offset + count], spread)
            total = total + column_sum(jnp.where(owner_mask(lay, lay.first[0], c_rel, owner), rows, 0.0))
        out_ref[:, at] = total


def repack(lay, plan, table_ref, grads, refs):
    sides = []
    for c_rel in range(2):
        parts = []
        for grad, (start, size, offset, count) in zip(grads, plan):
            owner, entry = owners(table_ref, slice(start, start + size), here()[2])
            spread = (lax.broadcasted_iota(jnp.int32, (count, size), 0) == entry).astype(F32).astype(BF)
            rows = jnp.where(owner_mask(lay, lay.first[1], c_rel, owner), grad, 0.0).astype(BF)
            parts.append(nt(rows, spread))
        used = sum(p.shape[1] for p in parts)
        sides.append(jnp.concatenate(parts + [jnp.zeros((2 * lay.img_count, PACKED - used), F32)], 1))
    if not lay.aligned:
        refs[1][...] = jnp.zeros(refs[1].shape, BF)
        for c_rel in range(2):
            refs[1][:, c_rel, :PACKED] = sides[c_rel].astype(BF)
        return
    half, count = lay.half_rows, lay.img_count
    for j in range(2 * count):
        ref = refs[2 + j // count]
        block = jnp.concatenate([side[j : j + 1] for side in sides] + [jnp.zeros((EXTRA - 2, PACKED), F32)], 0).astype(BF)
        ref[j % count, half:] = jnp.zeros((EXTRA, ref.shape[2]), BF)
        ref[j % count, half:, :PACKED] = block


def project_kernel(lay, n_w, t0, t1, t2, t3, *refs):
    w_refs = refs[:n_w]
    vec_ref, a_ref, q_ref, k_ref, v_ref, w_out, cos_ref, sin_ref, kp_ref, bias_ref, w_all = refs[n_w:]
    band, side, own, third = lay.band, lay.side, lay.own, lay.third
    g_ref, s_ref, b_ref = (vec_ref[:, lay.at[n]] for n in ("attn_gain", "attn_shift", "qkv_bias"))
    f_ref = vec_ref[:, lay.at["freqs"]]
    keeps = []
    for b, ref in enumerate((t0, t1, t2, t3)):
        at = slice(b * band, (b + 1) * band)
        normed, _ = normed_rows(ref[:band].astype(F32))
        a_ref[at] = (normed * g_ref + s_ref).astype(BF)
        keep = ref[2 * band : 2 * band + 16, :band].astype(F32)
        kp_ref[at] = jnp.transpose(keep)[:, 0:1]
        keeps.append(keep[0:1])
    bias_ref[...] = jnp.where(jnp.concatenate(keeps, 1) > 0, 0.0, MASKED_SCORE)
    lane = lax.broadcasted_iota(jnp.int32, (side, own), 1)
    sign = jnp.where((lane & (lay.head // 2)) == 0, -1.0, 1.0).astype(F32)
    col = lax.broadcasted_iota(jnp.int32, (side, own), 0).astype(F32) * f_ref[:, :own]
    col_cos, col_sin = jnp.cos(col), jnp.sin(col)
    row_index = here()[3]
    for b, flip in enumerate((0, 2, 1, 3)):
        first = ((row_index ^ flip) * lay.band_rows).astype(F32)
        rows = (lax.broadcasted_iota(jnp.int32, (8, own), 0).astype(F32) + first) * f_ref[:, own:]
        row_cos, row_sin = jnp.cos(rows), jnp.sin(rows)
        for r in range(lay.band_rows):
            at = slice(b * band + r * side, b * band + (r + 1) * side)
            rc, rs = row_cos[r : r + 1], row_sin[r : r + 1]
            cos_ref[at] = col_cos * rc - col_sin * rs
            sin_ref[at] = (col_sin * rc + col_cos * rs) * sign
    for y_rel in range(2):
        y_side = here()[1] ^ y_rel
        load_pieces(lay, lay.first, w_refs, y_rel, w_all.at[y_side], slice(0, 3 * third))
    acts = a_ref[...]
    w0, w1 = w_all[0].reshape(lay.width, -1), w_all[1].reshape(lay.width, -1)
    w_out[0], w_out[1] = w0, w1
    left = nn(acts, w0) + b_ref[:, : 3 * third]
    right = nn(acts, w1) + b_ref[:, 3 * third :]
    query, key = left[:, :own], jnp.concatenate([left[:, own:], right[:, :third]], 1)
    cos, sin = cos_ref[...], sin_ref[...]
    q_ref[...] = (query * cos + halves_of(lay, query) * sin).astype(BF)
    k_ref[...] = (key * cos + halves_of(lay, key) * sin).astype(BF)
    v_ref[...] = right[:, third:].astype(BF)


def proj_kernel(lay, n_w, *refs):
    out_ref, w_all = refs[n_w:]
    block = lay.width // 4
    columns = slice(refs[0].shape[-1] - block, None)
    for y_rel in range(2):
        y_side = here()[1] ^ y_rel
        load_pieces(lay, lay.gathered[0], refs[:n_w], y_rel, w_all.at[y_side], columns)
    for y_side in range(2):
        out_ref[:, y_side * block : (y_side + 1) * block] = w_all[y_side].reshape(lay.width, block)


def attend_kernel(lay, first, count, q_ref, k_ref, v_ref, bias_ref, o_ref, p_ref):
    head = lay.head
    pair = 2 * head
    scale = head**-0.5

    def step(n, carry):
        at = pl.ds(pl.multiple_of(n * pair, pair), pair)
        out = pl.ds(pl.multiple_of((n - first) * pair, pair), pair)
        keys, values = k_ref[:, at], v_ref[:, at]
        query = q_ref[:, at] * jnp.asarray(scale, BF)
        lane = lax.broadcasted_iota(jnp.int32, query.shape, 1)
        outs = []
        for h in range(2):
            mine = (lane < head) if h == 0 else (lane >= head)
            score = nt(jnp.where(mine, query, jnp.zeros_like(query)), keys) + bias_ref[...]
            power = jnp.exp(score - jnp.max(score, -1, keepdims=True))
            weights = (power * (1.0 / jnp.sum(power, -1, keepdims=True))).astype(BF)
            p_ref[2 * (n - first) + h] = weights
            outs.append(nn(weights, values))
        o_ref[:, out] = jnp.where(lane < head, outs[0], outs[1]).astype(BF)
        return carry

    lax.fori_loop(first, first + count, step, 0)


def both_heads(half, ob0, ob1, oo0, oo1):
    other = jnp.concatenate([oo0[...], oo1[...]], 1)
    return jnp.concatenate([ob0[...], ob1[...]], 1), jnp.concatenate([other[half:], other[:half]], 0)


def middle_kernel(lay, t0, t1, t2, t3, ob0, ob1, oo0, oo1, p_ref, po_ref, vec_ref, kp_ref, x1_ref, a2_ref, at_ref, dm_ref, dt_ref, dbg_ref, wp_ref):
    band, third, half = lay.band, lay.third, lay.length // 2
    c = here()[2]
    block = lay.width // 4
    pb_ref, g_ref, s_ref = (vec_ref[:, lay.at[n]] for n in ("proj_bias", "mlp_gain", "mlp_shift"))
    for y_side in range(2):
        mine, other = (ref[:, y_side * block : (y_side + 1) * block] for ref in (p_ref, po_ref))
        wp_ref[:, 2 * y_side * block : 2 * (y_side + 1) * block] = jnp.where(
            c == 0, jnp.concatenate([mine, other], 1), jnp.concatenate([other, mine], 1)
        )
    low = [pl.ds(pl.multiple_of((2 * s + c) * third, third), third) for s in range(2)]
    high = [pl.ds(pl.multiple_of((2 * s + 1 - c) * third, third), third) for s in range(2)]
    own_w = jnp.concatenate([wp_ref[low[0]], wp_ref[low[1]]], 0)
    other_w = jnp.concatenate([wp_ref[high[0]], wp_ref[high[1]]], 0)
    mine, other = both_heads(half, ob0, ob1, oo0, oo1)
    x1_ref[...] = nn(mine, own_w) + nn(other, other_w) + pb_ref
    for b, ref in enumerate((t0, t1, t2, t3)):
        at = slice(b * band, (b + 1) * band)
        x1 = x1_ref[at] + ref[:band].astype(F32)
        x1_ref[at] = x1
        normed, _ = normed_rows(x1)
        a2_ref[at] = (normed * g_ref + s_ref).astype(BF)
        dm_ref[at] = (ref[band : 2 * band].astype(F32) * kp_ref[at]).astype(BF)
    at_ref[...] = a2_ref[...].T
    dt_ref[...] = dm_ref[...].T
    dbg_ref[...] = column_sum(dm_ref[:half].astype(F32))


def mlp_kernel(lay, part, n_w, n_g, x1_ref, a2_ref, at_ref, dm_ref, dt_ref, vec_ref, *refs):
    w_refs, refs = refs[:n_w], refs[n_w:]
    last = part == len(PARTS) - 1
    if part:
        (m_in, dn_in), refs = refs[:2], refs[2:]
    count = n_g if last else 2 * n_g
    grads, refs = refs[:count], refs[count:]
    ubg_ref, refs = refs[0], refs[1:]
    if last:
        part_ref, msend_ref, dn_ref, dnsend_ref, m_ref, w_all, g_tmp = refs
    else:
        m_ref, dn_ref, w_all, g_tmp = refs
    width, half = lay.width, lay.length // 2
    chunk = lay.parts[part].stop - lay.parts[part].start
    up_bias = lay.at["up_bias"].start + lay.parts[part].start
    for y_rel in range(2):
        load_pieces(lay, lay.gathered[part], w_refs, y_rel, w_all, slice(0, 2 * chunk))
        y_side = here()[1] ^ y_rel
        up = w_all[:, :, :chunk].reshape(width, chunk)
        down = w_all[:, :, chunk:].reshape(width, chunk)
        pre = nn(a2_ref[...], up) + vec_ref[:, pl.ds(pl.multiple_of(y_side * width + up_bias, 128), chunk)]
        cdf = 0.5 * (1.0 + lax.erf(pre * 0.7071067811865476))
        slope = cdf + pre * (jnp.exp(-0.5 * pre * pre) * 0.3989422804014327)
        act = (pre * cdf).astype(BF)
        du = (nn(dm_ref[...], down) * slope).astype(BF)
        ubg_ref[:, pl.ds(pl.multiple_of(y_side * chunk, 128), chunk)] = column_sum(du.astype(F32))
        g_tmp[...] = nn(at_ref[...], du).astype(BF).reshape(g_tmp.shape)
        own, at = (grads[:n_g], slice(None)) if not last else (grads, slice(0, chunk))
        store_pieces(lay, lay.reduced[part], own, y_rel, at, g_tmp)
        g_tmp[...] = nn(dt_ref[...], act).astype(BF).reshape(g_tmp.shape)
        own, at = (grads[n_g:], slice(None)) if not last else (grads, slice(chunk, None))
        store_pieces(lay, lay.reduced[part], own, y_rel, at, g_tmp)
        m, dn = nt(act, down), nt(du, up)
        if y_rel == 0:
            m_ref[...] = m + m_in[...] if part else m
            dn_ref[...] = dn + dn_in[...] if part else dn
        else:
            m_ref[...] += m
            dn_ref[...] += dn
    if last:
        part_ref[...] = x1_ref[:half] + m_ref[:half] + vec_ref[:, lay.at["down_bias"]]
        msend_ref[...] = m_ref[half:].astype(BF)
        dnsend_ref[...] = dn_ref[...].astype(BF)


def attend_back(lay, first, count, base, q_ref, k_ref, v_ref, p_ref, dob_ref, dq_ref, dk_ref, dv_ref):
    head = lay.head
    pair = 2 * head
    scale = head**-0.5

    def step(n, carry):
        at = pl.ds(pl.multiple_of(n * pair, pair), pair)
        out = pl.ds(pl.multiple_of((n - base) * pair, pair), pair)
        keys, values = k_ref[:, at], v_ref[:, at]
        query, dob = q_ref[:, at], dob_ref[:, at]
        query_t, dob_t = query.T, dob.T
        lane = lax.broadcasted_iota(jnp.int32, query.shape, 1)
        row = lax.broadcasted_iota(jnp.int32, query_t.shape, 0)
        dqs, dks, dvs = [], [], []
        for h in range(2):
            mine = (lane < head) if h == 0 else (lane >= head)
            weights = p_ref[2 * (n - base) + h]
            soft = weights.astype(F32)
            dp = nt(jnp.where(mine, dob, jnp.zeros_like(dob)), values)
            ds = (soft * (dp - jnp.sum(soft * dp, -1, keepdims=True))).astype(BF)
            dqs.append(nn(ds, keys))
            dks.append(nn(query_t, ds))
            dvs.append(nn(dob_t, weights))
        dq_ref[:, out] = jnp.where(lane < head, dqs[0], dqs[1]) * scale
        dk_ref[:, out] = (jnp.where(row < head, dks[0], dks[1]) * scale).T
        dv_ref[:, out] = jnp.where(row < head, dvs[0], dvs[1]).T
        return carry

    lax.fori_loop(first, first + count, step, 0)


def back_kernel(
    lay, t0, t1, t2, t3, kp_ref, x1_ref, dn_ref, came_ref, vec_ref, wp_ref, ob0, ob1, oo0, oo1, q_ref, k_ref, v_ref,
    p_ref, dx_ref, dob_ref, pg_ref, sums_ref, dq_ref, dk_ref, dv_ref, dxb_ref,
):
    g_ref = vec_ref[:, lay.at["mlp_gain"]]
    band, third, half = lay.band, lay.third, lay.length // 2
    c = here()[2]
    gg, sg, pbg = 0.0, 0.0, 0.0
    for b, ref in enumerate((t0, t1, t2, t3)):
        at = slice(b * band, (b + 1) * band)
        away = slice((b ^ 2) * band, ((b ^ 2) + 1) * band)
        dn = dn_ref[at] + came_ref[away].astype(F32)
        normed, inverse = normed_rows(x1_ref[at])
        dx = ref[band : 2 * band].astype(F32) * kp_ref[at] + norm_back(dn, normed, inverse, g_ref)
        dxb = dx.astype(BF)
        dxb_ref[at] = dxb
        if b < 2:
            dx_ref[at] = dx
            gg = gg + column_sum(dn * normed)
            sg = sg + column_sum(dn)
            pbg = pbg + column_sum(dxb.astype(F32))
    low = [pl.ds(pl.multiple_of((2 * s + c) * third, third), third) for s in range(2)]
    own_w = jnp.concatenate([wp_ref[low[0]], wp_ref[low[1]]], 0)
    dxb = dxb_ref[...]
    dob_ref[...] = nt(dxb, own_w).astype(BF)
    block = lay.width // 4
    zero = jnp.concatenate([dxb[:, :block], dxb[:, 2 * block : 3 * block]], 1)
    one = jnp.concatenate([dxb[:, block : 2 * block], dxb[:, 3 * block :]], 1)
    cols = jnp.where(c == 0, zero, one)
    mine, other = both_heads(half, ob0, ob1, oo0, oo1)
    mine_g, other_g = tn(mine, cols).astype(BF), tn(other, cols).astype(BF)
    zero, one = jnp.where(c == 0, mine_g, other_g), jnp.where(c == 0, other_g, mine_g)
    p_grad = jnp.concatenate([zero[:third], one[:third], zero[third:], one[third:]], 0)
    pg_ref[...] = p_grad
    sums_ref[...] = jnp.concatenate([gg, sg, pbg], 0)
    attend_back(lay, 0, 1, 0, q_ref, k_ref, v_ref, p_ref, dob_ref, dq_ref, dk_ref, dv_ref)


def back_heads_kernel(lay, q_ref, k_ref, v_ref, p_ref, dob_ref, dq_ref, dk_ref, dv_ref):
    attend_back(lay, 1, HEADS // 4 - 1, 1, q_ref, k_ref, v_ref, p_ref, dob_ref, dq_ref, dk_ref, dv_ref)


def back_rest_kernel(
    lay, plan, n_g, t0, t1, t2, t3, q_ref, k_ref, cos_ref, sin_ref, a_ref, w_ref, table_ref, ubg0, ubg1, dbg_ref, pg_ref, sums_ref,
    dq0, dk0, dv0, dq1, dk1, dv1, *refs,
):
    keep_ref, send_ref = refs[:2]
    grads = refs[2 : 2 + n_g]
    dq_ref, g_tmp, dqkv_ref = refs[2 + n_g :]
    band, side, own, third, half, head = lay.band, lay.side, lay.own, lay.third, lay.length // 2, lay.head
    gg, sg, pbg = sums_ref[0:1], sums_ref[1:2], sums_ref[2:3]
    block = lay.width // 4
    sizes = [ref.shape[1] // 2 for ref in (ubg0, ubg1)]
    ubg = [ref[:, y_side * size : (y_side + 1) * size] for y_side in range(2) for ref, size in zip((ubg0, ubg1), sizes)]
    ubg = jnp.concatenate(ubg, 1)
    cos, sin = cos_ref[...], sin_ref[...]
    dq, dk, dv = (jnp.concatenate([a[...], b[...]], 1) for a, b in ((dq0, dq1), (dk0, dk1), (dv0, dv1)))
    dqkv_ref[:, :own] = (dq * cos + halves_of(lay, dq * sin)).astype(BF)
    dqkv_ref[:, own : 2 * own] = (dk * cos + halves_of(lay, dk * sin)).astype(BF)
    dqkv_ref[:, 2 * own :] = dv.astype(BF)
    dq_ref[...] = dq * halves_of(lay, q_ref[...].astype(F32)) + dk * halves_of(lay, k_ref[...].astype(F32))
    by_col = jnp.zeros((side, own), F32)
    by_row = jnp.zeros((side, own), F32)
    for b, flip in enumerate((0, 2, 1, 3)):
        first = ((here()[3] ^ flip) * lay.band_rows).astype(F32)
        for r in range(lay.band_rows):
            turn = dq_ref[b * band + r * side : b * band + (r + 1) * side]
            by_col = by_col + turn
            by_row = by_row + turn * (first + r)
    lane = lax.broadcasted_iota(jnp.int32, (2, own), 1)
    sign = jnp.where((lane & (head // 2)) == 0, -1.0, 1.0).astype(F32)
    place = lax.broadcasted_iota(jnp.int32, (side, own), 0).astype(F32)
    both = jnp.concatenate([column_sum(by_col * place), column_sum(by_row)], 0) * sign
    both = jnp.where(sign < 0, both + halves_of(lay, both), 0.0)
    freqs = jnp.concatenate([both[0:1], both[1:2]], 1)
    bqk = column_sum(dqkv_ref[:, : 2 * own].astype(F32))
    bv = column_sum(dqkv_ref[:, 2 * own :].astype(F32))
    grad = nt(dqkv_ref[:, : 3 * third], w_ref[0]) + nt(dqkv_ref[:, 3 * third :], w_ref[1])
    keep_ref[...] = grad[:half]
    send_ref[...] = grad[half:].astype(BF)
    g1, s1 = 0.0, 0.0
    for b, ref in enumerate((t0, t1, t2, t3)):
        part = grad[b * band : (b + 1) * band]
        normed, _ = normed_rows(ref[:band].astype(F32))
        g1 = g1 + column_sum(part * normed)
        s1 = s1 + column_sum(part)
    repack(lay, plan, table_ref, [bqk, bv, pbg, g1, s1, gg, sg, ubg, dbg_ref[...], freqs], grads)
    acts = a_ref[...]
    sides = []
    for y_side in range(2):
        grad = tn(acts, dqkv_ref[:, y_side * 3 * third : (y_side + 1) * 3 * third]).astype(BF)
        sides.append(jnp.concatenate([grad, pg_ref[:, y_side * block : (y_side + 1) * block]], 1))
    y = here()[1]
    for y_rel in range(2):
        g_tmp[...] = jnp.where((y ^ y_rel) == 0, sides[0], sides[1]).reshape(g_tmp.shape)
        store_pieces(lay, lay.first, grads, y_rel, slice(None), g_tmp)


def finish_kernel(lay, t0, t1, keep_ref, came_ref, dx_ref, vec_ref, out_ref, send_ref):
    band = lay.band
    g_ref = vec_ref[:, lay.at["attn_gain"]]
    for b, ref in enumerate((t0, t1)):
        at = slice(b * band, (b + 1) * band)
        dn = keep_ref[at] + came_ref[at].astype(F32)
        normed, inverse = normed_rows(ref[:band].astype(F32))
        result = (dx_ref[at] + norm_back(dn, normed, inverse, g_ref)).astype(BF)
        if b == 0:
            out_ref[...] = result
        else:
            send_ref[...] = result


def tail_second_kernel(lay, counts, *refs):
    up_ref, down_ref = refs[-2:]
    half = lay.half_rows
    for part, count in enumerate(counts):
        at = lay.parts[part]
        step = at.stop - at.start
        keep, *came = refs[sum(counts[:part]) : sum(counts[: part + 1])]
        if not came:
            up_ref[:, at], down_ref[:, at] = keep[:, :step].astype(F32), keep[:, step:].astype(F32)
        for rows, ref in zip((slice(0, half), slice(half, None)), came):
            up_ref[rows, at] = keep[rows, :step].astype(F32) + ref[:, :step].astype(F32)
            down_ref[rows, at] = keep[rows, step:].astype(F32) + ref[:, step:].astype(F32)


def tail_send_kernel(lay, sum_ref, out_ref):
    third, rows = lay.third, lay.rows
    out_ref[:, :third] = jnp.where(here()[2] == 0, sum_ref[:rows, 2 * third : 3 * third], sum_ref[:rows, :third])
    out_ref[:, third:] = jnp.zeros((rows, out_ref.shape[1] - third), BF)
    theirs = sum_ref[rows:, :PACKED].astype(F32)[1:2]
    out_ref[0:1, out_ref.shape[1] - PACKED :] = theirs.astype(BF)


def tail_kernel(lay, plan, sum_ref, came_ref, qkv_ref, proj_ref, *outs):
    third, rows = lay.third, lay.rows
    d0, d1, d2 = (sum_ref[:rows, k * third : (k + 1) * third] for k in range(3))
    c = here()[2]
    qkv_ref[:, :third] = jnp.where(c == 0, d0, d1).astype(F32)
    qkv_ref[:, third : 2 * third] = came_ref[:, :third].astype(F32)
    qkv_ref[:, 2 * third :] = jnp.where(c == 0, d1, d2).astype(F32)
    proj_ref[...] = sum_ref[:rows, 3 * third :].astype(F32)
    total = sum_ref[rows:, :PACKED].astype(F32)[0:1] + came_ref[0:1, came_ref.shape[1] - PACKED :].astype(F32)
    for ref, (_, _, offset, count) in zip(outs, plan):
        ref[...] = total[:, offset : offset + count]


def call(kernel, name, inputs, outs, scratch=(), limit=16, hbm=False):
    return pl.pallas_call(
        kernel,
        out_shape=[jax.ShapeDtypeStruct(shape, dtype) for shape, dtype in outs],
        in_specs=[HBM if hbm else VMEM] * len(inputs),
        out_specs=[VMEM] * len(outs),
        scratch_shapes=[s if not isinstance(s, tuple) else pltpu.VMEM(*s) for s in scratch],
        compiler_params=pltpu.CompilerParams(vmem_limit_bytes=limit * MIB),
        cost_estimate=pl.CostEstimate(flops=1000, bytes_accessed=1024, transcendentals=0),
        name=name,
    )(*inputs)


def after(value, *others):
    return lax.optimization_barrier((value, *others))[0]


class Slice:
    def __init__(self, lay):
        self.lay = lay
        self.img = lax.axis_index("img")
        self.row = lax.axis_index("row")
        self.y = self.row // 2
        self.c = self.row % 2
        self.orders = lay.first

    def swap(self, array, step):
        if step == "c":
            return lax.ppermute(array, "row", [(r, r ^ 1) for r in range(4)])
        if step == "y":
            return lax.ppermute(array, "row", [(r, r ^ 2) for r in range(4)])
        mask = sum(1 << bit for bit in self.lay.high) if step == "high" else 1 << step
        return lax.ppermute(array, "img", [(i, i ^ mask) for i in range(self.lay.img_count)])

    def gather(self, piece, order):
        held = piece[None]
        for step in order:
            held = jnp.concatenate([held, self.swap(held, step)], 0)
        return held

    def scatter(self, held, order):
        for step in reversed(order):
            half = held.shape[0] // 2
            came = self.swap(held[half:], step)
            held = (held[:half].astype(F32) + came.astype(F32)).astype(held.dtype)
        return held[0]

    def places(self, order):
        place = jnp.zeros((2, self.lay.img_count), jnp.int32)
        img = jnp.arange(self.lay.img_count, dtype=jnp.int32)[None, :] ^ self.img
        side = jnp.arange(2, dtype=jnp.int32)[:, None] ^ self.y
        for k, step in enumerate(order):
            bit = side if step == "y" else (img >> step) & 1
            place = place + (bit << k)
        return place

    def sources(self, order):
        place = self.places(order).reshape(-1)
        return jnp.zeros_like(place).at[place].set(jnp.arange(place.size, dtype=jnp.int32))

    def gather_whole(self, piece):
        lay = self.lay
        base = self.gather(piece, lay.high)
        whole = []
        for part, order in enumerate(self.orders):
            held = base[:, part * lay.half_rows : (part + 1) * lay.half_rows]
            held = self.gather(held, order[-2:]).reshape((-1,) + held.shape[1:])
            whole.append(jnp.take(held, self.places(order), axis=0))
        return jnp.concatenate(whole, 2).reshape((2,) + lay.tiles + piece.shape[1:])

    def high(self, *pieces):
        steps = self.lay.high + ["high"]
        pieces = list(pieces) * (3 if len(pieces) == 1 else 1)
        came = [None] * 3
        for k in (0, 2, 1):
            came[k] = self.swap(pieces[k], steps[k])
        return came

    def merge(self, pieces, name):
        lay = self.lay
        rows, columns = pieces[0].shape[-2:]
        count = len(pieces) * (pieces[0].shape[0] if pieces[0].ndim == 3 else 1)
        shapes = [((count, n, columns), BF) for n in (lay.half_rows, rows - lay.half_rows)]
        return call(functools.partial(merge_kernel, lay), name, pieces, shapes)

    def pairs(self, orders, place, top, bottom):
        return [self.swap(top, orders[0][place]), self.swap(bottom, orders[1][place])]

    def grad_shapes(self, columns, extra=0):
        lay = self.lay
        if lay.aligned:
            return [((lay.img_count, lay.half_rows + more, columns), BF) for more in (0, 0, extra, extra)]
        return [((2,) + lay.tiles + (columns,), BF)] + [((2 * lay.img_count, 2, columns), BF)] * (extra > 0)

    def scatter_rows(self, parts):
        lay = self.lay
        extra = []
        if not lay.aligned:
            if len(parts) > 1:
                extra = [jnp.pad(self.scatter(parts[1], self.orders[1]), ((0, EXTRA - 2), (0, 0)))]
            pieces = parts[0].reshape(2, lay.img_count, lay.rows, parts[0].shape[3])
            parts = []
            for part, order in enumerate(self.orders):
                mine = pieces[:, :, part * lay.half_rows : (part + 1) * lay.half_rows]
                mine = jnp.take(mine.reshape((-1,) + mine.shape[2:]), self.sources(order), axis=0)
                parts += [mine[: lay.img_count], mine[lay.img_count :]]
        sums = []
        for part, order in enumerate(self.orders):
            keep, send = parts[2 * part : 2 * part + 2]
            held = (keep.astype(F32) + self.swap(send, order[-1]).astype(F32)).astype(BF)
            half = lay.img_count // 2
            sums.append((held[:half].astype(F32) + self.swap(held[half:], order[-2]).astype(F32)).astype(BF))
        total = self.scatter(jnp.concatenate(sums, 1), lay.high)
        return jnp.concatenate([total] + extra, 0) if extra else total

    def fold(self, grads, came, name):
        shapes = [((g.shape[0] // 2,) + g.shape[1:], BF) for g in grads]
        return call(fold_kernel, name + "_fold", [grads[0], came[0], grads[2], came[1]], shapes)

    def rejoin(self, groups, name, n=2):
        count, rows, _ = groups[0][0].shape
        shape = (count // n, rows + groups[0][2].shape[1], sum(group[0].shape[2] for group in groups))
        arrays = [array for group in groups for array in group]
        return list(call(functools.partial(rejoin_kernel, n), name + "_rejoin", arrays, [(shape, BF)] * n))

    def halve(self, keep, came, name):
        shape = (keep.shape[0] // 2,) + keep.shape[1:]
        return call(halve_kernel, name + "_halve", [keep, came], [(shape, BF)] * 2)

    def split(self, keep, came, name):
        _, rows, columns = keep.shape
        half = self.lay.half_rows
        shapes = [((n, columns), BF) for n in (rows, half, rows - half)]
        out, top, bottom = call(split_kernel, name + "_split", [keep, came], shapes)
        return [out] + self.pairs(self.lay.second, 0, top, bottom)

    def end(self, shares, name):
        return call(end_kernel, name + "_end", shares, [(shares[0].shape[1:], BF)])[0]


NAMES = ("qkv_bias", "proj_bias", "attn_gain", "attn_shift", "mlp_gain", "mlp_shift", "up_bias", "down_bias", "freqs")


def plan_vectors(lay):
    width, third, pairs = lay.width, lay.third, lay.head // 2
    devices = lay.img_count * 4
    heads = np.arange(HEADS).reshape(2, 2, HEADS // 4)

    def by_core(count, shape):
        return [np.take(np.arange(count).reshape(shape), core, len(shape) - 2).reshape(-1) for core in range(2)]

    plain = [np.arange(width)] * 2
    up = by_core(4 * width, (2, 2, width))
    freqs = []
    for core in range(2):
        pick = np.arange(width).reshape(2, HEADS, pairs)[:, heads[:, core].reshape(-1)]
        freqs.append(np.stack([pick, pick], 2).reshape(-1))
    qkv, qk, v = (by_core(n * width, (n, 2, 2, third)) for n in (3, 2, 1))

    def lay_out(members):
        plan, tables, start, offset = [], [[], [], [], []], 0, 0
        for pick, count in members:
            count //= devices
            plan.append((start, pick[0].size, offset, count))
            for core in range(2):
                tables[2 * core].append(pick[core] // count)
                tables[2 * core + 1].append(pick[core] % count)
            start += pick[0].size
            offset += count
        return plan, jnp.asarray(np.stack([np.concatenate(t) for t in tables]).astype(np.int32))

    rest = [(plain, width)] * 5 + [(up, 4 * width), (plain, width), (freqs, width)]
    given = lay_out([(qkv, 3 * width)] + rest)
    lay.at = {name: slice(p[0], p[0] + p[1]) for name, p in zip(NAMES, given[0])}
    return given, lay_out([(qk, 2 * width), (v, width)] + rest)


def make_body(img_count):
    def body(
        tokens, keep_mask, cotangent, qkv_weight, qkv_bias, proj_weight, proj_bias, attn_gain, attn_shift,
        mlp_gain, mlp_shift, up_weight, up_bias, down_weight, down_bias, rope_freqs,
    ):
        lay = Layout(img_count, tokens, qkv_weight.shape[0])
        me = Slice(lay)
        y = me.y
        images, band, width, length = lay.images, lay.band, lay.width, lay.length
        heads = HEADS // 2
        own, third = lay.own, lay.third
        half = length // 2
        block = proj_weight.shape[1]
        hidden = up_weight.shape[1]
        vectors = (qkv_bias, proj_bias, attn_gain, attn_shift, mlp_gain, mlp_shift, up_bias, down_bias, rope_freqs)
        (plan, table), (grad_plan, grad_table) = plan_vectors(lay)

        def pick(flag, zero, one):
            return jnp.where(flag == 0, zero, one)

        def kernel(function, name, inputs, outs, scratch=(), **options):
            return call(functools.partial(function, lay), name, inputs, outs, scratch, **options)

        pack_rows = 2 * band + 16
        sizes = [part.stop - part.start for part in lay.parts]
        mine, other, third_send, first_piece, *second_pieces = kernel(
            pack_kernel, "pack",
            [tokens.reshape(images, band, width), cotangent.reshape(images, band, width), keep_mask.transpose(1, 0, 2), qkv_weight, proj_weight,
             up_weight, down_weight.T, *[v.reshape(1, -1) for v in vectors]],
            [((pack_rows, width), BF), ((pack_rows + lay.rows - lay.half_rows, width), BF), ((lay.rows, 256 + PACKED), BF),
             ((lay.rows + EXTRA, 2 * third), BF),
             ((lay.rows, 2 * sizes[0] + block), BF), ((lay.half_rows, 2 * sizes[1]), BF)],
            [((lay.band_rows, images, lay.side), jnp.int32), (qkv_weight.shape, F32), (proj_weight.shape, F32), (up_weight.shape, F32),
             (down_weight.T.shape, F32), *[((1, v.shape[0]), F32) for v in vectors], pltpu.SemaphoreType.DMA((18,))],
            limit=60, hbm=True,
        )
        third_came = me.swap(third_send, "c")
        (first_piece,) = kernel(fit_kernel, "fit", [third_came, first_piece], [((lay.rows, 3 * third + SPARE), BF)])
        mine_came = me.swap(mine, "c")
        near = me.swap(after(other, mine_came), 'y')
        bands = [mine, near, mine_came]
        if lay.aligned:
            part0, top1 = second_pieces
            near1 = me.swap(top1, lay.second[0][0])
            came = me.high(first_piece)
            bands.append(me.swap(after(near, *came), 'c'))
            part0 = part0
            top, bottom = me.merge([first_piece] + came, 'merge_first')
            came = me.pairs(lay.first, -2, top, bottom)
            high0 = [me.swap(part0, step) for step in lay.high]
            top = after(top, bands[3], near1, high0[0], high0[1])
            shapes = [((2 * held.shape[0],) + held.shape[1:], BF) for held in (top, bottom)]
            top, bottom = call(join_kernel, "join_first", [top, came[0], bottom, came[1]], shapes)
            came = me.pairs(lay.first, -1, top, bottom)
            first = [top, came[0], bottom, came[1]]
            high0.append(me.swap(after(high0[0], top), lay.high[1]))
            shape = (2, lay.rows, top1.shape[1])
            start1 = after(top1, high0[0])
            (both1,) = kernel(start_kernel, "start1", [start1, near1, other, near], [(shape, BF)])
            vec_parts = [after(first[0], first[3], high0[2], both1), first[1]]
            top0, bottom0 = me.merge([part0] + high0, "merge0")
            vec_parts[0] = after(vec_parts[0], top0, bottom0)
        else:
            bands.append(me.swap(near, "c"))
            first = [me.gather_whole(first_piece)]
            vec_parts = [me.gather(first_piece[: 2 * PACKED // SPARE, 3 * third :], me.orders[0])]
            second = [[me.gather_whole(p)] for p in (second_pieces[0], jnp.concatenate([second_pieces[1], other[pack_rows:]], 0))]
        (vec,) = call(
            functools.partial(unpack_kernel, lay, plan, len(vec_parts)), "unpack", [table, *vec_parts],
            [((1, table.shape[1]), F32)], limit=24,
        )

        n_w = len(first)
        n_g = len(me.grad_shapes(1))
        a1, q, k, v, w_qkv, cos, sin, kp, mask_bias = call(
            functools.partial(project_kernel, lay, n_w), "qkv", [*bands, *first, vec],
            [((length, width), BF), ((length, own), BF), ((length, own), BF), ((length, own), BF), ((2, width, 3 * third), BF),
             ((length, own), F32), ((length, own), F32), ((length, 1), F32), ((1, length), F32)],
            [((2,) + lay.tiles + (3 * third,), BF)], limit=16,
        )
        def attend(first, count, q):
            return call(
                functools.partial(attend_kernel, lay, first, count), "attend%d" % first, [q, k, v, mask_bias],
                [((length, count * 2 * lay.head), BF), ((2 * count, length, length), BF)], limit=8,
            )

        ob0, p0 = attend(0, 1, q)
        oo0 = me.swap(ob0, "c")
        if lay.aligned:
            near0 = me.pairs(lay.first, -2, top0, bottom0)
            high1 = [both1] + [me.swap(both1, step) for step in lay.high]
            shapes = [((2 * held.shape[0],) + held.shape[1:], BF) for held in (top0, bottom0)]
            top0 = after(top0, ob0, high1[1])
            top0, bottom0 = call(join_kernel, "join0", [top0, near0[0], bottom0, near0[1]], shapes)
            last0 = me.pairs(lay.first, -1, top0, bottom0)
            second = [[top0, last0[0], bottom0, last0[1]]]
            ob1, p1 = attend(1, HEADS // 4 - 1, after(q, top0, bottom0))
            high1.append(me.swap(after(high1[1], ob1), lay.high[1]))
            gate = [ob1]
            top1, bottom1 = me.merge(high1, "merge1")
            gate += [top1, bottom1]
        else:
            ob1, p1 = attend(1, HEADS // 4 - 1, q)
            gate = [ob1]
        oo1 = me.swap(ob1, 'c')
        (p_cols,) = call(
            functools.partial(proj_kernel, lay, len(second[0])), "proj", [after(second[0][0], *gate)] + second[0][1:], [((width, 2 * block), BF)],
            [((2,) + lay.tiles + (block,), BF)],
        )
        p_other = me.swap(p_cols, "c")
        x1, a2, a2_t, dm, dm_t, d_down_bias, w_proj = call(
            functools.partial(middle_kernel, lay), "middle", [*bands, ob0, ob1, oo0, oo1, p_cols, p_other, vec, kp],
            [((length, width), F32), ((length, width), BF), ((width, length), BF), ((length, width), BF), ((width, length), BF),
             ((1, width), F32), ((width, width), BF)], limit=10,
        )
        if lay.aligned:
            last1 = me.pairs(lay.second, -1, top1, bottom1)
            second.append([top1, last1[0], bottom1, last1[1]])
        sums, second_grads, d_up_bias = [], [], []
        for part, at in enumerate(lay.parts):
            step = at.stop - at.start
            shapes = (me.grad_shapes(2 * step) if part else me.grad_shapes(step) * 2) + [((1, 2 * step), F32)]
            scratch = [(lay.tiles + (2 * step,), BF), (lay.tiles + (step,), BF)]
            if part == len(PARTS) - 1:
                shapes += [((half, width), F32), ((half, width), BF), ((length, width), F32), ((length, width), BF)]
                scratch = [((length, width), F32)] + scratch
            else:
                shapes += [((length, width), F32)] * 2
            outs = call(
                functools.partial(mlp_kernel, lay, part, len(second[part]), n_g), "mlp%d" % part,
                [x1, a2, a2_t, dm, dm_t, vec, *second[part], *sums], shapes, scratch, limit=18,
            )
            count = n_g if part else 2 * n_g
            second_grads.append(outs[:count])
            d_up_bias.append(outs[count])
            sums = outs[count + 1 :]
        part, m_send, dn, dn_send = sums
        if lay.aligned:
            g = second_grads[0]
            came0 = me.pairs(lay.second, -1, g[1], g[3])
            dn_send = after(dn_send, *came0)
            came0 += me.pairs(lay.second, -1, g[5], g[7])
            dn_send = dn_send
        dn_came = me.swap(dn_send, "c")
        m_came = me.swap(m_send, "c")
        out_half = (kp[:half] * (part + m_came.astype(F32))).astype(BF)
        def to_images(keep, send):
            came = me.swap(send, "y")
            return pick(y, jnp.stack([keep, came]), jnp.stack([came, keep])).reshape(tokens.shape)

        if not lay.aligned:
            layer_out = to_images(out_half[:band], out_half[band:])
        pair = 2 * lay.head
        dx_half, dob, p_grad, norm_sums, dq0, dk0, dv0 = call(
            functools.partial(back_kernel, lay), "back",
            [*bands, kp, x1, dn, dn_came, vec, w_proj, ob0, ob1, oo0, oo1, q, k, v, p0],
            [((half, width), F32), ((length, own), BF), ((width, 2 * block), BF), ((3, width), F32), ((length, pair), F32),
             ((length, pair), F32), ((length, pair), F32)],
            [((length, width), BF)], limit=20,
        )
        if lay.aligned:
            g = second_grads[1]
            came1 = [after(send, dn_came) for send in (g[1], g[3])]
            came1 = me.pairs(lay.first, -1, *came1)
        else:
            g = [jnp.concatenate(second_grads[0], 3)], second_grads[1]
            d_second = [[me.scatter_rows(held)] for held in g]
        if lay.aligned:
            g = second_grads[0]
            came0[0] = after(came0[0], dob)
            keep0, send0 = me.rejoin([[g[k], came0[k // 2], g[k + 2], came0[k // 2 + 1]] for k in (0, 4)], "part0")
            dob = after(dob, keep0, send0)
            came0 = me.swap(send0, lay.high[1])
        dq1, dk1, dv1 = call(
            functools.partial(back_heads_kernel, lay), "back_heads", [q, k, v, p1, dob], [((length, own - pair), F32)] * 3
        )
        if lay.aligned:
            came1[0] = after(came1[0], dq1)
            folded1 = me.fold(second_grads[1], came1, "part1")
            came1 = me.pairs(lay.first, -2, folded1[1], folded1[3])
            dq1 = after(dq1, *folded1)
        if lay.aligned:
            keep0, send0 = me.halve(keep0, after(came0, dq1), "part0")
            dq1 = after(dq1, send0)
            came0, z0_0 = me.swap(send0, lay.high[0]), send0
        grad_shapes = me.grad_shapes(3 * third + block, EXTRA)
        dn1_keep, dn1_send, *first_grads = call(
            functools.partial(back_rest_kernel, lay, grad_plan, len(grad_shapes)), "back_rest",
            [*bands, q, k, cos, sin, a1, w_qkv, grad_table, *d_up_bias, d_down_bias, p_grad, norm_sums, dq0, dk0, dv0, dq1, dk1, dv1],
            [((half, width), F32), ((half, width), BF), *grad_shapes],
            [((length, own), F32), (lay.tiles + (3 * third + block,), BF), ((length, 3 * own), BF)], limit=24,
        )
        if lay.aligned:
            g = first_grads
            sends = [after(send, *came1, folded1[0]) for send in (g[1], g[3])]
            came = me.pairs(lay.first, -1, *sends)
            keep1, send1 = me.rejoin([[folded1[0], came1[0], folded1[2], came1[1]]], "part1")
            came1 = me.swap(send1, lay.high[1])
            folded = me.fold(g, came, "first")
            sends = [after(send, came1) for send in (folded[1], folded[3])]
            came = me.pairs(lay.first, -2, *sends)
            layer_out = to_images(out_half[:band], after(out_half[band:], *came))
            p2_came = came
            d_second = [me.split(keep0, came0, "part0")]
            keep1, send1 = me.halve(keep1, came1, "part1")
            came1 = me.swap(send1, lay.high[0])
            shares = me.rejoin([[folded[0], came[0], folded[2], came[1]]], "first", 4)
            d_second.append([me.end([keep1, came1], "part1")])
            d_up, d_down = call(
                functools.partial(tail_second_kernel, lay, [len(d) for d in d_second]), "tail_second",
                [held for d in d_second for held in d], [((lay.rows, n), F32) for n in (hidden, hidden)]
            )
            shares[1] = after(shares[1], d_second[0][0], d_second[1][0])
            d_first = me.end([after(shares[0], *d_second[0], d_up)] + me.high(*shares[1:]), 'first')
        else:
            d_up, d_down = call(
                functools.partial(tail_second_kernel, lay, [len(d) for d in d_second]), "tail_second",
                [held for d in d_second for held in d], [((lay.rows, n), F32) for n in (hidden, hidden)]
            )
            d_first = me.scatter_rows(first_grads)
        dn1_came = me.swap(dn1_send, "c")
        tg_keep, tg_send = call(
            functools.partial(finish_kernel, lay), "finish", [bands[0], bands[1], dn1_keep, dn1_came, dx_half, vec],
            [((band, width), BF), ((band, width), BF)],
        )

        if lay.aligned:
            tg_send = after(tg_send, *p2_came)
        tokens_grad = to_images(tg_keep, tg_send)

        d_down = d_down.T
        (tail_send,) = kernel(tail_send_kernel, "tail_send", [d_first], [((lay.rows, 256 + PACKED), BF)])
        tail_came = me.swap(tail_send, "c")
        d_qkv, d_proj, *r = call(
            functools.partial(tail_kernel, lay, grad_plan), "tail", [d_first, tail_came],
            [((lay.rows, 3 * third), F32), ((lay.rows, block), F32), *[((1, count), F32) for _, _, _, count in grad_plan]],
        )
        r = [v.reshape(-1) for v in r]
        return (
            layer_out, tokens_grad, d_qkv, r[0], r[1], d_proj, r[2], r[3], r[4], r[5], r[6], d_up, r[7], d_down, r[8], r[9],
        )

    return body


def solution(mesh):
    split = P(("img", "row"))
    both = P("img", "row")
    field = P("img", "row", None, None)
    return jax.shard_map(
        make_body(mesh.shape["img"]),
        mesh=mesh,
        in_specs=(
            field, P("img", "row", None), field, both, split, both, split, split, split, split, split, both, split,
            P("row", "img"), split, split,
        ),
        out_specs=(
            field, field, both, split, split, both, split, split, split, split, split, both, split, P("row", "img"),
            split, split,
        ),
        check_vma=False,
    )
```

```python
import functools

import jax
import jax.numpy as jnp
import numpy as np
from jax import lax
from jax.experimental import pallas as pl
from jax.experimental.pallas import tpu as pltpu
from jax.sharding import PartitionSpec as P

HEADS = 12
PARTS = (3, 3)
NORM_EPSILON = 1e-06
MASKED_SCORE = -1e30
BF = jnp.bfloat16
F32 = jnp.float32
MIB = 2**20
VMEM = pl.BlockSpec(memory_space=pltpu.VMEM)
HBM = pl.BlockSpec(memory_space=pltpu.MemorySpace.HBM)
PACKED = 384
SPARE = 64
EXTRA = 16


def dot(left, right, dims):
    return lax.dot_general(left, right, (dims, ((), ())), preferred_element_type=F32)


def nn(left, right):
    return dot(left, right, ((1,), (0,)))


def nt(left, right):
    return dot(left, right, ((1,), (1,)))


def tn(left, right):
    return dot(left, right, ((0,), (0,)))


def normed_rows(values):
    center = values - jnp.mean(values, -1, keepdims=True)
    inverse = lax.rsqrt(jnp.mean(center * center, -1, keepdims=True) + NORM_EPSILON)
    return center * inverse, inverse


def norm_back(grad, normed, inverse, gain):
    scaled = grad * gain
    centred = scaled - jnp.mean(scaled, -1, keepdims=True)
    return inverse * (centred - normed * jnp.mean(scaled * normed, -1, keepdims=True))


def column_sum(value):
    return jnp.sum(value, 0, keepdims=True)


def here():
    row = lax.axis_index("row")
    return lax.axis_index("img"), row >> 1, row & 1, row


class Layout:
    def __init__(self, img_count, tokens, rows):
        self.img_count = img_count
        self.bits = img_count.bit_length() - 1
        self.rows = rows
        self.half_rows = rows // 2
        self.aligned = rows % 32 == 0 and img_count == 8
        self.images, self.band_rows, self.side, self.width = tokens.shape
        self.band = self.band_rows * self.side
        self.length = 4 * self.band
        self.head = self.width // HEADS
        self.own = self.width // 2
        self.third = self.own // 2
        self.high = list(range(self.bits - 1, 0, -1))
        self.first = (self.high + [0, "y"], self.high + ["y", 0])
        self.second = ([0] + self.high + ["y"], ["y"] + self.high + [0])
        sizes = [self.width * sixths // 6 for sixths in PARTS]
        self.parts = [slice(sum(sizes[:n]), sum(sizes[: n + 1])) for n in range(len(sizes))]
        self.gathered = (self.first, self.second)
        self.reduced = (self.second, self.first)
        self.tiles = (img_count, rows) if self.aligned else (1, self.width)

    def slots(self, orders, img_rel, y_rel):
        found = []
        for order in orders:
            bits = [y_rel if step == "y" else (img_rel >> step) & 1 for step in order]
            found.append((sum(bit << k for k, bit in enumerate(bits[:-1])), bits[-1]))
        return found


def load_pieces(lay, orders, refs, y_rel, target, columns=slice(None)):
    if not lay.aligned:
        target[...] = refs[0][here()[1] ^ y_rel, :, :, columns]
        return
    half = lay.half_rows
    count = len(refs) // 2
    for img_rel in range(lay.img_count):
        for part, (slot, last) in enumerate(lay.slots(orders, img_rel, y_rel)):
            which, slot = divmod((slot + last * lay.img_count) * count, 2 * lay.img_count)
            ref, slot = refs[part * count + which], slot // count
            target[img_rel ^ here()[0], part * half : (part + 1) * half] = ref[slot, :half, columns]


def store_pieces(lay, orders, refs, y_rel, columns, source):
    if not lay.aligned:
        refs[0][here()[1] ^ y_rel, :, :, columns] = source[...]
        return
    half = lay.half_rows
    for img_rel in range(lay.img_count):
        for part, (slot, last) in enumerate(lay.slots(orders, img_rel, y_rel)):
            refs[2 * part + last][slot, :half, columns] = source[img_rel ^ here()[0], part * half : (part + 1) * half]


def halves_of(lay, value):
    pairs = lay.head // 2
    lane = lax.broadcasted_iota(jnp.int32, value.shape, 1)
    width = value.shape[1]
    first = (lane & pairs) == 0
    return jnp.where(first, pltpu.roll(value, width - pairs, 1), pltpu.roll(value, pairs, 1))


def pack_kernel(lay, *refs):
    tok, cot, mask, qkv, proj, up, down, *vectors = refs[:16]
    mine_ref, other_ref, third_ref, first_ref = refs[16:20]
    second, refs = [*refs[20:22], other_ref.at[2 * lay.band + 16 :]], refs[22:]
    mask_in, qkv_in, proj_in, up_in, down_in, *vectors_in = refs[:14]
    sems = refs[14]
    y = here()[1]
    band, third, width, rows = lay.band, lay.third, lay.width, lay.rows
    pairs = [(qkv, qkv_in), (proj, proj_in), *zip(vectors, vectors_in), (up, up_in), (down, down_in), (mask, mask_in)]
    for ref, which in ((other_ref, 1 - y), (mine_ref, y)):
        pairs += [(tok.at[which], ref.at[:band]), (cot.at[which], ref.at[band : 2 * band])]
    copies = [pltpu.make_async_copy(source, target, sems.at[n]) for n, (source, target) in enumerate(pairs)]
    for copy in copies:
        copy.start()
    for copy in copies[:11]:
        copy.wait()
    packed = jnp.concatenate([v[...] for v in vectors_in], 1)
    packed = jnp.concatenate([packed, jnp.zeros((1, PACKED - packed.shape[1]), F32)], 1).astype(BF)
    third_ref[:, :third] = qkv_in[:, third : 2 * third].astype(BF)
    third_ref[:, third:] = jnp.zeros((rows, third_ref.shape[1] - third), BF)
    blank = jnp.zeros((EXTRA - 1, PACKED), F32)
    packed = jnp.concatenate([packed.astype(F32), blank], 0).astype(BF)
    tall = min(rows, EXTRA)
    third_ref[:tall, third_ref.shape[1] - PACKED :] = packed[:tall]
    first_ref[:rows, :third] = qkv_in[:, :third].astype(BF)
    first_ref[:rows, third : 2 * third] = qkv_in[:, 2 * third :].astype(BF)
    first_ref[rows:, :PACKED] = packed
    for copy in copies[11:]:
        copy.wait()
    for ref, part, first_row in zip(second, (0, 1, 1), (0, 0, lay.half_rows)):
        at = lay.parts[part]
        step = at.stop - at.start
        side = slice(first_row, first_row + ref.shape[0])
        ref[:, :step] = up_in[side, at].astype(BF)
        ref[:, step : 2 * step] = down_in[side, at].astype(BF)
        if part == 0:
            ref[:, 2 * step :] = proj_in[side].astype(BF)
    for ref, which in ((mine_ref, y), (other_ref, 1 - y)):
        keep = [jnp.where(which == 0, mask_in[r, 0:1], mask_in[r, 1:2]).astype(F32) for r in range(lay.band_rows)]
        flat = jnp.concatenate(keep, 1)
        flat = jnp.concatenate([flat, jnp.zeros((1, width - band), F32)], 1)
        ref[2 * band : 2 * band + 16] = jnp.concatenate([flat, jnp.zeros((15, width), F32)], 0).astype(BF)


def fit_kernel(lay, came_ref, first_ref, out_ref):
    third, rows = lay.third, lay.rows
    c = here()[2]
    t0, t2, came = first_ref[:rows, :third], first_ref[:rows, third : 2 * third], came_ref[:, :third]
    out_ref[:, : 3 * third] = jnp.where(c == 0, jnp.concatenate([t0, t2, came], 1), jnp.concatenate([came, t0, t2], 1))
    tall = min(rows, EXTRA)
    lines = [first_ref[rows:, :PACKED].astype(F32)[0:1], came_ref[:tall, came_ref.shape[1] - PACKED :].astype(F32)[0:1]]
    lines = [line[:, k : k + SPARE] for line in lines for k in range(0, PACKED, SPARE)]
    if rows > len(lines):
        lines.append(jnp.zeros((rows - len(lines), SPARE), F32))
    out_ref[:, 3 * third :] = jnp.concatenate(lines, 0).astype(BF)


def merge_kernel(lay, *refs):
    pieces, (top_ref, bottom_ref) = refs[:-2], refs[-2:]
    half = lay.half_rows
    for k, ref in enumerate(pieces):
        if len(ref.shape) == 2:
            top_ref[k] = ref[:half]
            bottom_ref[k] = ref[half:]
        else:
            count = ref.shape[0]
            top_ref[k * count : (k + 1) * count] = ref[:, :half]
            bottom_ref[k * count : (k + 1) * count] = ref[:, half:]


def start_kernel(lay, top, top_came, bottom, bottom_came, out_ref):
    half = lay.half_rows
    out_ref[0, :half], out_ref[1, :half] = top[...], top_came[...]
    first = 2 * lay.band + 16
    out_ref[0, half:], out_ref[1, half:] = bottom[first:], bottom_came[first:]


def join_kernel(*refs):
    for part in range(2):
        own, came = refs[2 * part : 2 * part + 2]
        refs[4 + part][: own.shape[0]] = own[...]
        refs[4 + part][own.shape[0] :] = came[...]


def fold_kernel(*refs):
    for part in range(2):
        keep, came = refs[2 * part : 2 * part + 2]
        count = keep.shape[0] // 2
        for half in range(2):
            at = slice(half * count, (half + 1) * count)
            refs[4 + 2 * part + half][...] = (keep[at].astype(F32) + came[at].astype(F32)).astype(BF)


def rejoin_kernel(n, *refs):
    outs = refs[len(refs) - n :]
    top = refs[0].shape[1]
    count = refs[0].shape[0] // n
    column = 0
    for k in range(0, len(refs) - n, 4):
        columns = slice(column, column + refs[k].shape[2])
        column = columns.stop
        for part in range(2):
            keep, came = refs[k + 2 * part : k + 2 * part + 2]
            rows = slice(0, top) if part == 0 else slice(top, None)
            for share, out in enumerate(outs):
                at = slice(share * count, (share + 1) * count)
                out[:, rows, columns] = (keep[at].astype(F32) + came[at].astype(F32)).astype(BF)


def end_kernel(*refs):
    refs[-1][...] = sum(ref[0].astype(F32) for ref in refs[:-1]).astype(BF)


def halve_kernel(keep_ref, came_ref, *outs):
    count = keep_ref.shape[0] // len(outs)
    for half, ref in enumerate(outs):
        at = slice(half * count, (half + 1) * count)
        total = (keep_ref[at].astype(F32) + came_ref[at].astype(F32)).astype(BF)
        ref[...] = total.reshape(ref.shape)


def split_kernel(keep_ref, came_ref, out_ref, top_ref, bottom_ref):
    half = top_ref.shape[0]
    out_ref[...] = (keep_ref[0].astype(F32) + came_ref[0].astype(F32)).astype(BF)
    top_ref[...] = (keep_ref[1, :half].astype(F32) + came_ref[1, :half].astype(F32)).astype(BF)
    bottom_ref[...] = (keep_ref[1, half:].astype(F32) + came_ref[1, half:].astype(F32)).astype(BF)


def owner_mask(lay, order, c_rel, table_row):
    place = lax.broadcasted_iota(jnp.int32, (2 * lay.img_count, 1), 0)
    img_rel = jnp.zeros_like(place)
    row = here()[3] ^ c_rel
    for k, step in enumerate(order):
        bit = (place >> k) & 1
        if step == "y":
            row = row ^ (bit * 2)
        else:
            img_rel = img_rel | (bit << step)
    return ((img_rel ^ here()[0]) * 4 + row) == table_row


def owners(table_ref, at, c):
    owner = jnp.where(c == 0, table_ref[0:1, at], table_ref[2:3, at])
    entry = jnp.where(c == 0, table_ref[1:2, at], table_ref[3:4, at])
    return owner, entry


def unpack_kernel(lay, plan, n_v, table_ref, *refs):
    v_refs, out_ref = refs[:n_v], refs[n_v]
    lines = PACKED // SPARE
    if lay.aligned:
        blocks = [ref[k, :16, ref.shape[2] - SPARE :].astype(F32) for ref in v_refs for k in range(ref.shape[0])]
        blocks = [jnp.concatenate([block[n : n + 1] for block in blocks], 0) for n in range(2 * lines)]
    else:
        blocks = [v_refs[0][:, n].astype(F32) for n in range(2 * lines)]
    gathered = [jnp.concatenate(blocks[c_rel * lines : (c_rel + 1) * lines], 1).astype(BF) for c_rel in range(2)]
    for start, size, offset, count in plan:
        at = slice(start, start + size)
        owner, entry = owners(table_ref, at, here()[2])
        spread = (lax.broadcasted_iota(jnp.int32, (count, size), 0) == entry).astype(F32).astype(BF)
        total = 0.0
        for c_rel in range(2):
            rows = nn(gathered[c_rel][:, offset : offset + count], spread)
            total = total + column_sum(jnp.where(owner_mask(lay, lay.first[0], c_rel, owner), rows, 0.0))
        out_ref[:, at] = total


def repack(lay, plan, table_ref, grads, refs):
    sides = []
    for c_rel in range(2):
        parts = []
        for grad, (start, size, offset, count) in zip(grads, plan):
            owner, entry = owners(table_ref, slice(start, start + size), here()[2])
            spread = (lax.broadcasted_iota(jnp.int32, (count, size), 0) == entry).astype(F32).astype(BF)
            rows = jnp.where(owner_mask(lay, lay.first[1], c_rel, owner), grad, 0.0).astype(BF)
            parts.append(nt(rows, spread))
        used = sum(p.shape[1] for p in parts)
        sides.append(jnp.concatenate(parts + [jnp.zeros((2 * lay.img_count, PACKED - used), F32)], 1))
    if not lay.aligned:
        refs[1][...] = jnp.zeros(refs[1].shape, BF)
        for c_rel in range(2):
            refs[1][:, c_rel, :PACKED] = sides[c_rel].astype(BF)
        return
    half, count = lay.half_rows, lay.img_count
    for j in range(2 * count):
        ref = refs[2 + j // count]
        block = jnp.concatenate([side[j : j + 1] for side in sides] + [jnp.zeros((EXTRA - 2, PACKED), F32)], 0).astype(BF)
        ref[j % count, half:] = jnp.zeros((EXTRA, ref.shape[2]), BF)
        ref[j % count, half:, :PACKED] = block


def project_kernel(lay, n_w, t0, t1, t2, t3, *refs):
    w_refs = refs[:n_w]
    vec_ref, a_ref, q_ref, k_ref, v_ref, w_out, cos_ref, sin_ref, kp_ref, bias_ref, w_all = refs[n_w:]
    band, side, own, third = lay.band, lay.side, lay.own, lay.third
    g_ref, s_ref, b_ref = (vec_ref[:, lay.at[n]] for n in ("attn_gain", "attn_shift", "qkv_bias"))
    f_ref = vec_ref[:, lay.at["freqs"]]
    keeps = []
    for b, ref in enumerate((t0, t1, t2, t3)):
        at = slice(b * band, (b + 1) * band)
        normed, _ = normed_rows(ref[:band].astype(F32))
        a_ref[at] = (normed * g_ref + s_ref).astype(BF)
        keep = ref[2 * band : 2 * band + 16, :band].astype(F32)
        kp_ref[at] = jnp.transpose(keep)[:, 0:1]
        keeps.append(keep[0:1])
    bias_ref[...] = jnp.where(jnp.concatenate(keeps, 1) > 0, 0.0, MASKED_SCORE)
    lane = lax.broadcasted_iota(jnp.int32, (side, own), 1)
    sign = jnp.where((lane & (lay.head // 2)) == 0, -1.0, 1.0).astype(F32)
    col = lax.broadcasted_iota(jnp.int32, (side, own), 0).astype(F32) * f_ref[:, :own]
    col_cos, col_sin = jnp.cos(col), jnp.sin(col)
    row_index = here()[3]
    for b, flip in enumerate((0, 2, 1, 3)):
        first = ((row_index ^ flip) * lay.band_rows).astype(F32)
        rows = (lax.broadcasted_iota(jnp.int32, (8, own), 0).astype(F32) + first) * f_ref[:, own:]
        row_cos, row_sin = jnp.cos(rows), jnp.sin(rows)
        for r in range(lay.band_rows):
            at = slice(b * band + r * side, b * band + (r + 1) * side)
            rc, rs = row_cos[r : r + 1], row_sin[r : r + 1]
            cos_ref[at] = col_cos * rc - col_sin * rs
            sin_ref[at] = (col_sin * rc + col_cos * rs) * sign
    for y_rel in range(2):
        y_side = here()[1] ^ y_rel
        load_pieces(lay, lay.first, w_refs, y_rel, w_all.at[y_side], slice(0, 3 * third))
    acts = a_ref[...]
    w0, w1 = w_all[0].reshape(lay.width, -1), w_all[1].reshape(lay.width, -1)
    w_out[0], w_out[1] = w0, w1
    left = nn(acts, w0) + b_ref[:, : 3 * third]
    right = nn(acts, w1) + b_ref[:, 3 * third :]
    query, key = left[:, :own], jnp.concatenate([left[:, own:], right[:, :third]], 1)
    cos, sin = cos_ref[...], sin_ref[...]
    q_ref[...] = (query * cos + halves_of(lay, query) * sin).astype(BF)
    k_ref[...] = (key * cos + halves_of(lay, key) * sin).astype(BF)
    v_ref[...] = right[:, third:].astype(BF)


def proj_kernel(lay, n_w, *refs):
    out_ref, w_all = refs[n_w:]
    block = lay.width // 4
    columns = slice(refs[0].shape[-1] - block, None)
    for y_rel in range(2):
        y_side = here()[1] ^ y_rel
        load_pieces(lay, lay.gathered[0], refs[:n_w], y_rel, w_all.at[y_side], columns)
    for y_side in range(2):
        out_ref[:, y_side * block : (y_side + 1) * block] = w_all[y_side].reshape(lay.width, block)


def attend_kernel(lay, first, count, q_ref, k_ref, v_ref, bias_ref, o_ref, p_ref):
    head = lay.head
    pair = 2 * head
    scale = head**-0.5

    def step(n, carry):
        at = pl.ds(pl.multiple_of(n * pair, pair), pair)
        out = pl.ds(pl.multiple_of((n - first) * pair, pair), pair)
        keys, values = k_ref[:, at], v_ref[:, at]
        query = q_ref[:, at] * jnp.asarray(scale, BF)
        lane = lax.broadcasted_iota(jnp.int32, query.shape, 1)
        outs = []
        for h in range(2):
            mine = (lane < head) if h == 0 else (lane >= head)
            score = nt(jnp.where(mine, query, jnp.zeros_like(query)), keys) + bias_ref[...]
            power = jnp.exp(score - jnp.max(score, -1, keepdims=True))
            weights = (power * (1.0 / jnp.sum(power, -1, keepdims=True))).astype(BF)
            p_ref[2 * (n - first) + h] = weights
            outs.append(nn(weights, values))
        o_ref[:, out] = jnp.where(lane < head, outs[0], outs[1]).astype(BF)
        return carry

    lax.fori_loop(first, first + count, step, 0)


def both_heads(half, ob0, ob1, oo0, oo1):
    other = jnp.concatenate([oo0[...], oo1[...]], 1)
    return jnp.concatenate([ob0[...], ob1[...]], 1), jnp.concatenate([other[half:], other[:half]], 0)


def middle_kernel(lay, t0, t1, t2, t3, ob0, ob1, oo0, oo1, p_ref, po_ref, vec_ref, kp_ref, x1_ref, a2_ref, at_ref, dm_ref, dt_ref, dbg_ref, wp_ref):
    band, third, half = lay.band, lay.third, lay.length // 2
    c = here()[2]
    block = lay.width // 4
    pb_ref, g_ref, s_ref = (vec_ref[:, lay.at[n]] for n in ("proj_bias", "mlp_gain", "mlp_shift"))
    for y_side in range(2):
        mine, other = (ref[:, y_side * block : (y_side + 1) * block] for ref in (p_ref, po_ref))
        wp_ref[:, 2 * y_side * block : 2 * (y_side + 1) * block] = jnp.where(
            c == 0, jnp.concatenate([mine, other], 1), jnp.concatenate([other, mine], 1)
        )
    low = [pl.ds(pl.multiple_of((2 * s + c) * third, third), third) for s in range(2)]
    high = [pl.ds(pl.multiple_of((2 * s + 1 - c) * third, third), third) for s in range(2)]
    own_w = jnp.concatenate([wp_ref[low[0]], wp_ref[low[1]]], 0)
    other_w = jnp.concatenate([wp_ref[high[0]], wp_ref[high[1]]], 0)
    mine, other = both_heads(half, ob0, ob1, oo0, oo1)
    x1_ref[...] = nn(mine, own_w) + nn(other, other_w) + pb_ref
    for b, ref in enumerate((t0, t1, t2, t3)):
        at = slice(b * band, (b + 1) * band)
        x1 = x1_ref[at] + ref[:band].astype(F32)
        x1_ref[at] = x1
        normed, _ = normed_rows(x1)
        a2_ref[at] = (normed * g_ref + s_ref).astype(BF)
        dm_ref[at] = (ref[band : 2 * band].astype(F32) * kp_ref[at]).astype(BF)
    at_ref[...] = a2_ref[...].T
    dt_ref[...] = dm_ref[...].T
    dbg_ref[...] = column_sum(dm_ref[:half].astype(F32))


def mlp_kernel(lay, part, n_w, n_g, x1_ref, a2_ref, at_ref, dm_ref, dt_ref, vec_ref, *refs):
    w_refs, refs = refs[:n_w], refs[n_w:]
    last = part == len(PARTS) - 1
    if part:
        (m_in, dn_in), refs = refs[:2], refs[2:]
    count = n_g if last else 2 * n_g
    grads, refs = refs[:count], refs[count:]
    ubg_ref, refs = refs[0], refs[1:]
    if last:
        part_ref, msend_ref, dn_ref, dnsend_ref, m_ref, w_all, g_tmp = refs
    else:
        m_ref, dn_ref, w_all, g_tmp = refs
    width, half = lay.width, lay.length // 2
    chunk = lay.parts[part].stop - lay.parts[part].start
    up_bias = lay.at["up_bias"].start + lay.parts[part].start
    for y_rel in range(2):
        load_pieces(lay, lay.gathered[part], w_refs, y_rel, w_all, slice(0, 2 * chunk))
        y_side = here()[1] ^ y_rel
        up = w_all[:, :, :chunk].reshape(width, chunk)
        down = w_all[:, :, chunk:].reshape(width, chunk)
        pre = nn(a2_ref[...], up) + vec_ref[:, pl.ds(pl.multiple_of(y_side * width + up_bias, 128), chunk)]
        cdf = 0.5 * (1.0 + lax.erf(pre * 0.7071067811865476))
        slope = cdf + pre * (jnp.exp(-0.5 * pre * pre) * 0.3989422804014327)
        act = (pre * cdf).astype(BF)
        du = (nn(dm_ref[...], down) * slope).astype(BF)
        ubg_ref[:, pl.ds(pl.multiple_of(y_side * chunk, 128), chunk)] = column_sum(du.astype(F32))
        g_tmp[...] = nn(at_ref[...], du).astype(BF).reshape(g_tmp.shape)
        own, at = (grads[:n_g], slice(None)) if not last else (grads, slice(0, chunk))
        store_pieces(lay, lay.reduced[part], own, y_rel, at, g_tmp)
        g_tmp[...] = nn(dt_ref[...], act).astype(BF).reshape(g_tmp.shape)
        own, at = (grads[n_g:], slice(None)) if not last else (grads, slice(chunk, None))
        store_pieces(lay, lay.reduced[part], own, y_rel, at, g_tmp)
        m, dn = nt(act, down), nt(du, up)
        if y_rel == 0:
            m_ref[...] = m + m_in[...] if part else m
            dn_ref[...] = dn + dn_in[...] if part else dn
        else:
            m_ref[...] += m
            dn_ref[...] += dn
    if last:
        part_ref[...] = x1_ref[:half] + m_ref[:half] + vec_ref[:, lay.at["down_bias"]]
        msend_ref[...] = m_ref[half:].astype(BF)
        dnsend_ref[...] = dn_ref[...].astype(BF)


def attend_back(lay, first, count, base, q_ref, k_ref, v_ref, p_ref, dob_ref, dq_ref, dk_ref, dv_ref):
    head = lay.head
    pair = 2 * head
    scale = head**-0.5

    def step(n, carry):
        at = pl.ds(pl.multiple_of(n * pair, pair), pair)
        out = pl.ds(pl.multiple_of((n - base) * pair, pair), pair)
        keys, values = k_ref[:, at], v_ref[:, at]
        query, dob = q_ref[:, at], dob_ref[:, at]
        query_t, dob_t = query.T, dob.T
        lane = lax.broadcasted_iota(jnp.int32, query.shape, 1)
        row = lax.broadcasted_iota(jnp.int32, query_t.shape, 0)
        dqs, dks, dvs = [], [], []
        for h in range(2):
            mine = (lane < head) if h == 0 else (lane >= head)
            weights = p_ref[2 * (n - base) + h]
            soft = weights.astype(F32)
            dp = nt(jnp.where(mine, dob, jnp.zeros_like(dob)), values)
            ds = (soft * (dp - jnp.sum(soft * dp, -1, keepdims=True))).astype(BF)
            dqs.append(nn(ds, keys))
            dks.append(nn(query_t, ds))
            dvs.append(nn(dob_t, weights))
        dq_ref[:, out] = jnp.where(lane < head, dqs[0], dqs[1]) * scale
        dk_ref[:, out] = (jnp.where(row < head, dks[0], dks[1]) * scale).T
        dv_ref[:, out] = jnp.where(row < head, dvs[0], dvs[1]).T
        return carry

    lax.fori_loop(first, first + count, step, 0)


def back_kernel(
    lay, t0, t1, t2, t3, kp_ref, x1_ref, dn_ref, came_ref, vec_ref, wp_ref, ob0, ob1, oo0, oo1, q_ref, k_ref, v_ref,
    p_ref, dx_ref, dob_ref, pg_ref, sums_ref, dq_ref, dk_ref, dv_ref, dxb_ref,
):
    g_ref = vec_ref[:, lay.at["mlp_gain"]]
    band, third, half = lay.band, lay.third, lay.length // 2
    c = here()[2]
    gg, sg, pbg = 0.0, 0.0, 0.0
    for b, ref in enumerate((t0, t1, t2, t3)):
        at = slice(b * band, (b + 1) * band)
        away = slice((b ^ 2) * band, ((b ^ 2) + 1) * band)
        dn = dn_ref[at] + came_ref[away].astype(F32)
        normed, inverse = normed_rows(x1_ref[at])
        dx = ref[band : 2 * band].astype(F32) * kp_ref[at] + norm_back(dn, normed, inverse, g_ref)
        dxb = dx.astype(BF)
        dxb_ref[at] = dxb
        if b < 2:
            dx_ref[at] = dx
            gg = gg + column_sum(dn * normed)
            sg = sg + column_sum(dn)
            pbg = pbg + column_sum(dxb.astype(F32))
    low = [pl.ds(pl.multiple_of((2 * s + c) * third, third), third) for s in range(2)]
    own_w = jnp.concatenate([wp_ref[low[0]], wp_ref[low[1]]], 0)
    dxb = dxb_ref[...]
    dob_ref[...] = nt(dxb, own_w).astype(BF)
    block = lay.width // 4
    zero = jnp.concatenate([dxb[:, :block], dxb[:, 2 * block : 3 * block]], 1)
    one = jnp.concatenate([dxb[:, block : 2 * block], dxb[:, 3 * block :]], 1)
    cols = jnp.where(c == 0, zero, one)
    mine, other = both_heads(half, ob0, ob1, oo0, oo1)
    mine_g, other_g = tn(mine, cols).astype(BF), tn(other, cols).astype(BF)
    zero, one = jnp.where(c == 0, mine_g, other_g), jnp.where(c == 0, other_g, mine_g)
    p_grad = jnp.concatenate([zero[:third], one[:third], zero[third:], one[third:]], 0)
    pg_ref[...] = p_grad
    sums_ref[...] = jnp.concatenate([gg, sg, pbg], 0)
    attend_back(lay, 0, 1, 0, q_ref, k_ref, v_ref, p_ref, dob_ref, dq_ref, dk_ref, dv_ref)


def back_heads_kernel(lay, q_ref, k_ref, v_ref, p_ref, dob_ref, dq_ref, dk_ref, dv_ref):
    attend_back(lay, 1, HEADS // 4 - 1, 1, q_ref, k_ref, v_ref, p_ref, dob_ref, dq_ref, dk_ref, dv_ref)


def back_rest_kernel(
    lay, plan, n_g, t0, t1, t2, t3, q_ref, k_ref, cos_ref, sin_ref, a_ref, w_ref, table_ref, ubg0, ubg1, dbg_ref, pg_ref, sums_ref,
    dq0, dk0, dv0, dq1, dk1, dv1, *refs,
):
    keep_ref, send_ref = refs[:2]
    grads = refs[2 : 2 + n_g]
    dq_ref, g_tmp, dqkv_ref = refs[2 + n_g :]
    band, side, own, third, half, head = lay.band, lay.side, lay.own, lay.third, lay.length // 2, lay.head
    gg, sg, pbg = sums_ref[0:1], sums_ref[1:2], sums_ref[2:3]
    block = lay.width // 4
    sizes = [ref.shape[1] // 2 for ref in (ubg0, ubg1)]
    ubg = [ref[:, y_side * size : (y_side + 1) * size] for y_side in range(2) for ref, size in zip((ubg0, ubg1), sizes)]
    ubg = jnp.concatenate(ubg, 1)
    cos, sin = cos_ref[...], sin_ref[...]
    dq, dk, dv = (jnp.concatenate([a[...], b[...]], 1) for a, b in ((dq0, dq1), (dk0, dk1), (dv0, dv1)))
    dqkv_ref[:, :own] = (dq * cos + halves_of(lay, dq * sin)).astype(BF)
    dqkv_ref[:, own : 2 * own] = (dk * cos + halves_of(lay, dk * sin)).astype(BF)
    dqkv_ref[:, 2 * own :] = dv.astype(BF)
    dq_ref[...] = dq * halves_of(lay, q_ref[...].astype(F32)) + dk * halves_of(lay, k_ref[...].astype(F32))
    by_col = jnp.zeros((side, own), F32)
    by_row = jnp.zeros((side, own), F32)
    for b, flip in enumerate((0, 2, 1, 3)):
        first = ((here()[3] ^ flip) * lay.band_rows).astype(F32)
        for r in range(lay.band_rows):
            turn = dq_ref[b * band + r * side : b * band + (r + 1) * side]
            by_col = by_col + turn
            by_row = by_row + turn * (first + r)
    lane = lax.broadcasted_iota(jnp.int32, (2, own), 1)
    sign = jnp.where((lane & (head // 2)) == 0, -1.0, 1.0).astype(F32)
    place = lax.broadcasted_iota(jnp.int32, (side, own), 0).astype(F32)
    both = jnp.concatenate([column_sum(by_col * place), column_sum(by_row)], 0) * sign
    both = jnp.where(sign < 0, both + halves_of(lay, both), 0.0)
    freqs = jnp.concatenate([both[0:1], both[1:2]], 1)
    bqk = column_sum(dqkv_ref[:, : 2 * own].astype(F32))
    bv = column_sum(dqkv_ref[:, 2 * own :].astype(F32))
    grad = nt(dqkv_ref[:, : 3 * third], w_ref[0]) + nt(dqkv_ref[:, 3 * third :], w_ref[1])
    keep_ref[...] = grad[:half]
    send_ref[...] = grad[half:].astype(BF)
    g1, s1 = 0.0, 0.0
    for b, ref in enumerate((t0, t1, t2, t3)):
        part = grad[b * band : (b + 1) * band]
        normed, _ = normed_rows(ref[:band].astype(F32))
        g1 = g1 + column_sum(part * normed)
        s1 = s1 + column_sum(part)
    repack(lay, plan, table_ref, [bqk, bv, pbg, g1, s1, gg, sg, ubg, dbg_ref[...], freqs], grads)
    acts = a_ref[...]
    sides = []
    for y_side in range(2):
        grad = tn(acts, dqkv_ref[:, y_side * 3 * third : (y_side + 1) * 3 * third]).astype(BF)
        sides.append(jnp.concatenate([grad, pg_ref[:, y_side * block : (y_side + 1) * block]], 1))
    y = here()[1]
    for y_rel in range(2):
        g_tmp[...] = jnp.where((y ^ y_rel) == 0, sides[0], sides[1]).reshape(g_tmp.shape)
        store_pieces(lay, lay.first, grads, y_rel, slice(None), g_tmp)


def finish_kernel(lay, t0, t1, keep_ref, came_ref, dx_ref, vec_ref, out_ref, send_ref):
    band = lay.band
    g_ref = vec_ref[:, lay.at["attn_gain"]]
    for b, ref in enumerate((t0, t1)):
        at = slice(b * band, (b + 1) * band)
        dn = keep_ref[at] + came_ref[at].astype(F32)
        normed, inverse = normed_rows(ref[:band].astype(F32))
        result = (dx_ref[at] + norm_back(dn, normed, inverse, g_ref)).astype(BF)
        if b == 0:
            out_ref[...] = result
        else:
            send_ref[...] = result


def tail_second_kernel(lay, counts, *refs):
    up_ref, down_ref = refs[-2:]
    half = lay.half_rows
    for part, count in enumerate(counts):
        at = lay.parts[part]
        step = at.stop - at.start
        keep, *came = refs[sum(counts[:part]) : sum(counts[: part + 1])]
        if not came:
            up_ref[:, at], down_ref[:, at] = keep[:, :step].astype(F32), keep[:, step:].astype(F32)
        for rows, ref in zip((slice(0, half), slice(half, None)), came):
            up_ref[rows, at] = keep[rows, :step].astype(F32) + ref[:, :step].astype(F32)
            down_ref[rows, at] = keep[rows, step:].astype(F32) + ref[:, step:].astype(F32)


def tail_send_kernel(lay, sum_ref, out_ref):
    third, rows = lay.third, lay.rows
    out_ref[:, :third] = jnp.where(here()[2] == 0, sum_ref[:rows, 2 * third : 3 * third], sum_ref[:rows, :third])
    out_ref[:, third:] = jnp.zeros((rows, out_ref.shape[1] - third), BF)
    theirs = sum_ref[rows:, :PACKED].astype(F32)[1:2]
    tall = min(rows, EXTRA)
    theirs = jnp.concatenate([theirs, jnp.zeros((tall - 1, PACKED), F32)], 0)
    out_ref[:tall, out_ref.shape[1] - PACKED :] = theirs.astype(BF)


def tail_kernel(lay, plan, sum_ref, came_ref, qkv_ref, proj_ref, *outs):
    third, rows = lay.third, lay.rows
    d0, d1, d2 = (sum_ref[:rows, k * third : (k + 1) * third] for k in range(3))
    c = here()[2]
    qkv_ref[:, :third] = jnp.where(c == 0, d0, d1).astype(F32)
    qkv_ref[:, third : 2 * third] = came_ref[:, :third].astype(F32)
    qkv_ref[:, 2 * third :] = jnp.where(c == 0, d1, d2).astype(F32)
    proj_ref[...] = sum_ref[:rows, 3 * third :].astype(F32)
    total = sum_ref[rows:, :PACKED].astype(F32)[0:1] + came_ref[: min(rows, EXTRA), came_ref.shape[1] - PACKED :].astype(F32)[0:1]
    for ref, (_, _, offset, count) in zip(outs, plan):
        ref[...] = total[:, offset : offset + count]


def call(kernel, name, inputs, outs, scratch=(), limit=16, hbm=False):
    return pl.pallas_call(
        kernel,
        out_shape=[jax.ShapeDtypeStruct(shape, dtype) for shape, dtype in outs],
        in_specs=[HBM if hbm else VMEM] * len(inputs),
        out_specs=[VMEM] * len(outs),
        scratch_shapes=[s if not isinstance(s, tuple) else pltpu.VMEM(*s) for s in scratch],
        compiler_params=pltpu.CompilerParams(vmem_limit_bytes=limit * MIB),
        cost_estimate=pl.CostEstimate(flops=1000, bytes_accessed=1024, transcendentals=0),
        name=name,
    )(*inputs)


def after(value, *others):
    return lax.optimization_barrier((value, *others))[0]


class Slice:
    def __init__(self, lay):
        self.lay = lay
        self.img = lax.axis_index("img")
        self.row = lax.axis_index("row")
        self.y = self.row // 2
        self.c = self.row % 2
        self.orders = lay.first

    def swap(self, array, step):
        if step == "c":
            return lax.ppermute(array, "row", [(r, r ^ 1) for r in range(4)])
        if step == "y":
            return lax.ppermute(array, "row", [(r, r ^ 2) for r in range(4)])
        mask = sum(1 << bit for bit in self.lay.high) if step == "high" else 1 << step
        return lax.ppermute(array, "img", [(i, i ^ mask) for i in range(self.lay.img_count)])

    def gather(self, piece, order):
        held = piece[None]
        for step in order:
            held = jnp.concatenate([held, self.swap(held, step)], 0)
        return held

    def scatter(self, held, order):
        for step in reversed(order):
            half = held.shape[0] // 2
            came = self.swap(held[half:], step)
            held = (held[:half].astype(F32) + came.astype(F32)).astype(held.dtype)
        return held[0]

    def places(self, order):
        place = jnp.zeros((2, self.lay.img_count), jnp.int32)
        img = jnp.arange(self.lay.img_count, dtype=jnp.int32)[None, :] ^ self.img
        side = jnp.arange(2, dtype=jnp.int32)[:, None] ^ self.y
        for k, step in enumerate(order):
            bit = side if step == "y" else (img >> step) & 1
            place = place + (bit << k)
        return place

    def sources(self, order):
        place = self.places(order).reshape(-1)
        return jnp.zeros_like(place).at[place].set(jnp.arange(place.size, dtype=jnp.int32))

    def gather_whole(self, piece):
        lay = self.lay
        base = self.gather(piece, lay.high)
        whole = []
        for part, order in enumerate(self.orders):
            held = base[:, part * lay.half_rows : (part + 1) * lay.half_rows]
            held = self.gather(held, order[-2:]).reshape((-1,) + held.shape[1:])
            whole.append(jnp.take(held, self.places(order), axis=0))
        return jnp.concatenate(whole, 2).reshape((2,) + lay.tiles + piece.shape[1:])

    def high(self, *pieces):
        steps = self.lay.high + ["high"]
        pieces = list(pieces) * (3 if len(pieces) == 1 else 1)
        came = [None] * 3
        for k in (0, 2, 1):
            came[k] = self.swap(pieces[k], steps[k])
        return came

    def merge(self, pieces, name):
        lay = self.lay
        rows, columns = pieces[0].shape[-2:]
        count = len(pieces) * (pieces[0].shape[0] if pieces[0].ndim == 3 else 1)
        shapes = [((count, n, columns), BF) for n in (lay.half_rows, rows - lay.half_rows)]
        return call(functools.partial(merge_kernel, lay), name, pieces, shapes)

    def pairs(self, orders, place, top, bottom):
        return [self.swap(top, orders[0][place]), self.swap(bottom, orders[1][place])]

    def grad_shapes(self, columns, extra=0):
        lay = self.lay
        if lay.aligned:
            return [((lay.img_count, lay.half_rows + more, columns), BF) for more in (0, 0, extra, extra)]
        return [((2,) + lay.tiles + (columns,), BF)] + [((2 * lay.img_count, 2, columns), BF)] * (extra > 0)

    def scatter_rows(self, parts):
        lay = self.lay
        extra = []
        if not lay.aligned:
            if len(parts) > 1:
                extra = [jnp.pad(self.scatter(parts[1], self.orders[1]), ((0, EXTRA - 2), (0, 0)))]
            pieces = parts[0].reshape(2, lay.img_count, lay.rows, parts[0].shape[3])
            parts = []
            for part, order in enumerate(self.orders):
                mine = pieces[:, :, part * lay.half_rows : (part + 1) * lay.half_rows]
                mine = jnp.take(mine.reshape((-1,) + mine.shape[2:]), self.sources(order), axis=0)
                parts += [mine[: lay.img_count], mine[lay.img_count :]]
        sums = []
        for part, order in enumerate(self.orders):
            keep, send = parts[2 * part : 2 * part + 2]
            held = (keep.astype(F32) + self.swap(send, order[-1]).astype(F32)).astype(BF)
            half = lay.img_count // 2
            sums.append((held[:half].astype(F32) + self.swap(held[half:], order[-2]).astype(F32)).astype(BF))
        total = self.scatter(jnp.concatenate(sums, 1), lay.high)
        return jnp.concatenate([total] + extra, 0) if extra else total

    def fold(self, grads, came, name):
        shapes = [((g.shape[0] // 2,) + g.shape[1:], BF) for g in grads]
        return call(fold_kernel, name + "_fold", [grads[0], came[0], grads[2], came[1]], shapes)

    def rejoin(self, groups, name, n=2):
        count, rows, _ = groups[0][0].shape
        shape = (count // n, rows + groups[0][2].shape[1], sum(group[0].shape[2] for group in groups))
        arrays = [array for group in groups for array in group]
        return list(call(functools.partial(rejoin_kernel, n), name + "_rejoin", arrays, [(shape, BF)] * n))

    def halve(self, keep, came, name):
        shape = (keep.shape[0] // 2,) + keep.shape[1:]
        return call(halve_kernel, name + "_halve", [keep, came], [(shape, BF)] * 2)

    def split(self, keep, came, name):
        _, rows, columns = keep.shape
        half = self.lay.half_rows
        shapes = [((n, columns), BF) for n in (rows, half, rows - half)]
        out, top, bottom = call(split_kernel, name + "_split", [keep, came], shapes)
        return [out] + self.pairs(self.lay.second, 0, top, bottom)

    def end(self, shares, name):
        return call(end_kernel, name + "_end", shares, [(shares[0].shape[1:], BF)])[0]


NAMES = ("qkv_bias", "proj_bias", "attn_gain", "attn_shift", "mlp_gain", "mlp_shift", "up_bias", "down_bias", "freqs")


def plan_vectors(lay):
    width, third, pairs = lay.width, lay.third, lay.head // 2
    devices = lay.img_count * 4
    heads = np.arange(HEADS).reshape(2, 2, HEADS // 4)

    def by_core(count, shape):
        return [np.take(np.arange(count).reshape(shape), core, len(shape) - 2).reshape(-1) for core in range(2)]

    plain = [np.arange(width)] * 2
    up = by_core(4 * width, (2, 2, width))
    freqs = []
    for core in range(2):
        pick = np.arange(width).reshape(2, HEADS, pairs)[:, heads[:, core].reshape(-1)]
        freqs.append(np.stack([pick, pick], 2).reshape(-1))
    qkv, qk, v = (by_core(n * width, (n, 2, 2, third)) for n in (3, 2, 1))

    def lay_out(members):
        plan, tables, start, offset = [], [[], [], [], []], 0, 0
        for pick, count in members:
            count //= devices
            plan.append((start, pick[0].size, offset, count))
            for core in range(2):
                tables[2 * core].append(pick[core] // count)
                tables[2 * core + 1].append(pick[core] % count)
            start += pick[0].size
            offset += count
        return plan, jnp.asarray(np.stack([np.concatenate(t) for t in tables]).astype(np.int32))

    rest = [(plain, width)] * 5 + [(up, 4 * width), (plain, width), (freqs, width)]
    given = lay_out([(qkv, 3 * width)] + rest)
    lay.at = {name: slice(p[0], p[0] + p[1]) for name, p in zip(NAMES, given[0])}
    return given, lay_out([(qk, 2 * width), (v, width)] + rest)


def make_body(img_count):
    def body(
        tokens, keep_mask, cotangent, qkv_weight, qkv_bias, proj_weight, proj_bias, attn_gain, attn_shift,
        mlp_gain, mlp_shift, up_weight, up_bias, down_weight, down_bias, rope_freqs,
    ):
        lay = Layout(img_count, tokens, qkv_weight.shape[0])
        me = Slice(lay)
        y = me.y
        images, band, width, length = lay.images, lay.band, lay.width, lay.length
        heads = HEADS // 2
        own, third = lay.own, lay.third
        half = length // 2
        block = proj_weight.shape[1]
        hidden = up_weight.shape[1]
        vectors = (qkv_bias, proj_bias, attn_gain, attn_shift, mlp_gain, mlp_shift, up_bias, down_bias, rope_freqs)
        (plan, table), (grad_plan, grad_table) = plan_vectors(lay)

        def pick(flag, zero, one):
            return jnp.where(flag == 0, zero, one)

        def kernel(function, name, inputs, outs, scratch=(), **options):
            return call(functools.partial(function, lay), name, inputs, outs, scratch, **options)

        pack_rows = 2 * band + 16
        sizes = [part.stop - part.start for part in lay.parts]
        mine, other, third_send, first_piece, *second_pieces = kernel(
            pack_kernel, "pack",
            [tokens.reshape(images, band, width), cotangent.reshape(images, band, width), keep_mask.transpose(1, 0, 2), qkv_weight, proj_weight,
             up_weight, down_weight.T, *[v.reshape(1, -1) for v in vectors]],
            [((pack_rows, width), BF), ((pack_rows + lay.rows - lay.half_rows, width), BF), ((lay.rows, 256 + PACKED), BF),
             ((lay.rows + EXTRA, 2 * third), BF),
             ((lay.rows, 2 * sizes[0] + block), BF), ((lay.half_rows, 2 * sizes[1]), BF)],
            [((lay.band_rows, images, lay.side), jnp.int32), (qkv_weight.shape, F32), (proj_weight.shape, F32), (up_weight.shape, F32),
             (down_weight.T.shape, F32), *[((1, v.shape[0]), F32) for v in vectors], pltpu.SemaphoreType.DMA((18,))],
            limit=60, hbm=True,
        )
        third_came = me.swap(third_send, "c")
        (first_piece,) = kernel(fit_kernel, "fit", [third_came, first_piece], [((lay.rows, 3 * third + SPARE), BF)])
        mine_came = me.swap(mine, "c")
        near = me.swap(after(other, mine_came), 'y')
        bands = [mine, near, mine_came]
        if lay.aligned:
            part0, top1 = second_pieces
            near1 = me.swap(top1, lay.second[0][0])
            came = me.high(first_piece)
            bands.append(me.swap(after(near, *came), 'c'))
            part0 = part0
            top, bottom = me.merge([first_piece] + came, 'merge_first')
            came = me.pairs(lay.first, -2, top, bottom)
            high0 = [me.swap(part0, step) for step in lay.high]
            top = after(top, bands[3], near1, high0[0], high0[1])
            shapes = [((2 * held.shape[0],) + held.shape[1:], BF) for held in (top, bottom)]
            top, bottom = call(join_kernel, "join_first", [top, came[0], bottom, came[1]], shapes)
            came = me.pairs(lay.first, -1, top, bottom)
            first = [top, came[0], bottom, came[1]]
            high0.append(me.swap(after(high0[0], top), lay.high[1]))
            shape = (2, lay.rows, top1.shape[1])
            start1 = after(top1, high0[0])
            (both1,) = kernel(start_kernel, "start1", [start1, near1, other, near], [(shape, BF)])
            vec_parts = [after(first[0], first[3], high0[2], both1), first[1]]
            top0, bottom0 = me.merge([part0] + high0, "merge0")
            vec_parts[0] = after(vec_parts[0], top0, bottom0)
        else:
            bands.append(me.swap(near, "c"))
            first = [me.gather_whole(first_piece)]
            vec_parts = [me.gather(first_piece[: 2 * PACKED // SPARE, 3 * third :], me.orders[0])]
            second = [[me.gather_whole(p)] for p in (second_pieces[0], jnp.concatenate([second_pieces[1], other[pack_rows:]], 0))]
        (vec,) = call(
            functools.partial(unpack_kernel, lay, plan, len(vec_parts)), "unpack", [table, *vec_parts],
            [((1, table.shape[1]), F32)], limit=24,
        )

        n_w = len(first)
        n_g = len(me.grad_shapes(1))
        a1, q, k, v, w_qkv, cos, sin, kp, mask_bias = call(
            functools.partial(project_kernel, lay, n_w), "qkv", [*bands, *first, vec],
            [((length, width), BF), ((length, own), BF), ((length, own), BF), ((length, own), BF), ((2, width, 3 * third), BF),
             ((length, own), F32), ((length, own), F32), ((length, 1), F32), ((1, length), F32)],
            [((2,) + lay.tiles + (3 * third,), BF)], limit=16,
        )
        def attend(first, count, q):
            return call(
                functools.partial(attend_kernel, lay, first, count), "attend%d" % first, [q, k, v, mask_bias],
                [((length, count * 2 * lay.head), BF), ((2 * count, length, length), BF)], limit=8,
            )

        ob0, p0 = attend(0, 1, q)
        oo0 = me.swap(ob0, "c")
        if lay.aligned:
            near0 = me.pairs(lay.first, -2, top0, bottom0)
            high1 = [both1] + [me.swap(both1, step) for step in lay.high]
            shapes = [((2 * held.shape[0],) + held.shape[1:], BF) for held in (top0, bottom0)]
            top0 = after(top0, ob0, high1[1])
            top0, bottom0 = call(join_kernel, "join0", [top0, near0[0], bottom0, near0[1]], shapes)
            last0 = me.pairs(lay.first, -1, top0, bottom0)
            second = [[top0, last0[0], bottom0, last0[1]]]
            ob1, p1 = attend(1, HEADS // 4 - 1, after(q, top0, bottom0))
            high1.append(me.swap(after(high1[1], ob1), lay.high[1]))
            gate = [ob1]
            top1, bottom1 = me.merge(high1, "merge1")
            gate += [top1, bottom1]
        else:
            ob1, p1 = attend(1, HEADS // 4 - 1, q)
            gate = [ob1]
        oo1 = me.swap(ob1, 'c')
        (p_cols,) = call(
            functools.partial(proj_kernel, lay, len(second[0])), "proj", [after(second[0][0], *gate)] + second[0][1:], [((width, 2 * block), BF)],
            [((2,) + lay.tiles + (block,), BF)],
        )
        p_other = me.swap(p_cols, "c")
        x1, a2, a2_t, dm, dm_t, d_down_bias, w_proj = call(
            functools.partial(middle_kernel, lay), "middle", [*bands, ob0, ob1, oo0, oo1, p_cols, p_other, vec, kp],
            [((length, width), F32), ((length, width), BF), ((width, length), BF), ((length, width), BF), ((width, length), BF),
             ((1, width), F32), ((width, width), BF)], limit=10,
        )
        if lay.aligned:
            last1 = me.pairs(lay.second, -1, top1, bottom1)
            second.append([top1, last1[0], bottom1, last1[1]])
        sums, second_grads, d_up_bias = [], [], []
        for part, at in enumerate(lay.parts):
            step = at.stop - at.start
            shapes = (me.grad_shapes(2 * step) if part else me.grad_shapes(step) * 2) + [((1, 2 * step), F32)]
            scratch = [(lay.tiles + (2 * step,), BF), (lay.tiles + (step,), BF)]
            if part == len(PARTS) - 1:
                shapes += [((half, width), F32), ((half, width), BF), ((length, width), F32), ((length, width), BF)]
                scratch = [((length, width), F32)] + scratch
            else:
                shapes += [((length, width), F32)] * 2
            outs = call(
                functools.partial(mlp_kernel, lay, part, len(second[part]), n_g), "mlp%d" % part,
                [x1, a2, a2_t, dm, dm_t, vec, *second[part], *sums], shapes, scratch, limit=18,
            )
            count = n_g if part else 2 * n_g
            second_grads.append(outs[:count])
            d_up_bias.append(outs[count])
            sums = outs[count + 1 :]
        part, m_send, dn, dn_send = sums
        if lay.aligned:
            g = second_grads[0]
            came0 = me.pairs(lay.second, -1, g[1], g[3])
            dn_send = after(dn_send, *came0)
            came0 += me.pairs(lay.second, -1, g[5], g[7])
            dn_send = dn_send
        dn_came = me.swap(dn_send, "c")
        m_came = me.swap(m_send, "c")
        out_half = (kp[:half] * (part + m_came.astype(F32))).astype(BF)
        def to_images(keep, send):
            came = me.swap(send, "y")
            return pick(y, jnp.stack([keep, came]), jnp.stack([came, keep])).reshape(tokens.shape)

        if not lay.aligned:
            layer_out = to_images(out_half[:band], out_half[band:])
        pair = 2 * lay.head
        dx_half, dob, p_grad, norm_sums, dq0, dk0, dv0 = call(
            functools.partial(back_kernel, lay), "back",
            [*bands, kp, x1, dn, dn_came, vec, w_proj, ob0, ob1, oo0, oo1, q, k, v, p0],
            [((half, width), F32), ((length, own), BF), ((width, 2 * block), BF), ((3, width), F32), ((length, pair), F32),
             ((length, pair), F32), ((length, pair), F32)],
            [((length, width), BF)], limit=20,
        )
        if lay.aligned:
            g = second_grads[1]
            came1 = [after(send, dn_came) for send in (g[1], g[3])]
            came1 = me.pairs(lay.first, -1, *came1)
        else:
            g = [jnp.concatenate(second_grads[0], 3)], second_grads[1]
            d_second = [[me.scatter_rows(held)] for held in g]
        if lay.aligned:
            g = second_grads[0]
            came0[0] = after(came0[0], dob)
            keep0, send0 = me.rejoin([[g[k], came0[k // 2], g[k + 2], came0[k // 2 + 1]] for k in (0, 4)], "part0")
            dob = after(dob, keep0, send0)
            came0 = me.swap(send0, lay.high[1])
        dq1, dk1, dv1 = call(
            functools.partial(back_heads_kernel, lay), "back_heads", [q, k, v, p1, dob], [((length, own - pair), F32)] * 3
        )
        if lay.aligned:
            came1[0] = after(came1[0], dq1)
            folded1 = me.fold(second_grads[1], came1, "part1")
            came1 = me.pairs(lay.first, -2, folded1[1], folded1[3])
            dq1 = after(dq1, *folded1)
        if lay.aligned:
            keep0, send0 = me.halve(keep0, after(came0, dq1), "part0")
            dq1 = after(dq1, send0)
            came0, z0_0 = me.swap(send0, lay.high[0]), send0
        grad_shapes = me.grad_shapes(3 * third + block, EXTRA)
        dn1_keep, dn1_send, *first_grads = call(
            functools.partial(back_rest_kernel, lay, grad_plan, len(grad_shapes)), "back_rest",
            [*bands, q, k, cos, sin, a1, w_qkv, grad_table, *d_up_bias, d_down_bias, p_grad, norm_sums, dq0, dk0, dv0, dq1, dk1, dv1],
            [((half, width), F32), ((half, width), BF), *grad_shapes],
            [((length, own), F32), (lay.tiles + (3 * third + block,), BF), ((length, 3 * own), BF)], limit=24,
        )
        if lay.aligned:
            g = first_grads
            sends = [after(send, *came1, folded1[0]) for send in (g[1], g[3])]
            came = me.pairs(lay.first, -1, *sends)
            keep1, send1 = me.rejoin([[folded1[0], came1[0], folded1[2], came1[1]]], "part1")
            came1 = me.swap(send1, lay.high[1])
            folded = me.fold(g, came, "first")
            sends = [after(send, came1) for send in (folded[1], folded[3])]
            came = me.pairs(lay.first, -2, *sends)
            layer_out = to_images(out_half[:band], after(out_half[band:], *came))
            p2_came = came
            d_second = [me.split(keep0, came0, "part0")]
            keep1, send1 = me.halve(keep1, came1, "part1")
            came1 = me.swap(send1, lay.high[0])
            shares = me.rejoin([[folded[0], came[0], folded[2], came[1]]], "first", 4)
            d_second.append([me.end([keep1, came1], "part1")])
            d_up, d_down = call(
                functools.partial(tail_second_kernel, lay, [len(d) for d in d_second]), "tail_second",
                [held for d in d_second for held in d], [((lay.rows, n), F32) for n in (hidden, hidden)]
            )
            shares[1] = after(shares[1], d_second[0][0], d_second[1][0])
            d_first = me.end([after(shares[0], *d_second[0], d_up)] + me.high(*shares[1:]), 'first')
        else:
            d_up, d_down = call(
                functools.partial(tail_second_kernel, lay, [len(d) for d in d_second]), "tail_second",
                [held for d in d_second for held in d], [((lay.rows, n), F32) for n in (hidden, hidden)]
            )
            d_first = me.scatter_rows(first_grads)
        dn1_came = me.swap(dn1_send, "c")
        tg_keep, tg_send = call(
            functools.partial(finish_kernel, lay), "finish", [bands[0], bands[1], dn1_keep, dn1_came, dx_half, vec],
            [((band, width), BF), ((band, width), BF)],
        )

        if lay.aligned:
            tg_send = after(tg_send, *p2_came)
        tokens_grad = to_images(tg_keep, tg_send)

        d_down = d_down.T
        (tail_send,) = kernel(tail_send_kernel, "tail_send", [d_first], [((lay.rows, 256 + PACKED), BF)])
        tail_came = me.swap(tail_send, "c")
        d_qkv, d_proj, *r = call(
            functools.partial(tail_kernel, lay, grad_plan), "tail", [d_first, tail_came],
            [((lay.rows, 3 * third), F32), ((lay.rows, block), F32), *[((1, count), F32) for _, _, _, count in grad_plan]],
        )
        r = [v.reshape(-1) for v in r]
        return (
            layer_out, tokens_grad, d_qkv, r[0], r[1], d_proj, r[2], r[3], r[4], r[5], r[6], d_up, r[7], d_down, r[8], r[9],
        )

    return body


def solution(mesh):
    split = P(("img", "row"))
    both = P("img", "row")
    field = P("img", "row", None, None)
    return jax.shard_map(
        make_body(mesh.shape["img"]),
        mesh=mesh,
        in_specs=(
            field, P("img", "row", None), field, both, split, both, split, split, split, split, split, both, split,
            P("row", "img"), split, split,
        ),
        out_specs=(
            field, field, both, split, split, both, split, split, split, split, split, both, split, P("row", "img"),
            split, split,
        ),
        check_vma=False,
    )
```

```python
import functools

import jax
import jax.numpy as jnp
import numpy as np
from jax import lax
from jax.experimental import pallas as pl
from jax.experimental.pallas import tpu as pltpu
from jax.sharding import PartitionSpec as P

HEADS = 12
PARTS = (3, 3)
NORM_EPSILON = 1e-06
MASKED_SCORE = -1e30
BF = jnp.bfloat16
F32 = jnp.float32
MIB = 2**20
VMEM = pl.BlockSpec(memory_space=pltpu.VMEM)
HBM = pl.BlockSpec(memory_space=pltpu.MemorySpace.HBM)
PACKED = 384
SPARE = 64
EXTRA = 16


def dot(left, right, dims):
    return lax.dot_general(left, right, (dims, ((), ())), preferred_element_type=F32)


def nn(left, right):
    return dot(left, right, ((1,), (0,)))


def nt(left, right):
    return dot(left, right, ((1,), (1,)))


def tn(left, right):
    return dot(left, right, ((0,), (0,)))


def normed_rows(values):
    center = values - jnp.mean(values, -1, keepdims=True)
    inverse = lax.rsqrt(jnp.mean(center * center, -1, keepdims=True) + NORM_EPSILON)
    return center * inverse, inverse


def norm_back(grad, normed, inverse, gain):
    scaled = grad * gain
    centred = scaled - jnp.mean(scaled, -1, keepdims=True)
    return inverse * (centred - normed * jnp.mean(scaled * normed, -1, keepdims=True))


def column_sum(value):
    return jnp.sum(value, 0, keepdims=True)


def here():
    row = lax.axis_index("row")
    return lax.axis_index("img"), row >> 1, row & 1, row


class Layout:
    def __init__(self, img_count, tokens, rows):
        self.img_count = img_count
        self.bits = img_count.bit_length() - 1
        self.rows = rows
        self.half_rows = rows // 2
        self.aligned = rows % 32 == 0 and img_count == 8
        self.images, self.band_rows, self.side, self.width = tokens.shape
        self.band = self.band_rows * self.side
        self.length = 4 * self.band
        self.head = self.width // HEADS
        self.own = self.width // 2
        self.third = self.own // 2
        self.high = list(range(self.bits - 1, 0, -1))
        self.first = (self.high + [0, "y"], self.high + ["y", 0])
        self.second = ([0] + self.high + ["y"], ["y"] + self.high + [0])
        sizes = [self.width * sixths // 6 for sixths in PARTS]
        self.parts = [slice(sum(sizes[:n]), sum(sizes[: n + 1])) for n in range(len(sizes))]
        self.gathered = (self.first, self.second)
        self.reduced = (self.second, self.first)
        self.tiles = (img_count, rows) if self.aligned else (1, self.width)

    def slots(self, orders, img_rel, y_rel):
        found = []
        for order in orders:
            bits = [y_rel if step == "y" else (img_rel >> step) & 1 for step in order]
            found.append((sum(bit << k for k, bit in enumerate(bits[:-1])), bits[-1]))
        return found


def load_pieces(lay, orders, refs, y_rel, target, columns=slice(None)):
    if not lay.aligned:
        target[...] = refs[0][here()[1] ^ y_rel, :, :, columns]
        return
    half = lay.half_rows
    count = len(refs) // 2
    for img_rel in range(lay.img_count):
        for part, (slot, last) in enumerate(lay.slots(orders, img_rel, y_rel)):
            which, slot = divmod((slot + last * lay.img_count) * count, 2 * lay.img_count)
            ref, slot = refs[part * count + which], slot // count
            target[img_rel ^ here()[0], part * half : (part + 1) * half] = ref[slot, :half, columns]


def store_pieces(lay, orders, refs, y_rel, columns, source):
    if not lay.aligned:
        refs[0][here()[1] ^ y_rel, :, :, columns] = source[...]
        return
    half = lay.half_rows
    for img_rel in range(lay.img_count):
        for part, (slot, last) in enumerate(lay.slots(orders, img_rel, y_rel)):
            refs[2 * part + last][slot, :half, columns] = source[img_rel ^ here()[0], part * half : (part + 1) * half]


def halves_of(lay, value):
    pairs = lay.head // 2
    lane = lax.broadcasted_iota(jnp.int32, value.shape, 1)
    width = value.shape[1]
    first = (lane & pairs) == 0
    return jnp.where(first, pltpu.roll(value, width - pairs, 1), pltpu.roll(value, pairs, 1))


def pack_kernel(lay, *refs):
    tok, cot, mask, qkv, proj, up, down, *vectors = refs[:16]
    mine_ref, other_ref, third_ref, first_ref = refs[16:20]
    second, refs = [*refs[20:22], other_ref.at[2 * lay.band + 16 :]], refs[22:]
    mask_in, qkv_in, proj_in, up_in, down_in, *vectors_in = refs[:14]
    sems = refs[14]
    y = here()[1]
    band, third, width, rows = lay.band, lay.third, lay.width, lay.rows
    pairs = [(qkv, qkv_in), (proj, proj_in), *zip(vectors, vectors_in), (up, up_in), (down, down_in), (mask, mask_in)]
    for ref, which in ((other_ref, 1 - y), (mine_ref, y)):
        pairs += [(tok.at[which], ref.at[:band]), (cot.at[which], ref.at[band : 2 * band])]
    copies = [pltpu.make_async_copy(source, target, sems.at[n]) for n, (source, target) in enumerate(pairs)]
    for copy in copies:
        copy.start()
    for copy in copies[:11]:
        copy.wait()
    packed = jnp.concatenate([v[...] for v in vectors_in], 1)
    packed = jnp.concatenate([packed, jnp.zeros((1, PACKED - packed.shape[1]), F32)], 1).astype(BF)
    third_ref[:, :third] = qkv_in[:, third : 2 * third].astype(BF)
    third_ref[:, third:] = jnp.zeros((rows, third_ref.shape[1] - third), BF)
    blank = jnp.zeros((EXTRA - 1, PACKED), F32)
    packed = jnp.concatenate([packed.astype(F32), blank], 0).astype(BF)
    tall = min(rows, EXTRA)
    third_ref[:tall, third_ref.shape[1] - PACKED :] = packed[:tall]
    first_ref[:rows, :third] = qkv_in[:, :third].astype(BF)
    first_ref[:rows, third : 2 * third] = qkv_in[:, 2 * third :].astype(BF)
    first_ref[rows:, :PACKED] = packed
    for copy in copies[11:]:
        copy.wait()
    for ref, part, first_row in zip(second, (0, 1, 1), (0, 0, lay.half_rows)):
        at = lay.parts[part]
        step = at.stop - at.start
        side = slice(first_row, first_row + ref.shape[0])
        ref[:, :step] = up_in[side, at].astype(BF)
        ref[:, step : 2 * step] = down_in[side, at].astype(BF)
        if part == 0:
            ref[:, 2 * step :] = proj_in[side].astype(BF)
    for ref, which in ((mine_ref, y), (other_ref, 1 - y)):
        keep = [jnp.where(which == 0, mask_in[r, 0:1], mask_in[r, 1:2]).astype(F32) for r in range(lay.band_rows)]
        flat = jnp.concatenate(keep, 1)
        flat = jnp.concatenate([flat, jnp.zeros((1, width - band), F32)], 1)
        ref[2 * band : 2 * band + 16] = jnp.concatenate([flat, jnp.zeros((15, width), F32)], 0).astype(BF)


def fit_kernel(lay, came_ref, first_ref, out_ref):
    third, rows = lay.third, lay.rows
    c = here()[2]
    t0, t2, came = first_ref[:rows, :third], first_ref[:rows, third : 2 * third], came_ref[:, :third]
    out_ref[:, : 3 * third] = jnp.where(c == 0, jnp.concatenate([t0, t2, came], 1), jnp.concatenate([came, t0, t2], 1))
    tall = min(rows, EXTRA)
    lines = [first_ref[rows:, :PACKED].astype(F32)[0:1], came_ref[:tall, came_ref.shape[1] - PACKED :].astype(F32)[0:1]]
    lines = [line[:, k : k + SPARE] for line in lines for k in range(0, PACKED, SPARE)]
    if rows > len(lines):
        lines.append(jnp.zeros((rows - len(lines), SPARE), F32))
    out_ref[:, 3 * third :] = jnp.concatenate(lines, 0).astype(BF)


def merge_kernel(lay, *refs):
    pieces, (top_ref, bottom_ref) = refs[:-2], refs[-2:]
    half = lay.half_rows
    for k, ref in enumerate(pieces):
        if len(ref.shape) == 2:
            top_ref[k] = ref[:half]
            bottom_ref[k] = ref[half:]
        else:
            count = ref.shape[0]
            top_ref[k * count : (k + 1) * count] = ref[:, :half]
            bottom_ref[k * count : (k + 1) * count] = ref[:, half:]


def start_kernel(lay, top, top_came, bottom, bottom_came, out_ref):
    half = lay.half_rows
    out_ref[0, :half], out_ref[1, :half] = top[...], top_came[...]
    first = 2 * lay.band + 16
    out_ref[0, half:], out_ref[1, half:] = bottom[first:], bottom_came[first:]


def join_kernel(*refs):
    for part in range(2):
        own, came = refs[2 * part : 2 * part + 2]
        refs[4 + part][: own.shape[0]] = own[...]
        refs[4 + part][own.shape[0] :] = came[...]


def fold_kernel(*refs):
    for part in range(2):
        keep, came = refs[2 * part : 2 * part + 2]
        count = keep.shape[0] // 2
        for half in range(2):
            at = slice(half * count, (half + 1) * count)
            refs[4 + 2 * part + half][...] = (keep[at].astype(F32) + came[at].astype(F32)).astype(BF)


def rejoin_kernel(n, *refs):
    outs = refs[len(refs) - n :]
    top = refs[0].shape[1]
    count = refs[0].shape[0] // n
    column = 0
    for k in range(0, len(refs) - n, 4):
        columns = slice(column, column + refs[k].shape[2])
        column = columns.stop
        for part in range(2):
            keep, came = refs[k + 2 * part : k + 2 * part + 2]
            rows = slice(0, top) if part == 0 else slice(top, None)
            for share, out in enumerate(outs):
                at = slice(share * count, (share + 1) * count)
                out[:, rows, columns] = (keep[at].astype(F32) + came[at].astype(F32)).astype(BF)


def end_kernel(*refs):
    refs[-1][...] = sum(ref[0].astype(F32) for ref in refs[:-1]).astype(BF)


def halve_kernel(keep_ref, came_ref, *outs):
    count = keep_ref.shape[0] // len(outs)
    for half, ref in enumerate(outs):
        at = slice(half * count, (half + 1) * count)
        total = (keep_ref[at].astype(F32) + came_ref[at].astype(F32)).astype(BF)
        ref[...] = total.reshape(ref.shape)


def split_kernel(keep_ref, came_ref, out_ref, top_ref, bottom_ref):
    half = top_ref.shape[0]
    out_ref[...] = (keep_ref[0].astype(F32) + came_ref[0].astype(F32)).astype(BF)
    top_ref[...] = (keep_ref[1, :half].astype(F32) + came_ref[1, :half].astype(F32)).astype(BF)
    bottom_ref[...] = (keep_ref[1, half:].astype(F32) + came_ref[1, half:].astype(F32)).astype(BF)


def owner_mask(lay, order, c_rel, table_row):
    place = lax.broadcasted_iota(jnp.int32, (2 * lay.img_count, 1), 0)
    img_rel = jnp.zeros_like(place)
    row = here()[3] ^ c_rel
    for k, step in enumerate(order):
        bit = (place >> k) & 1
        if step == "y":
            row = row ^ (bit * 2)
        else:
            img_rel = img_rel | (bit << step)
    return ((img_rel ^ here()[0]) * 4 + row) == table_row


def owners(table_ref, at, c):
    owner = jnp.where(c == 0, table_ref[0:1, at], table_ref[2:3, at])
    entry = jnp.where(c == 0, table_ref[1:2, at], table_ref[3:4, at])
    return owner, entry


def unpack_kernel(lay, plan, n_v, table_ref, *refs):
    v_refs, out_ref = refs[:n_v], refs[n_v]
    lines = PACKED // SPARE
    if lay.aligned:
        blocks = [ref[k, :16, ref.shape[2] - SPARE :].astype(F32) for ref in v_refs for k in range(ref.shape[0])]
        blocks = [jnp.concatenate([block[n : n + 1] for block in blocks], 0) for n in range(2 * lines)]
    else:
        blocks = [v_refs[0][:, n].astype(F32) for n in range(2 * lines)]
    gathered = [jnp.concatenate(blocks[c_rel * lines : (c_rel + 1) * lines], 1).astype(BF) for c_rel in range(2)]
    for start, size, offset, count in plan:
        at = slice(start, start + size)
        owner, entry = owners(table_ref, at, here()[2])
        spread = (lax.broadcasted_iota(jnp.int32, (count, size), 0) == entry).astype(F32).astype(BF)
        total = 0.0
        for c_rel in range(2):
            rows = nn(gathered[c_rel][:, offset : offset + count], spread)
            total = total + column_sum(jnp.where(owner_mask(lay, lay.first[0], c_rel, owner), rows, 0.0))
        out_ref[:, at] = total


def repack(lay, plan, table_ref, grads, refs):
    sides = []
    for c_rel in range(2):
        parts = []
        for grad, (start, size, offset, count) in zip(grads, plan):
            owner, entry = owners(table_ref, slice(start, start + size), here()[2])
            spread = (lax.broadcasted_iota(jnp.int32, (count, size), 0) == entry).astype(F32).astype(BF)
            rows = jnp.where(owner_mask(lay, lay.first[1], c_rel, owner), grad, 0.0).astype(BF)
            parts.append(nt(rows, spread))
        used = sum(p.shape[1] for p in parts)
        sides.append(jnp.concatenate(parts + [jnp.zeros((2 * lay.img_count, PACKED - used), F32)], 1))
    if not lay.aligned:
        refs[1][...] = jnp.zeros(refs[1].shape, BF)
        for c_rel in range(2):
            refs[1][:, c_rel, :PACKED] = sides[c_rel].astype(BF)
        return
    half, count = lay.half_rows, lay.img_count
    for j in range(2 * count):
        ref = refs[2 + j // count]
        block = jnp.concatenate([side[j : j + 1] for side in sides] + [jnp.zeros((EXTRA - 2, PACKED), F32)], 0).astype(BF)
        ref[j % count, half:] = jnp.zeros((EXTRA, ref.shape[2]), BF)
        ref[j % count, half:, :PACKED] = block


def project_kernel(lay, n_w, t0, t1, t2, t3, *refs):
    w_refs = refs[:n_w]
    vec_ref, a_ref, q_ref, k_ref, v_ref, w_out, cos_ref, sin_ref, kp_ref, bias_ref, w_all = refs[n_w:]
    band, side, own, third = lay.band, lay.side, lay.own, lay.third
    g_ref, s_ref, b_ref = (vec_ref[:, lay.at[n]] for n in ("attn_gain", "attn_shift", "qkv_bias"))
    f_ref = vec_ref[:, lay.at["freqs"]]
    keeps = []
    for b, ref in enumerate((t0, t1, t2, t3)):
        at = slice(b * band, (b + 1) * band)
        normed, _ = normed_rows(ref[:band].astype(F32))
        a_ref[at] = (normed * g_ref + s_ref).astype(BF)
        keep = ref[2 * band : 2 * band + 16, :band].astype(F32)
        kp_ref[at] = jnp.transpose(keep)[:, 0:1]
        keeps.append(keep[0:1])
    bias_ref[...] = jnp.where(jnp.concatenate(keeps, 1) > 0, 0.0, MASKED_SCORE)
    lane = lax.broadcasted_iota(jnp.int32, (side, own), 1)
    sign = jnp.where((lane & (lay.head // 2)) == 0, -1.0, 1.0).astype(F32)
    col = lax.broadcasted_iota(jnp.int32, (side, own), 0).astype(F32) * f_ref[:, :own]
    col_cos, col_sin = jnp.cos(col), jnp.sin(col)
    row_index = here()[3]
    for b, flip in enumerate((0, 2, 1, 3)):
        first = ((row_index ^ flip) * lay.band_rows).astype(F32)
        rows = (lax.broadcasted_iota(jnp.int32, (8, own), 0).astype(F32) + first) * f_ref[:, own:]
        row_cos, row_sin = jnp.cos(rows), jnp.sin(rows)
        for r in range(lay.band_rows):
            at = slice(b * band + r * side, b * band + (r + 1) * side)
            rc, rs = row_cos[r : r + 1], row_sin[r : r + 1]
            cos_ref[at] = col_cos * rc - col_sin * rs
            sin_ref[at] = (col_sin * rc + col_cos * rs) * sign
    for y_rel in range(2):
        y_side = here()[1] ^ y_rel
        load_pieces(lay, lay.first, w_refs, y_rel, w_all.at[y_side], slice(0, 3 * third))
    acts = a_ref[...]
    w0, w1 = w_all[0].reshape(lay.width, -1), w_all[1].reshape(lay.width, -1)
    w_out[0], w_out[1] = w0, w1
    left = nn(acts, w0) + b_ref[:, : 3 * third]
    right = nn(acts, w1) + b_ref[:, 3 * third :]
    query, key = left[:, :own], jnp.concatenate([left[:, own:], right[:, :third]], 1)
    cos, sin = cos_ref[...], sin_ref[...]
    q_ref[...] = (query * cos + halves_of(lay, query) * sin).astype(BF)
    k_ref[...] = (key * cos + halves_of(lay, key) * sin).astype(BF)
    v_ref[...] = right[:, third:].astype(BF)


def proj_kernel(lay, n_w, *refs):
    out_ref, w_all = refs[n_w:]
    block = lay.width // 4
    columns = slice(refs[0].shape[-1] - block, None)
    for y_rel in range(2):
        y_side = here()[1] ^ y_rel
        load_pieces(lay, lay.gathered[0], refs[:n_w], y_rel, w_all.at[y_side], columns)
    for y_side in range(2):
        out_ref[:, y_side * block : (y_side + 1) * block] = w_all[y_side].reshape(lay.width, block)


def attend_kernel(lay, first, count, q_ref, k_ref, v_ref, bias_ref, o_ref, p_ref):
    head = lay.head
    pair = 2 * head
    scale = head**-0.5

    def step(n, carry):
        at = pl.ds(pl.multiple_of(n * pair, pair), pair)
        out = pl.ds(pl.multiple_of((n - first) * pair, pair), pair)
        keys, values = k_ref[:, at], v_ref[:, at]
        query = q_ref[:, at] * jnp.asarray(scale, BF)
        lane = lax.broadcasted_iota(jnp.int32, query.shape, 1)
        outs = []
        for h in range(2):
            mine = (lane < head) if h == 0 else (lane >= head)
            score = nt(jnp.where(mine, query, jnp.zeros_like(query)), keys) + bias_ref[...]
            power = jnp.exp(score - jnp.max(score, -1, keepdims=True))
            weights = (power * (1.0 / jnp.sum(power, -1, keepdims=True))).astype(BF)
            p_ref[2 * (n - first) + h] = weights
            outs.append(nn(weights, values))
        o_ref[:, out] = jnp.where(lane < head, outs[0], outs[1]).astype(BF)
        return carry

    lax.fori_loop(first, first + count, step, 0)


def both_heads(half, ob0, ob1, oo0, oo1):
    other = jnp.concatenate([oo0[...], oo1[...]], 1)
    return jnp.concatenate([ob0[...], ob1[...]], 1), jnp.concatenate([other[half:], other[:half]], 0)


def middle_kernel(lay, t0, t1, t2, t3, ob0, ob1, oo0, oo1, p_ref, po_ref, vec_ref, kp_ref, x1_ref, a2_ref, at_ref, dm_ref, dt_ref, dbg_ref, wp_ref):
    band, third, half = lay.band, lay.third, lay.length // 2
    c = here()[2]
    block = lay.width // 4
    pb_ref, g_ref, s_ref = (vec_ref[:, lay.at[n]] for n in ("proj_bias", "mlp_gain", "mlp_shift"))
    for y_side in range(2):
        mine, other = (ref[:, y_side * block : (y_side + 1) * block] for ref in (p_ref, po_ref))
        wp_ref[:, 2 * y_side * block : 2 * (y_side + 1) * block] = jnp.where(
            c == 0, jnp.concatenate([mine, other], 1), jnp.concatenate([other, mine], 1)
        )
    low = [pl.ds(pl.multiple_of((2 * s + c) * third, third), third) for s in range(2)]
    high = [pl.ds(pl.multiple_of((2 * s + 1 - c) * third, third), third) for s in range(2)]
    own_w = jnp.concatenate([wp_ref[low[0]], wp_ref[low[1]]], 0)
    other_w = jnp.concatenate([wp_ref[high[0]], wp_ref[high[1]]], 0)
    mine, other = both_heads(half, ob0, ob1, oo0, oo1)
    x1_ref[...] = nn(mine, own_w) + nn(other, other_w) + pb_ref
    for b, ref in enumerate((t0, t1, t2, t3)):
        at = slice(b * band, (b + 1) * band)
        x1 = x1_ref[at] + ref[:band].astype(F32)
        x1_ref[at] = x1
        normed, _ = normed_rows(x1)
        a2_ref[at] = (normed * g_ref + s_ref).astype(BF)
        dm_ref[at] = (ref[band : 2 * band].astype(F32) * kp_ref[at]).astype(BF)
    at_ref[...] = a2_ref[...].T
    dt_ref[...] = dm_ref[...].T
    dbg_ref[...] = column_sum(dm_ref[:half].astype(F32))


def mlp_kernel(lay, part, n_w, n_g, x1_ref, a2_ref, at_ref, dm_ref, dt_ref, vec_ref, *refs):
    w_refs, refs = refs[:n_w], refs[n_w:]
    last = part == len(PARTS) - 1
    if part:
        (m_in, dn_in), refs = refs[:2], refs[2:]
    count = n_g if last else 2 * n_g
    grads, refs = refs[:count], refs[count:]
    ubg_ref, refs = refs[0], refs[1:]
    if last:
        part_ref, msend_ref, dn_ref, dnsend_ref, m_ref, w_all, g_tmp = refs
    else:
        m_ref, dn_ref, w_all, g_tmp = refs
    width, half = lay.width, lay.length // 2
    chunk = lay.parts[part].stop - lay.parts[part].start
    up_bias = lay.at["up_bias"].start + lay.parts[part].start
    for y_rel in range(2):
        load_pieces(lay, lay.gathered[part], w_refs, y_rel, w_all, slice(0, 2 * chunk))
        y_side = here()[1] ^ y_rel
        up = w_all[:, :, :chunk].reshape(width, chunk)
        down = w_all[:, :, chunk:].reshape(width, chunk)
        pre = nn(a2_ref[...], up) + vec_ref[:, pl.ds(pl.multiple_of(y_side * width + up_bias, 128), chunk)]
        cdf = 0.5 * (1.0 + lax.erf(pre * 0.7071067811865476))
        slope = cdf + pre * (jnp.exp(-0.5 * pre * pre) * 0.3989422804014327)
        act = (pre * cdf).astype(BF)
        du = (nn(dm_ref[...], down) * slope).astype(BF)
        ubg_ref[:, pl.ds(pl.multiple_of(y_side * chunk, 128), chunk)] = column_sum(du.astype(F32))
        g_tmp[...] = nn(at_ref[...], du).astype(BF).reshape(g_tmp.shape)
        own, at = (grads[:n_g], slice(None)) if not last else (grads, slice(0, chunk))
        store_pieces(lay, lay.reduced[part], own, y_rel, at, g_tmp)
        g_tmp[...] = nn(dt_ref[...], act).astype(BF).reshape(g_tmp.shape)
        own, at = (grads[n_g:], slice(None)) if not last else (grads, slice(chunk, None))
        store_pieces(lay, lay.reduced[part], own, y_rel, at, g_tmp)
        m, dn = nt(act, down), nt(du, up)
        if y_rel == 0:
            m_ref[...] = m + m_in[...] if part else m
            dn_ref[...] = dn + dn_in[...] if part else dn
        else:
            m_ref[...] += m
            dn_ref[...] += dn
    if last:
        part_ref[...] = x1_ref[:half] + m_ref[:half] + vec_ref[:, lay.at["down_bias"]]
        msend_ref[...] = m_ref[half:].astype(BF)
        dnsend_ref[...] = dn_ref[...].astype(BF)


def attend_back(lay, first, count, base, q_ref, k_ref, v_ref, p_ref, dob_ref, dq_ref, dk_ref, dv_ref):
    head = lay.head
    pair = 2 * head
    scale = head**-0.5

    def step(n, carry):
        at = pl.ds(pl.multiple_of(n * pair, pair), pair)
        out = pl.ds(pl.multiple_of((n - base) * pair, pair), pair)
        keys, values = k_ref[:, at], v_ref[:, at]
        query, dob = q_ref[:, at], dob_ref[:, at]
        query_t, dob_t = query.T, dob.T
        lane = lax.broadcasted_iota(jnp.int32, query.shape, 1)
        row = lax.broadcasted_iota(jnp.int32, query_t.shape, 0)
        dqs, dks, dvs = [], [], []
        for h in range(2):
            mine = (lane < head) if h == 0 else (lane >= head)
            weights = p_ref[2 * (n - base) + h]
            soft = weights.astype(F32)
            dp = nt(jnp.where(mine, dob, jnp.zeros_like(dob)), values)
            ds = (soft * (dp - jnp.sum(soft * dp, -1, keepdims=True))).astype(BF)
            dqs.append(nn(ds, keys))
            dks.append(nn(query_t, ds))
            dvs.append(nn(dob_t, weights))
        dq_ref[:, out] = jnp.where(lane < head, dqs[0], dqs[1]) * scale
        dk_ref[:, out] = (jnp.where(row < head, dks[0], dks[1]) * scale).T
        dv_ref[:, out] = jnp.where(row < head, dvs[0], dvs[1]).T
        return carry

    lax.fori_loop(first, first + count, step, 0)


def back_kernel(
    lay, t0, t1, t2, t3, kp_ref, x1_ref, dn_ref, came_ref, vec_ref, wp_ref, ob0, ob1, oo0, oo1, q_ref, k_ref, v_ref,
    p_ref, dx_ref, dob_ref, pg_ref, sums_ref, dq_ref, dk_ref, dv_ref, dxb_ref,
):
    g_ref = vec_ref[:, lay.at["mlp_gain"]]
    band, third, half = lay.band, lay.third, lay.length // 2
    c = here()[2]
    gg, sg, pbg = 0.0, 0.0, 0.0
    for b, ref in enumerate((t0, t1, t2, t3)):
        at = slice(b * band, (b + 1) * band)
        away = slice((b ^ 2) * band, ((b ^ 2) + 1) * band)
        dn = dn_ref[at] + came_ref[away].astype(F32)
        normed, inverse = normed_rows(x1_ref[at])
        dx = ref[band : 2 * band].astype(F32) * kp_ref[at] + norm_back(dn, normed, inverse, g_ref)
        dxb = dx.astype(BF)
        dxb_ref[at] = dxb
        if b < 2:
            dx_ref[at] = dx
            gg = gg + column_sum(dn * normed)
            sg = sg + column_sum(dn)
            pbg = pbg + column_sum(dxb.astype(F32))
    low = [pl.ds(pl.multiple_of((2 * s + c) * third, third), third) for s in range(2)]
    own_w = jnp.concatenate([wp_ref[low[0]], wp_ref[low[1]]], 0)
    dxb = dxb_ref[...]
    dob_ref[...] = nt(dxb, own_w).astype(BF)
    block = lay.width // 4
    zero = jnp.concatenate([dxb[:, :block], dxb[:, 2 * block : 3 * block]], 1)
    one = jnp.concatenate([dxb[:, block : 2 * block], dxb[:, 3 * block :]], 1)
    cols = jnp.where(c == 0, zero, one)
    mine, other = both_heads(half, ob0, ob1, oo0, oo1)
    mine_g, other_g = tn(mine, cols).astype(BF), tn(other, cols).astype(BF)
    zero, one = jnp.where(c == 0, mine_g, other_g), jnp.where(c == 0, other_g, mine_g)
    p_grad = jnp.concatenate([zero[:third], one[:third], zero[third:], one[third:]], 0)
    pg_ref[...] = p_grad
    sums_ref[...] = jnp.concatenate([gg, sg, pbg], 0)
    attend_back(lay, 0, 1, 0, q_ref, k_ref, v_ref, p_ref, dob_ref, dq_ref, dk_ref, dv_ref)


def back_heads_kernel(lay, q_ref, k_ref, v_ref, p_ref, dob_ref, dq_ref, dk_ref, dv_ref):
    attend_back(lay, 1, HEADS // 4 - 1, 1, q_ref, k_ref, v_ref, p_ref, dob_ref, dq_ref, dk_ref, dv_ref)


def back_rest_kernel(
    lay, plan, n_g, t0, t1, t2, t3, q_ref, k_ref, cos_ref, sin_ref, a_ref, w_ref, table_ref, ubg0, ubg1, dbg_ref, pg_ref, sums_ref,
    dq0, dk0, dv0, dq1, dk1, dv1, *refs,
):
    keep_ref, send_ref = refs[:2]
    grads = refs[2 : 2 + n_g]
    dq_ref, g_tmp, dqkv_ref = refs[2 + n_g :]
    band, side, own, third, half, head = lay.band, lay.side, lay.own, lay.third, lay.length // 2, lay.head
    gg, sg, pbg = sums_ref[0:1], sums_ref[1:2], sums_ref[2:3]
    block = lay.width // 4
    sizes = [ref.shape[1] // 2 for ref in (ubg0, ubg1)]
    ubg = [ref[:, y_side * size : (y_side + 1) * size] for y_side in range(2) for ref, size in zip((ubg0, ubg1), sizes)]
    ubg = jnp.concatenate(ubg, 1)
    cos, sin = cos_ref[...], sin_ref[...]
    dq, dk, dv = (jnp.concatenate([a[...], b[...]], 1) for a, b in ((dq0, dq1), (dk0, dk1), (dv0, dv1)))
    dqkv_ref[:, :own] = (dq * cos + halves_of(lay, dq * sin)).astype(BF)
    dqkv_ref[:, own : 2 * own] = (dk * cos + halves_of(lay, dk * sin)).astype(BF)
    dqkv_ref[:, 2 * own :] = dv.astype(BF)
    dq_ref[...] = dq * halves_of(lay, q_ref[...].astype(F32)) + dk * halves_of(lay, k_ref[...].astype(F32))
    by_col = jnp.zeros((side, own), F32)
    by_row = jnp.zeros((side, own), F32)
    for b, flip in enumerate((0, 2, 1, 3)):
        first = ((here()[3] ^ flip) * lay.band_rows).astype(F32)
        for r in range(lay.band_rows):
            turn = dq_ref[b * band + r * side : b * band + (r + 1) * side]
            by_col = by_col + turn
            by_row = by_row + turn * (first + r)
    lane = lax.broadcasted_iota(jnp.int32, (2, own), 1)
    sign = jnp.where((lane & (head // 2)) == 0, -1.0, 1.0).astype(F32)
    place = lax.broadcasted_iota(jnp.int32, (side, own), 0).astype(F32)
    both = jnp.concatenate([column_sum(by_col * place), column_sum(by_row)], 0) * sign
    both = jnp.where(sign < 0, both + halves_of(lay, both), 0.0)
    freqs = jnp.concatenate([both[0:1], both[1:2]], 1)
    bqk = column_sum(dqkv_ref[:, : 2 * own].astype(F32))
    bv = column_sum(dqkv_ref[:, 2 * own :].astype(F32))
    grad = nt(dqkv_ref[:, : 3 * third], w_ref[0]) + nt(dqkv_ref[:, 3 * third :], w_ref[1])
    keep_ref[...] = grad[:half]
    send_ref[...] = grad[half:].astype(BF)
    g1, s1 = 0.0, 0.0
    for b, ref in enumerate((t0, t1, t2, t3)):
        part = grad[b * band : (b + 1) * band]
        normed, _ = normed_rows(ref[:band].astype(F32))
        g1 = g1 + column_sum(part * normed)
        s1 = s1 + column_sum(part)
    repack(lay, plan, table_ref, [bqk, bv, pbg, g1, s1, gg, sg, ubg, dbg_ref[...], freqs], grads)
    acts = a_ref[...]
    sides = []
    for y_side in range(2):
        grad = tn(acts, dqkv_ref[:, y_side * 3 * third : (y_side + 1) * 3 * third]).astype(BF)
        sides.append(jnp.concatenate([grad, pg_ref[:, y_side * block : (y_side + 1) * block]], 1))
    y = here()[1]
    for y_rel in range(2):
        g_tmp[...] = jnp.where((y ^ y_rel) == 0, sides[0], sides[1]).reshape(g_tmp.shape)
        store_pieces(lay, lay.first, grads, y_rel, slice(None), g_tmp)


def finish_kernel(lay, t0, t1, keep_ref, came_ref, dx_ref, vec_ref, kp_ref, part_ref, m_ref, layer_ref, out_ref, send_ref):
    band = lay.band
    g_ref = vec_ref[:, lay.at["attn_gain"]]
    for b, ref in enumerate((t0, t1)):
        at = slice(b * band, (b + 1) * band)
        layer = (kp_ref[at] * (part_ref[at] + m_ref[at].astype(F32))).astype(BF)
        dn = keep_ref[at] + came_ref[at].astype(F32)
        normed, inverse = normed_rows(ref[:band].astype(F32))
        result = (dx_ref[at] + norm_back(dn, normed, inverse, g_ref)).astype(BF)
        if b == 0:
            layer_ref[...], out_ref[...] = layer, result
        else:
            send_ref[:band], send_ref[band:] = layer, result


def tail_second_kernel(lay, counts, *refs):
    up_ref, down_ref = refs[-2:]
    half = lay.half_rows
    for part, count in enumerate(counts):
        at = lay.parts[part]
        step = at.stop - at.start
        keep, *came = refs[sum(counts[:part]) : sum(counts[: part + 1])]
        if not came:
            up_ref[:, at], down_ref[:, at] = keep[:, :step].astype(F32), keep[:, step:].astype(F32)
        for rows, ref in zip((slice(0, half), slice(half, None)), came):
            up_ref[rows, at] = keep[rows, :step].astype(F32) + ref[:, :step].astype(F32)
            down_ref[rows, at] = keep[rows, step:].astype(F32) + ref[:, step:].astype(F32)


def tail_send_kernel(lay, sum_ref, out_ref):
    third, rows = lay.third, lay.rows
    out_ref[:, :third] = jnp.where(here()[2] == 0, sum_ref[:rows, 2 * third : 3 * third], sum_ref[:rows, :third])
    out_ref[:, third:] = jnp.zeros((rows, out_ref.shape[1] - third), BF)
    theirs = sum_ref[rows:, :PACKED].astype(F32)[1:2]
    tall = min(rows, EXTRA)
    theirs = jnp.concatenate([theirs, jnp.zeros((tall - 1, PACKED), F32)], 0)
    out_ref[:tall, out_ref.shape[1] - PACKED :] = theirs.astype(BF)


def tail_kernel(lay, plan, sum_ref, came_ref, qkv_ref, proj_ref, *outs):
    third, rows = lay.third, lay.rows
    d0, d1, d2 = (sum_ref[:rows, k * third : (k + 1) * third] for k in range(3))
    c = here()[2]
    qkv_ref[:, :third] = jnp.where(c == 0, d0, d1).astype(F32)
    qkv_ref[:, third : 2 * third] = came_ref[:, :third].astype(F32)
    qkv_ref[:, 2 * third :] = jnp.where(c == 0, d1, d2).astype(F32)
    proj_ref[...] = sum_ref[:rows, 3 * third :].astype(F32)
    total = sum_ref[rows:, :PACKED].astype(F32)[0:1] + came_ref[: min(rows, EXTRA), came_ref.shape[1] - PACKED :].astype(F32)[0:1]
    for ref, (_, _, offset, count) in zip(outs, plan):
        ref[...] = total[:, offset : offset + count]


def call(kernel, name, inputs, outs, scratch=(), limit=16, hbm=False):
    return pl.pallas_call(
        kernel,
        out_shape=[jax.ShapeDtypeStruct(shape, dtype) for shape, dtype in outs],
        in_specs=[HBM if hbm else VMEM] * len(inputs),
        out_specs=[VMEM] * len(outs),
        scratch_shapes=[s if not isinstance(s, tuple) else pltpu.VMEM(*s) for s in scratch],
        compiler_params=pltpu.CompilerParams(vmem_limit_bytes=limit * MIB),
        cost_estimate=pl.CostEstimate(flops=1000, bytes_accessed=1024, transcendentals=0),
        name=name,
    )(*inputs)


def after(value, *others):
    return lax.optimization_barrier((value, *others))[0]


class Slice:
    def __init__(self, lay):
        self.lay = lay
        self.img = lax.axis_index("img")
        self.row = lax.axis_index("row")
        self.y = self.row // 2
        self.c = self.row % 2
        self.orders = lay.first

    def swap(self, array, step):
        if step == "c":
            return lax.ppermute(array, "row", [(r, r ^ 1) for r in range(4)])
        if step == "y":
            return lax.ppermute(array, "row", [(r, r ^ 2) for r in range(4)])
        mask = sum(1 << bit for bit in self.lay.high) if step == "high" else 1 << step
        return lax.ppermute(array, "img", [(i, i ^ mask) for i in range(self.lay.img_count)])

    def gather(self, piece, order):
        held = piece[None]
        for step in order:
            held = jnp.concatenate([held, self.swap(held, step)], 0)
        return held

    def scatter(self, held, order):
        for step in reversed(order):
            half = held.shape[0] // 2
            came = self.swap(held[half:], step)
            held = (held[:half].astype(F32) + came.astype(F32)).astype(held.dtype)
        return held[0]

    def places(self, order):
        place = jnp.zeros((2, self.lay.img_count), jnp.int32)
        img = jnp.arange(self.lay.img_count, dtype=jnp.int32)[None, :] ^ self.img
        side = jnp.arange(2, dtype=jnp.int32)[:, None] ^ self.y
        for k, step in enumerate(order):
            bit = side if step == "y" else (img >> step) & 1
            place = place + (bit << k)
        return place

    def sources(self, order):
        place = self.places(order).reshape(-1)
        return jnp.zeros_like(place).at[place].set(jnp.arange(place.size, dtype=jnp.int32))

    def gather_whole(self, piece):
        lay = self.lay
        base = self.gather(piece, lay.high)
        whole = []
        for part, order in enumerate(self.orders):
            held = base[:, part * lay.half_rows : (part + 1) * lay.half_rows]
            held = self.gather(held, order[-2:]).reshape((-1,) + held.shape[1:])
            whole.append(jnp.take(held, self.places(order), axis=0))
        return jnp.concatenate(whole, 2).reshape((2,) + lay.tiles + piece.shape[1:])

    def high(self, *pieces):
        steps = self.lay.high + ["high"]
        pieces = list(pieces) * (3 if len(pieces) == 1 else 1)
        came = [None] * 3
        for k in (0, 2, 1):
            came[k] = self.swap(pieces[k], steps[k])
        return came

    def merge(self, pieces, name):
        lay = self.lay
        rows, columns = pieces[0].shape[-2:]
        count = len(pieces) * (pieces[0].shape[0] if pieces[0].ndim == 3 else 1)
        shapes = [((count, n, columns), BF) for n in (lay.half_rows, rows - lay.half_rows)]
        return call(functools.partial(merge_kernel, lay), name, pieces, shapes)

    def pairs(self, orders, place, top, bottom):
        return [self.swap(top, orders[0][place]), self.swap(bottom, orders[1][place])]

    def grad_shapes(self, columns, extra=0):
        lay = self.lay
        if lay.aligned:
            return [((lay.img_count, lay.half_rows + more, columns), BF) for more in (0, 0, extra, extra)]
        return [((2,) + lay.tiles + (columns,), BF)] + [((2 * lay.img_count, 2, columns), BF)] * (extra > 0)

    def scatter_rows(self, parts):
        lay = self.lay
        extra = []
        if not lay.aligned:
            if len(parts) > 1:
                extra = [jnp.pad(self.scatter(parts[1], self.orders[1]), ((0, EXTRA - 2), (0, 0)))]
            pieces = parts[0].reshape(2, lay.img_count, lay.rows, parts[0].shape[3])
            parts = []
            for part, order in enumerate(self.orders):
                mine = pieces[:, :, part * lay.half_rows : (part + 1) * lay.half_rows]
                mine = jnp.take(mine.reshape((-1,) + mine.shape[2:]), self.sources(order), axis=0)
                parts += [mine[: lay.img_count], mine[lay.img_count :]]
        sums = []
        for part, order in enumerate(self.orders):
            keep, send = parts[2 * part : 2 * part + 2]
            held = (keep.astype(F32) + self.swap(send, order[-1]).astype(F32)).astype(BF)
            half = lay.img_count // 2
            sums.append((held[:half].astype(F32) + self.swap(held[half:], order[-2]).astype(F32)).astype(BF))
        total = self.scatter(jnp.concatenate(sums, 1), lay.high)
        return jnp.concatenate([total] + extra, 0) if extra else total

    def fold(self, grads, came, name):
        shapes = [((g.shape[0] // 2,) + g.shape[1:], BF) for g in grads]
        return call(fold_kernel, name + "_fold", [grads[0], came[0], grads[2], came[1]], shapes)

    def rejoin(self, groups, name, n=2):
        count, rows, _ = groups[0][0].shape
        shape = (count // n, rows + groups[0][2].shape[1], sum(group[0].shape[2] for group in groups))
        arrays = [array for group in groups for array in group]
        return list(call(functools.partial(rejoin_kernel, n), name + "_rejoin", arrays, [(shape, BF)] * n))

    def halve(self, keep, came, name):
        shape = (keep.shape[0] // 2,) + keep.shape[1:]
        return call(halve_kernel, name + "_halve", [keep, came], [(shape, BF)] * 2)

    def split(self, keep, came, name):
        _, rows, columns = keep.shape
        half = self.lay.half_rows
        shapes = [((n, columns), BF) for n in (rows, half, rows - half)]
        out, top, bottom = call(split_kernel, name + "_split", [keep, came], shapes)
        return [out] + self.pairs(self.lay.second, 0, top, bottom)

    def end(self, shares, name):
        return call(end_kernel, name + "_end", shares, [(shares[0].shape[1:], BF)])[0]


NAMES = ("qkv_bias", "proj_bias", "attn_gain", "attn_shift", "mlp_gain", "mlp_shift", "up_bias", "down_bias", "freqs")


def plan_vectors(lay):
    width, third, pairs = lay.width, lay.third, lay.head // 2
    devices = lay.img_count * 4
    heads = np.arange(HEADS).reshape(2, 2, HEADS // 4)

    def by_core(count, shape):
        return [np.take(np.arange(count).reshape(shape), core, len(shape) - 2).reshape(-1) for core in range(2)]

    plain = [np.arange(width)] * 2
    up = by_core(4 * width, (2, 2, width))
    freqs = []
    for core in range(2):
        pick = np.arange(width).reshape(2, HEADS, pairs)[:, heads[:, core].reshape(-1)]
        freqs.append(np.stack([pick, pick], 2).reshape(-1))
    qkv, qk, v = (by_core(n * width, (n, 2, 2, third)) for n in (3, 2, 1))

    def lay_out(members):
        plan, tables, start, offset = [], [[], [], [], []], 0, 0
        for pick, count in members:
            count //= devices
            plan.append((start, pick[0].size, offset, count))
            for core in range(2):
                tables[2 * core].append(pick[core] // count)
                tables[2 * core + 1].append(pick[core] % count)
            start += pick[0].size
            offset += count
        return plan, jnp.asarray(np.stack([np.concatenate(t) for t in tables]).astype(np.int32))

    rest = [(plain, width)] * 5 + [(up, 4 * width), (plain, width), (freqs, width)]
    given = lay_out([(qkv, 3 * width)] + rest)
    lay.at = {name: slice(p[0], p[0] + p[1]) for name, p in zip(NAMES, given[0])}
    return given, lay_out([(qk, 2 * width), (v, width)] + rest)


def make_body(img_count):
    def body(
        tokens, keep_mask, cotangent, qkv_weight, qkv_bias, proj_weight, proj_bias, attn_gain, attn_shift,
        mlp_gain, mlp_shift, up_weight, up_bias, down_weight, down_bias, rope_freqs,
    ):
        lay = Layout(img_count, tokens, qkv_weight.shape[0])
        me = Slice(lay)
        y = me.y
        images, band, width, length = lay.images, lay.band, lay.width, lay.length
        heads = HEADS // 2
        own, third = lay.own, lay.third
        half = length // 2
        block = proj_weight.shape[1]
        hidden = up_weight.shape[1]
        vectors = (qkv_bias, proj_bias, attn_gain, attn_shift, mlp_gain, mlp_shift, up_bias, down_bias, rope_freqs)
        (plan, table), (grad_plan, grad_table) = plan_vectors(lay)

        def pick(flag, zero, one):
            return jnp.where(flag == 0, zero, one)

        def kernel(function, name, inputs, outs, scratch=(), **options):
            return call(functools.partial(function, lay), name, inputs, outs, scratch, **options)

        pack_rows = 2 * band + 16
        sizes = [part.stop - part.start for part in lay.parts]
        mine, other, third_send, first_piece, *second_pieces = kernel(
            pack_kernel, "pack",
            [tokens.reshape(images, band, width), cotangent.reshape(images, band, width), keep_mask.transpose(1, 0, 2), qkv_weight, proj_weight,
             up_weight, down_weight.T, *[v.reshape(1, -1) for v in vectors]],
            [((pack_rows, width), BF), ((pack_rows + lay.rows - lay.half_rows, width), BF), ((lay.rows, 256 + PACKED), BF),
             ((lay.rows + EXTRA, 2 * third), BF),
             ((lay.rows, 2 * sizes[0] + block), BF), ((lay.half_rows, 2 * sizes[1]), BF)],
            [((lay.band_rows, images, lay.side), jnp.int32), (qkv_weight.shape, F32), (proj_weight.shape, F32), (up_weight.shape, F32),
             (down_weight.T.shape, F32), *[((1, v.shape[0]), F32) for v in vectors], pltpu.SemaphoreType.DMA((18,))],
            limit=60, hbm=True,
        )
        third_came = me.swap(third_send, "c")
        (first_piece,) = kernel(fit_kernel, "fit", [third_came, first_piece], [((lay.rows, 3 * third + SPARE), BF)])
        mine_came = me.swap(mine, "c")
        near = me.swap(after(other, mine_came), 'y')
        bands = [mine, near, mine_came]
        if lay.aligned:
            part0, top1 = second_pieces
            near1 = me.swap(top1, lay.second[0][0])
            came = me.high(first_piece)
            bands.append(me.swap(after(near, *came), 'c'))
            part0 = part0
            top, bottom = me.merge([first_piece] + came, 'merge_first')
            came = me.pairs(lay.first, -2, top, bottom)
            high0 = [me.swap(part0, step) for step in lay.high]
            top = after(top, bands[3], near1, high0[0], high0[1])
            shapes = [((2 * held.shape[0],) + held.shape[1:], BF) for held in (top, bottom)]
            top, bottom = call(join_kernel, "join_first", [top, came[0], bottom, came[1]], shapes)
            came = me.pairs(lay.first, -1, top, bottom)
            first = [top, came[0], bottom, came[1]]
            high0.append(me.swap(after(high0[0], top), lay.high[1]))
            shape = (2, lay.rows, top1.shape[1])
            start1 = after(top1, high0[0])
            (both1,) = kernel(start_kernel, "start1", [start1, near1, other, near], [(shape, BF)])
            vec_parts = [after(first[0], first[3], high0[2], both1), first[1]]
            top0, bottom0 = me.merge([part0] + high0, "merge0")
            vec_parts[0] = after(vec_parts[0], top0, bottom0)
        else:
            bands.append(me.swap(near, "c"))
            first = [me.gather_whole(first_piece)]
            vec_parts = [me.gather(first_piece[: 2 * PACKED // SPARE, 3 * third :], me.orders[0])]
            second = [[me.gather_whole(p)] for p in (second_pieces[0], jnp.concatenate([second_pieces[1], other[pack_rows:]], 0))]
        (vec,) = call(
            functools.partial(unpack_kernel, lay, plan, len(vec_parts)), "unpack", [table, *vec_parts],
            [((1, table.shape[1]), F32)], limit=24,
        )

        n_w = len(first)
        n_g = len(me.grad_shapes(1))
        a1, q, k, v, w_qkv, cos, sin, kp, mask_bias = call(
            functools.partial(project_kernel, lay, n_w), "qkv", [*bands, *first, vec],
            [((length, width), BF), ((length, own), BF), ((length, own), BF), ((length, own), BF), ((2, width, 3 * third), BF),
             ((length, own), F32), ((length, own), F32), ((length, 1), F32), ((1, length), F32)],
            [((2,) + lay.tiles + (3 * third,), BF)], limit=16,
        )
        def attend(first, count, q):
            return call(
                functools.partial(attend_kernel, lay, first, count), "attend%d" % first, [q, k, v, mask_bias],
                [((length, count * 2 * lay.head), BF), ((2 * count, length, length), BF)], limit=8,
            )

        ob0, p0 = attend(0, 1, q)
        oo0 = me.swap(ob0, "c")
        if lay.aligned:
            near0 = me.pairs(lay.first, -2, top0, bottom0)
            high1 = [both1] + [me.swap(both1, step) for step in lay.high]
            shapes = [((2 * held.shape[0],) + held.shape[1:], BF) for held in (top0, bottom0)]
            top0 = after(top0, ob0, high1[1])
            top0, bottom0 = call(join_kernel, "join0", [top0, near0[0], bottom0, near0[1]], shapes)
            last0 = me.pairs(lay.first, -1, top0, bottom0)
            second = [[top0, last0[0], bottom0, last0[1]]]
            ob1, p1 = attend(1, HEADS // 4 - 1, after(q, top0, bottom0))
            high1.append(me.swap(after(high1[1], ob1), lay.high[1]))
            gate = [ob1]
            top1, bottom1 = me.merge(high1, "merge1")
            gate += [top1, bottom1]
        else:
            ob1, p1 = attend(1, HEADS // 4 - 1, q)
            gate = [ob1]
        oo1 = me.swap(ob1, 'c')
        (p_cols,) = call(
            functools.partial(proj_kernel, lay, len(second[0])), "proj", [after(second[0][0], *gate)] + second[0][1:], [((width, 2 * block), BF)],
            [((2,) + lay.tiles + (block,), BF)],
        )
        p_other = me.swap(p_cols, "c")
        x1, a2, a2_t, dm, dm_t, d_down_bias, w_proj = call(
            functools.partial(middle_kernel, lay), "middle", [*bands, ob0, ob1, oo0, oo1, p_cols, p_other, vec, kp],
            [((length, width), F32), ((length, width), BF), ((width, length), BF), ((length, width), BF), ((width, length), BF),
             ((1, width), F32), ((width, width), BF)], limit=10,
        )
        if lay.aligned:
            last1 = me.pairs(lay.second, -1, top1, bottom1)
            second.append([top1, last1[0], bottom1, last1[1]])
        sums, second_grads, d_up_bias = [], [], []
        for part, at in enumerate(lay.parts):
            step = at.stop - at.start
            shapes = (me.grad_shapes(2 * step) if part else me.grad_shapes(step) * 2) + [((1, 2 * step), F32)]
            scratch = [(lay.tiles + (2 * step,), BF), (lay.tiles + (step,), BF)]
            if part == len(PARTS) - 1:
                shapes += [((half, width), F32), ((half, width), BF), ((length, width), F32), ((length, width), BF)]
                scratch = [((length, width), F32)] + scratch
            else:
                shapes += [((length, width), F32)] * 2
            outs = call(
                functools.partial(mlp_kernel, lay, part, len(second[part]), n_g), "mlp%d" % part,
                [x1, a2, a2_t, dm, dm_t, vec, *second[part], *sums], shapes, scratch, limit=18,
            )
            count = n_g if part else 2 * n_g
            second_grads.append(outs[:count])
            d_up_bias.append(outs[count])
            sums = outs[count + 1 :]
        part, m_send, dn, dn_send = sums
        if lay.aligned:
            g = second_grads[0]
            came0 = me.pairs(lay.second, -1, g[1], g[3])
            dn_send = after(dn_send, *came0)
            came0 += me.pairs(lay.second, -1, g[5], g[7])
            dn_send = dn_send
        dn_came = me.swap(dn_send, "c")
        m_came = me.swap(m_send, "c")
        pair = 2 * lay.head
        dx_half, dob, p_grad, norm_sums, dq0, dk0, dv0 = call(
            functools.partial(back_kernel, lay), "back",
            [*bands, kp, x1, dn, dn_came, vec, w_proj, ob0, ob1, oo0, oo1, q, k, v, p0],
            [((half, width), F32), ((length, own), BF), ((width, 2 * block), BF), ((3, width), F32), ((length, pair), F32),
             ((length, pair), F32), ((length, pair), F32)],
            [((length, width), BF)], limit=20,
        )
        if lay.aligned:
            g = second_grads[1]
            came1 = [after(send, dn_came) for send in (g[1], g[3])]
            came1 = me.pairs(lay.first, -1, *came1)
        else:
            g = [jnp.concatenate(second_grads[0], 3)], second_grads[1]
            d_second = [[me.scatter_rows(held)] for held in g]
        if lay.aligned:
            g = second_grads[0]
            came0[0] = after(came0[0], dob)
            keep0, send0 = me.rejoin([[g[k], came0[k // 2], g[k + 2], came0[k // 2 + 1]] for k in (0, 4)], "part0")
            dob = after(dob, keep0, send0)
            came0 = me.swap(send0, lay.high[1])
        dq1, dk1, dv1 = call(
            functools.partial(back_heads_kernel, lay), "back_heads", [q, k, v, p1, dob], [((length, own - pair), F32)] * 3
        )
        if lay.aligned:
            came1[0] = after(came1[0], dq1)
            folded1 = me.fold(second_grads[1], came1, "part1")
            came1 = me.pairs(lay.first, -2, folded1[1], folded1[3])
            dq1 = after(dq1, *folded1)
        if lay.aligned:
            keep0, send0 = me.halve(keep0, after(came0, dq1), "part0")
            dq1 = after(dq1, send0)
            came0, z0_0 = me.swap(send0, lay.high[0]), send0
        grad_shapes = me.grad_shapes(3 * third + block, EXTRA)
        dn1_keep, dn1_send, *first_grads = call(
            functools.partial(back_rest_kernel, lay, grad_plan, len(grad_shapes)), "back_rest",
            [*bands, q, k, cos, sin, a1, w_qkv, grad_table, *d_up_bias, d_down_bias, p_grad, norm_sums, dq0, dk0, dv0, dq1, dk1, dv1],
            [((half, width), F32), ((half, width), BF), *grad_shapes],
            [((length, own), F32), (lay.tiles + (3 * third + block,), BF), ((length, 3 * own), BF)], limit=24,
        )
        if lay.aligned:
            g = first_grads
            sends = [after(send, *came1, folded1[0]) for send in (g[1], g[3])]
            came = me.pairs(lay.first, -1, *sends)
            keep1, send1 = me.rejoin([[folded1[0], came1[0], folded1[2], came1[1]]], "part1")
            came1 = me.swap(send1, lay.high[1])
            folded = me.fold(g, came, "first")
            sends = [after(send, came1) for send in (folded[1], folded[3])]
            came = me.pairs(lay.first, -2, *sends)
            p2_came = came
            d_second = [me.split(keep0, came0, "part0")]
            keep1, send1 = me.halve(keep1, came1, "part1")
            came1 = me.swap(send1, lay.high[0])
            shares = me.rejoin([[folded[0], came[0], folded[2], came[1]]], "first", 4)
            d_second.append([me.end([keep1, came1], "part1")])
            d_up, d_down = call(
                functools.partial(tail_second_kernel, lay, [len(d) for d in d_second]), "tail_second",
                [held for d in d_second for held in d], [((lay.rows, n), F32) for n in (hidden, hidden)]
            )
            shares[1] = after(shares[1], d_second[0][0], d_second[1][0])
            d_first = me.end([after(shares[0], *d_second[0], d_up)] + me.high(*shares[1:]), 'first')
        else:
            d_up, d_down = call(
                functools.partial(tail_second_kernel, lay, [len(d) for d in d_second]), "tail_second",
                [held for d in d_second for held in d], [((lay.rows, n), F32) for n in (hidden, hidden)]
            )
            d_first = me.scatter_rows(first_grads)
        dn1_came = me.swap(dn1_send, "c")
        layer_keep, tg_keep, send = call(
            functools.partial(finish_kernel, lay), "finish",
            [bands[0], bands[1], dn1_keep, dn1_came, dx_half, vec, kp, part, m_came],
            [((band, width), BF), ((band, width), BF), ((2 * band, width), BF)],
        )
        if lay.aligned:
            send = after(send, *p2_came)
        came = me.swap(send, "y")

        def to_images(keep, came):
            return pick(y, jnp.stack([keep, came]), jnp.stack([came, keep])).reshape(tokens.shape)

        layer_out, tokens_grad = to_images(layer_keep, came[:band]), to_images(tg_keep, came[band:])
        d_down = d_down.T
        (tail_send,) = kernel(tail_send_kernel, "tail_send", [d_first], [((lay.rows, 256 + PACKED), BF)])
        tail_came = me.swap(tail_send, "c")
        d_qkv, d_proj, *r = call(
            functools.partial(tail_kernel, lay, grad_plan), "tail", [d_first, tail_came],
            [((lay.rows, 3 * third), F32), ((lay.rows, block), F32), *[((1, count), F32) for _, _, _, count in grad_plan]],
        )
        r = [v.reshape(-1) for v in r]
        return (
            layer_out, tokens_grad, d_qkv, r[0], r[1], d_proj, r[2], r[3], r[4], r[5], r[6], d_up, r[7], d_down, r[8], r[9],
        )

    return body


def solution(mesh):
    split = P(("img", "row"))
    both = P("img", "row")
    field = P("img", "row", None, None)
    return jax.shard_map(
        make_body(mesh.shape["img"]),
        mesh=mesh,
        in_specs=(
            field, P("img", "row", None), field, both, split, both, split, split, split, split, split, both, split,
            P("row", "img"), split, split,
        ),
        out_specs=(
            field, field, both, split, split, both, split, split, split, split, split, both, split, P("row", "img"),
            split, split,
        ),
        check_vma=False,
    )
```
